32 devices in a mesh: seq: 2 (over core), row: 4 (over y, x), col: 4 (over z).
Axes of the slice: x: 2, y: 2, z: 4, core: 2. Of those that a mesh axis runs over, the one named last changes fastest.
Arguments:
- layer_in: bfloat16 [2, 1024, 2048], P(None, ('seq', 'col'), 'row'), may hold values from -6 to 6
- per_layer_in: bfloat16 [2, 1024, 256], P(None, ('seq', 'col')), may hold values from -6 to 6
- doc_lengths: int32 [2, 4], replicated, may hold values from 1 to 512, 1024 in all within a row
- w_query: bfloat16 [2048, 2048], P('row', 'col'), may hold values from -0.125 to 0.125
- w_key: bfloat16 [2048, 512], P('row', 'col'), may hold values from -0.125 to 0.125
- w_value: bfloat16 [2048, 512], P('row', 'col'), may hold values from -0.125 to 0.125
- w_out: bfloat16 [2048, 2048], P('col', 'row'), may hold values from -0.125 to 0.125
- w_gate: bfloat16 [2048, 8192], P('row', 'col'), may hold values from -0.125 to 0.125
- w_up: bfloat16 [2048, 8192], P('row', 'col'), may hold values from -0.125 to 0.125
- w_down: bfloat16 [8192, 2048], P('col', 'row'), may hold values from -0.0625 to 0.0625
- laurel_left: bfloat16 [2048, 64], P('row'), may hold values from -0.125 to 0.125
- laurel_right: bfloat16 [64, 2048], P(None, 'row'), may hold values from -0.75 to 0.75
- per_gate: bfloat16 [2048, 256], P('row'), may hold values from -0.125 to 0.125
- per_proj: bfloat16 [256, 2048], P(None, 'row'), may hold values from -0.375 to 0.375
- norm_gains: float32 [6, 2048], P(None, 'row'), may hold values from 0.5 to 1.5
- head_gains: float32 [2, 256], replicated, may hold values from 0.25 to 0.4
- out_grad: bfloat16 [2, 1024, 2048], P(None, ('seq', 'col'), 'row'), may hold values from -6 to 6
Outputs:
- layer_out: bfloat16 [2, 1024, 2048], P(None, ('seq', 'col'), 'row')
- grad_in: bfloat16 [2, 1024, 2048], P(None, ('seq', 'col'), 'row')
- grad_w_query: float32 [2048, 2048], P('row', 'col')
- grad_w_key: float32 [2048, 512], P('row', 'col')
- grad_w_value: float32 [2048, 512], P('row', 'col')
- grad_w_out: float32 [2048, 2048], P('col', 'row')
- grad_w_gate: float32 [2048, 8192], P('row', 'col')
- grad_w_up: float32 [2048, 8192], P('row', 'col')
- grad_w_down: float32 [8192, 2048], P('col', 'row')
- grad_laurel_left: float32 [2048, 64], P('row')
- grad_laurel_right: float32 [64, 2048], P(None, 'row')
- grad_per_gate: float32 [2048, 256], P('row')
- grad_per_proj: float32 [256, 2048], P(None, 'row')
- grad_norm_gains: float32 [6, 2048], P(None, 'row')
- grad_head_gains: float32 [2, 256], replicated
- clipped_gains: float32 [2, 8, 256], replicated
The draws below stay inside these ranges and needn't reach their ends.
Inputs may be any that keep to these rules, and one draw needn't show every extreme that they name: `doc_lengths`: each row lists the lengths of one sequence's documents in order; they sum to 1024 and the longest is exactly 512.
All inputs are finite; a program needn't handle non-finite values.
Results may differ from the reference program's by a relative error of at most 0.017.
Values may be sent and summed in bfloat16 or wider, within the bound.
A program may use at most 128 MiB of HBM per device.

```python
import math
import jax
import jax.numpy as jnp
import numpy as np
from jax import lax

D = 2048
H = 8
KV = 2
HD = 256
FF = 8192
RANK = 64
PLD = 256
SEQS = 2
LEN = 1024
MOSTDOC = 512
NDOC = 4


def steps_of(stream_key, extent, shards, smallest, largest):
    loudness, own = 1.0, jax.random.fold_in(stream_key, 6)
    for dim, blocks in shards:
        heights = jnp.exp(jax.random.uniform(jax.random.fold_in(own, dim), (blocks,), jnp.float32, smallest / len(shards), largest / len(shards)))
        loudness = loudness * jnp.repeat(heights, extent[dim] // blocks).reshape([-1 if axis == dim else 1 for axis in range(len(extent))])
    return loudness


def length_profile(number_of, total, limit, lean):
    weights = [(1 << 20) // math.isqrt(standing ** lean) + 1 for standing in range(2, number_of + 1)]
    spare, counts = total - limit - (number_of - 1), [1] * (number_of - 1)
    while spare > 0:
        free = [i for i in range(number_of - 1) if counts[i] < limit]
        pool, left = sum([weights[i] for i in free]), spare
        for i in free:
            extra = min(limit - counts[i], max(1, left * weights[i] // pool), spare)
            counts[i] = counts[i] + extra
            spare = spare - extra
    return np.array([limit] + counts)


def uneven_parts(own_key, count, total, limit, skew):
    if count == 2:
        one = jax.random.randint(own_key, (), max(1, total - limit), min(limit, total - 1) + 1)
        return jnp.stack([one, total - one])
    tallies = jnp.asarray(length_profile(count, total, limit, skew), jnp.int32)
    couples = (count - 1) // 2
    giver, receiver = tallies[1:1 + 2 * couples:2], tallies[2:2 + 2 * couples:2]
    slack = jnp.minimum(giver - 1, limit - receiver)
    passed = jax.random.randint(jax.random.fold_in(own_key, 1), (couples,), 0, 1 << 20) % (slack + 1)
    tallies = tallies.at[1:1 + 2 * couples:2].set(giver - passed).at[2:2 + 2 * couples:2].set(receiver + passed)
    return tallies[jax.random.permutation(jax.random.fold_in(own_key, 2), count)]


def centred(key, dims, deviation, limit, shards=(), kind=jnp.bfloat16):
    entries = jax.random.normal(key, dims, jnp.float32) * deviation
    if len(shards) > 0:
        entries = steps_of(key, dims, shards, -0.22, 0.18) * entries
    return jnp.clip(entries, min=-limit, max=limit).astype(kind)


def setup_inputs(seed: int = 0) -> dict:
    arg_keys = jax.random.split(jax.random.key(seed), 18)
    return {
        "layer_in": centred(arg_keys[0], (SEQS, LEN, D), 1.0, 6.0, ((1, 8), (2, 4))),
        "per_layer_in": centred(arg_keys[1], (SEQS, LEN, PLD), 1.0, 6.0, ((1, 8),)),
        "doc_lengths": jax.vmap(lambda own: uneven_parts(own, NDOC, LEN, MOSTDOC, 1))(jax.random.split(arg_keys[2], SEQS)).reshape((SEQS, NDOC)).astype(jnp.int32),
        "w_query": centred(arg_keys[3], (D, H * HD), D ** -0.5, 0.125, ((0, 4), (1, 4))),
        "w_key": centred(arg_keys[4], (D, KV * HD), D ** -0.5, 0.125, ((0, 4), (1, 4))),
        "w_value": centred(arg_keys[5], (D, KV * HD), D ** -0.5, 0.125, ((0, 4), (1, 4))),
        "w_out": centred(arg_keys[6], (H * HD, D), (H * HD) ** -0.5, 0.125, ((0, 4), (1, 4))),
        "w_gate": centred(arg_keys[7], (D, FF), D ** -0.5, 0.125, ((0, 4), (1, 4))),
        "w_up": centred(arg_keys[8], (D, FF), D ** -0.5, 0.125, ((0, 4), (1, 4))),
        "w_down": centred(arg_keys[9], (FF, D), FF ** -0.5, 0.0625, ((0, 4), (1, 4))),
        "laurel_left": centred(arg_keys[10], (D, RANK), D ** -0.5, 0.125, ((0, 4),)),
        "laurel_right": centred(arg_keys[11], (RANK, D), RANK ** -0.5, 0.75, ((1, 4),)),
        "per_gate": centred(arg_keys[12], (D, PLD), D ** -0.5, 0.125, ((0, 4),)),
        "per_proj": centred(arg_keys[13], (PLD, D), PLD ** -0.5, 0.375, ((1, 4),)),
        "norm_gains": jnp.clip(1.0 + 0.1 * jax.random.normal(arg_keys[14], (6, D), jnp.float32), 0.5, 1.5),
        "head_gains": jnp.clip(jax.random.uniform(arg_keys[15], (2, HD), jnp.float32, 0.25, 0.4), 0.25, 0.4),
        "out_grad": centred(arg_keys[16], (SEQS, LEN, D), 1.0, 6.0, ((1, 8), (2, 4))),
    }


EPSILON = 1e-06
CLIP_LEVEL = 3.0
ROPE_BASE = 1000000.0
ROOT_HALF = 0.7071067811865476
MASK_FILL = -1e+30
PRECISE = lax.Precision.HIGHEST

@jax.custom_vjp
def low(v):
    return lax.optimization_barrier(v.astype(jnp.bfloat16)).astype(jnp.float32)

@jax.custom_vjp
def low_back(v):
    return v

def low_keep(v):
    return (low(v), None)

def low_pass(kept, grad):
    return (grad,)

def back_keep(v):
    return (v, None)

def back_low(kept, grad):
    return (low(grad),)
low.defvjp(low_keep, low_pass)
low_back.defvjp(back_keep, back_low)

def matmul(left_side, right_side):
    return jnp.matmul(left_side, right_side, precision=PRECISE)

def rms_norm(values, gain_vec):
    return values * lax.rsqrt(lax.optimization_barrier(jnp.mean(values * values, axis=-1, keepdims=True)) + EPSILON) * gain_vec

def rotation(position, width_all):
    half_width = width_all // 2
    frequency = ROPE_BASE ** (-2.0 * jnp.arange(half_width, dtype=jnp.float32) / width_all)
    angles = position.astype(jnp.float32)[..., None] * frequency
    cosine_table = jnp.concatenate([jnp.cos(angles), jnp.cos(angles)], axis=-1)
    sine_table = jnp.concatenate([jnp.sin(angles), jnp.sin(angles)], axis=-1)
    return (cosine_table, sine_table)

def rotate(values, cosine_table, sine_table):
    half_width = values.shape[-1] // 2
    turned = jnp.concatenate([-values[..., half_width:], values[..., :half_width]], axis=-1)
    return values * cosine_table + turned * sine_table

def doc_places(lengths, place_count):
    doc_ends = jnp.cumsum(lengths).astype(jnp.int32)
    places = jnp.arange(place_count, dtype=jnp.int32)
    before = (doc_ends[None, :] <= places[:, None]).astype(jnp.int32)
    segment = lax.optimization_barrier(jnp.sum(before, axis=1)).astype(jnp.int32)
    doc_start = lax.optimization_barrier(jnp.sum(before * lengths[None, :], axis=1)).astype(jnp.int32)
    return (segment, places, places - doc_start)

def attention(q_low, k_low, v_low, segment, places, group):
    head_dim = q_low.shape[-1]
    key_heads = jnp.repeat(k_low, group, axis=1)
    value_heads = jnp.repeat(v_low, group, axis=1)
    block_rows = min(512, q_low.shape[0])
    block_count = q_low.shape[0] // block_rows

    def one_block(item):
        q_part, seg_part, place_part = item
        scores = jnp.einsum('qhd,khd->hqk', q_part, key_heads, precision=PRECISE)
        scores = low_back(scores)
        allowed = (seg_part[:, None] == segment[None, :]) & (places[None, :] <= place_part[:, None])
        masked = jnp.where(allowed[None], scores, MASK_FILL)
        soft_probs = jax.nn.softmax(masked, axis=-1)
        mixed_out = jnp.einsum('hqk,khd->qhd', low(soft_probs), value_heads, precision=PRECISE)
        return (mixed_out, lax.optimization_barrier(jnp.max(masked, axis=(1, 2))))
    mixed_out, block_tops = lax.map(jax.checkpoint(one_block), (q_low.reshape(block_count, block_rows, q_low.shape[1], head_dim), segment.reshape(block_count, block_rows), places.reshape(block_count, block_rows)))
    return (mixed_out.reshape(q_low.shape), lax.optimization_barrier(jnp.max(block_tops, axis=0)))

def sequence_layer(inputs, per_input, lengths, weight_set):
    w_query, w_key, w_value, w_out, w_gate, w_up, w_down, laurel_left, laurel_right, per_gate, per_proj, norm_gains, head_gains = weight_set
    token_count = inputs.shape[0]
    head_dim = head_gains.shape[1]
    heads_all = w_query.shape[1] // head_dim
    kv_heads = w_key.shape[1] // head_dim
    segment, places, position = doc_places(lengths, token_count)
    cosine_table, sine_table = rotation(position, head_dim)
    x_norm = rms_norm(inputs, norm_gains[0])
    x_low = low(x_norm)
    q_raw = low_back(matmul(x_low, w_query)).reshape(token_count, heads_all, head_dim)
    k_raw = low_back(matmul(x_low, w_key)).reshape(token_count, kv_heads, head_dim)
    v_raw = low_back(matmul(x_low, w_value)).reshape(token_count, kv_heads, head_dim)
    q_low = low(rotate(rms_norm(q_raw, head_gains[0]), cosine_table[:, None], sine_table[:, None]))
    k_low = low(rotate(rms_norm(k_raw, head_gains[1]), cosine_table[:, None], sine_table[:, None]))
    v_low = low(rms_norm(v_raw, 1.0))
    attended, head_tops = attention(q_low, k_low, v_low, segment, places, heads_all // kv_heads)
    o_low = low(low_back(attended.reshape(token_count, heads_all * head_dim)))
    attn_val = low_back(matmul(o_low, w_out))
    h_one = inputs + rms_norm(attn_val, norm_gains[1])
    lr_low = low(low_back(matmul(x_low, laurel_left)))
    lo_val = low_back(matmul(lr_low, laurel_right))
    h_two = (h_one + (x_norm + rms_norm(lo_val, norm_gains[2]))) * ROOT_HALF
    f_low = low(rms_norm(h_two, norm_gains[3]))
    gate_val = low_back(matmul(f_low, w_gate))
    up_val = low_back(matmul(f_low, w_up))
    hid_low = low(jax.nn.gelu(gate_val, approximate=True) * up_val)
    ff_val = low_back(matmul(hid_low, w_down))
    h_three = h_two + rms_norm(ff_val, norm_gains[4])
    h_low = low(h_three)
    pg_val = low_back(matmul(h_low, per_gate))
    gp_low = low(jax.nn.gelu(pg_val, approximate=True) * per_input)
    pp_val = low_back(matmul(gp_low, per_proj))
    return (h_three + rms_norm(pp_val, norm_gains[5]), head_tops)

def reference(layer_in, per_layer_in, doc_lengths, w_query, w_key, w_value, w_out, w_gate, w_up, w_down, laurel_left, laurel_right, per_gate, per_proj, norm_gains, head_gains, out_grad):
    weights = tuple((weight.astype(jnp.float32) for weight in (w_query, w_key, w_value, w_out, w_gate, w_up, w_down, laurel_left, laurel_right, per_gate, per_proj, norm_gains, head_gains)))
    per_input = per_layer_in.astype(jnp.float32)

    def forward(inputs, weight_set):

        def one_seq(item):
            seq_in, seq_per, seq_lengths = item
            return sequence_layer(seq_in, seq_per, seq_lengths, weight_set)
        outputs, seq_tops = lax.map(one_seq, (inputs, per_input, doc_lengths))
        return (outputs, lax.optimization_barrier(jnp.max(seq_tops, axis=0)))
    outputs, back_fn, logit_top = jax.vjp(forward, layer_in.astype(jnp.float32), weights, has_aux=True)
    grad_inputs, grad_weights = back_fn(out_grad.astype(jnp.float32))
    gains = weights[12]
    clip_factor = jnp.sqrt(CLIP_LEVEL / jnp.maximum(logit_top, CLIP_LEVEL))
    clipped_gains = jnp.stack([clip_factor[:, None] * gains[0][None, :], clip_factor[:, None] * gains[1][None, :]])
    return (outputs.astype(jnp.bfloat16), grad_inputs.astype(jnp.bfloat16), grad_weights[0], grad_weights[1], grad_weights[2], grad_weights[3], grad_weights[4], grad_weights[5], grad_weights[6], grad_weights[7], grad_weights[8], grad_weights[9], grad_weights[10], grad_weights[11], grad_weights[12], clipped_gains)
```

```python
import functools

import jax
import jax.numpy as jnp
from jax import lax
from jax.experimental import pallas as pl
from jax.experimental.pallas import tpu as pltpu
from jax.sharding import PartitionSpec as P

EPSILON = 1e-06
CLIP_LEVEL = 3.0
ROPE_BASE = 1000000.0
ROOT_HALF = 0.7071067811865476
MASK_FILL = -1e30
MESH = pl.DeviceIdType.MESH
BF = jnp.bfloat16
F32 = jnp.float32


def swapped(value, axis, apart):
    mask = 2**apart
    pairs = [(source, source ^ mask) for source in range(lax.axis_size(axis))]
    return lax.ppermute(value, axis, pairs)


def width_total(values):
    return lax.psum(values, "row")


def gather_tokens(values):
    return lax.all_gather(values, "col", axis=1, tiled=True)


def spread_rows(values, project):
    gathered = gather_tokens(values)
    return (gathered, lax.psum_scatter(project(gathered), "row", scatter_dimension=1, tiled=True))


def spread_cols(values, project):
    gathered = lax.all_gather(values, "row", axis=1, tiled=True)
    return (gathered, lax.psum_scatter(project(gathered), "col", scatter_dimension=1, tiled=True))


def times_right(left_side, right_side):
    return jnp.einsum("std,dn->stn", left_side, right_side, preferred_element_type=jnp.float32)


def times_back(left_side, right_side):
    return jnp.einsum("stn,dn->std", left_side, right_side, preferred_element_type=jnp.float32)


def outer_sum(left_side, right_side):
    return jnp.einsum("std,stn->dn", left_side, right_side, preferred_element_type=jnp.float32)


def norm_forward(values, gain_vec, width_all):
    square_sum = width_total(jnp.sum(values * values, axis=-1, keepdims=True))
    factor = lax.rsqrt(square_sum / width_all + EPSILON)
    normed = values * factor
    return (normed * gain_vec, normed, factor)


def norm_backward(grad_values, normed, factor, gain_vec, width_all):
    grad_normed = grad_values * gain_vec
    inner_sum = width_total(jnp.sum(grad_normed * normed, axis=-1, keepdims=True))
    result = factor * (grad_normed - normed * (inner_sum / width_all))
    return (result, jnp.sum(grad_values * normed, axis=(0, 1)))


def head_norm(values, gain_vec):
    return (
        values * lax.rsqrt(jnp.mean(values * values, axis=-1, keepdims=True) + EPSILON) * gain_vec
    )


def rotation(position, width_all):
    half_width = width_all // 2
    frequency = ROPE_BASE ** (-2.0 * jnp.arange(half_width, dtype=jnp.float32) / width_all)
    angles = position.astype(jnp.float32)[..., None] * frequency
    cosine_table = jnp.concatenate([jnp.cos(angles), jnp.cos(angles)], axis=-1)
    sine_table = jnp.concatenate([jnp.sin(angles), jnp.sin(angles)], axis=-1)
    return (cosine_table, sine_table)


def rotate(values, cosine_table, sine_table):
    half_width = values.shape[-1] // 2
    turned = jnp.concatenate([-values[..., half_width:], values[..., :half_width]], axis=-1)
    return values * cosine_table + turned * sine_table


def doc_places(doc_lengths, first_place, place_count):
    upto = jnp.tril(jnp.ones((doc_lengths.shape[1], doc_lengths.shape[1]), jnp.int32))
    doc_ends = jnp.sum(doc_lengths[:, None, :] * upto[None], axis=2)
    places = first_place + jnp.arange(place_count, dtype=jnp.int32)
    before = (doc_ends[:, None, :] <= places[None, :, None]).astype(jnp.int32)
    segment = jnp.sum(before, axis=2)
    doc_start = jnp.sum(before * doc_lengths[:, None, :], axis=2)
    return (segment, places, places[None, :] - doc_start)


def block_scores(queries, keys_all, block_start, block_size, query_seg, query_place, key_seg):
    keys_part = lax.dynamic_slice_in_dim(keys_all, block_start, block_size, 1)
    scores = jnp.einsum("sqhd,skd->shqk", queries, keys_part, preferred_element_type=jnp.float32)
    seg_part = lax.dynamic_slice_in_dim(key_seg, block_start, block_size, 1)
    key_place = block_start + jnp.arange(block_size, dtype=jnp.int32)
    allowed = (query_seg[:, None, :, None] == seg_part[:, None, None, :]) & (
        key_place[None, None, None, :] <= query_place[None, None, :, None]
    )
    return (scores, allowed)


def body_any(
    layer_in,
    per_layer_in,
    doc_lengths,
    w_query,
    w_key,
    w_value,
    w_out,
    w_gate,
    w_up,
    w_down,
    laurel_left,
    laurel_right,
    per_gate,
    per_proj,
    norm_gains,
    head_gains,
    out_grad,
):
    seq_count = layer_in.shape[0]
    width_all = layer_in.shape[2] * lax.axis_size("row")
    head_dim = head_gains.shape[1]
    heads_here = w_query.shape[1] // head_dim
    heads_all = heads_here * lax.axis_size("col")
    key_width = w_key.shape[1]
    ff_here = w_gate.shape[1]
    local_len = layer_in.shape[1] * lax.axis_size("col")
    tokens_row = local_len // lax.axis_size("row")
    seq_len = local_len * lax.axis_size("seq")
    col_index = lax.axis_index("col")
    even_col = col_index % 2 == 0
    q_width = heads_here * head_dim
    partner_key, partner_value = swapped((w_key, w_value), "col", 0)
    key_head = jnp.where(
        even_col,
        jnp.concatenate([w_key, partner_key], axis=1),
        jnp.concatenate([partner_key, w_key], axis=1),
    )
    value_head = jnp.where(
        even_col,
        jnp.concatenate([w_value, partner_value], axis=1),
        jnp.concatenate([partner_value, w_value], axis=1),
    )
    w_heads = jnp.concatenate([w_query, key_head, value_head], axis=1)
    w_back = jnp.concatenate([w_query, w_key, w_value], axis=1)
    w_gate_up = jnp.concatenate([w_gate, w_up], axis=1)
    inputs = layer_in.astype(jnp.float32)
    x_norm, x_normed, x_factor = norm_forward(inputs, norm_gains[0], width_all)
    x_low = x_norm.astype(jnp.bfloat16)
    x_rows, head_raw = spread_rows(x_low, lambda gathered: times_right(gathered, w_heads))
    q_raw = head_raw[:, :, :q_width].reshape(seq_count, tokens_row, heads_here, head_dim)
    k_raw = head_raw[:, :, q_width : q_width + head_dim]
    v_raw = head_raw[:, :, q_width + head_dim :]
    query_seg, query_place, query_pos = doc_places(
        doc_lengths, lax.axis_index(("seq", "row")) * tokens_row, tokens_row
    )
    key_seg, unused_place, unused_pos = doc_places(doc_lengths, 0, seq_len)
    cosine_table, sine_table = rotation(query_pos, head_dim)

    def query_prep(raw_part, gain_vec):
        return rotate(
            head_norm(raw_part, gain_vec), cosine_table[:, :, None], sine_table[:, :, None]
        )

    def key_prep(raw_part, gain_vec):
        return rotate(head_norm(raw_part, gain_vec), cosine_table, sine_table)

    def value_prep(raw_part):
        return head_norm(raw_part, 1.0)

    q_rot, query_back = jax.vjp(query_prep, q_raw, head_gains[0])
    k_rot, key_back = jax.vjp(key_prep, k_raw, head_gains[1])
    v_normed, value_back = jax.vjp(value_prep, v_raw)
    q_low = q_rot.astype(jnp.bfloat16)
    keys_all, values_all = (
        lax.all_gather(k_rot.astype(jnp.bfloat16), ("seq", "row"), axis=1, tiled=True),
        lax.all_gather(v_normed.astype(jnp.bfloat16), ("seq", "row"), axis=1, tiled=True),
    )
    block_size = min(512, seq_len)
    block_count = seq_len // block_size
    blocks = jnp.arange(block_count, dtype=jnp.int32)

    def scored(block_index):
        return block_scores(
            q_low, keys_all, block_index * block_size, block_size, query_seg, query_place, key_seg
        )

    def values_at(block_index):
        return lax.dynamic_slice_in_dim(values_all, block_index * block_size, block_size, 1)

    def stats_step(carry, block_index):
        row_top, row_total = carry
        scores, allowed = scored(block_index)
        new_top = jnp.maximum(row_top, jnp.max(jnp.where(allowed, scores, MASK_FILL), axis=3))
        weights = jnp.where(allowed, jnp.exp(scores - new_top[..., None]), 0.0)
        row_total = row_total * jnp.exp(row_top - new_top) + jnp.sum(weights, axis=3)
        return ((new_top, row_total), None)

    start_top = jnp.full((seq_count, heads_here, tokens_row), MASK_FILL, jnp.float32)
    (row_top, row_total), unused = lax.scan(
        stats_step, (start_top, jnp.zeros_like(start_top)), blocks
    )
    log_total = row_top + jnp.log(row_total)

    def probs_at(block_index):
        scores, allowed = scored(block_index)
        return jnp.where(allowed, jnp.exp(scores - log_total[..., None]), 0.0)

    def out_step(total_out, block_index):
        probs_low = probs_at(block_index).astype(jnp.bfloat16)
        total_out = total_out + jnp.einsum(
            "shqk,skd->sqhd", probs_low, values_at(block_index), preferred_element_type=jnp.float32
        )
        return (total_out, None)

    attended, unused = lax.scan(
        out_step, jnp.zeros((seq_count, tokens_row, heads_here, head_dim), jnp.float32), blocks
    )
    o_low = attended.astype(jnp.bfloat16).reshape(seq_count, tokens_row, q_width)
    head_slots = lax.dynamic_update_slice_in_dim(
        jnp.full((heads_all,), MASK_FILL, jnp.float32),
        jnp.max(row_top, axis=(0, 2)),
        col_index * heads_here,
        0,
    )
    logit_top = lax.pmax(head_slots, ("seq", "row", "col"))
    o_rows, attn_val = spread_cols(o_low, lambda gathered: times_right(gathered, w_out))
    attn_norm, attn_normed, attn_factor = norm_forward(attn_val, norm_gains[1], width_all)
    h_one = inputs + attn_norm
    lr_low = width_total(times_right(x_low, laurel_left)).astype(jnp.bfloat16)
    lo_val = times_right(lr_low, laurel_right)
    lo_norm, lo_normed, lo_factor = norm_forward(lo_val, norm_gains[2], width_all)
    h_two = (h_one + (x_norm + lo_norm)) * ROOT_HALF
    f_norm, f_normed, f_factor = norm_forward(h_two, norm_gains[3], width_all)
    f_low = f_norm.astype(jnp.bfloat16)
    f_rows, gate_up = spread_rows(f_low, lambda gathered: times_right(gathered, w_gate_up))
    gate_val = gate_up[:, :, :ff_here]
    up_val = gate_up[:, :, ff_here:]

    def geglu(gate_part, up_part):
        return jax.nn.gelu(gate_part, approximate=True) * up_part

    hidden, geglu_back = jax.vjp(geglu, gate_val, up_val)
    hid_low = hidden.astype(jnp.bfloat16)
    hid_rows, ff_val = spread_cols(hid_low, lambda gathered: times_right(gathered, w_down))
    ff_norm, ff_normed, ff_factor = norm_forward(ff_val, norm_gains[4], width_all)
    h_three = h_two + ff_norm
    h_low = h_three.astype(jnp.bfloat16)
    pg_val = width_total(times_right(h_low, per_gate))
    per_input = per_layer_in.astype(jnp.float32)

    def per_mix(gate_part):
        return jax.nn.gelu(gate_part, approximate=True) * per_input

    gp_val, per_back = jax.vjp(per_mix, pg_val)
    gp_low = gp_val.astype(jnp.bfloat16)
    pp_val = times_right(gp_low, per_proj)
    pp_norm, pp_normed, pp_factor = norm_forward(pp_val, norm_gains[5], width_all)
    layer_out = (h_three + pp_norm).astype(jnp.bfloat16)
    grad_top = out_grad.astype(jnp.float32)
    d_pp, gain_five = norm_backward(grad_top, pp_normed, pp_factor, norm_gains[5], width_all)
    d_pp_low = d_pp.astype(jnp.bfloat16)
    grad_per_proj = outer_sum(gp_low, d_pp_low)
    (d_pg,) = per_back(width_total(times_back(d_pp_low, per_proj)))
    d_pg_low = d_pg.astype(jnp.bfloat16)
    grad_per_gate = outer_sum(h_low, d_pg_low)
    d_three = grad_top + times_back(d_pg_low, per_gate)
    d_ff, gain_four = norm_backward(d_three, ff_normed, ff_factor, norm_gains[4], width_all)
    d_ff_low = d_ff.astype(jnp.bfloat16)
    dff_rows, d_hidden = spread_rows(d_ff_low, lambda gathered: times_back(gathered, w_down))
    grad_down = outer_sum(hid_rows, dff_rows)
    d_gate, d_up = geglu_back(d_hidden)
    d_gate_up = jnp.concatenate([d_gate, d_up], axis=2).astype(jnp.bfloat16)
    dgu_rows, d_f_low = spread_cols(d_gate_up, lambda gathered: times_back(gathered, w_gate_up))
    grad_gate_up = outer_sum(f_rows, dgu_rows)
    d_f, gain_three = norm_backward(d_f_low, f_normed, f_factor, norm_gains[3], width_all)
    d_half = (d_three + d_f) * ROOT_HALF
    d_lo, gain_two = norm_backward(d_half, lo_normed, lo_factor, norm_gains[2], width_all)
    d_lo_low = d_lo.astype(jnp.bfloat16)
    grad_laurel_right = outer_sum(lr_low, d_lo_low)
    d_lr_low = width_total(times_back(d_lo_low, laurel_right)).astype(jnp.bfloat16)
    grad_laurel_left = outer_sum(x_low, d_lr_low)
    d_attn, gain_one = norm_backward(d_half, attn_normed, attn_factor, norm_gains[1], width_all)
    d_attn_low = d_attn.astype(jnp.bfloat16)
    dattn_rows, d_o = spread_rows(d_attn_low, lambda gathered: times_back(gathered, w_out))
    grad_w_out = outer_sum(o_rows, dattn_rows)
    d_o_low = d_o.astype(jnp.bfloat16).reshape(seq_count, tokens_row, heads_here, head_dim)

    def delta_step(total_delta, block_index):
        d_probs = jnp.einsum(
            "sqhd,skd->shqk", d_o_low, values_at(block_index), preferred_element_type=jnp.float32
        )
        return (total_delta + jnp.sum(probs_at(block_index) * d_probs, axis=3), None)

    row_delta, unused = lax.scan(delta_step, jnp.zeros_like(log_total), blocks)

    def grad_step(carry, block_index):
        d_query, d_keys, d_values = carry
        block_start = block_index * block_size
        prob_vals = probs_at(block_index)
        d_probs = jnp.einsum(
            "sqhd,skd->shqk", d_o_low, values_at(block_index), preferred_element_type=jnp.float32
        )
        d_scores = (prob_vals * (d_probs - row_delta[..., None])).astype(jnp.bfloat16)
        keys_part = lax.dynamic_slice_in_dim(keys_all, block_start, block_size, 1)
        d_query = d_query + jnp.einsum(
            "shqk,skd->sqhd", d_scores, keys_part, preferred_element_type=jnp.float32
        )
        key_part = jnp.einsum("shqk,sqhd->skd", d_scores, q_low, preferred_element_type=jnp.float32)
        value_part = jnp.einsum(
            "shqk,sqhd->skd",
            prob_vals.astype(jnp.bfloat16),
            d_o_low,
            preferred_element_type=jnp.float32,
        )
        d_keys = lax.dynamic_update_slice_in_dim(d_keys, key_part, block_start, 1)
        d_values = lax.dynamic_update_slice_in_dim(d_values, value_part, block_start, 1)
        return ((d_query, d_keys, d_values), None)

    zero_keys = jnp.zeros((seq_count, seq_len, head_dim), jnp.float32)
    (d_query, d_keys, d_values), unused = lax.scan(
        grad_step, (jnp.zeros_like(attended), zero_keys, zero_keys), blocks
    )
    own_keys, own_values = (
        lax.psum_scatter(d_keys, ("seq", "row"), scatter_dimension=1, tiled=True),
        lax.psum_scatter(d_values, ("seq", "row"), scatter_dimension=1, tiled=True),
    )
    pair_keys, pair_values = swapped((own_keys, own_values), "col", 0)
    d_q_raw, d_q_gain = query_back(d_query)
    d_k_raw, d_k_gain = key_back(own_keys + pair_keys)
    (d_v_raw,) = value_back(own_values + pair_values)
    key_offset = col_index % 2 * key_width
    d_heads_low = jnp.concatenate(
        [
            d_q_raw.reshape(seq_count, tokens_row, q_width),
            lax.dynamic_slice_in_dim(d_k_raw, key_offset, key_width, 2),
            lax.dynamic_slice_in_dim(d_v_raw, key_offset, key_width, 2),
        ],
        axis=2,
    ).astype(jnp.bfloat16)
    dhead_rows, d_x_heads = spread_cols(d_heads_low, lambda gathered: times_back(gathered, w_back))
    grad_heads = outer_sum(x_rows, dhead_rows)
    d_x_low = d_x_heads + times_back(d_lr_low, laurel_left)
    d_x_part, gain_zero = norm_backward(
        d_half + d_x_low, x_normed, x_factor, norm_gains[0], width_all
    )
    grad_in = (d_half + d_x_part).astype(jnp.bfloat16)
    head_part = width_total(jnp.stack([d_q_gain, d_k_gain * 0.5]))
    sum_heads, sum_out, sum_gate_up, sum_down = lax.psum(
        (grad_heads, grad_w_out, grad_gate_up, grad_down), "seq"
    )
    sum_left, sum_right, sum_per_gate, sum_per_proj, sum_gains, sum_head_gains = lax.psum(
        (
            grad_laurel_left,
            grad_laurel_right,
            grad_per_gate,
            grad_per_proj,
            jnp.stack([gain_zero, gain_one, gain_two, gain_three, gain_four, gain_five]),
            head_part,
        ),
        ("seq", "col"),
    )
    clip_factor = jnp.sqrt(CLIP_LEVEL / jnp.maximum(logit_top, CLIP_LEVEL))
    clipped_gains = jnp.stack(
        [
            clip_factor[:, None] * head_gains[0][None, :],
            clip_factor[:, None] * head_gains[1][None, :],
        ]
    )
    return (
        layer_out,
        grad_in,
        sum_heads[:, :q_width],
        sum_heads[:, q_width : q_width + key_width],
        sum_heads[:, q_width + key_width :],
        sum_out,
        sum_gate_up[:, :ff_here],
        sum_gate_up[:, ff_here:],
        sum_down,
        sum_left,
        sum_right,
        sum_per_gate,
        sum_per_proj,
        sum_gains,
        sum_head_gains,
        clipped_gains,
    )


def group_gather(values):
    return lax.all_gather(values, ("seq", "col"), axis=0, tiled=True)


def group_scatter(partial):
    return lax.psum_scatter(
        partial.astype(jnp.bfloat16), ("seq", "col"), scatter_dimension=0, tiled=True
    ).astype(jnp.float32)


def to_owner(values):
    seq_count, tokens, width = values.shape
    rows = lax.axis_size("row")
    parts = values.reshape(rows, seq_count * tokens // rows, width)
    moved = lax.all_to_all(parts, "row", split_axis=0, concat_axis=0)
    return moved.transpose(1, 0, 2).reshape(parts.shape[1], rows * width)


def from_owner(values, seq_count):
    tokens, width = values.shape
    rows = lax.axis_size("row")
    parts = values.reshape(tokens, rows, width // rows).transpose(1, 0, 2)
    moved = lax.all_to_all(parts, "row", split_axis=0, concat_axis=0)
    return moved.reshape(seq_count, rows * tokens // seq_count, width // rows)


def mm(left_side, right_side):
    return jnp.dot(left_side, right_side, preferred_element_type=jnp.float32)


def mm_nt(left_side, right_side):
    return lax.dot_general(
        left_side, right_side, (((1,), (1,)), ((), ())), preferred_element_type=jnp.float32
    )


def mm_tn(left_side, right_side):
    return lax.dot_general(
        left_side, right_side, (((0,), (0,)), ((), ())), preferred_element_type=jnp.float32
    )


def rms(values):
    factor = lax.rsqrt(jnp.mean(values * values, axis=-1, keepdims=True) + EPSILON)
    return values * factor, factor


def rms_back(grad_values, normed, factor, gain_vec):
    grad_normed = grad_values * gain_vec
    inner = jnp.mean(grad_normed * normed, axis=-1, keepdims=True)
    return (
        factor * (grad_normed - normed * inner),
        jnp.sum(grad_values * normed, axis=0, keepdims=True),
    )


def gather_rows(values, axis):
    return lax.all_gather(values, "row", axis=axis, tiled=True)


def scatter_rows(values, axis):
    return lax.psum_scatter(
        values.astype(jnp.bfloat16), "row", scatter_dimension=axis, tiled=True
    ).astype(jnp.float32)


def both_cores(values, axis):
    return lax.all_gather(values, "seq", axis=axis, tiled=True)


def remote(src, dst, send_sem, recv_sem, device):
    return pltpu.make_async_remote_copy(
        src_ref=src,
        dst_ref=dst,
        send_sem=send_sem,
        recv_sem=recv_sem,
        device_id=device,
        device_id_type=MESH,
    )


def greet(core, row, col):
    barrier = pltpu.get_barrier_semaphore()
    near = [(core, row ^ 1, col), (core, row ^ 2, col), (core, row ^ 3, col), (1 - core, row, col)]
    for device in near:
        pl.semaphore_signal(barrier, inc=1, device_id=device, device_id_type=MESH)

    @pl.when(col > 0)
    def _():
        pl.semaphore_signal(barrier, inc=1, device_id=(core, row, col - 1), device_id_type=MESH)

    @pl.when(col < 3)
    def _():
        pl.semaphore_signal(barrier, inc=1, device_id=(core, row, col + 1), device_id_type=MESH)

    ends = jnp.where((col == 0) | (col == 3), 1, 2)
    pl.semaphore_wait(barrier, 4 + ends)


class Gather:
    def __init__(self, place, buf, rows, sems):
        self.core, self.row, self.col = place
        self.buf, self.rows = buf, rows
        self.send_z, self.recv_z, self.send_s, self.recv_s = sems

    def part(self, core, col):
        return self.buf.at[pl.ds(pl.multiple_of((core * 4 + col) * self.rows, self.rows), self.rows)]

    def to_right(self, dist):
        part = self.part(self.core, self.col - dist)
        return remote(
            part, part, self.send_z.at[dist], self.recv_z.at[dist], (self.core, self.row, self.col + 1)
        )

    def to_left(self, dist):
        part = self.part(self.core, self.col + dist)
        return remote(
            part,
            part,
            self.send_z.at[3 + dist],
            self.recv_z.at[3 + dist],
            (self.core, self.row, self.col - 1),
        )

    def to_sibling(self, col):
        part = self.part(self.core, col)
        return remote(
            part, part, self.send_s.at[col], self.recv_s.at[col], (1 - self.core, self.row, self.col)
        )

    def start(self):
        col = self.col

        @pl.when(col < 3)
        def _():
            self.to_right(0).start()

        @pl.when(col > 0)
        def _():
            self.to_left(0).start()

        self.to_sibling(col).start()

    def forward(self):
        col = self.col
        for dist in (1, 2, 3):

            @pl.when(col >= dist)
            def _():
                part = self.part(self.core, col - dist)
                remote(
                    part, part, self.send_z.at[0], self.recv_z.at[dist - 1], (self.core, self.row, col)
                ).wait_recv()

                @pl.when(col < 3)
                def _():
                    if dist < 3:
                        self.to_right(dist).start()

                self.to_sibling(col - dist).start()

            @pl.when(col + dist <= 3)
            def _():
                part = self.part(self.core, col + dist)
                remote(
                    part,
                    part,
                    self.send_z.at[0],
                    self.recv_z.at[3 + dist - 1],
                    (self.core, self.row, col),
                ).wait_recv()

                @pl.when(col > 0)
                def _():
                    if dist < 3:
                        self.to_left(dist).start()

                self.to_sibling(col + dist).start()

    def finish(self):
        for col in range(4):
            part = self.part(1 - self.core, col)
            remote(
                part, part, self.send_s.at[col], self.recv_s.at[col], (1 - self.core, self.row, self.col)
            ).wait_recv()
        for col in range(4):
            self.to_sibling(col).wait_send()
        for dist in (0, 1, 2):

            @pl.when((self.col < 3) & (self.col >= dist))
            def _():
                self.to_right(dist).wait_send()

            @pl.when((self.col > 0) & (self.col + dist <= 3))
            def _():
                self.to_left(dist).wait_send()


class Scatter:
    def __init__(self, place, rows, bufs, sems):
        self.core, self.row, self.col = place
        self.rows = rows
        self.give, self.keep, self.got, self.sent, self.left, self.right = bufs
        self.send_z, self.recv_z, self.send_s, self.recv_s = sems

    def sibling(self):
        return remote(
            self.give,
            self.got,
            self.send_s.at[0],
            self.recv_s.at[0],
            (1 - self.core, self.row, self.col),
        )

    def mine(self, dest):
        rows = pl.ds(dest * self.rows, self.rows)
        return self.keep[rows] + self.got[rows].astype(F32)

    def hop(self, dest, right):
        step = 1 if right else -1
        lane = 0 if right else 4
        return remote(
            self.sent.at[dest],
            (self.left if right else self.right).at[dest],
            self.send_z.at[lane + dest],
            self.recv_z.at[lane + dest],
            (self.core, self.row, self.col + step),
        )

    def chain(self, dest, right):
        col = self.col
        inner = (col > 0) if right else (col < 3)

        @pl.when((col < dest) if right else (col > dest))
        def _():
            @pl.when(inner)
            def _():
                self.hop(dest, right).wait_recv()
                came = (self.left if right else self.right)[dest].astype(F32)
                self.sent[dest] = (self.mine(dest) + came).astype(BF)

            @pl.when(jnp.logical_not(inner))
            def _():
                self.sent[dest] = self.mine(dest).astype(BF)

            self.hop(dest, right).start()

    def run(self, result):
        col = self.col
        self.sibling().wait_recv()
        for dest in (3, 2, 1):
            self.chain(dest, True)
            self.chain(3 - dest, False)
        own = pl.ds(pl.multiple_of(col * self.rows, self.rows), self.rows)
        result[...] = self.keep[own] + self.got[own].astype(F32)
        for dest in range(4):

            @pl.when((col == dest) & (dest > 0))
            def _():
                self.hop(dest, True).wait_recv()
                result[...] += self.left[dest].astype(F32)

            @pl.when((col == dest) & (dest < 3))
            def _():
                self.hop(dest, False).wait_recv()
                result[...] += self.right[dest].astype(F32)

        self.sibling().wait_send()
        for dest in range(4):

            @pl.when(col < dest)
            def _():
                self.hop(dest, True).wait_send()

            @pl.when(col > dest)
            def _():
                self.hop(dest, False).wait_send()


class RowGather:
    def __init__(self, place, source, block, halves, sems):
        self.core, self.row, self.col = place
        self.source, self.block, self.halves = source, block, halves
        self.sems = sems

    def neighbour(self, mask):
        return (self.core, self.row ^ mask, self.col)

    def own(self):
        return pltpu.make_async_copy(self.source, self.block(self.row), self.sems.at[8])

    def first(self, mask, block=None):
        lane = mask - 1
        return remote(
            self.source,
            self.block(self.row) if block is None else block,
            self.sems.at[lane],
            self.sems.at[4 + lane],
            self.neighbour(mask),
        )

    def second(self, mask):
        part = self.halves(self.row ^ (3 - mask))[mask - 1]
        return remote(
            part, part, self.sems.at[1 + mask], self.sems.at[5 + mask], self.neighbour(mask)
        )

    def start(self):
        self.first(1).start()
        self.first(2).start()
        self.own().start()

    def forward(self):
        self.first(1, self.block(self.row ^ 1)).wait_recv()
        self.second(2).start()
        self.first(2, self.block(self.row ^ 2)).wait_recv()
        self.second(1).start()

    def finish(self):
        for mask in (1, 2):
            part = self.halves(self.row ^ 3)[mask - 1]
            remote(
                part, part, self.sems.at[1 + mask], self.sems.at[5 + mask], self.neighbour(mask)
            ).wait_recv()
        self.own().wait()
        self.first(1).wait_send()
        self.first(2).wait_send()
        self.second(1).wait_send()
        self.second(2).wait_send()


def by_rows(buf, block_rows):
    half = block_rows // 2

    def block(index):
        return buf.at[pl.ds(pl.multiple_of(index * block_rows, block_rows), block_rows)]

    def halves(index):
        return [
            buf.at[pl.ds(pl.multiple_of(index * block_rows + part * half, half), half)]
            for part in range(2)
        ]

    return block, halves


def by_cols(buf, block_cols):
    rows = buf.shape[0] // 2

    def block(index):
        return buf.at[:, pl.ds(pl.multiple_of(index * block_cols, block_cols), block_cols)]

    def halves(index):
        cols = pl.ds(pl.multiple_of(index * block_cols, block_cols), block_cols)
        return [buf.at[pl.ds(part * rows, rows), cols] for part in range(2)]

    return block, halves


def gelu(values):
    inner = 0.7978845608028654 * (values + 0.044715 * values * values * values)
    return 0.5 * values * (1.0 + jnp.tanh(inner))


def head_parts(raw, gain, cosine, sine):
    factor = lax.rsqrt(jnp.mean(raw * raw, axis=1, keepdims=True) + EPSILON)
    half = raw.shape[1] // 2
    scaled = raw * factor * gain
    first, second = scaled[:, :half], scaled[:, half:]
    return jnp.concatenate([first * cosine - second * sine, second * cosine + first * sine], axis=1)


def forward_kernel(
    x_in,
    gains_in,
    w_query,
    w_kv,
    w_out,
    w_gate,
    w_up,
    w_down,
    small_in,
    small_out,
    cosine,
    sine,
    start,
    head_gains,
    x_own,
    gains,
    xg,
    raw_q,
    raw_kv,
    q_low,
    kv,
    lse,
    top,
    o_low,
    attn_val,
    lr_low,
    fg,
    gate,
    up,
    hid,
    ff_val,
    wq_all,
    wkv_all,
    wo_all,
    wg_all,
    wu_all,
    wd_all,
    si_all,
    so_all,
    w_kv_pair,
    gains_pad,
    vq,
    vkv,
    vo,
    vg,
    vu,
    vd,
    vsi,
    vso,
    give,
    keep,
    got,
    sent,
    left,
    right,
    give2,
    keep2,
    got2,
    sent2,
    left2,
    right2,
    row_sems,
    z_send,
    z_recv,
    s_send,
    s_recv,
    misc_send,
    misc_recv,
    out_sems,
):
    core, row, col = lax.axis_index("seq"), lax.axis_index("row"), lax.axis_index("col")
    place = (core, row, col)
    own_tokens, width = x_own.shape
    block = x_in.shape[2]
    head_dim = head_gains.shape[1]
    tokens = xg.shape[0]
    ff_part = gate.shape[1]
    chunk = 2 * own_tokens
    key_width = w_kv.shape[1]
    half = row % 2
    greet(core, row, col)

    my_cols = pl.ds(pl.multiple_of(row * block, block), block)

    def hand_over(mask):
        return remote(
            x_in.at[row ^ mask],
            x_own.at[:, my_cols],
            misc_send.at[mask],
            misc_recv.at[mask],
            (core, row ^ mask, col),
        )

    def hand_gains(mask):
        return remote(
            gains_pad,
            gains.at[:, my_cols],
            misc_send.at[3 + mask],
            misc_recv.at[3 + mask],
            (core, row ^ mask, col),
        )

    for mask in (3, 1, 2):
        hand_over(mask).start()
    gains_pad[pl.ds(0, 6)] = gains_in[...]
    gains_pad[pl.ds(6, 2)] = jnp.zeros((2, block), F32)
    for mask in (3, 1, 2):
        hand_gains(mask).start()
    x_own[:, my_cols] = x_in[row]
    gains[:, my_cols] = gains_pad[...]

    pair_cols = pl.ds(pl.multiple_of(col % 2 * key_width, key_width), key_width)
    pair = remote(
        w_kv, w_kv_pair.at[:, pair_cols], misc_send.at[7], misc_recv.at[7], (core, row, col ^ 1)
    )
    pair.start()
    w_kv_pair[:, pair_cols] = w_kv[...]

    def rows_of(array, source, buf, lane, split=by_rows, size=None):
        block_of, halves_of = split(buf, size)
        return RowGather(place, source, block_of, halves_of, row_sems.at[lane])

    core_head = pl.ds(pl.multiple_of(core * head_dim, head_dim), head_dim)
    core_ff = pl.ds(pl.multiple_of(core * ff_part, ff_part), ff_part)
    get_q = rows_of(0, w_query.at[:, core_head], vq, 0, by_rows, block)
    get_kv = rows_of(0, w_kv_pair, vkv, 1, by_rows, block)
    get_o = rows_of(0, w_out.at[core_head], vo, 2, by_cols, block)
    get_g = rows_of(0, w_gate.at[:, core_ff], vg, 3, by_rows, block)
    get_u = rows_of(0, w_up.at[:, core_ff], vu, 4, by_rows, block)
    get_d = rows_of(0, w_down.at[core_ff], vd, 5, by_cols, block)
    get_si = rows_of(0, small_in, vsi, 6, by_rows, block)
    get_so = rows_of(0, small_out, vso, 7, by_cols, block)
    get_q.start()
    pair.wait_recv()
    get_kv.start()
    get_o.start()

    for mask in (1, 2, 3):
        remote(
            x_in.at[row],
            x_own.at[:, pl.ds(pl.multiple_of((row ^ mask) * block, block), block)],
            misc_send.at[mask],
            misc_recv.at[mask],
            (core, row, col),
        ).wait_recv()
        remote(
            gains_pad,
            gains.at[:, pl.ds(pl.multiple_of((row ^ mask) * block, block), block)],
            misc_send.at[3 + mask],
            misc_recv.at[3 + mask],
            (core, row, col),
        ).wait_recv()

    def own_norm():
        values = x_own[...].astype(F32)
        factor = lax.rsqrt(jnp.mean(values * values, axis=1, keepdims=True) + EPSILON)
        return values, values * factor * gains[pl.ds(0, 1)]

    mine = pl.ds(pl.multiple_of((core * 4 + col) * own_tokens, own_tokens), own_tokens)
    xg[mine] = own_norm()[1].astype(BF)
    sems = lambda lane: (z_send.at[lane], z_recv.at[lane], s_send.at[lane], s_recv.at[lane])
    gather_x = Gather(place, xg, own_tokens, sems(0))
    gather_x.start()
    get_q.forward()
    get_kv.forward()
    get_o.forward()
    get_si.start()
    get_so.start()
    get_g.start()
    gather_x.forward()
    gather_x.finish()
    get_q.finish()
    get_kv.finish()

    raw_q[...] = mm(xg[...], vq[...])
    raw_kv[...] = mm(xg[...], vkv[...])
    q_low[...] = head_parts(raw_q[...], head_gains[pl.ds(0, 1)], cosine[...], sine[...]).astype(BF)
    is_key = core == 0
    kv_here = head_parts(
        raw_kv[...],
        jnp.where(is_key, head_gains[pl.ds(1, 1)], 1.0),
        jnp.where(is_key, cosine[...], 1.0),
        jnp.where(is_key, sine[...], 0.0),
    ).astype(BF)

    def kv_part(kind, which):
        return kv.at[kind, pl.ds(pl.multiple_of(which * tokens, tokens), tokens)]

    kv[core, pl.ds(pl.multiple_of(half * tokens, tokens), tokens)] = kv_here
    here = kv_part(core, half)
    to_x = remote(here, here, misc_send.at[8], misc_recv.at[8], (core, row ^ 1, col))
    to_s = remote(here, here, misc_send.at[9], misc_recv.at[9], (1 - core, row, col))
    to_x.start()
    to_s.start()
    came = kv_part(core, half ^ 1)
    remote(here, came, misc_send.at[8], misc_recv.at[8], (core, row, col)).wait_recv()
    on_s = remote(came, came, misc_send.at[10], misc_recv.at[10], (1 - core, row, col))
    on_s.start()
    other = kv_part(1 - core, half)
    remote(other, other, misc_send.at[9], misc_recv.at[9], (core, row, col)).wait_recv()
    other_came = kv_part(1 - core, half ^ 1)
    remote(other_came, other_came, misc_send.at[10], misc_recv.at[10], (core, row, col)).wait_recv()

    q_rows = 128
    key_token = lax.broadcasted_iota(jnp.int32, (1, 2 * tokens), 1)
    in_half = key_token % tokens
    key_place = in_half // own_tokens * chunk + key_token // tokens * own_tokens + in_half % own_tokens
    top[...] = jnp.full(top.shape, MASK_FILL, F32)

    def attend(step, carry):
        first = pl.multiple_of(step * q_rows, q_rows)
        rows = pl.ds(first, q_rows)
        token = first + lax.broadcasted_iota(jnp.int32, (q_rows, 1), 0)
        q_place = token // own_tokens * chunk + half * own_tokens + token % own_tokens
        allowed = (key_place <= q_place) & (key_place >= start[rows])
        scores = jnp.where(allowed, mm_nt(q_low[rows], kv[0]), MASK_FILL)
        row_top = jnp.max(scores, axis=1, keepdims=True)
        weights = jnp.exp(scores - row_top)
        total = jnp.sum(weights, axis=1, keepdims=True)
        probs = (weights * (1.0 / total)).astype(BF)
        o_low[rows] = mm(probs, kv[1]).astype(BF)
        lse[rows] = row_top + jnp.log(total)
        top[...] = jnp.maximum(top[...], jnp.max(row_top))
        return carry

    lax.fori_loop(0, tokens // q_rows, attend, 0)
    get_si.forward()
    get_so.forward()
    get_g.forward()
    get_u.start()
    get_o.finish()

    away = pl.multiple_of((1 - core) * 4 * own_tokens, 4 * own_tokens)
    home = pl.multiple_of(core * 4 * own_tokens, 4 * own_tokens)
    scatter = Scatter(place, own_tokens, (give, keep, got, sent, left, right), sems(1))

    def project(source, weights, target, first):
        def step(index, carry):
            cols = pl.ds(pl.multiple_of(index * block, block), block)
            value = mm(source[pl.ds(first, 4 * own_tokens)], weights[:, cols])
            target[:, cols] = value.astype(target.dtype)
            return carry

        lax.fori_loop(0, width // block, step, 0)

    project(o_low, vo, give, away)
    scatter.sibling().start()
    project(o_low, vo, keep, home)
    scatter.run(attn_val)

    get_si.finish()
    get_so.finish()
    inputs, x_norm = own_norm()
    attn_normed = rms(attn_val[...])[0]
    rank = lr_low.shape[1]
    lr_low[...] = mm(xg[mine], vsi[:, pl.ds(0, rank)]).astype(BF)
    lo_normed = rms(mm(lr_low[...], vso[pl.ds(0, rank)]))[0]
    h_two = (
        inputs + attn_normed * gains[pl.ds(1, 1)] + (x_norm + lo_normed * gains[pl.ds(2, 1)])
    ) * ROOT_HALF
    fg[mine] = (rms(h_two)[0] * gains[pl.ds(3, 1)]).astype(BF)
    gather_f = Gather(place, fg, own_tokens, sems(2))
    gather_f.start()
    get_u.forward()
    get_d.start()
    get_g.finish()
    gather_f.forward()
    gather_f.finish()
    get_u.finish()

    tile = 256

    def units(index, carry):
        cols = pl.ds(pl.multiple_of(index * tile, tile), tile)
        gate_part = mm(fg[...], vg[:, cols])
        gate[:, cols] = gate_part
        up_part = mm(fg[...], vu[:, cols])
        up[:, cols] = up_part
        hid[:, cols] = (gelu(gate_part) * up_part).astype(BF)
        return carry

    lax.fori_loop(0, ff_part // tile, units, 0)
    get_d.forward()
    keep_weights = [
        pltpu.make_async_copy(source, target, out_sems.at[lane])
        for lane, (source, target) in enumerate(
            [
                (vq, wq_all),
                (vkv, wkv_all),
                (vo, wo_all),
                (vg, wg_all),
                (vu, wu_all),
                (vd, wd_all),
                (vsi, si_all),
                (vso, so_all),
            ]
        )
    ]
    get_d.finish()
    for copy in keep_weights:
        copy.start()
    scatter_ff = Scatter(place, own_tokens, (give2, keep2, got2, sent2, left2, right2), sems(3))
    project(hid, vd, give2, away)
    scatter_ff.sibling().start()
    project(hid, vd, keep2, home)
    scatter_ff.run(ff_val)

    for mask in (1, 2, 3):
        hand_over(mask).wait_send()
        hand_gains(mask).wait_send()
    pair.wait_send()
    to_x.wait_send()
    to_s.wait_send()
    on_s.wait_send()
    for copy in keep_weights:
        copy.wait()


def run_forward(x_in, gains_in, w_query, w_kv, w_out, w_gate, w_up, w_down, small_in, small_out, tables, head_gains):
    cosine, sine, start = tables
    block = x_in.shape[2]
    own, width = x_in.shape[1], 4 * block
    tokens, head_dim, ff_part = 8 * own, head_gains.shape[1], w_gate.shape[1] // 2
    rank = small_in.shape[1] - small_out.shape[0]
    vm = pl.BlockSpec(memory_space=pltpu.VMEM)
    hbm = pl.BlockSpec(memory_space=pl.ANY)
    shape = jax.ShapeDtypeStruct
    weights = [
        (width, head_dim),
        (width, head_dim),
        (head_dim, width),
        (width, ff_part),
        (width, ff_part),
        (ff_part, width),
        (width, small_in.shape[1]),
        (small_out.shape[0], width),
    ]
    outs = [
        shape((own, width), BF),
        shape((8, width), F32),
        shape((tokens, width), BF),
        shape((tokens, head_dim), F32),
        shape((tokens, head_dim), F32),
        shape((tokens, head_dim), BF),
        shape((2, 2 * tokens, head_dim), BF),
        shape((tokens, 1), F32),
        shape((8, 128), F32),
        shape((tokens, head_dim), BF),
        shape((own, width), F32),
        shape((own, rank), BF),
        shape((tokens, width), BF),
        shape((tokens, ff_part), F32),
        shape((tokens, ff_part), F32),
        shape((tokens, ff_part), BF),
        shape((own, width), F32),
    ] + [shape(size, BF) for size in weights]
    scatter_bufs = [
        pltpu.VMEM((4 * own, width), BF),
        pltpu.VMEM((4 * own, width), F32),
        pltpu.VMEM((4 * own, width), BF),
        pltpu.VMEM((4, own, width), BF),
        pltpu.VMEM((4, own, width), BF),
        pltpu.VMEM((4, own, width), BF),
    ]
    dma = pltpu.SemaphoreType.DMA
    return pl.pallas_call(
        forward_kernel,
        out_shape=outs,
        in_specs=[vm, vm, hbm, vm, hbm, hbm, hbm, hbm, hbm, hbm, vm, vm, vm, vm],
        out_specs=[vm] * 17 + [hbm] * 8,
        scratch_shapes=[pltpu.VMEM((block, head_dim), BF), pltpu.VMEM((8, block), F32)]
        + [pltpu.VMEM(size, BF) for size in weights]
        + scatter_bufs * 2
        + [
            dma((8, 10)),
            dma((4, 8)),
            dma((4, 8)),
            dma((4, 4)),
            dma((4, 4)),
            dma((12,)),
            dma((12,)),
            dma((8,)),
        ],
        compiler_params=pltpu.CompilerParams(
            collective_id=0, has_side_effects=True, vmem_limit_bytes=60 * 2**20
        ),
        cost_estimate=pl.CostEstimate(flops=2 * 10**10, bytes_accessed=5 * 10**7, transcendentals=10**6),
    )(x_in, gains_in, w_query, w_kv, w_out, w_gate, w_up, w_down, small_in, small_out, cosine, sine, start, head_gains)


def body_pair(
    layer_in,
    per_layer_in,
    doc_lengths,
    w_query,
    w_key,
    w_value,
    w_out,
    w_gate,
    w_up,
    w_down,
    laurel_left,
    laurel_right,
    per_gate,
    per_proj,
    norm_gains,
    head_gains,
    out_grad,
):
    core, row, col = lax.axis_index("seq"), lax.axis_index("row"), lax.axis_index("col")
    rows, cols, cores = lax.axis_size("row"), lax.axis_size("col"), lax.axis_size("seq")
    seq_count = layer_in.shape[0]
    head_dim = head_gains.shape[1]
    key_width = w_key.shape[1]
    ff_part = w_gate.shape[1] // cores
    chunk = layer_in.shape[1]
    halves = rows // seq_count
    own_tokens = chunk // halves
    group_tokens = own_tokens * cores * cols
    even_col = col % 2 == 0

    lengths = doc_lengths[row // halves]
    count = doc_lengths.shape[1]
    upto = jnp.tril(jnp.ones((count, count), jnp.int32))
    doc_ends = jnp.sum(lengths[None, :] * upto, axis=1)

    def places_of(half):
        token = jnp.arange(group_tokens, dtype=jnp.int32)
        place = token // own_tokens * chunk + half * own_tokens + token % own_tokens
        before = (doc_ends[None, :] <= place[:, None]).astype(jnp.int32)
        start = jnp.sum(before * lengths[None, :], axis=1)
        return place, start

    half = row % halves
    place, start = places_of(half)
    other_place, other_start = places_of(half ^ 1)
    key_place = jnp.stack([place, other_place])[jnp.array([0, 1]) ^ half].reshape(-1)
    allowed = (key_place[None, :] <= place[:, None]) & (key_place[None, :] >= start[:, None])
    cosine_table, sine_table = rotation(place - start, head_dim)

    w_kv = jnp.where(core == 0, w_key, w_value)
    rank = laurel_left.shape[1]
    small_in = jnp.concatenate(
        [laurel_left, jnp.zeros((laurel_left.shape[0], rank), BF), per_gate], axis=1
    )
    small_out = jnp.concatenate([laurel_right, per_proj], axis=0)
    (
        x_own,
        gains,
        x_all,
        raw_q,
        raw_kv,
        q_low,
        kv,
        lse,
        top_tile,
        o_low,
        attn_val,
        lr_low,
        f_all,
        gate_val,
        up_val,
        hid_low,
        ff_val,
        w_q,
        w_kv_all,
        w_o,
        w_g,
        w_u,
        w_d,
        small_in_all,
        small_out_all,
    ) = run_forward(
        layer_in.reshape(rows, own_tokens, -1),
        norm_gains,
        w_query,
        w_kv,
        w_out,
        w_gate,
        w_up,
        w_down,
        small_in,
        small_out,
        (
            cosine_table[:, : head_dim // 2],
            sine_table[:, : head_dim // 2],
            start[:, None],
        ),
        head_gains,
    )
    w_gu = jnp.concatenate([w_g, w_u], axis=1)
    l_left, p_gate = small_in_all[:, :rank], small_in_all[:, 2 * rank :]
    l_right, p_proj = small_out_all[:rank], small_out_all[rank:]
    inputs = x_own.astype(jnp.float32)
    grad_top = to_owner(out_grad).astype(jnp.float32)
    per_input = per_layer_in.reshape(rows, own_tokens, -1)[row].astype(jnp.float32)
    x_normed, x_factor = rms(inputs)
    x_norm = x_normed * gains[0]
    x_low = x_norm.astype(jnp.bfloat16)

    def head_prep(raw_part, gain_vec):
        return rotate(head_norm(raw_part, gain_vec), cosine_table, sine_table)

    other_kv = swapped(raw_kv, "seq", 0)
    raw_k = jnp.where(core == 0, raw_kv, other_kv)
    raw_v = jnp.where(core == 0, other_kv, raw_kv)
    other_w = swapped(w_kv_all, "seq", 0)
    w_heads = jnp.concatenate(
        [w_q, jnp.where(core == 0, w_kv_all, other_w), jnp.where(core == 0, other_w, w_kv_all)], axis=1
    )
    q_rot, query_back = jax.vjp(head_prep, raw_q, head_gains[0])
    k_rot, key_back = jax.vjp(head_prep, raw_k, head_gains[1])
    v_rot, value_back = jax.vjp(lambda part: head_norm(part, 1.0), raw_v)
    keys, values = kv[0], kv[1]
    scores = jnp.where(allowed, mm_nt(q_low, keys), MASK_FILL)
    probs = jnp.exp(scores - lse)
    probs_low = probs.astype(jnp.bfloat16)
    attn_normed, attn_factor = rms(attn_val)
    lo_normed, lo_factor = rms(mm(lr_low, l_right))
    h_two = (inputs + attn_normed * gains[1] + (x_norm + lo_normed * gains[2])) * ROOT_HALF
    f_normed, f_factor = rms(h_two)

    def geglu(gate_part, up_part):
        return jax.nn.gelu(gate_part, approximate=True) * up_part

    hidden, geglu_back = jax.vjp(geglu, gate_val, up_val)
    ff_normed, ff_factor = rms(ff_val)
    h_three = h_two + ff_normed * gains[4]
    h_low = h_three.astype(jnp.bfloat16)

    def per_mix(gate_part):
        return jax.nn.gelu(gate_part, approximate=True) * per_input

    gp_val, per_back = jax.vjp(per_mix, mm(h_low, p_gate))
    gp_low = gp_val.astype(jnp.bfloat16)
    pp_normed, pp_factor = rms(mm(gp_low, p_proj))
    layer_out = from_owner((h_three + pp_normed * gains[5]).astype(jnp.bfloat16), seq_count)

    d_pp, gain_five = rms_back(grad_top, pp_normed, pp_factor, gains[5])
    d_pp_low = d_pp.astype(jnp.bfloat16)
    g_per_proj = mm_tn(gp_low, d_pp_low)
    (d_pg,) = per_back(mm_nt(d_pp_low, p_proj))
    d_pg_low = d_pg.astype(jnp.bfloat16)
    g_per_gate = mm_tn(h_low, d_pg_low)
    d_three = grad_top + mm_nt(d_pg_low, p_gate)
    d_ff, gain_four = rms_back(d_three, ff_normed, ff_factor, gains[4])
    d_ff_all = group_gather(d_ff.astype(jnp.bfloat16))
    d_hidden = mm_nt(d_ff_all, w_d)
    d_gate, d_up = geglu_back(d_hidden)
    d_gu = jnp.concatenate([d_gate, d_up], axis=1).astype(jnp.bfloat16)
    d_f = group_scatter(mm_nt(d_gu, w_gu))
    g_down = both_cores(scatter_rows(mm_tn(hid_low, d_ff_all), 1), 0)
    g_gu = scatter_rows(mm_tn(f_all, d_gu), 0)
    g_gate, g_up = both_cores(g_gu[:, :ff_part], 1), both_cores(g_gu[:, ff_part:], 1)
    d_f, gain_three = rms_back(d_f, f_normed, f_factor, gains[3])
    d_half = (d_three + d_f) * ROOT_HALF
    d_lo, gain_two = rms_back(d_half, lo_normed, lo_factor, gains[2])
    d_attn, gain_one = rms_back(d_half, attn_normed, attn_factor, gains[1])
    d_attn_all = group_gather(d_attn.astype(jnp.bfloat16))
    d_lo_low = d_lo.astype(jnp.bfloat16)
    g_right = mm_tn(lr_low, d_lo_low)
    d_lr_low = mm_nt(d_lo_low, l_right).astype(jnp.bfloat16)
    g_left = mm_tn(x_low, d_lr_low)

    d_o_low = mm_nt(d_attn_all, w_o).astype(jnp.bfloat16)
    g_out = both_cores(scatter_rows(mm_tn(o_low, d_attn_all), 1), 0)
    d_probs = mm_nt(d_o_low, values)
    delta = jnp.sum(probs * d_probs, axis=1, keepdims=True)
    d_scores = (probs * (d_probs - delta)).astype(jnp.bfloat16)
    d_query = mm(d_scores, keys)
    d_kv = jnp.concatenate([mm_tn(d_scores, q_low), mm_tn(probs_low, d_o_low)], axis=1)
    d_kv = d_kv.reshape(2, group_tokens, -1)
    d_kv = d_kv[half] + swapped(d_kv[half ^ 1], "row", 0)
    d_kv = lax.psum(d_kv, "seq")
    d_kv = d_kv + swapped(d_kv, "col", 0)
    d_q_raw, d_q_gain = query_back(d_query)
    d_k_raw, d_k_gain = key_back(d_kv[:, :head_dim])
    (d_v_raw,) = value_back(d_kv[:, head_dim:])
    d_kv_low = jnp.concatenate([d_k_raw, d_v_raw], axis=1).astype(jnp.bfloat16)
    kv_offset = core * head_dim + col % 2 * key_width
    d_heads = jnp.concatenate(
        [
            d_q_raw.astype(jnp.bfloat16),
            lax.dynamic_slice_in_dim(d_kv_low, kv_offset, key_width, 1),
        ],
        axis=1,
    )
    w_back = jnp.concatenate(
        [
            w_heads[:, :head_dim],
            lax.dynamic_slice_in_dim(w_heads, head_dim + kv_offset, key_width, 1),
        ],
        axis=1,
    )
    d_xn = group_scatter(mm_nt(d_heads, w_back)) + mm_nt(d_lr_low, l_left)
    g_heads = scatter_rows(mm_tn(x_all, d_heads), 0)
    g_query = both_cores(g_heads[:, :head_dim], 1)
    g_kv = both_cores(g_heads[:, head_dim:], 1)
    d_in, gain_zero = rms_back(d_half + d_xn, x_normed, x_factor, gains[0])
    grad_in = from_owner((d_half + d_in).astype(jnp.bfloat16), seq_count)

    g_gains = jnp.concatenate(
        [gain_zero, gain_one, gain_two, gain_three, gain_four, gain_five], axis=0
    )
    g_small_in = lax.psum_scatter(
        jnp.concatenate([g_left, g_per_gate], axis=1), "row", scatter_dimension=0, tiled=True
    )
    g_small_out = lax.psum_scatter(
        jnp.concatenate([g_right, g_per_proj, g_gains], axis=0),
        "row",
        scatter_dimension=1,
        tiled=True,
    )
    g_small_in, g_small_out = lax.psum((g_small_in, g_small_out), ("seq", "col"))
    g_head_gains = lax.psum(jnp.stack([d_q_gain, d_k_gain * 0.25]), ("seq", "row", "col"))
    top = lax.pmax(top_tile[0, 0], "row")
    tops = lax.all_gather(top, ("seq", "col"))
    logit_top = tops.reshape(cores, cols).T.reshape(-1)
    clip_factor = jnp.sqrt(CLIP_LEVEL / jnp.maximum(logit_top, CLIP_LEVEL))
    clipped_gains = clip_factor[None, :, None] * head_gains[:, None, :]
    proj_rows = rank + per_proj.shape[0]
    return (
        layer_out,
        grad_in,
        g_query,
        g_kv[:, :key_width],
        g_kv[:, key_width:],
        g_out,
        g_gate,
        g_up,
        g_down,
        g_small_in[:, :rank],
        g_small_out[:rank],
        g_small_in[:, rank:],
        g_small_out[rank:proj_rows],
        g_small_out[proj_rows:],
        g_head_gains,
        clipped_gains,
    )


def solution(mesh):
    sizes = tuple(mesh.shape[axis] for axis in ("seq", "row", "col"))
    body = body_pair if sizes == (2, 4, 4) else body_any
    return jax.shard_map(
        body,
        mesh=mesh,
        in_specs=(
            P(None, ("seq", "col"), "row"),
            P(None, ("seq", "col"), None),
            P(),
            P("row", "col"),
            P("row", "col"),
            P("row", "col"),
            P("col", "row"),
            P("row", "col"),
            P("row", "col"),
            P("col", "row"),
            P("row", None),
            P(None, "row"),
            P("row", None),
            P(None, "row"),
            P(None, "row"),
            P(),
            P(None, ("seq", "col"), "row"),
        ),
        out_specs=(
            P(None, ("seq", "col"), "row"),
            P(None, ("seq", "col"), "row"),
            P("row", "col"),
            P("row", "col"),
            P("row", "col"),
            P("col", "row"),
            P("row", "col"),
            P("row", "col"),
            P("col", "row"),
            P("row", None),
            P(None, "row"),
            P("row", None),
            P(None, "row"),
            P(None, "row"),
            P(),
            P(),
        ),
        check_vma=False,
    )
```

```python
import functools

import jax
import jax.numpy as jnp
from jax import lax
from jax.experimental import pallas as pl
from jax.experimental.pallas import tpu as pltpu
from jax.sharding import PartitionSpec as P

EPSILON = 1e-06
CLIP_LEVEL = 3.0
ROPE_BASE = 1000000.0
ROOT_HALF = 0.7071067811865476
MASK_FILL = -1e30
MESH = pl.DeviceIdType.MESH
BF = jnp.bfloat16
F32 = jnp.float32
VMEM_BYTES = 63 * 2**20


def swapped(value, axis, apart):
    mask = 2**apart
    pairs = [(source, source ^ mask) for source in range(lax.axis_size(axis))]
    return lax.ppermute(value, axis, pairs)


def width_total(values):
    return lax.psum(values, "row")


def gather_tokens(values):
    return lax.all_gather(values, "col", axis=1, tiled=True)


def spread_rows(values, project):
    gathered = gather_tokens(values)
    return (gathered, lax.psum_scatter(project(gathered), "row", scatter_dimension=1, tiled=True))


def spread_cols(values, project):
    gathered = lax.all_gather(values, "row", axis=1, tiled=True)
    return (gathered, lax.psum_scatter(project(gathered), "col", scatter_dimension=1, tiled=True))


def times_right(left_side, right_side):
    return jnp.einsum("std,dn->stn", left_side, right_side, preferred_element_type=jnp.float32)


def times_back(left_side, right_side):
    return jnp.einsum("stn,dn->std", left_side, right_side, preferred_element_type=jnp.float32)


def outer_sum(left_side, right_side):
    return jnp.einsum("std,stn->dn", left_side, right_side, preferred_element_type=jnp.float32)


def norm_forward(values, gain_vec, width_all):
    square_sum = width_total(jnp.sum(values * values, axis=-1, keepdims=True))
    factor = lax.rsqrt(square_sum / width_all + EPSILON)
    normed = values * factor
    return (normed * gain_vec, normed, factor)


def norm_backward(grad_values, normed, factor, gain_vec, width_all):
    grad_normed = grad_values * gain_vec
    inner_sum = width_total(jnp.sum(grad_normed * normed, axis=-1, keepdims=True))
    result = factor * (grad_normed - normed * (inner_sum / width_all))
    return (result, jnp.sum(grad_values * normed, axis=(0, 1)))


def head_norm(values, gain_vec):
    return (
        values * lax.rsqrt(jnp.mean(values * values, axis=-1, keepdims=True) + EPSILON) * gain_vec
    )


def rotation(position, width_all):
    half_width = width_all // 2
    frequency = ROPE_BASE ** (-2.0 * jnp.arange(half_width, dtype=jnp.float32) / width_all)
    angles = position.astype(jnp.float32)[..., None] * frequency
    cosine_table = jnp.concatenate([jnp.cos(angles), jnp.cos(angles)], axis=-1)
    sine_table = jnp.concatenate([jnp.sin(angles), jnp.sin(angles)], axis=-1)
    return (cosine_table, sine_table)


def rotate(values, cosine_table, sine_table):
    half_width = values.shape[-1] // 2
    turned = jnp.concatenate([-values[..., half_width:], values[..., :half_width]], axis=-1)
    return values * cosine_table + turned * sine_table


def doc_places(doc_lengths, first_place, place_count):
    upto = jnp.tril(jnp.ones((doc_lengths.shape[1], doc_lengths.shape[1]), jnp.int32))
    doc_ends = jnp.sum(doc_lengths[:, None, :] * upto[None], axis=2)
    places = first_place + jnp.arange(place_count, dtype=jnp.int32)
    before = (doc_ends[:, None, :] <= places[None, :, None]).astype(jnp.int32)
    segment = jnp.sum(before, axis=2)
    doc_start = jnp.sum(before * doc_lengths[:, None, :], axis=2)
    return (segment, places, places[None, :] - doc_start)


def block_scores(queries, keys_all, block_start, block_size, query_seg, query_place, key_seg):
    keys_part = lax.dynamic_slice_in_dim(keys_all, block_start, block_size, 1)
    scores = jnp.einsum("sqhd,skd->shqk", queries, keys_part, preferred_element_type=jnp.float32)
    seg_part = lax.dynamic_slice_in_dim(key_seg, block_start, block_size, 1)
    key_place = block_start + jnp.arange(block_size, dtype=jnp.int32)
    allowed = (query_seg[:, None, :, None] == seg_part[:, None, None, :]) & (
        key_place[None, None, None, :] <= query_place[None, None, :, None]
    )
    return (scores, allowed)


def body_any(
    layer_in,
    per_layer_in,
    doc_lengths,
    w_query,
    w_key,
    w_value,
    w_out,
    w_gate,
    w_up,
    w_down,
    laurel_left,
    laurel_right,
    per_gate,
    per_proj,
    norm_gains,
    head_gains,
    out_grad,
):
    seq_count = layer_in.shape[0]
    width_all = layer_in.shape[2] * lax.axis_size("row")
    head_dim = head_gains.shape[1]
    heads_here = w_query.shape[1] // head_dim
    heads_all = heads_here * lax.axis_size("col")
    key_width = w_key.shape[1]
    ff_here = w_gate.shape[1]
    local_len = layer_in.shape[1] * lax.axis_size("col")
    tokens_row = local_len // lax.axis_size("row")
    seq_len = local_len * lax.axis_size("seq")
    col_index = lax.axis_index("col")
    even_col = col_index % 2 == 0
    q_width = heads_here * head_dim
    partner_key, partner_value = swapped((w_key, w_value), "col", 0)
    key_head = jnp.where(
        even_col,
        jnp.concatenate([w_key, partner_key], axis=1),
        jnp.concatenate([partner_key, w_key], axis=1),
    )
    value_head = jnp.where(
        even_col,
        jnp.concatenate([w_value, partner_value], axis=1),
        jnp.concatenate([partner_value, w_value], axis=1),
    )
    w_heads = jnp.concatenate([w_query, key_head, value_head], axis=1)
    w_back = jnp.concatenate([w_query, w_key, w_value], axis=1)
    w_gate_up = jnp.concatenate([w_gate, w_up], axis=1)
    inputs = layer_in.astype(jnp.float32)
    x_norm, x_normed, x_factor = norm_forward(inputs, norm_gains[0], width_all)
    x_low = x_norm.astype(jnp.bfloat16)
    x_rows, head_raw = spread_rows(x_low, lambda gathered: times_right(gathered, w_heads))
    q_raw = head_raw[:, :, :q_width].reshape(seq_count, tokens_row, heads_here, head_dim)
    k_raw = head_raw[:, :, q_width : q_width + head_dim]
    v_raw = head_raw[:, :, q_width + head_dim :]
    query_seg, query_place, query_pos = doc_places(
        doc_lengths, lax.axis_index(("seq", "row")) * tokens_row, tokens_row
    )
    key_seg, unused_place, unused_pos = doc_places(doc_lengths, 0, seq_len)
    cosine_table, sine_table = rotation(query_pos, head_dim)

    def query_prep(raw_part, gain_vec):
        return rotate(
            head_norm(raw_part, gain_vec), cosine_table[:, :, None], sine_table[:, :, None]
        )

    def key_prep(raw_part, gain_vec):
        return rotate(head_norm(raw_part, gain_vec), cosine_table, sine_table)

    def value_prep(raw_part):
        return head_norm(raw_part, 1.0)

    q_rot, query_back = jax.vjp(query_prep, q_raw, head_gains[0])
    k_rot, key_back = jax.vjp(key_prep, k_raw, head_gains[1])
    v_normed, value_back = jax.vjp(value_prep, v_raw)
    q_low = q_rot.astype(jnp.bfloat16)
    keys_all, values_all = (
        lax.all_gather(k_rot.astype(jnp.bfloat16), ("seq", "row"), axis=1, tiled=True),
        lax.all_gather(v_normed.astype(jnp.bfloat16), ("seq", "row"), axis=1, tiled=True),
    )
    block_size = min(512, seq_len)
    block_count = seq_len // block_size
    blocks = jnp.arange(block_count, dtype=jnp.int32)

    def scored(block_index):
        return block_scores(
            q_low, keys_all, block_index * block_size, block_size, query_seg, query_place, key_seg
        )

    def values_at(block_index):
        return lax.dynamic_slice_in_dim(values_all, block_index * block_size, block_size, 1)

    def stats_step(carry, block_index):
        row_top, row_total = carry
        scores, allowed = scored(block_index)
        new_top = jnp.maximum(row_top, jnp.max(jnp.where(allowed, scores, MASK_FILL), axis=3))
        weights = jnp.where(allowed, jnp.exp(scores - new_top[..., None]), 0.0)
        row_total = row_total * jnp.exp(row_top - new_top) + jnp.sum(weights, axis=3)
        return ((new_top, row_total), None)

    start_top = jnp.full((seq_count, heads_here, tokens_row), MASK_FILL, jnp.float32)
    (row_top, row_total), unused = lax.scan(
        stats_step, (start_top, jnp.zeros_like(start_top)), blocks
    )
    log_total = row_top + jnp.log(row_total)

    def probs_at(block_index):
        scores, allowed = scored(block_index)
        return jnp.where(allowed, jnp.exp(scores - log_total[..., None]), 0.0)

    def out_step(total_out, block_index):
        probs_low = probs_at(block_index).astype(jnp.bfloat16)
        total_out = total_out + jnp.einsum(
            "shqk,skd->sqhd", probs_low, values_at(block_index), preferred_element_type=jnp.float32
        )
        return (total_out, None)

    attended, unused = lax.scan(
        out_step, jnp.zeros((seq_count, tokens_row, heads_here, head_dim), jnp.float32), blocks
    )
    o_low = attended.astype(jnp.bfloat16).reshape(seq_count, tokens_row, q_width)
    head_slots = lax.dynamic_update_slice_in_dim(
        jnp.full((heads_all,), MASK_FILL, jnp.float32),
        jnp.max(row_top, axis=(0, 2)),
        col_index * heads_here,
        0,
    )
    logit_top = lax.pmax(head_slots, ("seq", "row", "col"))
    o_rows, attn_val = spread_cols(o_low, lambda gathered: times_right(gathered, w_out))
    attn_norm, attn_normed, attn_factor = norm_forward(attn_val, norm_gains[1], width_all)
    h_one = inputs + attn_norm
    lr_low = width_total(times_right(x_low, laurel_left)).astype(jnp.bfloat16)
    lo_val = times_right(lr_low, laurel_right)
    lo_norm, lo_normed, lo_factor = norm_forward(lo_val, norm_gains[2], width_all)
    h_two = (h_one + (x_norm + lo_norm)) * ROOT_HALF
    f_norm, f_normed, f_factor = norm_forward(h_two, norm_gains[3], width_all)
    f_low = f_norm.astype(jnp.bfloat16)
    f_rows, gate_up = spread_rows(f_low, lambda gathered: times_right(gathered, w_gate_up))
    gate_val = gate_up[:, :, :ff_here]
    up_val = gate_up[:, :, ff_here:]

    def geglu(gate_part, up_part):
        return jax.nn.gelu(gate_part, approximate=True) * up_part

    hidden, geglu_back = jax.vjp(geglu, gate_val, up_val)
    hid_low = hidden.astype(jnp.bfloat16)
    hid_rows, ff_val = spread_cols(hid_low, lambda gathered: times_right(gathered, w_down))
    ff_norm, ff_normed, ff_factor = norm_forward(ff_val, norm_gains[4], width_all)
    h_three = h_two + ff_norm
    h_low = h_three.astype(jnp.bfloat16)
    pg_val = width_total(times_right(h_low, per_gate))
    per_input = per_layer_in.astype(jnp.float32)

    def per_mix(gate_part):
        return jax.nn.gelu(gate_part, approximate=True) * per_input

    gp_val, per_back = jax.vjp(per_mix, pg_val)
    gp_low = gp_val.astype(jnp.bfloat16)
    pp_val = times_right(gp_low, per_proj)
    pp_norm, pp_normed, pp_factor = norm_forward(pp_val, norm_gains[5], width_all)
    layer_out = (h_three + pp_norm).astype(jnp.bfloat16)
    grad_top = out_grad.astype(jnp.float32)
    d_pp, gain_five = norm_backward(grad_top, pp_normed, pp_factor, norm_gains[5], width_all)
    d_pp_low = d_pp.astype(jnp.bfloat16)
    grad_per_proj = outer_sum(gp_low, d_pp_low)
    (d_pg,) = per_back(width_total(times_back(d_pp_low, per_proj)))
    d_pg_low = d_pg.astype(jnp.bfloat16)
    grad_per_gate = outer_sum(h_low, d_pg_low)
    d_three = grad_top + times_back(d_pg_low, per_gate)
    d_ff, gain_four = norm_backward(d_three, ff_normed, ff_factor, norm_gains[4], width_all)
    d_ff_low = d_ff.astype(jnp.bfloat16)
    dff_rows, d_hidden = spread_rows(d_ff_low, lambda gathered: times_back(gathered, w_down))
    grad_down = outer_sum(hid_rows, dff_rows)
    d_gate, d_up = geglu_back(d_hidden)
    d_gate_up = jnp.concatenate([d_gate, d_up], axis=2).astype(jnp.bfloat16)
    dgu_rows, d_f_low = spread_cols(d_gate_up, lambda gathered: times_back(gathered, w_gate_up))
    grad_gate_up = outer_sum(f_rows, dgu_rows)
    d_f, gain_three = norm_backward(d_f_low, f_normed, f_factor, norm_gains[3], width_all)
    d_half = (d_three + d_f) * ROOT_HALF
    d_lo, gain_two = norm_backward(d_half, lo_normed, lo_factor, norm_gains[2], width_all)
    d_lo_low = d_lo.astype(jnp.bfloat16)
    grad_laurel_right = outer_sum(lr_low, d_lo_low)
    d_lr_low = width_total(times_back(d_lo_low, laurel_right)).astype(jnp.bfloat16)
    grad_laurel_left = outer_sum(x_low, d_lr_low)
    d_attn, gain_one = norm_backward(d_half, attn_normed, attn_factor, norm_gains[1], width_all)
    d_attn_low = d_attn.astype(jnp.bfloat16)
    dattn_rows, d_o = spread_rows(d_attn_low, lambda gathered: times_back(gathered, w_out))
    grad_w_out = outer_sum(o_rows, dattn_rows)
    d_o_low = d_o.astype(jnp.bfloat16).reshape(seq_count, tokens_row, heads_here, head_dim)

    def delta_step(total_delta, block_index):
        d_probs = jnp.einsum(
            "sqhd,skd->shqk", d_o_low, values_at(block_index), preferred_element_type=jnp.float32
        )
        return (total_delta + jnp.sum(probs_at(block_index) * d_probs, axis=3), None)

    row_delta, unused = lax.scan(delta_step, jnp.zeros_like(log_total), blocks)

    def grad_step(carry, block_index):
        d_query, d_keys, d_values = carry
        block_start = block_index * block_size
        prob_vals = probs_at(block_index)
        d_probs = jnp.einsum(
            "sqhd,skd->shqk", d_o_low, values_at(block_index), preferred_element_type=jnp.float32
        )
        d_scores = (prob_vals * (d_probs - row_delta[..., None])).astype(jnp.bfloat16)
        keys_part = lax.dynamic_slice_in_dim(keys_all, block_start, block_size, 1)
        d_query = d_query + jnp.einsum(
            "shqk,skd->sqhd", d_scores, keys_part, preferred_element_type=jnp.float32
        )
        key_part = jnp.einsum("shqk,sqhd->skd", d_scores, q_low, preferred_element_type=jnp.float32)
        value_part = jnp.einsum(
            "shqk,sqhd->skd",
            prob_vals.astype(jnp.bfloat16),
            d_o_low,
            preferred_element_type=jnp.float32,
        )
        d_keys = lax.dynamic_update_slice_in_dim(d_keys, key_part, block_start, 1)
        d_values = lax.dynamic_update_slice_in_dim(d_values, value_part, block_start, 1)
        return ((d_query, d_keys, d_values), None)

    zero_keys = jnp.zeros((seq_count, seq_len, head_dim), jnp.float32)
    (d_query, d_keys, d_values), unused = lax.scan(
        grad_step, (jnp.zeros_like(attended), zero_keys, zero_keys), blocks
    )
    own_keys, own_values = (
        lax.psum_scatter(d_keys, ("seq", "row"), scatter_dimension=1, tiled=True),
        lax.psum_scatter(d_values, ("seq", "row"), scatter_dimension=1, tiled=True),
    )
    pair_keys, pair_values = swapped((own_keys, own_values), "col", 0)
    d_q_raw, d_q_gain = query_back(d_query)
    d_k_raw, d_k_gain = key_back(own_keys + pair_keys)
    (d_v_raw,) = value_back(own_values + pair_values)
    key_offset = col_index % 2 * key_width
    d_heads_low = jnp.concatenate(
        [
            d_q_raw.reshape(seq_count, tokens_row, q_width),
            lax.dynamic_slice_in_dim(d_k_raw, key_offset, key_width, 2),
            lax.dynamic_slice_in_dim(d_v_raw, key_offset, key_width, 2),
        ],
        axis=2,
    ).astype(jnp.bfloat16)
    dhead_rows, d_x_heads = spread_cols(d_heads_low, lambda gathered: times_back(gathered, w_back))
    grad_heads = outer_sum(x_rows, dhead_rows)
    d_x_low = d_x_heads + times_back(d_lr_low, laurel_left)
    d_x_part, gain_zero = norm_backward(
        d_half + d_x_low, x_normed, x_factor, norm_gains[0], width_all
    )
    grad_in = (d_half + d_x_part).astype(jnp.bfloat16)
    head_part = width_total(jnp.stack([d_q_gain, d_k_gain * 0.5]))
    sum_heads, sum_out, sum_gate_up, sum_down = lax.psum(
        (grad_heads, grad_w_out, grad_gate_up, grad_down), "seq"
    )
    sum_left, sum_right, sum_per_gate, sum_per_proj, sum_gains, sum_head_gains = lax.psum(
        (
            grad_laurel_left,
            grad_laurel_right,
            grad_per_gate,
            grad_per_proj,
            jnp.stack([gain_zero, gain_one, gain_two, gain_three, gain_four, gain_five]),
            head_part,
        ),
        ("seq", "col"),
    )
    clip_factor = jnp.sqrt(CLIP_LEVEL / jnp.maximum(logit_top, CLIP_LEVEL))
    clipped_gains = jnp.stack(
        [
            clip_factor[:, None] * head_gains[0][None, :],
            clip_factor[:, None] * head_gains[1][None, :],
        ]
    )
    return (
        layer_out,
        grad_in,
        sum_heads[:, :q_width],
        sum_heads[:, q_width : q_width + key_width],
        sum_heads[:, q_width + key_width :],
        sum_out,
        sum_gate_up[:, :ff_here],
        sum_gate_up[:, ff_here:],
        sum_down,
        sum_left,
        sum_right,
        sum_per_gate,
        sum_per_proj,
        sum_gains,
        sum_head_gains,
        clipped_gains,
    )


def group_gather(values):
    return lax.all_gather(values, ("seq", "col"), axis=0, tiled=True)


def group_scatter(partial):
    return lax.psum_scatter(
        partial.astype(jnp.bfloat16), ("seq", "col"), scatter_dimension=0, tiled=True
    ).astype(jnp.float32)


def to_owner(values):
    seq_count, tokens, width = values.shape
    rows = lax.axis_size("row")
    parts = values.reshape(rows, seq_count * tokens // rows, width)
    moved = lax.all_to_all(parts, "row", split_axis=0, concat_axis=0)
    return moved.transpose(1, 0, 2).reshape(parts.shape[1], rows * width)


def from_owner(values, seq_count):
    tokens, width = values.shape
    rows = lax.axis_size("row")
    parts = values.reshape(tokens, rows, width // rows).transpose(1, 0, 2)
    moved = lax.all_to_all(parts, "row", split_axis=0, concat_axis=0)
    return moved.reshape(seq_count, rows * tokens // seq_count, width // rows)


def mm(left_side, right_side):
    return jnp.dot(left_side, right_side, preferred_element_type=jnp.float32)


def mm_nt(left_side, right_side):
    return lax.dot_general(
        left_side, right_side, (((1,), (1,)), ((), ())), preferred_element_type=jnp.float32
    )


def mm_tn(left_side, right_side):
    return lax.dot_general(
        left_side, right_side, (((0,), (0,)), ((), ())), preferred_element_type=jnp.float32
    )


def rms(values):
    factor = lax.rsqrt(jnp.mean(values * values, axis=-1, keepdims=True) + EPSILON)
    return values * factor, factor


def rms_back(grad_values, normed, factor, gain_vec):
    grad_normed = grad_values * gain_vec
    inner = jnp.mean(grad_normed * normed, axis=-1, keepdims=True)
    return (
        factor * (grad_normed - normed * inner),
        jnp.sum(grad_values * normed, axis=0, keepdims=True),
    )


def gather_rows(values, axis):
    return lax.all_gather(values, "row", axis=axis, tiled=True)


def scatter_rows(values, axis):
    return lax.psum_scatter(
        values.astype(jnp.bfloat16), "row", scatter_dimension=axis, tiled=True
    ).astype(jnp.float32)


def both_cores(values, axis):
    return lax.all_gather(values, "seq", axis=axis, tiled=True)


def remote(src, dst, send_sem, recv_sem, device):
    return pltpu.make_async_remote_copy(
        src_ref=src,
        dst_ref=dst,
        send_sem=send_sem,
        recv_sem=recv_sem,
        device_id=device,
        device_id_type=MESH,
    )


def greet(core, row, col):
    barrier = pltpu.get_barrier_semaphore()
    near = [(core, row ^ 1, col), (core, row ^ 2, col), (core, row ^ 3, col), (1 - core, row, col)]
    for device in near:
        pl.semaphore_signal(barrier, inc=1, device_id=device, device_id_type=MESH)

    @pl.when(col > 0)
    def _():
        pl.semaphore_signal(barrier, inc=1, device_id=(core, row, col - 1), device_id_type=MESH)

    @pl.when(col < 3)
    def _():
        pl.semaphore_signal(barrier, inc=1, device_id=(core, row, col + 1), device_id_type=MESH)

    ends = jnp.where((col == 0) | (col == 3), 1, 2)
    pl.semaphore_wait(barrier, 4 + ends)


class Gather:
    def __init__(self, place, buf, rows, sems):
        self.core, self.row, self.col = place
        self.buf, self.rows = buf, rows
        self.send_z, self.recv_z, self.send_s, self.recv_s = sems

    def part(self, core, col):
        return self.buf.at[pl.ds(pl.multiple_of((core * 4 + col) * self.rows, self.rows), self.rows)]

    def to_right(self, dist):
        part = self.part(self.core, self.col - dist)
        return remote(
            part, part, self.send_z.at[dist], self.recv_z.at[dist], (self.core, self.row, self.col + 1)
        )

    def to_left(self, dist):
        part = self.part(self.core, self.col + dist)
        return remote(
            part,
            part,
            self.send_z.at[3 + dist],
            self.recv_z.at[3 + dist],
            (self.core, self.row, self.col - 1),
        )

    def to_sibling(self, col):
        part = self.part(self.core, col)
        return remote(
            part, part, self.send_s.at[col], self.recv_s.at[col], (1 - self.core, self.row, self.col)
        )

    def start(self):
        col = self.col

        @pl.when(col < 3)
        def _():
            self.to_right(0).start()

        @pl.when(col > 0)
        def _():
            self.to_left(0).start()

        self.to_sibling(col).start()

    def forward(self):
        col = self.col
        for dist in (1, 2, 3):

            @pl.when(col >= dist)
            def _():
                part = self.part(self.core, col - dist)
                remote(
                    part, part, self.send_z.at[0], self.recv_z.at[dist - 1], (self.core, self.row, col)
                ).wait_recv()

                @pl.when(col < 3)
                def _():
                    if dist < 3:
                        self.to_right(dist).start()

                self.to_sibling(col - dist).start()

            @pl.when(col + dist <= 3)
            def _():
                part = self.part(self.core, col + dist)
                remote(
                    part,
                    part,
                    self.send_z.at[0],
                    self.recv_z.at[3 + dist - 1],
                    (self.core, self.row, col),
                ).wait_recv()

                @pl.when(col > 0)
                def _():
                    if dist < 3:
                        self.to_left(dist).start()

                self.to_sibling(col + dist).start()

    def finish(self):
        for col in range(4):
            part = self.part(1 - self.core, col)
            remote(
                part, part, self.send_s.at[col], self.recv_s.at[col], (1 - self.core, self.row, self.col)
            ).wait_recv()
        for col in range(4):
            self.to_sibling(col).wait_send()
        for dist in (0, 1, 2):

            @pl.when((self.col < 3) & (self.col >= dist))
            def _():
                self.to_right(dist).wait_send()

            @pl.when((self.col > 0) & (self.col + dist <= 3))
            def _():
                self.to_left(dist).wait_send()


class Scatter:
    def __init__(self, place, rows, bufs, sems):
        self.core, self.row, self.col = place
        self.rows = rows
        self.give, self.keep, self.got, self.sent, self.left, self.right = bufs
        self.send_z, self.recv_z, self.send_s, self.recv_s = sems

    def sibling(self):
        return remote(
            self.give,
            self.got,
            self.send_s.at[0],
            self.recv_s.at[0],
            (1 - self.core, self.row, self.col),
        )

    def mine(self, dest):
        rows = pl.ds(dest * self.rows, self.rows)
        return self.keep[rows] + self.got[rows].astype(F32)

    def hop(self, dest, right):
        step = 1 if right else -1
        lane = 0 if right else 4
        return remote(
            self.sent.at[dest],
            self.left.at[dest - 1] if right else self.right.at[dest],
            self.send_z.at[lane + dest],
            self.recv_z.at[lane + dest],
            (self.core, self.row, self.col + step),
        )

    def chain(self, dest, right):
        col = self.col
        inner = (col > 0) if right else (col < 3)

        @pl.when((col < dest) if right else (col > dest))
        def _():
            @pl.when(inner)
            def _():
                self.hop(dest, right).wait_recv()
                came = (self.left[dest - 1] if right else self.right[dest]).astype(F32)
                self.sent[dest] = (self.mine(dest) + came).astype(BF)

            @pl.when(jnp.logical_not(inner))
            def _():
                self.sent[dest] = self.mine(dest).astype(BF)

            self.hop(dest, right).start()

    def run(self, result, work=()):
        col = self.col
        work = list(work)
        self.sibling().wait_recv()
        for dest in (3, 2, 1):
            self.chain(dest, True)
            self.chain(3 - dest, False)
            if work:
                work.pop(0)()
        own = pl.ds(pl.multiple_of(col * self.rows, self.rows), self.rows)
        result[...] = self.keep[own] + self.got[own].astype(F32)
        for dest in range(4):

            @pl.when(col == dest)
            def _():
                if dest > 0:
                    self.hop(dest, True).wait_recv()
                    result[...] += self.left[dest - 1].astype(F32)
                if dest < 3:
                    self.hop(dest, False).wait_recv()
                    result[...] += self.right[dest].astype(F32)

        self.sibling().wait_send()
        for dest in (1, 2, 3):

            @pl.when(col < dest)
            def _():
                self.hop(dest, True).wait_send()

            @pl.when(col > 3 - dest)
            def _():
                self.hop(3 - dest, False).wait_send()


class RowGather:
    def __init__(self, place, source, block, halves, sems):
        self.core, self.row, self.col = place
        self.source, self.block, self.halves = source, block, halves
        self.sems = sems

    def neighbour(self, mask):
        return (self.core, self.row ^ mask, self.col)

    def own(self):
        return pltpu.make_async_copy(self.source, self.block(self.row), self.sems.at[8])

    def first(self, mask, block=None):
        lane = mask - 1
        return remote(
            self.source,
            self.block(self.row) if block is None else block,
            self.sems.at[lane],
            self.sems.at[4 + lane],
            self.neighbour(mask),
        )

    def second(self, mask):
        part = self.halves(self.row ^ (3 - mask))[mask - 1]
        return remote(
            part, part, self.sems.at[1 + mask], self.sems.at[5 + mask], self.neighbour(mask)
        )

    def start(self):
        self.first(1).start()
        self.first(2).start()
        self.own().start()

    def forward(self):
        self.first(1, self.block(self.row ^ 1)).wait_recv()
        self.second(2).start()
        self.first(2, self.block(self.row ^ 2)).wait_recv()
        self.second(1).start()

    def finish(self):
        for mask in (1, 2):
            part = self.halves(self.row ^ 3)[mask - 1]
            remote(
                part, part, self.sems.at[1 + mask], self.sems.at[5 + mask], self.neighbour(mask)
            ).wait_recv()
        self.own().wait()
        self.first(1).wait_send()
        self.first(2).wait_send()
        self.second(1).wait_send()
        self.second(2).wait_send()


def by_rows(buf, block_rows):
    half = block_rows // 2

    def block(index):
        return buf.at[pl.ds(pl.multiple_of(index * block_rows, block_rows), block_rows)]

    def halves(index):
        return [
            buf.at[pl.ds(pl.multiple_of(index * block_rows + part * half, half), half)]
            for part in range(2)
        ]

    return block, halves


def by_cols(buf, block_cols):
    rows = buf.shape[0] // 2

    def block(index):
        return buf.at[:, pl.ds(pl.multiple_of(index * block_cols, block_cols), block_cols)]

    def halves(index):
        cols = pl.ds(pl.multiple_of(index * block_cols, block_cols), block_cols)
        return [buf.at[pl.ds(part * rows, rows), cols] for part in range(2)]

    return block, halves


def gelu_both(values):
    inner = 0.7978845608028654 * (values + 0.044715 * values * values * values)
    bend = jnp.tanh(inner)
    slope = 0.7978845608028654 * (1.0 + 3.0 * 0.044715 * values * values)
    return 0.5 * values * (1.0 + bend), 0.5 * (1.0 + bend) + 0.5 * values * (1.0 - bend * bend) * slope


def head_parts(raw, gain, cosine, sine):
    factor = lax.rsqrt(jnp.mean(raw * raw, axis=1, keepdims=True) + EPSILON)
    half = raw.shape[1] // 2
    scaled = raw * factor * gain
    first, second = scaled[:, :half], scaled[:, half:]
    return jnp.concatenate([first * cosine - second * sine, second * cosine + first * sine], axis=1)


def forward_kernel(
    x_in,
    g_in,
    gains_in,
    w_query,
    w_kv,
    w_out,
    w_gate,
    w_up,
    w_down,
    small_in,
    small_out,
    cosine,
    sine,
    start,
    head_gains,
    x_own,
    g_own,
    gains,
    xg,
    raw_q,
    raw_kv,
    q_low,
    kv,
    lse,
    top,
    o_low,
    attn_val,
    lr_low,
    fg,
    gate,
    up,
    hid,
    ff_val,
    wq_all,
    wkv_all,
    wo_all,
    wg_all,
    wu_all,
    wd_all,
    si_all,
    so_all,
    w_kv_pair,
    gains_pad,
    vq,
    vkv,
    vo,
    vg,
    vu,
    vd,
    vsi,
    vso,
    give,
    keep,
    got,
    sent,
    left,
    right,
    give2,
    keep2,
    got2,
    sent2,
    left2,
    right2,
    row_sems,
    z_send,
    z_recv,
    s_send,
    s_recv,
    misc_send,
    misc_recv,
    out_sems,
):
    core, row, col = lax.axis_index("seq"), lax.axis_index("row"), lax.axis_index("col")
    place = (core, row, col)
    own_tokens, width = x_own.shape
    block = x_in.shape[2]
    head_dim = head_gains.shape[1]
    tokens = xg.shape[0]
    ff_part = gate.shape[1]
    chunk = 2 * own_tokens
    key_width = w_kv.shape[1]
    half = row % 2
    greet(core, row, col)

    my_cols = pl.ds(pl.multiple_of(row * block, block), block)

    def hand_over(mask):
        return remote(
            x_in.at[row ^ mask],
            x_own.at[:, my_cols],
            misc_send.at[mask],
            misc_recv.at[mask],
            (core, row ^ mask, col),
        )

    def hand_grad(mask):
        return remote(
            g_in.at[row ^ mask],
            g_own.at[:, my_cols],
            misc_send.at[11 + mask],
            misc_recv.at[11 + mask],
            (core, row ^ mask, col),
        )

    def hand_gains(mask):
        return remote(
            gains_pad,
            gains.at[:, my_cols],
            misc_send.at[3 + mask],
            misc_recv.at[3 + mask],
            (core, row ^ mask, col),
        )

    for mask in (3, 1, 2):
        hand_over(mask).start()
    gains_pad[pl.ds(0, 6)] = gains_in[...]
    gains_pad[pl.ds(6, 2)] = jnp.zeros((2, block), F32)
    for mask in (3, 1, 2):
        hand_gains(mask).start()
    x_own[:, my_cols] = x_in[row]
    g_own[:, my_cols] = g_in[row]
    gains[:, my_cols] = gains_pad[...]

    pair_cols = pl.ds(pl.multiple_of(col % 2 * key_width, key_width), key_width)
    pair = remote(
        w_kv, w_kv_pair.at[:, pair_cols], misc_send.at[7], misc_recv.at[7], (core, row, col ^ 1)
    )
    pair.start()
    w_kv_pair[:, pair_cols] = w_kv[...]

    def rows_of(array, source, buf, lane, split=by_rows, size=None):
        block_of, halves_of = split(buf, size)
        return RowGather(place, source, block_of, halves_of, row_sems.at[lane])

    core_head = pl.ds(pl.multiple_of(core * head_dim, head_dim), head_dim)
    core_ff = pl.ds(pl.multiple_of(core * ff_part, ff_part), ff_part)
    get_q = rows_of(0, w_query.at[:, core_head], vq, 0, by_rows, block)
    get_kv = rows_of(0, w_kv_pair, vkv, 1, by_rows, block)
    get_o = rows_of(0, w_out.at[core_head], vo, 2, by_cols, block)
    get_g = rows_of(0, w_gate.at[:, core_ff], vg, 3, by_rows, block)
    get_u = rows_of(0, w_up.at[:, core_ff], vu, 4, by_rows, block)
    get_d = rows_of(0, w_down.at[core_ff], vd, 5, by_cols, block)
    get_si = rows_of(0, small_in, vsi, 6, by_rows, block)
    get_so = rows_of(0, small_out, vso, 7, by_cols, block)
    get_q.start()
    pair.wait_recv()
    get_kv.start()
    get_o.start()

    for mask in (1, 2, 3):
        remote(
            x_in.at[row],
            x_own.at[:, pl.ds(pl.multiple_of((row ^ mask) * block, block), block)],
            misc_send.at[mask],
            misc_recv.at[mask],
            (core, row, col),
        ).wait_recv()
        remote(
            gains_pad,
            gains.at[:, pl.ds(pl.multiple_of((row ^ mask) * block, block), block)],
            misc_send.at[3 + mask],
            misc_recv.at[3 + mask],
            (core, row, col),
        ).wait_recv()

    def own_norm():
        values = x_own[...].astype(F32)
        factor = lax.rsqrt(jnp.mean(values * values, axis=1, keepdims=True) + EPSILON)
        return values, values * factor * gains[pl.ds(0, 1)]

    mine = pl.ds(pl.multiple_of((core * 4 + col) * own_tokens, own_tokens), own_tokens)
    xg[mine] = own_norm()[1].astype(BF)
    sems = lambda lane: (z_send.at[lane], z_recv.at[lane], s_send.at[lane], s_recv.at[lane])
    gather_x = Gather(place, xg, own_tokens, sems(0))
    gather_x.start()
    get_q.forward()
    get_kv.forward()
    get_o.forward()
    get_si.start()
    get_so.start()
    get_g.start()
    for mask in (1, 2, 3):
        hand_grad(mask).start()
    gather_x.forward()
    gather_x.finish()
    get_q.finish()
    get_kv.finish()

    raw_q[...] = mm(xg[...], vq[...])
    raw_kv[...] = mm(xg[...], vkv[...])
    q_low[...] = head_parts(raw_q[...], head_gains[pl.ds(0, 1)], cosine[...], sine[...]).astype(BF)
    is_key = core == 0
    kv_here = head_parts(
        raw_kv[...],
        jnp.where(is_key, head_gains[pl.ds(1, 1)], 1.0),
        jnp.where(is_key, cosine[...], 1.0),
        jnp.where(is_key, sine[...], 0.0),
    ).astype(BF)

    def kv_part(kind, which):
        return kv.at[kind, pl.ds(pl.multiple_of(which * tokens, tokens), tokens)]

    kv[core, pl.ds(pl.multiple_of(half * tokens, tokens), tokens)] = kv_here
    here = kv_part(core, half)
    to_x = remote(here, here, misc_send.at[8], misc_recv.at[8], (core, row ^ 1, col))
    to_s = remote(here, here, misc_send.at[9], misc_recv.at[9], (1 - core, row, col))
    to_x.start()
    to_s.start()
    came = kv_part(core, half ^ 1)
    remote(here, came, misc_send.at[8], misc_recv.at[8], (core, row, col)).wait_recv()
    on_s = remote(came, came, misc_send.at[10], misc_recv.at[10], (1 - core, row, col))
    on_s.start()
    other = kv_part(1 - core, half)
    remote(other, other, misc_send.at[9], misc_recv.at[9], (core, row, col)).wait_recv()
    other_came = kv_part(1 - core, half ^ 1)
    remote(other_came, other_came, misc_send.at[10], misc_recv.at[10], (core, row, col)).wait_recv()

    q_rows = 128
    key_token = lax.broadcasted_iota(jnp.int32, (1, 2 * tokens), 1)
    in_half = key_token % tokens
    key_place = in_half // own_tokens * chunk + key_token // tokens * own_tokens + in_half % own_tokens
    top[...] = jnp.full(top.shape, MASK_FILL, F32)

    def attend(step, carry):
        first = pl.multiple_of(step * q_rows, q_rows)
        rows = pl.ds(first, q_rows)
        token = first + lax.broadcasted_iota(jnp.int32, (q_rows, 1), 0)
        q_place = token // own_tokens * chunk + half * own_tokens + token % own_tokens
        allowed = (key_place <= q_place) & (key_place >= start[rows])
        scores = jnp.where(allowed, mm_nt(q_low[rows], kv[0]), MASK_FILL)
        row_top = jnp.max(scores, axis=1, keepdims=True)
        weights = jnp.exp(scores - row_top)
        total = jnp.sum(weights, axis=1, keepdims=True)
        probs = (weights * (1.0 / total)).astype(BF)
        o_low[rows] = mm(probs, kv[1]).astype(BF)
        lse[rows] = row_top + jnp.log(total)
        top[...] = jnp.maximum(top[...], jnp.max(row_top))
        return carry

    lax.fori_loop(0, tokens // q_rows, attend, 0)
    get_si.forward()
    get_so.forward()
    get_g.forward()
    get_u.start()
    get_o.finish()

    away = pl.multiple_of((1 - core) * 4 * own_tokens, 4 * own_tokens)
    home = pl.multiple_of(core * 4 * own_tokens, 4 * own_tokens)
    scatter = Scatter(place, own_tokens, (give, keep, got, sent, left, right), sems(1))

    def project(source, weights, target, first):
        def step(index, carry):
            cols = pl.ds(pl.multiple_of(index * block, block), block)
            value = mm(source[pl.ds(first, 4 * own_tokens)], weights[:, cols])
            target[:, cols] = value.astype(target.dtype)
            return carry

        lax.fori_loop(0, width // block, step, 0)

    project(o_low, vo, give, away)
    scatter.sibling().start()
    project(o_low, vo, keep, home)
    scatter.run(attn_val)

    get_si.finish()
    get_so.finish()
    inputs, x_norm = own_norm()
    attn_normed = rms(attn_val[...])[0]
    rank = lr_low.shape[1]
    lr_low[...] = mm(xg[mine], vsi[:, pl.ds(0, rank)]).astype(BF)
    lo_normed = rms(mm(lr_low[...], vso[pl.ds(0, rank)]))[0]
    h_two = (
        inputs + attn_normed * gains[pl.ds(1, 1)] + (x_norm + lo_normed * gains[pl.ds(2, 1)])
    ) * ROOT_HALF
    fg[mine] = (rms(h_two)[0] * gains[pl.ds(3, 1)]).astype(BF)
    gather_f = Gather(place, fg, own_tokens, sems(2))
    gather_f.start()
    get_u.forward()
    get_d.start()
    get_g.finish()
    gather_f.forward()
    gather_f.finish()
    get_u.finish()

    tile = 256

    def units(index, carry):
        cols = pl.ds(pl.multiple_of(index * tile, tile), tile)
        bent, slope = gelu_both(mm(fg[...], vg[:, cols]))
        up_part = mm(fg[...], vu[:, cols])
        gate[:, cols] = (up_part * slope).astype(BF)
        up[:, cols] = bent.astype(BF)
        hid[:, cols] = (bent * up_part).astype(BF)
        return carry

    lax.fori_loop(0, ff_part // tile, units, 0)
    get_d.forward()
    keep_weights = [
        pltpu.make_async_copy(source, target, out_sems.at[lane])
        for lane, (source, target) in enumerate(
            [
                (vq, wq_all),
                (vkv, wkv_all),
                (vo, wo_all),
                (vg, wg_all),
                (vu, wu_all),
                (vd, wd_all),
                (vsi, si_all),
                (vso, so_all),
            ]
        )
    ]
    get_d.finish()
    for copy in keep_weights:
        copy.start()
    scatter_ff = Scatter(place, own_tokens, (give2, keep2, got2, sent2, left2, right2), sems(3))
    project(hid, vd, give2, away)
    scatter_ff.sibling().start()
    project(hid, vd, keep2, home)
    scatter_ff.run(ff_val)

    for mask in (1, 2, 3):
        hand_over(mask).wait_send()
        hand_gains(mask).wait_send()
        hand_grad(mask).wait_send()
        remote(
            g_in.at[row],
            g_own.at[:, pl.ds(pl.multiple_of((row ^ mask) * block, block), block)],
            misc_send.at[11 + mask],
            misc_recv.at[11 + mask],
            (core, row, col),
        ).wait_recv()
    pair.wait_send()
    to_x.wait_send()
    to_s.wait_send()
    on_s.wait_send()
    for copy in keep_weights:
        copy.wait()


def run_forward(x_in, g_in, gains_in, w_query, w_kv, w_out, w_gate, w_up, w_down, small_in, small_out, tables, head_gains):
    cosine, sine, start = tables
    block = x_in.shape[2]
    own, width = x_in.shape[1], 4 * block
    tokens, head_dim, ff_part = 8 * own, head_gains.shape[1], w_gate.shape[1] // 2
    rank = small_in.shape[1] - small_out.shape[0]
    vm = pl.BlockSpec(memory_space=pltpu.VMEM)
    hbm = pl.BlockSpec(memory_space=pl.ANY)
    shape = jax.ShapeDtypeStruct
    weights = [
        (width, head_dim),
        (width, head_dim),
        (head_dim, width),
        (width, ff_part),
        (width, ff_part),
        (ff_part, width),
        (width, small_in.shape[1]),
        (small_out.shape[0], width),
    ]
    outs = [
        shape((own, width), BF),
        shape((own, width), BF),
        shape((8, width), F32),
        shape((tokens, width), BF),
        shape((tokens, head_dim), F32),
        shape((tokens, head_dim), F32),
        shape((tokens, head_dim), BF),
        shape((2, 2 * tokens, head_dim), BF),
        shape((tokens, 1), F32),
        shape((8, 128), F32),
        shape((tokens, head_dim), BF),
        shape((own, width), F32),
        shape((own, rank), BF),
        shape((tokens, width), BF),
        shape((tokens, ff_part), BF),
        shape((tokens, ff_part), BF),
        shape((tokens, ff_part), BF),
        shape((own, width), F32),
    ] + [shape(size, BF) for size in weights]
    scatter_bufs = [
        pltpu.VMEM((4 * own, width), BF),
        pltpu.VMEM((4 * own, width), F32),
        pltpu.VMEM((4 * own, width), BF),
        pltpu.VMEM((4, own, width), BF),
        pltpu.VMEM((3, own, width), BF),
        pltpu.VMEM((3, own, width), BF),
    ]
    dma = pltpu.SemaphoreType.DMA
    return pl.pallas_call(
        forward_kernel,
        out_shape=outs,
        in_specs=[vm, vm, vm, hbm, vm, hbm, hbm, hbm, hbm, hbm, hbm, vm, vm, vm, vm],
        out_specs=[vm] * 18 + [hbm] * 8,
        scratch_shapes=[pltpu.VMEM((block, head_dim), BF), pltpu.VMEM((8, block), F32)]
        + [pltpu.VMEM(size, BF) for size in weights]
        + scatter_bufs * 2
        + [
            dma((8, 10)),
            dma((4, 8)),
            dma((4, 8)),
            dma((4, 4)),
            dma((4, 4)),
            dma((16,)),
            dma((16,)),
            dma((8,)),
        ],
        compiler_params=pltpu.CompilerParams(
            collective_id=0, has_side_effects=True, vmem_limit_bytes=60 * 2**20
        ),
        cost_estimate=pl.CostEstimate(flops=2 * 10**10, bytes_accessed=5 * 10**7, transcendentals=10**6),
    )(x_in, g_in, gains_in, w_query, w_kv, w_out, w_gate, w_up, w_down, small_in, small_out, cosine, sine, start, head_gains)


class RowScatter:
    def __init__(self, place, halves, came, sems, stage=None):
        self.core, self.row, self.col = place
        self.halves, self.came, self.sems = halves, came, sems
        self.stage = stage

    def send(self, lane, index, half, mask):
        return remote(
            self.halves(index)[half],
            self.came.at[lane],
            self.sems.at[lane],
            self.sems.at[6 + lane],
            (self.core, self.row ^ mask, self.col),
        )

    def lane(self, lane):
        index, half, mask = ((1, 0, 1), (3, 0, 1), (2, 1, 2), (3, 1, 2), (2, 0, 2), (1, 1, 1))[lane]
        return self.send(lane, self.row ^ index, half, mask)

    def start(self):
        for lane in (1, 3, 0, 2):
            self.lane(lane).start()

    def value(self, lane):
        return (self.came if self.stage is None else self.stage[0])[
            lane if self.stage is None else lane % 2
        ].astype(F32)

    def fetch(self, *wanted):
        for lane in wanted:
            self.lane(lane).wait_recv()
        if self.stage is None:
            return
        copies = [
            pltpu.make_async_copy(
                self.came.at[lane], self.stage[0].at[lane % 2], self.stage[1].at[lane % 2]
            )
            for lane in wanted
        ]
        for copy in copies:
            copy.start()
        for copy in copies:
            copy.wait()

    def middle(self):
        row = self.row
        for lane, out, index, half in ((1, 4, row ^ 2, 0), (3, 5, row ^ 1, 1)):
            self.fetch(lane)
            part = self.halves(index)[half]
            part[...] = (part[...].astype(F32) + self.value(lane)).astype(BF)
            self.lane(out).start()

    def finish(self):
        row = self.row
        for pair, half in (((0, 4), 0), ((2, 5), 1)):
            part = self.halves(row)[half]
            total = part[...].astype(F32)
            for lane in pair:
                self.fetch(lane)
                total = total + self.value(lane)
            part[...] = total.astype(BF)

    def drain(self):
        for lane in range(6):
            self.lane(lane).wait_send()


def head_back(grad, raw, gain, cosine, sine):
    factor = lax.rsqrt(jnp.mean(raw * raw, axis=1, keepdims=True) + EPSILON)
    half = raw.shape[1] // 2
    normed = raw * factor
    first, second = grad[:, :half], grad[:, half:]
    back = jnp.concatenate([first * cosine + second * sine, second * cosine - first * sine], axis=1)
    gain_grad = jnp.sum(back * normed, axis=0, keepdims=True)
    inner = back * gain
    return factor * (inner - normed * jnp.mean(inner * normed, axis=1, keepdims=True)), gain_grad


def backward_kernel(
    x_own,
    g_own,
    per_in,
    gains,
    head_gains,
    attn_val,
    lr_low,
    ff_val,
    raw_q,
    raw_kv,
    q_low,
    kv,
    lse,
    top,
    o_low,
    cosine,
    sine,
    start,
    vsi,
    vso,
    xg_in,
    fg_in,
    gate_in,
    up_in,
    hid_in,
    wq_in,
    wkv_in,
    wo_in,
    wg_in,
    wu_in,
    wd_in,
    y_out,
    x_grad,
    g_gain,
    tops,
    small_a,
    gq,
    gkv,
    gout,
    ggate,
    gup,
    gdown,
    came_g,
    came_u,
    came_d,
    vq,
    vkv,
    vo,
    vg,
    vu,
    vd,
    fg,
    gate,
    up,
    hid,
    dffg,
    dattng,
    dgate,
    dup,
    give,
    keep,
    got,
    sent,
    left,
    right,
    own_sum,
    h_two_ref,
    d_three_ref,
    low_ref,
    gpart,
    gcame,
    gpart2,
    gcame2,
    small_give,
    small_keep,
    small_got,
    small_row,
    small_z,
    d_o,
    d_kv,
    kv_give,
    kv_got,
    kv_x,
    kv_x_got,
    kv_p_got,
    pkv,
    came_q,
    came_kv,
    came_o,
    stage_g,
    stage_d,
    stage_sems,
    load_sems,
    row_sems,
    z_send,
    z_recv,
    s_send,
    s_recv,
    misc_send,
    misc_recv,
    gain_send,
    gain_recv,
    done_sems,
):
    core, row, col = lax.axis_index("seq"), lax.axis_index("row"), lax.axis_index("col")
    place = (core, row, col)
    own_tokens, width = x_own.shape
    block = width // 4
    tokens, head_dim = raw_q.shape
    ff_part = gate.shape[1]
    chunk = 2 * own_tokens
    key_width = head_dim // 2
    half = row % 2
    rank = lr_low.shape[1]
    my_cols = pl.ds(pl.multiple_of(row * block, block), block)
    mine = pl.ds(pl.multiple_of((core * 4 + col) * own_tokens, own_tokens), own_tokens)
    away = pl.multiple_of((1 - core) * 4 * own_tokens, 4 * own_tokens)
    home = pl.multiple_of(core * 4 * own_tokens, 4 * own_tokens)

    barrier = pltpu.get_barrier_semaphore()
    for mask in (1, 2, 3):
        pl.semaphore_signal(barrier, inc=1, device_id=(core, row ^ mask, col), device_id_type=MESH)
        for other in (0, 1):
            pl.semaphore_signal(
                barrier, inc=1, device_id=(core ^ other, row, col ^ mask), device_id_type=MESH
            )
    pl.semaphore_signal(barrier, inc=1, device_id=(1 - core, row, col), device_id_type=MESH)
    loads = [
        pltpu.make_async_copy(source, target, load_sems.at[lane])
        for lane, (source, target) in enumerate(
            [
                (wd_in, vd),
                (gate_in, gate),
                (up_in, up),
                (wg_in, vg),
                (wu_in, vu),
                (hid_in, hid),
                (fg_in, fg),
                (wo_in, vo),
                (wq_in, vq),
                (wkv_in, vkv),
            ]
        )
    ]
    for load in loads:
        load.start()
    pl.semaphore_wait(barrier, 10)

    def gain(index):
        return gains[pl.ds(index, 1)]

    inputs = x_own[...].astype(F32)
    x_norm = rms(inputs)[0] * gain(0)
    attn_normed = rms(attn_val[...])[0]
    lo_normed = rms(mm(lr_low[...], vso[pl.ds(0, rank)]))[0]
    h_two = (inputs + attn_normed * gain(1) + (x_norm + lo_normed * gain(2))) * ROOT_HALF
    h_two_ref[...] = h_two
    ff_normed, ff_factor = rms(ff_val[...])
    h_three = h_two + ff_normed * gain(4)
    h_low = h_three.astype(BF)
    p_gate = vsi[:, pl.ds(2 * rank, vsi.shape[1] - 2 * rank)]
    p_proj = vso[pl.ds(rank, vso.shape[0] - rank)]
    pg_gelu, pg_slope = gelu_both(mm(h_low, p_gate))
    per_input = per_in[row].astype(F32)
    gp_low = (pg_gelu * per_input).astype(BF)
    pp_normed, pp_factor = rms(mm(gp_low, p_proj))
    low_ref[...] = (h_three + pp_normed * gain(5)).astype(BF)

    def hand_back(source, target, mask, lane):
        return remote(
            source.at[:, pl.ds(pl.multiple_of((row ^ mask) * block, block), block)],
            target.at[row],
            misc_send.at[lane + mask],
            misc_recv.at[lane + mask],
            (core, row ^ mask, col),
        )

    def came_back(target, mask, lane):
        return remote(
            target.at[row ^ mask],
            target.at[row ^ mask],
            misc_send.at[lane + mask],
            misc_recv.at[lane + mask],
            (core, row, col),
        )

    for mask in (1, 2, 3):
        hand_back(low_ref, y_out, mask, 0).start()
    y_out[row] = low_ref[:, my_cols]

    grad_top = g_own[...].astype(F32)
    d_pp, gain_five = rms_back(grad_top, pp_normed, pp_factor, gain(5))
    d_pp_low = d_pp.astype(BF)
    d_pg_low = (mm_nt(d_pp_low, p_proj) * per_input * pg_slope).astype(BF)
    d_three = grad_top + mm_nt(d_pg_low, p_gate)
    d_three_ref[...] = d_three
    d_ff, gain_four = rms_back(d_three, ff_normed, ff_factor, gain(4))
    gpart[...] = jnp.zeros(gpart.shape, F32)
    gpart[pl.ds(5, 1)] = gain_five
    gpart[pl.ds(4, 1)] = gain_four
    dffg[mine] = d_ff.astype(BF)
    sems = lambda lane: (z_send.at[lane], z_recv.at[lane], s_send.at[lane], s_recv.at[lane])
    gather_ff = Gather(place, dffg, own_tokens, sems(0))
    gather_ff.start()

    def small(kind, first, value):
        rows = pl.ds(first, value.shape[0])
        value = value.astype(BF)

        @pl.when(core == kind)
        def _():
            small_keep[rows] = value

        @pl.when(core != kind)
        def _():
            small_give[rows] = value

    small(0, rank, mm_tn(gp_low, d_pp_low))
    small(1, rank, mm_tn(d_pg_low, h_low))
    gather_ff.forward()
    gather_ff.finish()

    tile = 256
    for load in loads[:3]:
        load.wait()

    def units(index, carry):
        cols = pl.ds(pl.multiple_of(index * tile, tile), tile)
        d_hid = mm_nt(dffg[...], vd[cols])
        dgate[:, cols] = (d_hid * gate[:, cols].astype(F32)).astype(BF)
        dup[:, cols] = (d_hid * up[:, cols].astype(F32)).astype(BF)
        return carry

    lax.fori_loop(0, ff_part // tile, units, 0)
    for load in loads[3:5]:
        load.wait()

    def back_ff(target, first):
        rows = pl.ds(first, 4 * own_tokens)

        def step(index, carry):
            cols = pl.ds(pl.multiple_of(index * block, block), block)
            value = mm_nt(dgate[rows], vg[cols]) + mm_nt(dup[rows], vu[cols])
            target[:, cols] = value.astype(target.dtype)
            return carry

        lax.fori_loop(0, width // block, step, 0)

    scatter_f = Scatter(place, own_tokens, (give, keep, got, sent, left, right), sems(1))
    back_ff(give, away)
    scatter_f.sibling().start()
    back_ff(keep, home)

    put_d = RowScatter(place, by_cols(vd, block)[1], came_d, row_sems.at[0], (stage_d, stage_sems))
    put_g = RowScatter(place, by_rows(vg, block)[1], came_g, row_sems.at[1], (stage_g, stage_sems))
    put_u = RowScatter(place, by_rows(vu, block)[1], came_u, row_sems.at[2], (stage_g, stage_sems))

    def down_grad():
        loads[5].wait()

        def step(index, carry):
            cols = pl.ds(pl.multiple_of(index * tile, tile), tile)
            for part in range(2):
                wide = pl.ds(part * (width // 2), width // 2)
                vd[cols, wide] = mm_tn(hid[:, cols], dffg[:, wide]).astype(BF)
            return carry

        lax.fori_loop(0, ff_part // tile, step, 0)
        put_d.start()

    def gate_grad(target, grad, put):
        def step(index, carry):
            rows = pl.ds(pl.multiple_of(index * tile, tile), tile)
            target[rows] = mm_tn(fg[:, rows], grad[...]).astype(BF)
            return carry

        lax.fori_loop(0, width // tile, step, 0)
        put.start()

    def both_gates():
        loads[6].wait()
        gate_grad(vg, dgate, put_g)

    scatter_f.run(own_sum, [down_grad, both_gates, lambda: gate_grad(vu, dup, put_u)])

    f_normed, f_factor = rms(h_two_ref[...])
    d_f, gain_three = rms_back(own_sum[...], f_normed, f_factor, gain(3))
    d_half = (d_three_ref[...] + d_f) * ROOT_HALF
    d_three_ref[...] = d_half
    attn_normed, attn_factor = rms(attn_val[...])
    d_attn, gain_one = rms_back(d_half, attn_normed, attn_factor, gain(1))
    dattng[mine] = d_attn.astype(BF)
    gather_a = Gather(place, dattng, own_tokens, sems(2))
    gather_a.start()
    lo_normed, lo_factor = rms(mm(lr_low[...], vso[pl.ds(0, rank)]))
    d_lo, gain_two = rms_back(d_half, lo_normed, lo_factor, gain(2))
    d_lo_low = d_lo.astype(BF)
    d_lr_low = mm_nt(d_lo_low, vso[pl.ds(0, rank)]).astype(BF)
    small(0, 0, mm_tn(lr_low[...], d_lo_low))
    x_low = (rms(x_own[...].astype(F32))[0] * gain(0)).astype(BF)
    small(1, 0, mm_tn(d_lr_low, x_low))
    own_sum[...] = d_half + mm_nt(d_lr_low, vsi[:, pl.ds(0, rank)])
    gpart[pl.ds(3, 1)] = gain_three
    gpart[pl.ds(2, 1)] = gain_two
    gpart[pl.ds(1, 1)] = gain_one
    small_swap = remote(
        small_give, small_got, misc_send.at[8], misc_recv.at[8], (1 - core, row, col)
    )
    small_swap.start()
    gather_a.forward()
    put_d.middle()
    gather_a.finish()

    loads[7].wait()
    d_o[...] = mm_nt(dattng[...], vo[...]).astype(BF)
    q_rows = 128
    key_token = lax.broadcasted_iota(jnp.int32, (1, 2 * tokens), 1)
    in_half = key_token % tokens
    key_place = in_half // own_tokens * chunk + key_token // tokens * own_tokens + in_half % own_tokens
    d_kv[...] = jnp.zeros(d_kv.shape, F32)

    def attend(step, carry):
        first = pl.multiple_of(step * q_rows, q_rows)
        rows = pl.ds(first, q_rows)
        token = first + lax.broadcasted_iota(jnp.int32, (q_rows, 1), 0)
        q_place = token // own_tokens * chunk + half * own_tokens + token % own_tokens
        allowed = (key_place <= q_place) & (key_place >= start[rows])
        scores = jnp.where(allowed, mm_nt(q_low[rows], kv[0]), MASK_FILL)
        probs = jnp.exp(scores - lse[rows])
        d_probs = mm_nt(d_o[rows], kv[1])
        delta = jnp.sum(probs * d_probs, axis=1, keepdims=True)
        d_scores = (probs * (d_probs - delta)).astype(BF)
        d_kv[0] += mm_tn(d_scores, q_low[rows])
        d_kv[1] += mm_tn(probs.astype(BF), d_o[rows])
        d_raw, gain_part = head_back(
            mm(d_scores, kv[0]), raw_q[rows], head_gains[pl.ds(0, 1)], cosine[rows], sine[rows]
        )
        d_o[rows] = d_raw.astype(BF)
        return carry + gain_part

    gain_q = lax.fori_loop(0, tokens // q_rows, attend, jnp.zeros((1, head_dim), F32))

    kv_give[...] = d_kv[1 - core].astype(BF)
    swap_kv = remote(kv_give, kv_got, misc_send.at[9], misc_recv.at[9], (1 - core, row, col))
    swap_kv.start()

    def out_grad():
        for part in range(2):
            wide = pl.ds(part * (width // 2), width // 2)
            vo[:, wide] = mm_tn(o_low[...], dattng[:, wide]).astype(BF)

    put_o = RowScatter(place, by_cols(vo, block)[1], came_o, row_sems.at[3])
    swap_kv.wait_recv()
    theirs = pl.ds(pl.multiple_of((half ^ 1) * tokens, tokens), tokens)
    ours = pl.ds(pl.multiple_of(half * tokens, tokens), tokens)
    kv_x[...] = (d_kv[core, theirs] + kv_got[theirs].astype(F32)).astype(BF)
    over_x = remote(kv_x, kv_x_got, misc_send.at[10], misc_recv.at[10], (core, row ^ 1, col))
    over_x.start()
    load_x = pltpu.make_async_copy(xg_in, dffg, load_sems.at[10])
    load_x.start()
    out_grad()
    put_o.start()
    loads[8].wait()
    loads[9].wait()
    over_x.wait_recv()
    d_kind = d_kv[core, ours] + kv_got[ours].astype(F32) + kv_x_got[...].astype(F32)
    kv_p = kv_got.at[pl.ds(0, tokens)]
    kv_p[...] = d_kind.astype(BF)
    over_p = remote(kv_p, kv_p_got, misc_send.at[11], misc_recv.at[11], (core, row, col ^ 1))
    over_p.start()
    put_g.middle()
    over_p.wait()
    d_kind = kv_p[...].astype(F32) + kv_p_got[...].astype(F32)
    is_key = core == 0
    d_kind_raw, gain_k = head_back(
        d_kind,
        raw_kv[...],
        jnp.where(is_key, head_gains[pl.ds(1, 1)], 1.0),
        jnp.where(is_key, cosine[...], 1.0),
        jnp.where(is_key, sine[...], 0.0),
    )
    for part in range(4):
        gpart[pl.ds(6, 1), pl.ds(part * block, head_dim)] = gain_q
        gpart[pl.ds(6, 1), pl.ds(part * block + head_dim, head_dim)] = gain_k * jnp.where(
            is_key, 0.5, 0.0
        )
    kv_p[...] = d_kind_raw.astype(BF)
    pair_cols = pl.ds(pl.multiple_of(col % 2 * key_width, key_width), key_width)

    def back_heads(target, first):
        rows = pl.ds(first, 4 * own_tokens)

        def step(index, carry):
            cols = pl.ds(pl.multiple_of(index * block, block), block)
            value = mm_nt(d_o[rows], vq[cols]) + mm_nt(kv_p[rows, pair_cols], vkv[cols, pair_cols])
            target[:, cols] = value.astype(target.dtype)
            return carry

        lax.fori_loop(0, width // block, step, 0)

    scatter_x = Scatter(place, own_tokens, (give, keep, got, sent, left, right), sems(3))
    back_heads(give, away)
    scatter_x.sibling().start()
    back_heads(keep, home)
    put_q = RowScatter(place, by_rows(vq, block)[1], came_q, row_sems.at[4])
    put_kv = RowScatter(place, by_rows(pkv, block)[1], came_kv, row_sems.at[5])
    put_s = RowScatter(place, by_cols(small_keep, block)[1], small_row, row_sems.at[6])

    def query_grad():
        load_x.wait()

        def step(index, carry):
            rows = pl.ds(pl.multiple_of(index * tile, tile), tile)
            vq[rows] = mm_tn(dffg[:, rows], d_o[...]).astype(BF)
            pkv[rows] = mm_tn(dffg[:, rows], kv_p[:, pair_cols]).astype(BF)
            return carry

        lax.fori_loop(0, width // tile, step, 0)
        put_q.start()
        put_kv.start()

    def small_sum():
        small_swap.wait_recv()
        small_keep[...] = (small_keep[...].astype(F32) + small_got[...].astype(F32)).astype(BF)
        put_s.start()

    d_half_here = d_three_ref
    scatter_x.run(h_two_ref, [query_grad, small_sum, put_u.middle])
    d_xn = own_sum[...] + h_two_ref[...]
    x_normed, x_factor = rms(x_own[...].astype(F32))
    d_in, gain_zero = rms_back(d_xn, x_normed, x_factor, gain(0))
    gpart[pl.ds(0, 1)] = gain_zero
    for mask in (1, 2, 3):
        hand_back(low_ref, y_out, mask, 0).wait_send()
    low_ref[...] = (d_half_here[...] + d_in).astype(BF)
    for mask in (1, 2, 3):
        hand_back(low_ref, x_grad, mask, 4).start()
    x_grad[row] = low_ref[:, my_cols]

    gpart[pl.ds(8, 8)] = jnp.full((8, width), jnp.max(top[...]), F32)

    def gain_row(mask):
        return remote(
            gpart.at[:, pl.ds(pl.multiple_of((row ^ mask) * block, block), block)],
            gcame.at[mask],
            gain_send.at[mask],
            gain_recv.at[mask],
            (core, row ^ mask, col),
        )

    for mask in (1, 2, 3):
        gain_row(mask).start()
    gcame[0] = gpart[:, my_cols]
    for mask in (1, 2, 3):
        gain_row(mask).wait_recv()
    summed = gcame[0] + gcame[1] + gcame[2] + gcame[3]
    largest = jnp.maximum(jnp.maximum(gcame[0], gcame[1]), jnp.maximum(gcame[2], gcame[3]))
    gpart2[pl.ds(0, 8)] = summed[:8]
    gpart2[pl.ds(8, 8)] = largest[8:]
    me = core * 4 + col
    members = [(other, mask) for other in (0, 1) for mask in range(4) if other or mask]

    def gain_group(other, mask):
        lane = 4 + other * 4 + mask
        return remote(
            gpart2,
            gcame2.at[me],
            gain_send.at[lane],
            gain_recv.at[lane],
            (core ^ other, row, col ^ mask),
        )

    for other, mask in members:
        gain_group(other, mask).start()
    gcame2[me] = gpart2[...]
    put_s.middle()
    put_kv.middle()
    put_o.middle()
    put_q.middle()

    def deliver(lane, source, target):
        local = pltpu.make_async_copy(source, target, done_sems.at[lane])
        over = remote(
            source, target, done_sems.at[8 + lane], done_sems.at[16 + lane], (1 - core, row, col)
        )
        local.start()
        over.start()
        return local, over

    core_ff = pl.ds(pl.multiple_of(core * ff_part, ff_part), ff_part)
    core_head = pl.ds(pl.multiple_of(core * head_dim, head_dim), head_dim)
    sib_ff = pl.ds(pl.multiple_of((1 - core) * ff_part, ff_part), ff_part)
    sib_head = pl.ds(pl.multiple_of((1 - core) * head_dim, head_dim), head_dim)
    row_block = pl.ds(pl.multiple_of(row * block, block), block)
    done = []
    put_d.finish()
    done.append(deliver(0, vd.at[:, row_block], gdown.at[core_ff]))
    put_g.finish()
    done.append(deliver(1, vg.at[row_block], ggate.at[:, core_ff]))
    put_s.finish()

    quarter = block // 4

    def small_quarter(mask):
        return remote(
            small_keep.at[
                :, pl.ds(pl.multiple_of(row * block + (col ^ mask) * quarter, quarter), quarter)
            ],
            small_z.at[mask],
            misc_send.at[11 + mask],
            misc_recv.at[11 + mask],
            (core, row, col ^ mask),
        )

    def small_share(other, mask):
        lane = 16 + other * 4 + mask
        return remote(
            kv_x.at[pl.ds(0, small_keep.shape[0]), pl.ds(0, quarter)],
            small_a.at[core, col],
            misc_send.at[lane],
            misc_recv.at[lane],
            (core ^ other, row, col ^ mask),
        )

    for mask in (1, 2, 3):
        small_quarter(mask).start()
    put_u.finish()
    done.append(deliver(2, vu.at[row_block], gup.at[:, core_ff]))
    for mask in (1, 2, 3):
        small_quarter(mask).wait_recv()
    small_total = small_keep[
        :, pl.ds(pl.multiple_of(row * block + col * quarter, quarter), quarter)
    ].astype(F32)
    for mask in (1, 2, 3):
        small_total = small_total + small_z[mask].astype(F32)
    over_x.wait_send()
    kv_x[pl.ds(0, small_keep.shape[0]), pl.ds(0, quarter)] = small_total.astype(BF)
    for other, mask in members:
        small_share(other, mask).start()
    small_a[core, col] = small_total.astype(BF)
    put_kv.finish()
    done.append(deliver(3, pkv.at[row_block], gkv.at[core]))
    put_o.finish()
    done.append(deliver(4, vo.at[:, row_block], gout.at[core_head]))
    put_q.finish()
    done.append(deliver(5, vq.at[row_block], gq.at[:, core_head]))

    for other, mask in members:
        who = (core ^ other) * 4 + (col ^ mask)
        lane = 4 + other * 4 + mask
        remote(
            gpart2, gcame2.at[who], gain_send.at[lane], gain_recv.at[lane], (core, row, col)
        ).wait_recv()
    total = gcame2[0]
    for who in range(1, 8):
        total = total + gcame2[who]
    g_gain[...] = total[:8]
    for who in range(8):
        head = 2 * (who % 4) + who // 4
        tops[pl.ds(head, 1)] = gcame2[who, pl.ds(8, 1), pl.ds(0, 128)]

    for other, mask in members:
        part = small_a.at[core ^ other, col ^ mask]
        lane = 16 + other * 4 + mask
        remote(part, part, misc_send.at[lane], misc_recv.at[lane], (core, row, col)).wait_recv()
        small_share(other, mask).wait_send()
        gain_group(other, mask).wait_send()
    for mask in (1, 2, 3):
        came_back(y_out, mask, 0).wait_recv()
        came_back(x_grad, mask, 4).wait_recv()
        hand_back(low_ref, x_grad, mask, 4).wait_send()
        gain_row(mask).wait_send()
        small_quarter(mask).wait_send()
    small_swap.wait_send()
    swap_kv.wait_send()
    for put in (put_d, put_g, put_u, put_o, put_q, put_kv, put_s):
        put.drain()
    sib_targets = [
        gdown.at[sib_ff],
        ggate.at[:, sib_ff],
        gup.at[:, sib_ff],
        gkv.at[1 - core],
        gout.at[sib_head],
        gq.at[:, sib_head],
    ]
    for lane, (local, over) in enumerate(done):
        local.wait()
        over.wait_send()
        target = sib_targets[lane]
        remote(
            target, target, done_sems.at[8 + lane], done_sems.at[16 + lane], (core, row, col)
        ).wait_recv()


def run_backward(small_args, big_args):
    x_own, per_in, head_gains = small_args[0], small_args[2], small_args[4]
    own, width = x_own.shape
    block = width // 4
    gate = big_args[2]
    tokens, ff_part = gate.shape
    head_dim = head_gains.shape[1]
    rank = small_args[6].shape[1]
    small_rows = small_args[19].shape[0]
    vm = pl.BlockSpec(memory_space=pltpu.VMEM)
    hbm = pl.BlockSpec(memory_space=pl.ANY)
    shape = jax.ShapeDtypeStruct
    vmem = pltpu.VMEM
    dma = pltpu.SemaphoreType.DMA
    outs = [
        shape((4, own, block), BF),
        shape((4, own, block), BF),
        shape((8, block), F32),
        shape((8, 128), F32),
        shape((2, 4, small_rows, block // 4), BF),
        shape((block, 2 * head_dim), BF),
        shape((2, block, head_dim // 2), BF),
        shape((2 * head_dim, block), BF),
        shape((block, 2 * ff_part), BF),
        shape((block, 2 * ff_part), BF),
        shape((2 * ff_part, block), BF),
        shape((6, block // 2, ff_part), BF),
        shape((6, block // 2, ff_part), BF),
        shape((6, ff_part // 2, block), BF),
    ]
    scratch = [
        vmem((width, head_dim), BF),
        vmem((width, head_dim), BF),
        vmem((head_dim, width), BF),
        vmem((width, ff_part), BF),
        vmem((width, ff_part), BF),
        vmem((ff_part, width), BF),
        vmem((tokens, width), BF),
        vmem((tokens, ff_part), BF),
        vmem((tokens, ff_part), BF),
        vmem((tokens, ff_part), BF),
        vmem((tokens, width), BF),
        vmem((tokens, width), BF),
        vmem((tokens, ff_part), BF),
        vmem((tokens, ff_part), BF),
        vmem((4 * own, width), BF),
        vmem((4 * own, width), F32),
        vmem((4 * own, width), BF),
        vmem((4, own, width), BF),
        vmem((3, own, width), BF),
        vmem((3, own, width), BF),
        vmem((own, width), F32),
        vmem((own, width), F32),
        vmem((own, width), F32),
        vmem((own, width), BF),
        vmem((16, width), F32),
        vmem((4, 16, block), F32),
        vmem((16, block), F32),
        vmem((8, 16, block), F32),
        vmem((small_rows, width), BF),
        vmem((small_rows, width), BF),
        vmem((small_rows, width), BF),
        vmem((6, small_rows // 2, block), BF),
        vmem((4, small_rows, block // 4), BF),
        vmem((tokens, head_dim), BF),
        vmem((2, 2 * tokens, head_dim), F32),
        vmem((2 * tokens, head_dim), BF),
        vmem((2 * tokens, head_dim), BF),
        vmem((tokens, head_dim), BF),
        vmem((tokens, head_dim), BF),
        vmem((tokens, head_dim), BF),
        vmem((width, head_dim // 2), BF),
        vmem((6, block // 2, head_dim), BF),
        vmem((6, block // 2, head_dim // 2), BF),
        vmem((6, head_dim // 2, block), BF),
        vmem((2, block // 2, ff_part), BF),
        vmem((2, ff_part // 2, block), BF),
        dma((2,)),
        dma((11,)),
        dma((7, 12)),
        dma((4, 8)),
        dma((4, 8)),
        dma((4, 4)),
        dma((4, 4)),
        dma((24,)),
        dma((24,)),
        dma((12,)),
        dma((12,)),
        dma((24,)),
    ]
    return pl.pallas_call(
        backward_kernel,
        out_shape=outs,
        in_specs=[vm] * 20 + [hbm] * 11,
        out_specs=[vm] * 5 + [hbm] * 9,
        scratch_shapes=scratch,
        compiler_params=pltpu.CompilerParams(
            collective_id=1, has_side_effects=True, vmem_limit_bytes=VMEM_BYTES
        ),
        cost_estimate=pl.CostEstimate(
            flops=4 * 10**10, bytes_accessed=10**8, transcendentals=2 * 10**6
        ),
    )(*small_args, *big_args)


def body_pair(
    layer_in,
    per_layer_in,
    doc_lengths,
    w_query,
    w_key,
    w_value,
    w_out,
    w_gate,
    w_up,
    w_down,
    laurel_left,
    laurel_right,
    per_gate,
    per_proj,
    norm_gains,
    head_gains,
    out_grad,
):
    core, row, col = lax.axis_index("seq"), lax.axis_index("row"), lax.axis_index("col")
    rows, cols, cores = lax.axis_size("row"), lax.axis_size("col"), lax.axis_size("seq")
    seq_count = layer_in.shape[0]
    head_dim = head_gains.shape[1]
    key_width = w_key.shape[1]
    ff_part = w_gate.shape[1] // cores
    chunk = layer_in.shape[1]
    halves = rows // seq_count
    own_tokens = chunk // halves
    group_tokens = own_tokens * cores * cols
    even_col = col % 2 == 0

    lengths = doc_lengths[row // halves]
    count = doc_lengths.shape[1]
    upto = jnp.tril(jnp.ones((count, count), jnp.int32))
    doc_ends = jnp.sum(lengths[None, :] * upto, axis=1)

    def places_of(half):
        token = jnp.arange(group_tokens, dtype=jnp.int32)
        place = token // own_tokens * chunk + half * own_tokens + token % own_tokens
        before = (doc_ends[None, :] <= place[:, None]).astype(jnp.int32)
        start = jnp.sum(before * lengths[None, :], axis=1)
        return place, start

    half = row % halves
    place, start = places_of(half)
    other_place, other_start = places_of(half ^ 1)
    key_place = jnp.stack([place, other_place])[jnp.array([0, 1]) ^ half].reshape(-1)
    allowed = (key_place[None, :] <= place[:, None]) & (key_place[None, :] >= start[:, None])
    cosine_table, sine_table = rotation(place - start, head_dim)

    w_kv = jnp.where(core == 0, w_key, w_value)
    rank = laurel_left.shape[1]
    small_in = jnp.concatenate(
        [laurel_left, jnp.zeros((laurel_left.shape[0], rank), BF), per_gate], axis=1
    )
    small_out = jnp.concatenate([laurel_right, per_proj], axis=0)
    (
        x_own,
        g_own,
        gains,
        x_all,
        raw_q,
        raw_kv,
        q_low,
        kv,
        lse,
        top_tile,
        o_low,
        attn_val,
        lr_low,
        f_all,
        gate_val,
        up_val,
        hid_low,
        ff_val,
        w_q,
        w_kv_all,
        w_o,
        w_g,
        w_u,
        w_d,
        small_in_all,
        small_out_all,
    ) = run_forward(
        layer_in.reshape(rows, own_tokens, -1),
        out_grad.reshape(rows, own_tokens, -1),
        norm_gains,
        w_query,
        w_kv,
        w_out,
        w_gate,
        w_up,
        w_down,
        small_in,
        small_out,
        (
            cosine_table[:, : head_dim // 2],
            sine_table[:, : head_dim // 2],
            start[:, None],
        ),
        head_gains,
    )
    half_table = head_dim // 2
    (
        y_out,
        x_grad,
        g_gain,
        tops,
        small_sums,
        g_q,
        g_kv,
        g_o,
        g_g,
        g_u,
        g_d,
        *came,
    ) = run_backward(
        (
            x_own,
            g_own,
            per_layer_in.reshape(rows, own_tokens, -1),
            gains,
            head_gains,
            attn_val,
            lr_low,
            ff_val,
            raw_q,
            raw_kv,
            q_low,
            kv,
            lse,
            top_tile,
            o_low,
            cosine_table[:, :half_table],
            sine_table[:, :half_table],
            start[:, None],
            small_in_all,
            small_out_all,
        ),
        (x_all, f_all, gate_val, up_val, hid_low, w_q, w_kv_all, w_o, w_g, w_u, w_d),
    )
    sums_a = small_sums[0].transpose(1, 0, 2).reshape(small_sums.shape[2], -1).astype(F32)
    sums_b = small_sums[1].transpose(0, 2, 1).reshape(-1, small_sums.shape[2]).astype(F32)
    logit_top = tops[:, 0]
    clip_factor = jnp.sqrt(CLIP_LEVEL / jnp.maximum(logit_top, CLIP_LEVEL))
    clipped_gains = clip_factor[None, :, None] * head_gains[:, None, :]
    return (
        y_out.reshape(layer_in.shape),
        x_grad.reshape(layer_in.shape),
        g_q.astype(F32),
        g_kv[0].astype(F32),
        g_kv[1].astype(F32),
        g_o.astype(F32),
        g_g.astype(F32),
        g_u.astype(F32),
        g_d.astype(F32),
        sums_b[:, :rank],
        sums_a[:rank],
        sums_b[:, rank:],
        sums_a[rank:],
        g_gain[:6],
        g_gain[6].reshape(head_gains.shape),
        clipped_gains,
    )


def solution(mesh):
    sizes = tuple(mesh.shape[axis] for axis in ("seq", "row", "col"))
    body = body_pair if sizes == (2, 4, 4) else body_any
    return jax.shard_map(
        body,
        mesh=mesh,
        in_specs=(
            P(None, ("seq", "col"), "row"),
            P(None, ("seq", "col"), None),
            P(),
            P("row", "col"),
            P("row", "col"),
            P("row", "col"),
            P("col", "row"),
            P("row", "col"),
            P("row", "col"),
            P("col", "row"),
            P("row", None),
            P(None, "row"),
            P("row", None),
            P(None, "row"),
            P(None, "row"),
            P(),
            P(None, ("seq", "col"), "row"),
        ),
        out_specs=(
            P(None, ("seq", "col"), "row"),
            P(None, ("seq", "col"), "row"),
            P("row", "col"),
            P("row", "col"),
            P("row", "col"),
            P("col", "row"),
            P("row", "col"),
            P("row", "col"),
            P("col", "row"),
            P("row", None),
            P(None, "row"),
            P("row", None),
            P(None, "row"),
            P(None, "row"),
            P(),
            P(),
        ),
        check_vma=False,
    )
```

```python
import functools

import jax
import jax.numpy as jnp
from jax import lax
from jax.experimental import pallas as pl
from jax.experimental.pallas import tpu as pltpu
from jax.sharding import PartitionSpec as P

EPSILON = 1e-06
CLIP_LEVEL = 3.0
ROPE_BASE = 1000000.0
ROOT_HALF = 0.7071067811865476
MASK_FILL = -1e30
MESH = pl.DeviceIdType.MESH
BF = jnp.bfloat16
F32 = jnp.float32
VMEM_BYTES = 63 * 2**20


def swapped(value, axis, apart):
    mask = 2**apart
    pairs = [(source, source ^ mask) for source in range(lax.axis_size(axis))]
    return lax.ppermute(value, axis, pairs)


def width_total(values):
    return lax.psum(values, "row")


def gather_tokens(values):
    return lax.all_gather(values, "col", axis=1, tiled=True)


def spread_rows(values, project):
    gathered = gather_tokens(values)
    return (gathered, lax.psum_scatter(project(gathered), "row", scatter_dimension=1, tiled=True))


def spread_cols(values, project):
    gathered = lax.all_gather(values, "row", axis=1, tiled=True)
    return (gathered, lax.psum_scatter(project(gathered), "col", scatter_dimension=1, tiled=True))


def times_right(left_side, right_side):
    return jnp.einsum("std,dn->stn", left_side, right_side, preferred_element_type=jnp.float32)


def times_back(left_side, right_side):
    return jnp.einsum("stn,dn->std", left_side, right_side, preferred_element_type=jnp.float32)


def outer_sum(left_side, right_side):
    return jnp.einsum("std,stn->dn", left_side, right_side, preferred_element_type=jnp.float32)


def norm_forward(values, gain_vec, width_all):
    square_sum = width_total(jnp.sum(values * values, axis=-1, keepdims=True))
    factor = lax.rsqrt(square_sum / width_all + EPSILON)
    normed = values * factor
    return (normed * gain_vec, normed, factor)


def norm_backward(grad_values, normed, factor, gain_vec, width_all):
    grad_normed = grad_values * gain_vec
    inner_sum = width_total(jnp.sum(grad_normed * normed, axis=-1, keepdims=True))
    result = factor * (grad_normed - normed * (inner_sum / width_all))
    return (result, jnp.sum(grad_values * normed, axis=(0, 1)))


def head_norm(values, gain_vec):
    return (
        values * lax.rsqrt(jnp.mean(values * values, axis=-1, keepdims=True) + EPSILON) * gain_vec
    )


def rotation(position, width_all):
    half_width = width_all // 2
    frequency = ROPE_BASE ** (-2.0 * jnp.arange(half_width, dtype=jnp.float32) / width_all)
    angles = position.astype(jnp.float32)[..., None] * frequency
    cosine_table = jnp.concatenate([jnp.cos(angles), jnp.cos(angles)], axis=-1)
    sine_table = jnp.concatenate([jnp.sin(angles), jnp.sin(angles)], axis=-1)
    return (cosine_table, sine_table)


def rotate(values, cosine_table, sine_table):
    half_width = values.shape[-1] // 2
    turned = jnp.concatenate([-values[..., half_width:], values[..., :half_width]], axis=-1)
    return values * cosine_table + turned * sine_table


def doc_places(doc_lengths, first_place, place_count):
    upto = jnp.tril(jnp.ones((doc_lengths.shape[1], doc_lengths.shape[1]), jnp.int32))
    doc_ends = jnp.sum(doc_lengths[:, None, :] * upto[None], axis=2)
    places = first_place + jnp.arange(place_count, dtype=jnp.int32)
    before = (doc_ends[:, None, :] <= places[None, :, None]).astype(jnp.int32)
    segment = jnp.sum(before, axis=2)
    doc_start = jnp.sum(before * doc_lengths[:, None, :], axis=2)
    return (segment, places, places[None, :] - doc_start)


def block_scores(queries, keys_all, block_start, block_size, query_seg, query_place, key_seg):
    keys_part = lax.dynamic_slice_in_dim(keys_all, block_start, block_size, 1)
    scores = jnp.einsum("sqhd,skd->shqk", queries, keys_part, preferred_element_type=jnp.float32)
    seg_part = lax.dynamic_slice_in_dim(key_seg, block_start, block_size, 1)
    key_place = block_start + jnp.arange(block_size, dtype=jnp.int32)
    allowed = (query_seg[:, None, :, None] == seg_part[:, None, None, :]) & (
        key_place[None, None, None, :] <= query_place[None, None, :, None]
    )
    return (scores, allowed)


def body_any(
    layer_in,
    per_layer_in,
    doc_lengths,
    w_query,
    w_key,
    w_value,
    w_out,
    w_gate,
    w_up,
    w_down,
    laurel_left,
    laurel_right,
    per_gate,
    per_proj,
    norm_gains,
    head_gains,
    out_grad,
):
    seq_count = layer_in.shape[0]
    width_all = layer_in.shape[2] * lax.axis_size("row")
    head_dim = head_gains.shape[1]
    heads_here = w_query.shape[1] // head_dim
    heads_all = heads_here * lax.axis_size("col")
    key_width = w_key.shape[1]
    ff_here = w_gate.shape[1]
    local_len = layer_in.shape[1] * lax.axis_size("col")
    tokens_row = local_len // lax.axis_size("row")
    seq_len = local_len * lax.axis_size("seq")
    col_index = lax.axis_index("col")
    even_col = col_index % 2 == 0
    q_width = heads_here * head_dim
    partner_key, partner_value = swapped((w_key, w_value), "col", 0)
    key_head = jnp.where(
        even_col,
        jnp.concatenate([w_key, partner_key], axis=1),
        jnp.concatenate([partner_key, w_key], axis=1),
    )
    value_head = jnp.where(
        even_col,
        jnp.concatenate([w_value, partner_value], axis=1),
        jnp.concatenate([partner_value, w_value], axis=1),
    )
    w_heads = jnp.concatenate([w_query, key_head, value_head], axis=1)
    w_back = jnp.concatenate([w_query, w_key, w_value], axis=1)
    w_gate_up = jnp.concatenate([w_gate, w_up], axis=1)
    inputs = layer_in.astype(jnp.float32)
    x_norm, x_normed, x_factor = norm_forward(inputs, norm_gains[0], width_all)
    x_low = x_norm.astype(jnp.bfloat16)
    x_rows, head_raw = spread_rows(x_low, lambda gathered: times_right(gathered, w_heads))
    q_raw = head_raw[:, :, :q_width].reshape(seq_count, tokens_row, heads_here, head_dim)
    k_raw = head_raw[:, :, q_width : q_width + head_dim]
    v_raw = head_raw[:, :, q_width + head_dim :]
    query_seg, query_place, query_pos = doc_places(
        doc_lengths, lax.axis_index(("seq", "row")) * tokens_row, tokens_row
    )
    key_seg, unused_place, unused_pos = doc_places(doc_lengths, 0, seq_len)
    cosine_table, sine_table = rotation(query_pos, head_dim)

    def query_prep(raw_part, gain_vec):
        return rotate(
            head_norm(raw_part, gain_vec), cosine_table[:, :, None], sine_table[:, :, None]
        )

    def key_prep(raw_part, gain_vec):
        return rotate(head_norm(raw_part, gain_vec), cosine_table, sine_table)

    def value_prep(raw_part):
        return head_norm(raw_part, 1.0)

    q_rot, query_back = jax.vjp(query_prep, q_raw, head_gains[0])
    k_rot, key_back = jax.vjp(key_prep, k_raw, head_gains[1])
    v_normed, value_back = jax.vjp(value_prep, v_raw)
    q_low = q_rot.astype(jnp.bfloat16)
    keys_all, values_all = (
        lax.all_gather(k_rot.astype(jnp.bfloat16), ("seq", "row"), axis=1, tiled=True),
        lax.all_gather(v_normed.astype(jnp.bfloat16), ("seq", "row"), axis=1, tiled=True),
    )
    block_size = min(512, seq_len)
    block_count = seq_len // block_size
    blocks = jnp.arange(block_count, dtype=jnp.int32)

    def scored(block_index):
        return block_scores(
            q_low, keys_all, block_index * block_size, block_size, query_seg, query_place, key_seg
        )

    def values_at(block_index):
        return lax.dynamic_slice_in_dim(values_all, block_index * block_size, block_size, 1)

    def stats_step(carry, block_index):
        row_top, row_total = carry
        scores, allowed = scored(block_index)
        new_top = jnp.maximum(row_top, jnp.max(jnp.where(allowed, scores, MASK_FILL), axis=3))
        weights = jnp.where(allowed, jnp.exp(scores - new_top[..., None]), 0.0)
        row_total = row_total * jnp.exp(row_top - new_top) + jnp.sum(weights, axis=3)
        return ((new_top, row_total), None)

    start_top = jnp.full((seq_count, heads_here, tokens_row), MASK_FILL, jnp.float32)
    (row_top, row_total), unused = lax.scan(
        stats_step, (start_top, jnp.zeros_like(start_top)), blocks
    )
    log_total = row_top + jnp.log(row_total)

    def probs_at(block_index):
        scores, allowed = scored(block_index)
        return jnp.where(allowed, jnp.exp(scores - log_total[..., None]), 0.0)

    def out_step(total_out, block_index):
        probs_low = probs_at(block_index).astype(jnp.bfloat16)
        total_out = total_out + jnp.einsum(
            "shqk,skd->sqhd", probs_low, values_at(block_index), preferred_element_type=jnp.float32
        )
        return (total_out, None)

    attended, unused = lax.scan(
        out_step, jnp.zeros((seq_count, tokens_row, heads_here, head_dim), jnp.float32), blocks
    )
    o_low = attended.astype(jnp.bfloat16).reshape(seq_count, tokens_row, q_width)
    head_slots = lax.dynamic_update_slice_in_dim(
        jnp.full((heads_all,), MASK_FILL, jnp.float32),
        jnp.max(row_top, axis=(0, 2)),
        col_index * heads_here,
        0,
    )
    logit_top = lax.pmax(head_slots, ("seq", "row", "col"))
    o_rows, attn_val = spread_cols(o_low, lambda gathered: times_right(gathered, w_out))
    attn_norm, attn_normed, attn_factor = norm_forward(attn_val, norm_gains[1], width_all)
    h_one = inputs + attn_norm
    lr_low = width_total(times_right(x_low, laurel_left)).astype(jnp.bfloat16)
    lo_val = times_right(lr_low, laurel_right)
    lo_norm, lo_normed, lo_factor = norm_forward(lo_val, norm_gains[2], width_all)
    h_two = (h_one + (x_norm + lo_norm)) * ROOT_HALF
    f_norm, f_normed, f_factor = norm_forward(h_two, norm_gains[3], width_all)
    f_low = f_norm.astype(jnp.bfloat16)
    f_rows, gate_up = spread_rows(f_low, lambda gathered: times_right(gathered, w_gate_up))
    gate_val = gate_up[:, :, :ff_here]
    up_val = gate_up[:, :, ff_here:]

    def geglu(gate_part, up_part):
        return jax.nn.gelu(gate_part, approximate=True) * up_part

    hidden, geglu_back = jax.vjp(geglu, gate_val, up_val)
    hid_low = hidden.astype(jnp.bfloat16)
    hid_rows, ff_val = spread_cols(hid_low, lambda gathered: times_right(gathered, w_down))
    ff_norm, ff_normed, ff_factor = norm_forward(ff_val, norm_gains[4], width_all)
    h_three = h_two + ff_norm
    h_low = h_three.astype(jnp.bfloat16)
    pg_val = width_total(times_right(h_low, per_gate))
    per_input = per_layer_in.astype(jnp.float32)

    def per_mix(gate_part):
        return jax.nn.gelu(gate_part, approximate=True) * per_input

    gp_val, per_back = jax.vjp(per_mix, pg_val)
    gp_low = gp_val.astype(jnp.bfloat16)
    pp_val = times_right(gp_low, per_proj)
    pp_norm, pp_normed, pp_factor = norm_forward(pp_val, norm_gains[5], width_all)
    layer_out = (h_three + pp_norm).astype(jnp.bfloat16)
    grad_top = out_grad.astype(jnp.float32)
    d_pp, gain_five = norm_backward(grad_top, pp_normed, pp_factor, norm_gains[5], width_all)
    d_pp_low = d_pp.astype(jnp.bfloat16)
    grad_per_proj = outer_sum(gp_low, d_pp_low)
    (d_pg,) = per_back(width_total(times_back(d_pp_low, per_proj)))
    d_pg_low = d_pg.astype(jnp.bfloat16)
    grad_per_gate = outer_sum(h_low, d_pg_low)
    d_three = grad_top + times_back(d_pg_low, per_gate)
    d_ff, gain_four = norm_backward(d_three, ff_normed, ff_factor, norm_gains[4], width_all)
    d_ff_low = d_ff.astype(jnp.bfloat16)
    dff_rows, d_hidden = spread_rows(d_ff_low, lambda gathered: times_back(gathered, w_down))
    grad_down = outer_sum(hid_rows, dff_rows)
    d_gate, d_up = geglu_back(d_hidden)
    d_gate_up = jnp.concatenate([d_gate, d_up], axis=2).astype(jnp.bfloat16)
    dgu_rows, d_f_low = spread_cols(d_gate_up, lambda gathered: times_back(gathered, w_gate_up))
    grad_gate_up = outer_sum(f_rows, dgu_rows)
    d_f, gain_three = norm_backward(d_f_low, f_normed, f_factor, norm_gains[3], width_all)
    d_half = (d_three + d_f) * ROOT_HALF
    d_lo, gain_two = norm_backward(d_half, lo_normed, lo_factor, norm_gains[2], width_all)
    d_lo_low = d_lo.astype(jnp.bfloat16)
    grad_laurel_right = outer_sum(lr_low, d_lo_low)
    d_lr_low = width_total(times_back(d_lo_low, laurel_right)).astype(jnp.bfloat16)
    grad_laurel_left = outer_sum(x_low, d_lr_low)
    d_attn, gain_one = norm_backward(d_half, attn_normed, attn_factor, norm_gains[1], width_all)
    d_attn_low = d_attn.astype(jnp.bfloat16)
    dattn_rows, d_o = spread_rows(d_attn_low, lambda gathered: times_back(gathered, w_out))
    grad_w_out = outer_sum(o_rows, dattn_rows)
    d_o_low = d_o.astype(jnp.bfloat16).reshape(seq_count, tokens_row, heads_here, head_dim)

    def delta_step(total_delta, block_index):
        d_probs = jnp.einsum(
            "sqhd,skd->shqk", d_o_low, values_at(block_index), preferred_element_type=jnp.float32
        )
        return (total_delta + jnp.sum(probs_at(block_index) * d_probs, axis=3), None)

    row_delta, unused = lax.scan(delta_step, jnp.zeros_like(log_total), blocks)

    def grad_step(carry, block_index):
        d_query, d_keys, d_values = carry
        block_start = block_index * block_size
        prob_vals = probs_at(block_index)
        d_probs = jnp.einsum(
            "sqhd,skd->shqk", d_o_low, values_at(block_index), preferred_element_type=jnp.float32
        )
        d_scores = (prob_vals * (d_probs - row_delta[..., None])).astype(jnp.bfloat16)
        keys_part = lax.dynamic_slice_in_dim(keys_all, block_start, block_size, 1)
        d_query = d_query + jnp.einsum(
            "shqk,skd->sqhd", d_scores, keys_part, preferred_element_type=jnp.float32
        )
        key_part = jnp.einsum("shqk,sqhd->skd", d_scores, q_low, preferred_element_type=jnp.float32)
        value_part = jnp.einsum(
            "shqk,sqhd->skd",
            prob_vals.astype(jnp.bfloat16),
            d_o_low,
            preferred_element_type=jnp.float32,
        )
        d_keys = lax.dynamic_update_slice_in_dim(d_keys, key_part, block_start, 1)
        d_values = lax.dynamic_update_slice_in_dim(d_values, value_part, block_start, 1)
        return ((d_query, d_keys, d_values), None)

    zero_keys = jnp.zeros((seq_count, seq_len, head_dim), jnp.float32)
    (d_query, d_keys, d_values), unused = lax.scan(
        grad_step, (jnp.zeros_like(attended), zero_keys, zero_keys), blocks
    )
    own_keys, own_values = (
        lax.psum_scatter(d_keys, ("seq", "row"), scatter_dimension=1, tiled=True),
        lax.psum_scatter(d_values, ("seq", "row"), scatter_dimension=1, tiled=True),
    )
    pair_keys, pair_values = swapped((own_keys, own_values), "col", 0)
    d_q_raw, d_q_gain = query_back(d_query)
    d_k_raw, d_k_gain = key_back(own_keys + pair_keys)
    (d_v_raw,) = value_back(own_values + pair_values)
    key_offset = col_index % 2 * key_width
    d_heads_low = jnp.concatenate(
        [
            d_q_raw.reshape(seq_count, tokens_row, q_width),
            lax.dynamic_slice_in_dim(d_k_raw, key_offset, key_width, 2),
            lax.dynamic_slice_in_dim(d_v_raw, key_offset, key_width, 2),
        ],
        axis=2,
    ).astype(jnp.bfloat16)
    dhead_rows, d_x_heads = spread_cols(d_heads_low, lambda gathered: times_back(gathered, w_back))
    grad_heads = outer_sum(x_rows, dhead_rows)
    d_x_low = d_x_heads + times_back(d_lr_low, laurel_left)
    d_x_part, gain_zero = norm_backward(
        d_half + d_x_low, x_normed, x_factor, norm_gains[0], width_all
    )
    grad_in = (d_half + d_x_part).astype(jnp.bfloat16)
    head_part = width_total(jnp.stack([d_q_gain, d_k_gain * 0.5]))
    sum_heads, sum_out, sum_gate_up, sum_down = lax.psum(
        (grad_heads, grad_w_out, grad_gate_up, grad_down), "seq"
    )
    sum_left, sum_right, sum_per_gate, sum_per_proj, sum_gains, sum_head_gains = lax.psum(
        (
            grad_laurel_left,
            grad_laurel_right,
            grad_per_gate,
            grad_per_proj,
            jnp.stack([gain_zero, gain_one, gain_two, gain_three, gain_four, gain_five]),
            head_part,
        ),
        ("seq", "col"),
    )
    clip_factor = jnp.sqrt(CLIP_LEVEL / jnp.maximum(logit_top, CLIP_LEVEL))
    clipped_gains = jnp.stack(
        [
            clip_factor[:, None] * head_gains[0][None, :],
            clip_factor[:, None] * head_gains[1][None, :],
        ]
    )
    return (
        layer_out,
        grad_in,
        sum_heads[:, :q_width],
        sum_heads[:, q_width : q_width + key_width],
        sum_heads[:, q_width + key_width :],
        sum_out,
        sum_gate_up[:, :ff_here],
        sum_gate_up[:, ff_here:],
        sum_down,
        sum_left,
        sum_right,
        sum_per_gate,
        sum_per_proj,
        sum_gains,
        sum_head_gains,
        clipped_gains,
    )


def group_gather(values):
    return lax.all_gather(values, ("seq", "col"), axis=0, tiled=True)


def group_scatter(partial):
    return lax.psum_scatter(
        partial.astype(jnp.bfloat16), ("seq", "col"), scatter_dimension=0, tiled=True
    ).astype(jnp.float32)


def to_owner(values):
    seq_count, tokens, width = values.shape
    rows = lax.axis_size("row")
    parts = values.reshape(rows, seq_count * tokens // rows, width)
    moved = lax.all_to_all(parts, "row", split_axis=0, concat_axis=0)
    return moved.transpose(1, 0, 2).reshape(parts.shape[1], rows * width)


def from_owner(values, seq_count):
    tokens, width = values.shape
    rows = lax.axis_size("row")
    parts = values.reshape(tokens, rows, width // rows).transpose(1, 0, 2)
    moved = lax.all_to_all(parts, "row", split_axis=0, concat_axis=0)
    return moved.reshape(seq_count, rows * tokens // seq_count, width // rows)


def mm(left_side, right_side):
    return jnp.dot(left_side, right_side, preferred_element_type=jnp.float32)


def mm_nt(left_side, right_side):
    return lax.dot_general(
        left_side, right_side, (((1,), (1,)), ((), ())), preferred_element_type=jnp.float32
    )


def mm_tn(left_side, right_side):
    return lax.dot_general(
        left_side, right_side, (((0,), (0,)), ((), ())), preferred_element_type=jnp.float32
    )


def rms(values):
    factor = lax.rsqrt(jnp.mean(values * values, axis=-1, keepdims=True) + EPSILON)
    return values * factor, factor


def rms_back(grad_values, normed, factor, gain_vec):
    grad_normed = grad_values * gain_vec
    inner = jnp.mean(grad_normed * normed, axis=-1, keepdims=True)
    return (
        factor * (grad_normed - normed * inner),
        jnp.sum(grad_values * normed, axis=0, keepdims=True),
    )


def gather_rows(values, axis):
    return lax.all_gather(values, "row", axis=axis, tiled=True)


def scatter_rows(values, axis):
    return lax.psum_scatter(
        values.astype(jnp.bfloat16), "row", scatter_dimension=axis, tiled=True
    ).astype(jnp.float32)


def both_cores(values, axis):
    return lax.all_gather(values, "seq", axis=axis, tiled=True)


def remote(src, dst, send_sem, recv_sem, device):
    return pltpu.make_async_remote_copy(
        src_ref=src,
        dst_ref=dst,
        send_sem=send_sem,
        recv_sem=recv_sem,
        device_id=device,
        device_id_type=MESH,
    )


def greet(core, row, col):
    barrier = pltpu.get_barrier_semaphore()
    near = [(core, row ^ 1, col), (core, row ^ 2, col), (core, row ^ 3, col), (1 - core, row, col)]
    for device in near:
        pl.semaphore_signal(barrier, inc=1, device_id=device, device_id_type=MESH)

    @pl.when(col > 0)
    def _():
        pl.semaphore_signal(barrier, inc=1, device_id=(core, row, col - 1), device_id_type=MESH)

    @pl.when(col < 3)
    def _():
        pl.semaphore_signal(barrier, inc=1, device_id=(core, row, col + 1), device_id_type=MESH)

    ends = jnp.where((col == 0) | (col == 3), 1, 2)
    pl.semaphore_wait(barrier, 4 + ends)


class Gather:
    def __init__(self, place, buf, rows, sems):
        self.core, self.row, self.col = place
        self.buf, self.rows = buf, rows
        self.send_z, self.recv_z, self.send_s, self.recv_s = sems

    def part(self, core, col):
        return self.buf.at[pl.ds(pl.multiple_of((core * 4 + col) * self.rows, self.rows), self.rows)]

    def to_right(self, dist):
        part = self.part(self.core, self.col - dist)
        return remote(
            part, part, self.send_z.at[dist], self.recv_z.at[dist], (self.core, self.row, self.col + 1)
        )

    def to_left(self, dist):
        part = self.part(self.core, self.col + dist)
        return remote(
            part,
            part,
            self.send_z.at[3 + dist],
            self.recv_z.at[3 + dist],
            (self.core, self.row, self.col - 1),
        )

    def to_sibling(self, col):
        part = self.part(self.core, col)
        return remote(
            part, part, self.send_s.at[col], self.recv_s.at[col], (1 - self.core, self.row, self.col)
        )

    def start(self):
        col = self.col

        @pl.when(col < 3)
        def _():
            self.to_right(0).start()

        @pl.when(col > 0)
        def _():
            self.to_left(0).start()

        self.to_sibling(col).start()

    def forward(self, work=()):
        col = self.col
        work = list(work)
        for dist in (1, 2, 3):

            @pl.when(col >= dist)
            def _():
                part = self.part(self.core, col - dist)
                remote(
                    part, part, self.send_z.at[0], self.recv_z.at[dist - 1], (self.core, self.row, col)
                ).wait_recv()

                @pl.when(col < 3)
                def _():
                    if dist < 3:
                        self.to_right(dist).start()

                self.to_sibling(col - dist).start()

            @pl.when(col + dist <= 3)
            def _():
                part = self.part(self.core, col + dist)
                remote(
                    part,
                    part,
                    self.send_z.at[0],
                    self.recv_z.at[3 + dist - 1],
                    (self.core, self.row, col),
                ).wait_recv()

                @pl.when(col > 0)
                def _():
                    if dist < 3:
                        self.to_left(dist).start()

                self.to_sibling(col + dist).start()

            if work:
                work.pop(0)()

    def finish(self):
        for col in range(4):
            part = self.part(1 - self.core, col)
            remote(
                part, part, self.send_s.at[col], self.recv_s.at[col], (1 - self.core, self.row, self.col)
            ).wait_recv()
        for col in range(4):
            self.to_sibling(col).wait_send()
        for dist in (0, 1, 2):

            @pl.when((self.col < 3) & (self.col >= dist))
            def _():
                self.to_right(dist).wait_send()

            @pl.when((self.col > 0) & (self.col + dist <= 3))
            def _():
                self.to_left(dist).wait_send()


class Scatter:
    def __init__(self, place, rows, bufs, sems):
        self.core, self.row, self.col = place
        self.rows = rows
        self.give, self.keep, self.got, self.sent, self.left, self.right = bufs
        self.send_z, self.recv_z, self.send_s, self.recv_s = sems

    def sibling(self):
        return remote(
            self.give,
            self.got,
            self.send_s.at[0],
            self.recv_s.at[0],
            (1 - self.core, self.row, self.col),
        )

    def mine(self, dest):
        rows = pl.ds(dest * self.rows, self.rows)
        return self.keep[rows] + self.got[rows].astype(F32)

    def hop(self, dest, right):
        step = 1 if right else -1
        lane = 0 if right else 4
        return remote(
            self.sent.at[dest],
            self.left.at[dest - 1] if right else self.right.at[dest],
            self.send_z.at[lane + dest],
            self.recv_z.at[lane + dest],
            (self.core, self.row, self.col + step),
        )

    def chain(self, dest, right):
        col = self.col
        inner = (col > 0) if right else (col < 3)

        @pl.when((col < dest) if right else (col > dest))
        def _():
            @pl.when(inner)
            def _():
                self.hop(dest, right).wait_recv()
                came = (self.left[dest - 1] if right else self.right[dest]).astype(F32)
                self.sent[dest] = (self.mine(dest) + came).astype(BF)

            @pl.when(jnp.logical_not(inner))
            def _():
                self.sent[dest] = self.mine(dest).astype(BF)

            self.hop(dest, right).start()

    def run(self, result, work=()):
        col = self.col
        work = list(work)
        self.sibling().wait_recv()
        for dest in (3, 2, 1):
            self.chain(dest, True)
            self.chain(3 - dest, False)
            if work:
                work.pop(0)()
        own = pl.ds(pl.multiple_of(col * self.rows, self.rows), self.rows)
        result[...] = self.keep[own] + self.got[own].astype(F32)
        for dest in range(4):

            @pl.when(col == dest)
            def _():
                if dest > 0:
                    self.hop(dest, True).wait_recv()
                    result[...] += self.left[dest - 1].astype(F32)
                if dest < 3:
                    self.hop(dest, False).wait_recv()
                    result[...] += self.right[dest].astype(F32)

        self.sibling().wait_send()
        for dest in (1, 2, 3):

            @pl.when(col < dest)
            def _():
                self.hop(dest, True).wait_send()

            @pl.when(col > 3 - dest)
            def _():
                self.hop(3 - dest, False).wait_send()


class RowGather:
    def __init__(self, place, source, block, halves, sems):
        self.core, self.row, self.col = place
        self.source, self.block, self.halves = source, block, halves
        self.sems = sems

    def neighbour(self, mask):
        return (self.core, self.row ^ mask, self.col)

    def own(self):
        return pltpu.make_async_copy(self.source, self.block(self.row), self.sems.at[8])

    def first(self, mask, block=None):
        lane = mask - 1
        return remote(
            self.source,
            self.block(self.row) if block is None else block,
            self.sems.at[lane],
            self.sems.at[4 + lane],
            self.neighbour(mask),
        )

    def second(self, mask):
        part = self.halves(self.row ^ (3 - mask))[mask - 1]
        return remote(
            part, part, self.sems.at[1 + mask], self.sems.at[5 + mask], self.neighbour(mask)
        )

    def start(self):
        self.first(1).start()
        self.first(2).start()
        self.own().start()

    def forward(self):
        self.first(1, self.block(self.row ^ 1)).wait_recv()
        self.second(2).start()
        self.first(2, self.block(self.row ^ 2)).wait_recv()
        self.second(1).start()

    def finish(self):
        for mask in (1, 2):
            part = self.halves(self.row ^ 3)[mask - 1]
            remote(
                part, part, self.sems.at[1 + mask], self.sems.at[5 + mask], self.neighbour(mask)
            ).wait_recv()
        self.own().wait()
        self.first(1).wait_send()
        self.first(2).wait_send()
        self.second(1).wait_send()
        self.second(2).wait_send()


def by_rows(buf, block_rows):
    half = block_rows // 2

    def block(index):
        return buf.at[pl.ds(pl.multiple_of(index * block_rows, block_rows), block_rows)]

    def halves(index):
        return [
            buf.at[pl.ds(pl.multiple_of(index * block_rows + part * half, half), half)]
            for part in range(2)
        ]

    return block, halves


def by_core_rows(core):
    def split(buf, block_rows):
        own = block_rows // 2

        def piece(index, part, count):
            first = index * block_rows + core * own + part * (own // count)
            return buf.at[pl.ds(pl.multiple_of(first, own // count), own // count)]

        return (
            lambda index: piece(index, 0, 1),
            lambda index: [piece(index, part, 2) for part in range(2)],
        )

    return split


def by_cols(buf, block_cols):
    rows = buf.shape[0] // 2

    def block(index):
        return buf.at[:, pl.ds(pl.multiple_of(index * block_cols, block_cols), block_cols)]

    def halves(index):
        cols = pl.ds(pl.multiple_of(index * block_cols, block_cols), block_cols)
        return [buf.at[pl.ds(part * rows, rows), cols] for part in range(2)]

    return block, halves


def gelu_both(values):
    inner = 0.7978845608028654 * (values + 0.044715 * values * values * values)
    bend = jnp.tanh(inner)
    slope = 0.7978845608028654 * (1.0 + 3.0 * 0.044715 * values * values)
    return 0.5 * values * (1.0 + bend), 0.5 * (1.0 + bend) + 0.5 * values * (1.0 - bend * bend) * slope


def head_parts(raw, gain, cosine, sine):
    factor = lax.rsqrt(jnp.mean(raw * raw, axis=1, keepdims=True) + EPSILON)
    half = raw.shape[1] // 2
    scaled = raw * factor * gain
    first, second = scaled[:, :half], scaled[:, half:]
    return jnp.concatenate([first * cosine - second * sine, second * cosine + first * sine], axis=1)


def forward_kernel(
    x_in,
    g_in,
    gains_in,
    w_query,
    w_kv,
    w_out,
    w_gate,
    w_up,
    w_down,
    laurel_left,
    laurel_right,
    per_gate,
    per_proj,
    cosine,
    sine,
    start,
    head_gains,
    x_own,
    g_own,
    gains,
    raw_q,
    raw_kv,
    q_low,
    kv,
    lse,
    top,
    o_low,
    attn_val,
    lr_low,
    ff_val,
    vll,
    vlr,
    vpg,
    vpp,
    wq_all,
    wkv_all,
    wo_all,
    wg_all,
    wu_all,
    wd_all,
    xg_all,
    fg_all,
    gate_all,
    up_all,
    turned_all,
    w_kv_pair,
    gains_pad,
    vq,
    vkv,
    vo,
    vg,
    vu,
    vd,
    xg,
    fg,
    gate,
    up,
    hid,
    turned,
    give,
    keep,
    got,
    sent,
    left,
    right,
    give2,
    keep2,
    got2,
    sent2,
    left2,
    right2,
    row_sems,
    z_send,
    z_recv,
    s_send,
    s_recv,
    misc_send,
    misc_recv,
    out_sems,
):
    core, row, col = lax.axis_index("seq"), lax.axis_index("row"), lax.axis_index("col")
    place = (core, row, col)
    own_tokens, width = x_own.shape
    block = x_in.shape[2]
    head_dim = head_gains.shape[1]
    tokens = xg.shape[0]
    ff_part = gate.shape[1]
    chunk = 2 * own_tokens
    key_width = w_kv.shape[1]
    half = row % 2
    greet(core, row, col)

    my_cols = pl.ds(pl.multiple_of(row * block, block), block)

    def hand_over(mask):
        return remote(
            x_in.at[row ^ mask],
            x_own.at[:, my_cols],
            misc_send.at[mask],
            misc_recv.at[mask],
            (core, row ^ mask, col),
        )

    def hand_grad(mask):
        return remote(
            g_in.at[row ^ mask],
            g_own.at[:, my_cols],
            misc_send.at[11 + mask],
            misc_recv.at[11 + mask],
            (core, row ^ mask, col),
        )

    def hand_gains(mask):
        return remote(
            gains_pad,
            gains.at[:, my_cols],
            misc_send.at[3 + mask],
            misc_recv.at[3 + mask],
            (core, row ^ mask, col),
        )

    for mask in (3, 1, 2):
        hand_over(mask).start()
    gains_pad[pl.ds(0, 6)] = gains_in[...]
    gains_pad[pl.ds(6, 2)] = jnp.zeros((2, block), F32)
    for mask in (3, 1, 2):
        hand_gains(mask).start()
    x_own[:, my_cols] = x_in[row]
    g_own[:, my_cols] = g_in[row]
    gains[:, my_cols] = gains_pad[...]

    pair_cols = pl.ds(pl.multiple_of(col % 2 * key_width, key_width), key_width)
    pair = remote(
        w_kv, w_kv_pair.at[:, pair_cols], misc_send.at[7], misc_recv.at[7], (core, row, col ^ 1)
    )
    pair.start()
    w_kv_pair[:, pair_cols] = w_kv[...]

    lanes = iter(range(32))

    def rows_of(source, buf, split=by_rows, size=block):
        block_of, halves_of = split(buf, size)
        return RowGather(place, source, block_of, halves_of, row_sems.at[next(lanes)])

    tile = 256
    core_head = pl.ds(pl.multiple_of(core * head_dim, head_dim), head_dim)

    def core_tile(index):
        return pl.ds(pl.multiple_of(core * ff_part + index * tile, tile), tile)

    get_q = rows_of(w_query.at[:, core_head], vq)
    get_kv = rows_of(w_kv_pair, vkv)
    get_o = rows_of(w_out.at[core_head], vo, by_cols)
    get_laurel = [rows_of(laurel_left, vll), rows_of(laurel_right, vlr, by_cols)]
    per_rows, per_cols = per_gate.shape[0] // 2, per_proj.shape[0] // 2
    own_rows = pl.ds(pl.multiple_of(core * per_rows, per_rows), per_rows)
    own_cols = pl.ds(pl.multiple_of(core * per_cols, per_cols), per_cols)
    get_per = [
        rows_of(per_gate.at[own_rows], vpg, by_core_rows(core)),
        rows_of(per_proj.at[own_cols], vpp.at[own_cols], by_cols),
    ]
    tiles = ff_part // tile
    get_gu = [
        [
            rows_of(whole.at[:, core_tile(index)], buf.at[:, pl.ds(index * tile, tile)])
            for whole, buf in ((w_gate, vg), (w_up, vu))
        ]
        for index in range(tiles)
    ]
    half_ff = ff_part // 2
    get_d = [
        rows_of(
            w_down.at[pl.ds(pl.multiple_of(core * ff_part + part * half_ff, half_ff), half_ff)],
            vd.at[pl.ds(part * half_ff, half_ff)],
            by_cols,
        )
        for part in range(2)
    ]

    def per_parts(which, lane):
        parts = [
            vpg.at[pl.ds(pl.multiple_of(index * block + which * per_rows, per_rows), per_rows)]
            for index in range(4)
        ]
        parts.append(vpp.at[pl.ds(pl.multiple_of(which * per_cols, per_cols), per_cols)])
        return list(enumerate(parts, lane))

    def begin(jobs):
        for job in jobs:
            job.start()

    def push(jobs):
        for job in jobs:
            job.forward()

    def complete(jobs):
        for job in jobs:
            job.finish()

    get_q.start()
    pair.wait_recv()
    get_kv.start()

    for mask in (1, 2, 3):
        remote(
            x_in.at[row],
            x_own.at[:, pl.ds(pl.multiple_of((row ^ mask) * block, block), block)],
            misc_send.at[mask],
            misc_recv.at[mask],
            (core, row, col),
        ).wait_recv()
        remote(
            gains_pad,
            gains.at[:, pl.ds(pl.multiple_of((row ^ mask) * block, block), block)],
            misc_send.at[3 + mask],
            misc_recv.at[3 + mask],
            (core, row, col),
        ).wait_recv()

    def own_norm():
        values = x_own[...].astype(F32)
        factor = lax.rsqrt(jnp.mean(values * values, axis=1, keepdims=True) + EPSILON)
        return values, values * factor * gains[pl.ds(0, 1)]

    mine = pl.ds(pl.multiple_of((core * 4 + col) * own_tokens, own_tokens), own_tokens)
    xg[mine] = own_norm()[1].astype(BF)
    sems = lambda lane: (z_send.at[lane], z_recv.at[lane], s_send.at[lane], s_recv.at[lane])
    gather_x = Gather(place, xg, own_tokens, sems(0))
    gather_x.start()
    gather_x.forward(
        [
            lambda: begin([get_o] + get_laurel),
            lambda: push([get_q, get_kv]),
            lambda: push([get_o] + get_laurel),
        ]
    )
    gather_x.finish()
    complete([get_q, get_kv])

    raw_q[...] = mm(xg[...], vq[...])
    raw_kv[...] = mm(xg[...], vkv[...])
    q_low[...] = head_parts(raw_q[...], head_gains[pl.ds(0, 1)], cosine[...], sine[...]).astype(BF)
    is_key = core == 0
    kv_here = head_parts(
        raw_kv[...],
        jnp.where(is_key, head_gains[pl.ds(1, 1)], 1.0),
        jnp.where(is_key, cosine[...], 1.0),
        jnp.where(is_key, sine[...], 0.0),
    ).astype(BF)

    def kv_part(kind, which):
        return kv.at[kind, pl.ds(pl.multiple_of(which * tokens, tokens), tokens)]

    kv[core, pl.ds(pl.multiple_of(half * tokens, tokens), tokens)] = kv_here
    here = kv_part(core, half)
    to_x = remote(here, here, misc_send.at[8], misc_recv.at[8], (core, row ^ 1, col))
    to_s = remote(here, here, misc_send.at[9], misc_recv.at[9], (1 - core, row, col))
    to_x.start()
    to_s.start()
    begin(get_gu[0])
    begin(get_gu[1])
    came = kv_part(core, half ^ 1)
    remote(here, came, misc_send.at[8], misc_recv.at[8], (core, row, col)).wait_recv()
    on_s = remote(came, came, misc_send.at[10], misc_recv.at[10], (1 - core, row, col))
    on_s.start()
    other = kv_part(1 - core, half)
    remote(other, other, misc_send.at[9], misc_recv.at[9], (core, row, col)).wait_recv()
    other_came = kv_part(1 - core, half ^ 1)
    remote(other_came, other_came, misc_send.at[10], misc_recv.at[10], (core, row, col)).wait_recv()

    q_rows = 128
    key_token = lax.broadcasted_iota(jnp.int32, (1, 2 * tokens), 1)
    in_half = key_token % tokens
    key_place = in_half // own_tokens * chunk + key_token // tokens * own_tokens + in_half % own_tokens
    top[...] = jnp.full(top.shape, MASK_FILL, F32)

    def attend(step, carry):
        first = pl.multiple_of(step * q_rows, q_rows)
        rows = pl.ds(first, q_rows)
        token = first + lax.broadcasted_iota(jnp.int32, (q_rows, 1), 0)
        q_place = token // own_tokens * chunk + half * own_tokens + token % own_tokens
        allowed = (key_place <= q_place) & (key_place >= start[rows])
        scores = jnp.where(allowed, mm_nt(q_low[rows], kv[0]), MASK_FILL)
        row_top = jnp.max(scores, axis=1, keepdims=True)
        weights = jnp.exp(scores - row_top)
        total = jnp.sum(weights, axis=1, keepdims=True)
        probs = (weights * (1.0 / total)).astype(BF)
        o_low[rows] = mm(probs, kv[1]).astype(BF)
        lse[rows] = row_top + jnp.log(total)
        top[...] = jnp.maximum(top[...], jnp.max(row_top))
        return carry

    lax.fori_loop(0, tokens // q_rows, attend, 0)
    get_o.finish()

    away = pl.multiple_of((1 - core) * 4 * own_tokens, 4 * own_tokens)
    home = pl.multiple_of(core * 4 * own_tokens, 4 * own_tokens)
    scatter = Scatter(place, own_tokens, (give, keep, got, sent, left, right), sems(1))

    def project(source, weights, target, first):
        def step(index, carry):
            cols = pl.ds(pl.multiple_of(index * block, block), block)
            value = mm(source[pl.ds(first, 4 * own_tokens)], weights[:, cols])
            target[:, cols] = value.astype(target.dtype)
            return carry

        lax.fori_loop(0, width // block, step, 0)

    project(o_low, vo, give, away)
    scatter.sibling().start()
    push(get_gu[0])
    begin(get_gu[2])
    project(o_low, vo, keep, home)
    scatter.run(
        attn_val,
        [lambda: None, lambda: push(get_gu[1]), lambda: begin(get_gu[3])],
    )

    complete(get_laurel)
    inputs, x_norm = own_norm()
    attn_normed = rms(attn_val[...])[0]
    lr_low[...] = mm(xg[mine], vll[...]).astype(BF)
    lo_normed = rms(mm(lr_low[...], vlr[...]))[0]
    h_two = (
        inputs + attn_normed * gains[pl.ds(1, 1)] + (x_norm + lo_normed * gains[pl.ds(2, 1)])
    ) * ROOT_HALF
    fg[mine] = (rms(h_two)[0] * gains[pl.ds(3, 1)]).astype(BF)
    gather_f = Gather(place, fg, own_tokens, sems(2))
    gather_f.start()
    gather_f.forward(
        [
            lambda: push(get_gu[2]),
            lambda: None,
            lambda: None,
        ]
    )
    gather_f.finish()

    def unit_tile(index):
        complete(get_gu[index])
        cols = pl.ds(index * tile, tile)
        bent, slope = gelu_both(mm(fg[...], vg[:, cols]))
        up_part = mm(fg[...], vu[:, cols])
        gate[:, cols] = (up_part * slope).astype(BF)
        up[:, cols] = bent.astype(BF)
        hid[:, cols] = (bent * up_part).astype(BF)

    for index in range(tiles):
        if index == 1:
            push(get_gu[3])
            begin(get_d)
        unit_tile(index)
    turned[...] = hid[...].T
    for job in get_d:
        job.forward()
    keep_weights = [
        pltpu.make_async_copy(source, target, out_sems.at[lane])
        for lane, (source, target) in enumerate(
            [
                (vq, wq_all),
                (vkv, wkv_all),
                (vo, wo_all),
                (vg, wg_all),
                (vu, wu_all),
                (vd, wd_all),
                (xg, xg_all),
                (fg, fg_all),
                (gate, gate_all),
                (up, up_all),
                (turned, turned_all),
            ]
        )
    ]
    begin(get_per)
    for mask in (1, 2, 3):
        hand_grad(mask).start()
    complete(get_d)
    for copy in keep_weights:
        copy.start()
    scatter_ff = Scatter(place, own_tokens, (give2, keep2, got2, sent2, left2, right2), sems(3))
    project(hid, vd, give2, away)
    scatter_ff.sibling().start()
    project(hid, vd, keep2, home)
    scatter_ff.run(ff_val, [lambda: None, lambda: push(get_per)])
    complete(get_per)
    share = [
        remote(part, part, misc_send.at[lane], misc_recv.at[lane], (1 - core, row, col))
        for lane, part in per_parts(core, 16)
    ]
    for copy in share:
        copy.start()
    for lane, part in per_parts(1 - core, 16):
        remote(part, part, misc_send.at[lane], misc_recv.at[lane], (core, row, col)).wait_recv()
    for copy in share:
        copy.wait_send()

    for mask in (1, 2, 3):
        hand_over(mask).wait_send()
        hand_gains(mask).wait_send()
        hand_grad(mask).wait_send()
        remote(
            g_in.at[row],
            g_own.at[:, pl.ds(pl.multiple_of((row ^ mask) * block, block), block)],
            misc_send.at[11 + mask],
            misc_recv.at[11 + mask],
            (core, row, col),
        ).wait_recv()
    pair.wait_send()
    to_x.wait_send()
    to_s.wait_send()
    on_s.wait_send()
    for copy in keep_weights:
        copy.wait()


def run_forward(x_in, g_in, gains_in, weights_in, tables, head_gains):
    cosine, sine, start = tables
    w_gate, laurel_left, per_gate, per_proj = (weights_in[i] for i in (3, 6, 8, 9))
    block = x_in.shape[2]
    own, width = x_in.shape[1], 4 * block
    tokens, head_dim, ff_part = 8 * own, head_gains.shape[1], w_gate.shape[1] // 2
    rank = laurel_left.shape[1]
    vm = pl.BlockSpec(memory_space=pltpu.VMEM)
    hbm = pl.BlockSpec(memory_space=pl.ANY)
    shape = jax.ShapeDtypeStruct
    weights = [
        (width, head_dim),
        (width, head_dim),
        (head_dim, width),
        (width, ff_part),
        (width, ff_part),
        (ff_part, width),
    ]
    acts = [
        (tokens, width),
        (tokens, width),
        (tokens, ff_part),
        (tokens, ff_part),
    ]
    outs = [
        shape((own, width), BF),
        shape((own, width), BF),
        shape((8, width), F32),
        shape((tokens, head_dim), F32),
        shape((tokens, head_dim), F32),
        shape((tokens, head_dim), BF),
        shape((2, 2 * tokens, head_dim), BF),
        shape((tokens, 1), F32),
        shape((8, 128), F32),
        shape((tokens, head_dim), BF),
        shape((own, width), F32),
        shape((own, rank), BF),
        shape((own, width), F32),
        shape((width, rank), BF),
        shape((rank, width), BF),
        shape((width, per_gate.shape[1]), BF),
        shape((per_proj.shape[0], width), BF),
    ] + [shape(size, BF) for size in weights + acts + [(ff_part, tokens)]]
    scatter_bufs = [
        pltpu.VMEM((4 * own, width), BF),
        pltpu.VMEM((4 * own, width), F32),
        pltpu.VMEM((4 * own, width), BF),
        pltpu.VMEM((4, own, width), BF),
        pltpu.VMEM((3, own, width), BF),
        pltpu.VMEM((3, own, width), BF),
    ]
    dma = pltpu.SemaphoreType.DMA
    return pl.pallas_call(
        forward_kernel,
        out_shape=outs,
        in_specs=[vm, vm, vm, hbm, vm] + [hbm] * 8 + [vm] * 4,
        out_specs=[vm] * 17 + [hbm] * 11,
        scratch_shapes=[pltpu.VMEM((block, head_dim), BF), pltpu.VMEM((8, block), F32)]
        + [pltpu.VMEM(size, BF) for size in weights + acts]
        + [pltpu.VMEM((tokens, ff_part), BF), pltpu.VMEM((ff_part, tokens), BF)]
        + scatter_bufs * 2
        + [
            dma((17, 10)),
            dma((4, 8)),
            dma((4, 8)),
            dma((4, 4)),
            dma((4, 4)),
            dma((24,)),
            dma((24,)),
            dma((11,)),
        ],
        compiler_params=pltpu.CompilerParams(
            collective_id=0, has_side_effects=True, vmem_limit_bytes=VMEM_BYTES
        ),
        cost_estimate=pl.CostEstimate(flops=2 * 10**10, bytes_accessed=5 * 10**7, transcendentals=10**6),
    )(x_in, g_in, gains_in, *weights_in, cosine, sine, start, head_gains)


class RowScatter:
    def __init__(self, place, halves, came, sems, stage=None):
        self.core, self.row, self.col = place
        self.halves, self.came, self.sems = halves, came, sems
        self.stage = stage

    def send(self, lane, index, half, mask):
        return remote(
            self.halves(index)[half],
            self.came.at[lane],
            self.sems.at[lane],
            self.sems.at[6 + lane],
            (self.core, self.row ^ mask, self.col),
        )

    def lane(self, lane):
        index, half, mask = ((1, 0, 1), (3, 0, 1), (2, 1, 2), (3, 1, 2), (2, 0, 2), (1, 1, 1))[lane]
        return self.send(lane, self.row ^ index, half, mask)

    def start(self, lanes=(1, 3, 0, 2)):
        for lane in lanes:
            self.lane(lane).start()

    def load(self, lane):
        slot = {0: 0, 1: 0, 4: 0, 2: 1, 3: 1, 5: 1}[lane]
        return slot, pltpu.make_async_copy(
            self.came.at[lane], self.stage[0].at[slot], self.stage[1].at[slot]
        )

    def fetch(self, *lanes):
        for lane in lanes:
            self.lane(lane).wait_recv()
            if self.stage is not None:
                self.load(lane)[1].start()

    def add(self, lane, index, half):
        if self.stage is None:
            value = self.came[lane]
        else:
            slot, copy = self.load(lane)
            copy.wait()
            value = self.stage[0][slot]
        part = self.halves(self.row ^ index)[half]
        part[...] = (part[...].astype(F32) + value.astype(F32)).astype(BF)

    def middle(self):
        for lane, out, index, half in ((1, 4, 2, 0), (3, 5, 1, 1)):
            self.add(lane, index, half)
            self.lane(out).start()

    def early(self):
        self.add(0, 0, 0)
        self.add(2, 0, 1)

    def finish(self):
        self.add(4, 0, 0)
        self.add(5, 0, 1)

    def drain(self):
        for lane in range(6):
            self.lane(lane).wait_send()


def head_back(grad, raw, gain, cosine, sine):
    factor = lax.rsqrt(jnp.mean(raw * raw, axis=1, keepdims=True) + EPSILON)
    half = raw.shape[1] // 2
    normed = raw * factor
    first, second = grad[:, :half], grad[:, half:]
    back = jnp.concatenate([first * cosine + second * sine, second * cosine - first * sine], axis=1)
    gain_grad = jnp.sum(back * normed, axis=0, keepdims=True)
    inner = back * gain
    return factor * (inner - normed * jnp.mean(inner * normed, axis=1, keepdims=True)), gain_grad


def backward_kernel(
    x_own,
    g_own,
    per_in,
    gains,
    head_gains,
    attn_val,
    lr_low,
    ff_val,
    raw_q,
    raw_kv,
    q_low,
    kv,
    lse,
    top,
    o_low,
    cosine,
    sine,
    start,
    vll,
    vlr,
    vpg,
    vpp,
    xg_in,
    fg_in,
    gate_in,
    up_in,
    turned_in,
    wq_in,
    wkv_in,
    wo_in,
    wg_in,
    wu_in,
    wd_in,
    y_out,
    x_grad,
    g_gain,
    tops,
    small_a,
    gq,
    gkv,
    gout,
    ggate,
    gup,
    gdown,
    came_g,
    came_u,
    turned_all,
    vq,
    vkv,
    vo,
    vg,
    vu,
    vd,
    fg,
    gate,
    up,
    dff_all,
    down_stage,
    dffg,
    dattng,
    dgate,
    dup,
    give,
    keep,
    got,
    sent,
    left,
    right,
    own_sum,
    h_two_ref,
    d_three_ref,
    low_ref,
    gpart,
    gcame,
    gpart2,
    gcame2,
    small_give,
    small_keep,
    small_got,
    small_row,
    small_z,
    d_o,
    d_kv,
    kv_give,
    kv_got,
    kv_x_got,
    kv_p_got,
    pkv,
    came_q,
    came_kv,
    came_o,
    stage_g,
    stage_sems,
    load_sems,
    row_sems,
    z_send,
    z_recv,
    s_send,
    s_recv,
    misc_send,
    misc_recv,
    gain_send,
    gain_recv,
    done_sems,
    ff_sems,
    down_sems,
):
    core, row, col = lax.axis_index("seq"), lax.axis_index("row"), lax.axis_index("col")
    place = (core, row, col)
    own_tokens, width = x_own.shape
    block = width // 4
    tokens, head_dim = raw_q.shape
    ff_part = gate.shape[1]
    chunk = 2 * own_tokens
    key_width = head_dim // 2
    half = row % 2
    rank = lr_low.shape[1]
    my_cols = pl.ds(pl.multiple_of(row * block, block), block)
    mine = pl.ds(pl.multiple_of((core * 4 + col) * own_tokens, own_tokens), own_tokens)
    away = pl.multiple_of((1 - core) * 4 * own_tokens, 4 * own_tokens)
    home = pl.multiple_of(core * 4 * own_tokens, 4 * own_tokens)

    barrier = pltpu.get_barrier_semaphore()
    for mask in (1, 2, 3):
        pl.semaphore_signal(barrier, inc=1, device_id=(core, row ^ mask, col), device_id_type=MESH)
        for other in (0, 1):
            pl.semaphore_signal(
                barrier, inc=1, device_id=(core ^ other, row, col ^ mask), device_id_type=MESH
            )
    pl.semaphore_signal(barrier, inc=1, device_id=(1 - core, row, col), device_id_type=MESH)
    loads = [
        pltpu.make_async_copy(source, target, load_sems.at[lane])
        for lane, (source, target) in enumerate(
            [
                (wd_in, vd),
                (gate_in, gate),
                (up_in, up),
                (wg_in, vg),
                (wu_in, vu),
                (fg_in, fg),
                (wo_in, vo),
                (wq_in, vq),
                (wkv_in, vkv),
            ]
        )
    ]
    for load in loads:
        load.start()
    pl.semaphore_wait(barrier, 10)
    block_of, halves_of = by_cols(turned_all, tokens)
    get_turned = RowGather(place, turned_in, block_of, halves_of, row_sems.at[0])
    get_turned.start()

    def gain(index):
        return gains[pl.ds(index, 1)]

    inputs = x_own[...].astype(F32)
    x_norm = rms(inputs)[0] * gain(0)
    attn_normed = rms(attn_val[...])[0]
    lo_normed = rms(mm(lr_low[...], vlr[...]))[0]
    h_two = (inputs + attn_normed * gain(1) + (x_norm + lo_normed * gain(2))) * ROOT_HALF
    h_two_ref[...] = h_two
    ff_normed, ff_factor = rms(ff_val[...])
    h_three = h_two + ff_normed * gain(4)
    h_low = h_three.astype(BF)
    p_gate, p_proj = vpg[...], vpp[...]
    pg_gelu, pg_slope = gelu_both(mm(h_low, p_gate))
    per_input = per_in[row].astype(F32)
    gp_low = (pg_gelu * per_input).astype(BF)
    pp_normed, pp_factor = rms(mm(gp_low, p_proj))
    low_ref[...] = (h_three + pp_normed * gain(5)).astype(BF)

    def hand_back(source, target, mask, lane):
        return remote(
            source.at[:, pl.ds(pl.multiple_of((row ^ mask) * block, block), block)],
            target.at[row],
            misc_send.at[lane + mask],
            misc_recv.at[lane + mask],
            (core, row ^ mask, col),
        )

    def came_back(target, mask, lane):
        return remote(
            target.at[row ^ mask],
            target.at[row ^ mask],
            misc_send.at[lane + mask],
            misc_recv.at[lane + mask],
            (core, row, col),
        )

    for mask in (1, 2, 3):
        hand_back(low_ref, y_out, mask, 0).start()
    y_out[row] = low_ref[:, my_cols]

    grad_top = g_own[...].astype(F32)
    d_pp, gain_five = rms_back(grad_top, pp_normed, pp_factor, gain(5))
    d_pp_low = d_pp.astype(BF)
    d_pg_low = (mm_nt(d_pp_low, p_proj) * per_input * pg_slope).astype(BF)
    d_three = grad_top + mm_nt(d_pg_low, p_gate)
    d_three_ref[...] = d_three
    d_ff, gain_four = rms_back(d_three, ff_normed, ff_factor, gain(4))
    gpart[...] = jnp.zeros(gpart.shape, F32)
    gpart[pl.ds(5, 1)] = gain_five
    gpart[pl.ds(4, 1)] = gain_four
    dffg[mine] = d_ff.astype(BF)
    sems = lambda lane: (z_send.at[lane], z_recv.at[lane], s_send.at[lane], s_recv.at[lane])
    gather_ff = Gather(place, dffg, own_tokens, sems(0))
    gather_ff.start()

    def small(kind, first, value):
        rows = pl.ds(first, value.shape[0])
        value = value.astype(BF)

        @pl.when(core == kind)
        def _():
            small_keep[rows] = value

        @pl.when(core != kind)
        def _():
            small_give[rows] = value

    small(0, rank, mm_tn(gp_low, d_pp_low))
    small(1, rank, mm_tn(d_pg_low, h_low))
    gather_ff.forward([lambda: None, lambda: None, get_turned.forward])
    gather_ff.finish()

    part_rows = tokens // 2

    def ff_piece(group, which):
        return dff_all.at[
            pl.ds(pl.multiple_of(group * tokens + which * part_rows, part_rows), part_rows)
        ]

    def ff_over(mask):
        return remote(
            dffg.at[
                pl.ds(pl.multiple_of(core * part_rows, part_rows), part_rows),
                pl.ds(pl.multiple_of((row ^ mask) * block, block), block),
            ],
            ff_piece(row, core),
            ff_sems.at[mask],
            ff_sems.at[4 + mask],
            (core, row ^ mask, col),
        )

    def ff_came(mask):
        part = ff_piece(row ^ mask, core)
        return remote(part, part, ff_sems.at[mask], ff_sems.at[4 + mask], (core, row, col))

    def ff_share(mask, which):
        part = ff_piece(row ^ mask, which)
        return remote(
            part, part, ff_sems.at[8 + mask], ff_sems.at[12 + mask], (1 - core, row, col)
        )

    for mask in (1, 2, 3):
        ff_over(mask).start()
    dff_all[pl.ds(pl.multiple_of(row * tokens, tokens), tokens)] = dffg[:, my_cols]

    tile = 256
    for load in loads[:3]:
        load.wait()

    def units(index, carry):
        cols = pl.ds(pl.multiple_of(index * tile, tile), tile)
        d_hid = mm_nt(dffg[...], vd[cols])
        dgate[:, cols] = (d_hid * gate[:, cols].astype(F32)).astype(BF)
        dup[:, cols] = (d_hid * up[:, cols].astype(F32)).astype(BF)
        return carry

    lax.fori_loop(0, ff_part // tile, units, 0)
    for load in loads[3:5]:
        load.wait()

    def back_ff(target, first):
        rows = pl.ds(first, 4 * own_tokens)

        def step(index, carry):
            cols = pl.ds(pl.multiple_of(index * block, block), block)
            value = mm_nt(dgate[rows], vg[cols]) + mm_nt(dup[rows], vu[cols])
            target[:, cols] = value.astype(target.dtype)
            return carry

        lax.fori_loop(0, width // block, step, 0)

    scatter_f = Scatter(place, own_tokens, (give, keep, got, sent, left, right), sems(1))
    back_ff(give, away)
    scatter_f.sibling().start()
    back_ff(keep, home)

    put_g = RowScatter(place, by_rows(vg, block)[1], came_g, row_sems.at[1], (stage_g, stage_sems))
    put_u = RowScatter(place, by_rows(vu, block)[1], came_u, row_sems.at[2], (stage_g, stage_sems))

    load_turned = pltpu.make_async_copy(turned_all, vd, load_sems.at[5])

    def down_ready():
        get_turned.finish()
        load_turned.start()
        for mask in (1, 2, 3):
            ff_came(mask).wait_recv()
            ff_share(mask, core).start()

    def down_tile(index):
        slot = index % 2
        rows = pl.ds(index * tile, tile)
        target = gdown.at[pl.ds(pl.multiple_of(core * ff_part + index * tile, tile), tile)]
        local = pltpu.make_async_copy(down_stage.at[slot], target, down_sems.at[index])
        over = remote(
            down_stage.at[slot],
            target,
            down_sems.at[4 + index],
            down_sems.at[8 + index],
            (1 - core, row, col),
        )
        return slot, rows, local, over

    def down_grad():
        load_turned.wait()
        for mask in (1, 2, 3):
            ff_share(mask, 1 - core).wait_recv()
        for index in range(ff_part // tile):
            slot, rows, local, over = down_tile(index)
            if index >= 2:
                before = down_tile(index - 2)
                before[2].wait()
                before[3].wait_send()
            down_stage[slot] = mm(vd[rows], dff_all[...]).astype(BF)
            local.start()
            over.start()

    def gate_grad(target, grad, put):
        def step(index, carry):
            rows = pl.ds(pl.multiple_of(index * tile, tile), tile)
            target[rows] = mm_tn(fg[:, rows], grad[...]).astype(BF)
            return carry

        lax.fori_loop(0, width // tile, step, 0)

    def start_gate():
        loads[5].wait()
        gate_grad(vg, dgate, put_g)
        put_g.start()

    def start_up():
        gate_grad(vu, dup, put_u)
        put_u.start((1, 3))

    scatter_f.run(own_sum, [start_gate, start_up, down_ready])

    f_normed, f_factor = rms(h_two_ref[...])
    d_f, gain_three = rms_back(own_sum[...], f_normed, f_factor, gain(3))
    d_half = (d_three_ref[...] + d_f) * ROOT_HALF
    d_three_ref[...] = d_half
    attn_normed, attn_factor = rms(attn_val[...])
    d_attn, gain_one = rms_back(d_half, attn_normed, attn_factor, gain(1))
    dattng[mine] = d_attn.astype(BF)
    gather_a = Gather(place, dattng, own_tokens, sems(2))
    gather_a.start()
    lo_normed, lo_factor = rms(mm(lr_low[...], vlr[...]))
    d_lo, gain_two = rms_back(d_half, lo_normed, lo_factor, gain(2))
    d_lo_low = d_lo.astype(BF)
    d_lr_low = mm_nt(d_lo_low, vlr[...]).astype(BF)
    small(0, 0, mm_tn(lr_low[...], d_lo_low))
    x_low = (rms(x_own[...].astype(F32))[0] * gain(0)).astype(BF)
    small(1, 0, mm_tn(d_lr_low, x_low))
    own_sum[...] = d_half + mm_nt(d_lr_low, vll[...])
    gpart[pl.ds(3, 1)] = gain_three
    gpart[pl.ds(2, 1)] = gain_two
    gpart[pl.ds(1, 1)] = gain_one
    small_swap = remote(
        small_give, small_got, misc_send.at[8], misc_recv.at[8], (1 - core, row, col)
    )
    small_swap.start()
    put_s = RowScatter(place, by_cols(small_keep, block)[1], small_row, row_sems.at[6])

    def small_sum():
        small_swap.wait_recv()
        small_keep[...] = (small_keep[...].astype(F32) + small_got[...].astype(F32)).astype(BF)
        put_s.start()

    def middle_gate():
        put_g.fetch(1, 3)
        down_grad()
        put_g.middle()

    def more_up():
        put_u.start((0, 2))
        small_sum()
        put_g.fetch(0, 2)

    gather_a.forward([middle_gate, more_up, put_g.early])
    gather_a.finish()

    loads[6].wait()
    d_o[...] = mm_nt(dattng[...], vo[...]).astype(BF)
    q_rows = 128
    key_token = lax.broadcasted_iota(jnp.int32, (1, 2 * tokens), 1)
    in_half = key_token % tokens
    key_place = in_half // own_tokens * chunk + key_token // tokens * own_tokens + in_half % own_tokens
    d_kv[...] = jnp.zeros(d_kv.shape, F32)

    def attend(step, carry):
        first = pl.multiple_of(step * q_rows, q_rows)
        rows = pl.ds(first, q_rows)
        token = first + lax.broadcasted_iota(jnp.int32, (q_rows, 1), 0)
        q_place = token // own_tokens * chunk + half * own_tokens + token % own_tokens
        allowed = (key_place <= q_place) & (key_place >= start[rows])
        scores = jnp.where(allowed, mm_nt(q_low[rows], kv[0]), MASK_FILL)
        probs = jnp.exp(scores - lse[rows])
        d_probs = mm_nt(d_o[rows], kv[1])
        delta = jnp.sum(probs * d_probs, axis=1, keepdims=True)
        d_scores = (probs * (d_probs - delta)).astype(BF)
        d_kv[0] += mm_tn(d_scores, q_low[rows])
        d_kv[1] += mm_tn(probs.astype(BF), d_o[rows])
        d_raw, gain_part = head_back(
            mm(d_scores, kv[0]), raw_q[rows], head_gains[pl.ds(0, 1)], cosine[rows], sine[rows]
        )
        d_o[rows] = d_raw.astype(BF)
        return carry + gain_part

    gain_q = lax.fori_loop(0, tokens // q_rows, attend, jnp.zeros((1, head_dim), F32))

    kv_give[...] = d_kv[1 - core].astype(BF)
    swap_kv = remote(kv_give, kv_got, misc_send.at[9], misc_recv.at[9], (1 - core, row, col))
    swap_kv.start()

    def out_grad():
        for part in range(2):
            wide = pl.ds(part * (width // 2), width // 2)
            vo[:, wide] = mm_tn(o_low[...], dattng[:, wide]).astype(BF)

    put_o = RowScatter(place, by_cols(vo, block)[1], came_o, row_sems.at[3])
    swap_kv.wait()
    kv_x = kv_give.at[pl.ds(0, tokens)]
    theirs = pl.ds(pl.multiple_of((half ^ 1) * tokens, tokens), tokens)
    ours = pl.ds(pl.multiple_of(half * tokens, tokens), tokens)
    kv_x[...] = (d_kv[core, theirs] + kv_got[theirs].astype(F32)).astype(BF)
    over_x = remote(kv_x, kv_x_got, misc_send.at[10], misc_recv.at[10], (core, row ^ 1, col))
    over_x.start()
    load_x = pltpu.make_async_copy(xg_in, dffg, load_sems.at[10])
    for mask in (1, 2, 3):
        ff_over(mask).wait_send()
    load_x.start()
    put_u.fetch(1, 3)
    out_grad()
    put_u.middle()
    put_o.start()
    put_s.fetch(1, 3)
    put_s.middle()
    loads[7].wait()
    loads[8].wait()
    over_x.wait_recv()
    d_kind = d_kv[core, ours] + kv_got[ours].astype(F32) + kv_x_got[...].astype(F32)
    kv_p = kv_got.at[pl.ds(0, tokens)]
    kv_p[...] = d_kind.astype(BF)
    over_p = remote(kv_p, kv_p_got, misc_send.at[11], misc_recv.at[11], (core, row, col ^ 1))
    over_p.start()
    put_u.fetch(0, 2)
    put_u.early()
    over_p.wait()
    d_kind = kv_p[...].astype(F32) + kv_p_got[...].astype(F32)
    is_key = core == 0
    d_kind_raw, gain_k = head_back(
        d_kind,
        raw_kv[...],
        jnp.where(is_key, head_gains[pl.ds(1, 1)], 1.0),
        jnp.where(is_key, cosine[...], 1.0),
        jnp.where(is_key, sine[...], 0.0),
    )
    for part in range(4):
        gpart[pl.ds(6, 1), pl.ds(part * block, head_dim)] = gain_q
        gpart[pl.ds(6, 1), pl.ds(part * block + head_dim, head_dim)] = gain_k * jnp.where(
            is_key, 0.5, 0.0
        )
    kv_p[...] = d_kind_raw.astype(BF)
    pair_cols = pl.ds(pl.multiple_of(col % 2 * key_width, key_width), key_width)

    def back_heads(target, first):
        rows = pl.ds(first, 4 * own_tokens)

        def step(index, carry):
            cols = pl.ds(pl.multiple_of(index * block, block), block)
            value = mm_nt(d_o[rows], vq[cols]) + mm_nt(kv_p[rows, pair_cols], vkv[cols, pair_cols])
            target[:, cols] = value.astype(target.dtype)
            return carry

        lax.fori_loop(0, width // block, step, 0)

    scatter_x = Scatter(place, own_tokens, (give, keep, got, sent, left, right), sems(3))
    back_heads(give, away)
    scatter_x.sibling().start()
    back_heads(keep, home)
    put_q = RowScatter(place, by_rows(vq, block)[1], came_q, row_sems.at[4])
    put_kv = RowScatter(place, by_rows(pkv, block)[1], came_kv, row_sems.at[5])

    def query_grad():
        load_x.wait()

        def step(index, carry):
            rows = pl.ds(pl.multiple_of(index * tile, tile), tile)
            vq[rows] = mm_tn(dffg[:, rows], d_o[...]).astype(BF)
            pkv[rows] = mm_tn(dffg[:, rows], kv_p[:, pair_cols]).astype(BF)
            return carry

        lax.fori_loop(0, width // tile, step, 0)
        put_q.start()
        put_kv.start()

    def deliver(lane, source, target):
        local = pltpu.make_async_copy(source, target, done_sems.at[lane])
        over = remote(
            source, target, done_sems.at[8 + lane], done_sems.at[16 + lane], (1 - core, row, col)
        )
        local.start()
        over.start()
        done.append((local, over))

    core_ff = pl.ds(pl.multiple_of(core * ff_part, ff_part), ff_part)
    core_head = pl.ds(pl.multiple_of(core * head_dim, head_dim), head_dim)
    sib_ff = pl.ds(pl.multiple_of((1 - core) * ff_part, ff_part), ff_part)
    sib_head = pl.ds(pl.multiple_of((1 - core) * head_dim, head_dim), head_dim)
    row_block = pl.ds(pl.multiple_of(row * block, block), block)
    done = []

    quarter = block // 4

    def small_quarter(mask):
        return remote(
            small_keep.at[
                :, pl.ds(pl.multiple_of(row * block + (col ^ mask) * quarter, quarter), quarter)
            ],
            small_z.at[mask],
            misc_send.at[11 + mask],
            misc_recv.at[11 + mask],
            (core, row, col ^ mask),
        )

    def small_finish():
        put_s.fetch(0, 2, 4, 5)
        put_s.early()
        put_s.finish()
        for mask in (1, 2, 3):
            small_quarter(mask).start()

    def gate_finish():
        put_o.fetch(1, 3)
        put_o.middle()
        put_g.fetch(4, 5)
        put_g.finish()
        deliver(1, vg.at[row_block], ggate.at[:, core_ff])

    d_half_here = d_three_ref
    scatter_x.run(h_two_ref, [query_grad, small_finish, gate_finish])
    d_xn = own_sum[...] + h_two_ref[...]
    x_normed, x_factor = rms(x_own[...].astype(F32))
    d_in, gain_zero = rms_back(d_xn, x_normed, x_factor, gain(0))
    gpart[pl.ds(0, 1)] = gain_zero
    for mask in (1, 2, 3):
        hand_back(low_ref, y_out, mask, 0).wait_send()
    low_ref[...] = (d_half_here[...] + d_in).astype(BF)
    for mask in (1, 2, 3):
        hand_back(low_ref, x_grad, mask, 4).start()
    x_grad[row] = low_ref[:, my_cols]

    gpart[pl.ds(8, 8)] = jnp.full((8, width), jnp.max(top[...]), F32)

    def gain_row(mask):
        return remote(
            gpart.at[:, pl.ds(pl.multiple_of((row ^ mask) * block, block), block)],
            gcame.at[mask],
            gain_send.at[mask],
            gain_recv.at[mask],
            (core, row ^ mask, col),
        )

    for mask in (1, 2, 3):
        gain_row(mask).start()
    gcame[0] = gpart[:, my_cols]
    for mask in (1, 2, 3):
        gain_row(mask).wait_recv()
    summed = gcame[0] + gcame[1] + gcame[2] + gcame[3]
    largest = jnp.maximum(jnp.maximum(gcame[0], gcame[1]), jnp.maximum(gcame[2], gcame[3]))
    gpart2[pl.ds(0, 8)] = summed[:8]
    gpart2[pl.ds(8, 8)] = largest[8:]
    me = core * 4 + col
    members = [(other, mask) for other in (0, 1) for mask in range(4) if other or mask]

    def gain_group(other, mask):
        lane = 4 + other * 4 + mask
        return remote(
            gpart2,
            gcame2.at[me],
            gain_send.at[lane],
            gain_recv.at[lane],
            (core ^ other, row, col ^ mask),
        )

    for other, mask in members:
        gain_group(other, mask).start()
    gcame2[me] = gpart2[...]
    put_kv.fetch(1, 3)
    put_kv.middle()
    put_q.fetch(1, 3)
    put_q.middle()
    put_u.fetch(4, 5)

    def small_share(other, mask):
        lane = 16 + other * 4 + mask
        return remote(
            kv_x.at[pl.ds(0, small_keep.shape[0]), pl.ds(0, quarter)],
            small_a.at[core, col],
            misc_send.at[lane],
            misc_recv.at[lane],
            (core ^ other, row, col ^ mask),
        )

    put_u.finish()
    deliver(2, vu.at[row_block], gup.at[:, core_ff])
    for mask in (1, 2, 3):
        small_quarter(mask).wait_recv()
    small_total = small_keep[
        :, pl.ds(pl.multiple_of(row * block + col * quarter, quarter), quarter)
    ].astype(F32)
    for mask in (1, 2, 3):
        small_total = small_total + small_z[mask].astype(F32)
    over_x.wait_send()
    kv_x[pl.ds(0, small_keep.shape[0]), pl.ds(0, quarter)] = small_total.astype(BF)
    for other, mask in members:
        small_share(other, mask).start()
    small_a[core, col] = small_total.astype(BF)
    for put, lane, source, target in (
        (put_o, 4, vo.at[:, row_block], gout.at[core_head]),
        (put_kv, 3, pkv.at[row_block], gkv.at[core]),
        (put_q, 5, vq.at[row_block], gq.at[:, core_head]),
    ):
        put.fetch(0, 2, 4, 5)
        put.early()
        put.finish()
        deliver(lane, source, target)

    for other, mask in members:
        who = (core ^ other) * 4 + (col ^ mask)
        lane = 4 + other * 4 + mask
        remote(
            gpart2, gcame2.at[who], gain_send.at[lane], gain_recv.at[lane], (core, row, col)
        ).wait_recv()
    total = gcame2[0]
    for who in range(1, 8):
        total = total + gcame2[who]
    g_gain[...] = total[:8]
    for who in range(8):
        head = 2 * (who % 4) + who // 4
        tops[pl.ds(head, 1)] = gcame2[who, pl.ds(8, 1), pl.ds(0, 128)]

    for other, mask in members:
        part = small_a.at[core ^ other, col ^ mask]
        lane = 16 + other * 4 + mask
        remote(part, part, misc_send.at[lane], misc_recv.at[lane], (core, row, col)).wait_recv()
        small_share(other, mask).wait_send()
        gain_group(other, mask).wait_send()
    for mask in (1, 2, 3):
        came_back(y_out, mask, 0).wait_recv()
        came_back(x_grad, mask, 4).wait_recv()
        hand_back(low_ref, x_grad, mask, 4).wait_send()
        gain_row(mask).wait_send()
        small_quarter(mask).wait_send()
    small_swap.wait_send()
    for put in (put_g, put_u, put_o, put_q, put_kv, put_s):
        put.drain()
    for mask in (1, 2, 3):
        ff_share(mask, core).wait_send()
    for index in range(ff_part // tile):
        slot, rows, local, over = down_tile(index)
        if index >= 2:
            local.wait()
            over.wait_send()
        target = gdown.at[pl.ds(pl.multiple_of((1 - core) * ff_part + index * tile, tile), tile)]
        remote(
            target, target, down_sems.at[4 + index], down_sems.at[8 + index], (core, row, col)
        ).wait_recv()
    theirs_at = {
        1: ggate.at[:, sib_ff],
        2: gup.at[:, sib_ff],
        3: gkv.at[1 - core],
        4: gout.at[sib_head],
        5: gq.at[:, sib_head],
    }
    for lane, (local, over) in zip((1, 2, 4, 3, 5), done):
        local.wait()
        over.wait_send()
        target = theirs_at[lane]
        remote(
            target, target, done_sems.at[8 + lane], done_sems.at[16 + lane], (core, row, col)
        ).wait_recv()


def run_backward(small_args, big_args):
    x_own, per_in, head_gains = small_args[0], small_args[2], small_args[4]
    own, width = x_own.shape
    block = width // 4
    gate = big_args[2]
    tokens, ff_part = gate.shape
    head_dim = head_gains.shape[1]
    rank = small_args[6].shape[1]
    small_rows = sum(small_args[lane].shape[0] for lane in (19, 21))
    vm = pl.BlockSpec(memory_space=pltpu.VMEM)
    hbm = pl.BlockSpec(memory_space=pl.ANY)
    shape = jax.ShapeDtypeStruct
    vmem = pltpu.VMEM
    dma = pltpu.SemaphoreType.DMA
    outs = [
        shape((4, own, block), BF),
        shape((4, own, block), BF),
        shape((8, block), F32),
        shape((8, 128), F32),
        shape((2, 4, small_rows, block // 4), BF),
        shape((block, 2 * head_dim), BF),
        shape((2, block, head_dim // 2), BF),
        shape((2 * head_dim, block), BF),
        shape((block, 2 * ff_part), BF),
        shape((block, 2 * ff_part), BF),
        shape((2 * ff_part, block), BF),
        shape((6, block // 2, ff_part), BF),
        shape((6, block // 2, ff_part), BF),
        shape((ff_part, 4 * tokens), BF),
    ]
    scratch = [
        vmem((width, head_dim), BF),
        vmem((width, head_dim), BF),
        vmem((head_dim, width), BF),
        vmem((width, ff_part), BF),
        vmem((width, ff_part), BF),
        vmem((ff_part, width), BF),
        vmem((tokens, width), BF),
        vmem((tokens, ff_part), BF),
        vmem((tokens, ff_part), BF),
        vmem((4 * tokens, block), BF),
        vmem((2, 256, block), BF),
        vmem((tokens, width), BF),
        vmem((tokens, width), BF),
        vmem((tokens, ff_part), BF),
        vmem((tokens, ff_part), BF),
        vmem((4 * own, width), BF),
        vmem((4 * own, width), F32),
        vmem((4 * own, width), BF),
        vmem((4, own, width), BF),
        vmem((3, own, width), BF),
        vmem((3, own, width), BF),
        vmem((own, width), F32),
        vmem((own, width), F32),
        vmem((own, width), F32),
        vmem((own, width), BF),
        vmem((16, width), F32),
        vmem((4, 16, block), F32),
        vmem((16, block), F32),
        vmem((8, 16, block), F32),
        vmem((small_rows, width), BF),
        vmem((small_rows, width), BF),
        vmem((small_rows, width), BF),
        vmem((6, small_rows // 2, block), BF),
        vmem((4, small_rows, block // 4), BF),
        vmem((tokens, head_dim), BF),
        vmem((2, 2 * tokens, head_dim), F32),
        vmem((2 * tokens, head_dim), BF),
        vmem((2 * tokens, head_dim), BF),
        vmem((tokens, head_dim), BF),
        vmem((tokens, head_dim), BF),
        vmem((width, head_dim // 2), BF),
        vmem((6, block // 2, head_dim), BF),
        vmem((6, block // 2, head_dim // 2), BF),
        vmem((6, head_dim // 2, block), BF),
        vmem((2, block // 2, ff_part), BF),
        dma((2,)),
        dma((11,)),
        dma((7, 12)),
        dma((4, 8)),
        dma((4, 8)),
        dma((4, 4)),
        dma((4, 4)),
        dma((24,)),
        dma((24,)),
        dma((12,)),
        dma((12,)),
        dma((24,)),
        dma((16,)),
        dma((12,)),
    ]
    return pl.pallas_call(
        backward_kernel,
        out_shape=outs,
        in_specs=[vm] * 22 + [hbm] * 11,
        out_specs=[vm] * 5 + [hbm] * 9,
        scratch_shapes=scratch,
        compiler_params=pltpu.CompilerParams(
            collective_id=1, has_side_effects=True, vmem_limit_bytes=VMEM_BYTES
        ),
        cost_estimate=pl.CostEstimate(
            flops=4 * 10**10, bytes_accessed=10**8, transcendentals=2 * 10**6
        ),
    )(*small_args, *big_args)


def body_pair(
    layer_in,
    per_layer_in,
    doc_lengths,
    w_query,
    w_key,
    w_value,
    w_out,
    w_gate,
    w_up,
    w_down,
    laurel_left,
    laurel_right,
    per_gate,
    per_proj,
    norm_gains,
    head_gains,
    out_grad,
):
    core, row, col = lax.axis_index("seq"), lax.axis_index("row"), lax.axis_index("col")
    rows, cols, cores = lax.axis_size("row"), lax.axis_size("col"), lax.axis_size("seq")
    seq_count = layer_in.shape[0]
    head_dim = head_gains.shape[1]
    key_width = w_key.shape[1]
    ff_part = w_gate.shape[1] // cores
    chunk = layer_in.shape[1]
    halves = rows // seq_count
    own_tokens = chunk // halves
    group_tokens = own_tokens * cores * cols
    even_col = col % 2 == 0

    lengths = doc_lengths[row // halves]
    count = doc_lengths.shape[1]
    upto = jnp.tril(jnp.ones((count, count), jnp.int32))
    doc_ends = jnp.sum(lengths[None, :] * upto, axis=1)

    def places_of(half):
        token = jnp.arange(group_tokens, dtype=jnp.int32)
        place = token // own_tokens * chunk + half * own_tokens + token % own_tokens
        before = (doc_ends[None, :] <= place[:, None]).astype(jnp.int32)
        start = jnp.sum(before * lengths[None, :], axis=1)
        return place, start

    half = row % halves
    place, start = places_of(half)
    other_place, other_start = places_of(half ^ 1)
    key_place = jnp.stack([place, other_place])[jnp.array([0, 1]) ^ half].reshape(-1)
    allowed = (key_place[None, :] <= place[:, None]) & (key_place[None, :] >= start[:, None])
    cosine_table, sine_table = rotation(place - start, head_dim)

    w_kv = jnp.where(core == 0, w_key, w_value)
    rank = laurel_left.shape[1]
    saved = run_forward(
        layer_in.reshape(rows, own_tokens, -1),
        out_grad.reshape(rows, own_tokens, -1),
        norm_gains,
        (
            w_query,
            w_kv,
            w_out,
            w_gate,
            w_up,
            w_down,
            laurel_left,
            laurel_right,
            per_gate,
            per_proj,
        ),
        (
            cosine_table[:, : head_dim // 2],
            sine_table[:, : head_dim // 2],
            start[:, None],
        ),
        head_gains,
    )
    (x_own, g_own, gains, raw_q, raw_kv, q_low, kv, lse, top_tile, o_low, attn_val, lr_low, ff_val) = saved[
        :13
    ]
    l_left, l_right, p_gate, p_proj = saved[13:17]
    w_q, w_kv_all, w_o, w_g, w_u, w_d, x_all, f_all, gate_val, up_val, turned = saved[17:]
    half_table = head_dim // 2
    (
        y_out,
        x_grad,
        g_gain,
        tops,
        small_sums,
        g_q,
        g_kv,
        g_o,
        g_g,
        g_u,
        g_d,
        *came,
    ) = run_backward(
        (
            x_own,
            g_own,
            per_layer_in.reshape(rows, own_tokens, -1),
            gains,
            head_gains,
            attn_val,
            lr_low,
            ff_val,
            raw_q,
            raw_kv,
            q_low,
            kv,
            lse,
            top_tile,
            o_low,
            cosine_table[:, :half_table],
            sine_table[:, :half_table],
            start[:, None],
            l_left,
            l_right,
            p_gate,
            p_proj,
        ),
        (x_all, f_all, gate_val, up_val, turned, w_q, w_kv_all, w_o, w_g, w_u, w_d),
    )
    sums_a = small_sums[0].transpose(1, 0, 2).reshape(small_sums.shape[2], -1).astype(F32)
    sums_b = small_sums[1].transpose(0, 2, 1).reshape(-1, small_sums.shape[2]).astype(F32)
    logit_top = tops[:, 0]
    clip_factor = jnp.sqrt(CLIP_LEVEL / jnp.maximum(logit_top, CLIP_LEVEL))
    clipped_gains = clip_factor[None, :, None] * head_gains[:, None, :]
    return (
        y_out.reshape(layer_in.shape),
        x_grad.reshape(layer_in.shape),
        g_q.astype(F32),
        g_kv[0].astype(F32),
        g_kv[1].astype(F32),
        g_o.astype(F32),
        g_g.astype(F32),
        g_u.astype(F32),
        g_d.astype(F32),
        sums_b[:, :rank],
        sums_a[:rank],
        sums_b[:, rank:],
        sums_a[rank:],
        g_gain[:6],
        g_gain[6].reshape(head_gains.shape),
        clipped_gains,
    )


def solution(mesh):
    sizes = tuple(mesh.shape[axis] for axis in ("seq", "row", "col"))
    body = body_pair if sizes == (2, 4, 4) else body_any
    return jax.shard_map(
        body,
        mesh=mesh,
        in_specs=(
            P(None, ("seq", "col"), "row"),
            P(None, ("seq", "col"), None),
            P(),
            P("row", "col"),
            P("row", "col"),
            P("row", "col"),
            P("col", "row"),
            P("row", "col"),
            P("row", "col"),
            P("col", "row"),
            P("row", None),
            P(None, "row"),
            P("row", None),
            P(None, "row"),
            P(None, "row"),
            P(),
            P(None, ("seq", "col"), "row"),
        ),
        out_specs=(
            P(None, ("seq", "col"), "row"),
            P(None, ("seq", "col"), "row"),
            P("row", "col"),
            P("row", "col"),
            P("row", "col"),
            P("col", "row"),
            P("row", "col"),
            P("row", "col"),
            P("col", "row"),
            P("row", None),
            P(None, "row"),
            P("row", None),
            P(None, "row"),
            P(None, "row"),
            P(),
            P(),
        ),
        check_vma=False,
    )
```

```python
import functools

import jax
import jax.numpy as jnp
from jax import lax
from jax.experimental import pallas as pl
from jax.experimental.pallas import tpu as pltpu
from jax.sharding import PartitionSpec as P

EPSILON = 1e-06
CLIP_LEVEL = 3.0
ROPE_BASE = 1000000.0
ROOT_HALF = 0.7071067811865476
MASK_FILL = -1e30
MESH = pl.DeviceIdType.MESH
BF = jnp.bfloat16
F32 = jnp.float32
VMEM_BYTES = 63 * 2**20
PIECES = 4


def swapped(value, axis, apart):
    mask = 2**apart
    pairs = [(source, source ^ mask) for source in range(lax.axis_size(axis))]
    return lax.ppermute(value, axis, pairs)


def width_total(values):
    return lax.psum(values, "row")


def gather_tokens(values):
    return lax.all_gather(values, "col", axis=1, tiled=True)


def spread_rows(values, project):
    gathered = gather_tokens(values)
    return (gathered, lax.psum_scatter(project(gathered), "row", scatter_dimension=1, tiled=True))


def spread_cols(values, project):
    gathered = lax.all_gather(values, "row", axis=1, tiled=True)
    return (gathered, lax.psum_scatter(project(gathered), "col", scatter_dimension=1, tiled=True))


def times_right(left_side, right_side):
    return jnp.einsum("std,dn->stn", left_side, right_side, preferred_element_type=jnp.float32)


def times_back(left_side, right_side):
    return jnp.einsum("stn,dn->std", left_side, right_side, preferred_element_type=jnp.float32)


def outer_sum(left_side, right_side):
    return jnp.einsum("std,stn->dn", left_side, right_side, preferred_element_type=jnp.float32)


def norm_forward(values, gain_vec, width_all):
    square_sum = width_total(jnp.sum(values * values, axis=-1, keepdims=True))
    factor = lax.rsqrt(square_sum / width_all + EPSILON)
    normed = values * factor
    return (normed * gain_vec, normed, factor)


def norm_backward(grad_values, normed, factor, gain_vec, width_all):
    grad_normed = grad_values * gain_vec
    inner_sum = width_total(jnp.sum(grad_normed * normed, axis=-1, keepdims=True))
    result = factor * (grad_normed - normed * (inner_sum / width_all))
    return (result, jnp.sum(grad_values * normed, axis=(0, 1)))


def head_norm(values, gain_vec):
    return (
        values * lax.rsqrt(jnp.mean(values * values, axis=-1, keepdims=True) + EPSILON) * gain_vec
    )


def rotation(position, width_all):
    half_width = width_all // 2
    frequency = ROPE_BASE ** (-2.0 * jnp.arange(half_width, dtype=jnp.float32) / width_all)
    angles = position.astype(jnp.float32)[..., None] * frequency
    cosine_table = jnp.concatenate([jnp.cos(angles), jnp.cos(angles)], axis=-1)
    sine_table = jnp.concatenate([jnp.sin(angles), jnp.sin(angles)], axis=-1)
    return (cosine_table, sine_table)


def rotate(values, cosine_table, sine_table):
    half_width = values.shape[-1] // 2
    turned = jnp.concatenate([-values[..., half_width:], values[..., :half_width]], axis=-1)
    return values * cosine_table + turned * sine_table


def doc_places(doc_lengths, first_place, place_count):
    upto = jnp.tril(jnp.ones((doc_lengths.shape[1], doc_lengths.shape[1]), jnp.int32))
    doc_ends = jnp.sum(doc_lengths[:, None, :] * upto[None], axis=2)
    places = first_place + jnp.arange(place_count, dtype=jnp.int32)
    before = (doc_ends[:, None, :] <= places[None, :, None]).astype(jnp.int32)
    segment = jnp.sum(before, axis=2)
    doc_start = jnp.sum(before * doc_lengths[:, None, :], axis=2)
    return (segment, places, places[None, :] - doc_start)


def block_scores(queries, keys_all, block_start, block_size, query_seg, query_place, key_seg):
    keys_part = lax.dynamic_slice_in_dim(keys_all, block_start, block_size, 1)
    scores = jnp.einsum("sqhd,skd->shqk", queries, keys_part, preferred_element_type=jnp.float32)
    seg_part = lax.dynamic_slice_in_dim(key_seg, block_start, block_size, 1)
    key_place = block_start + jnp.arange(block_size, dtype=jnp.int32)
    allowed = (query_seg[:, None, :, None] == seg_part[:, None, None, :]) & (
        key_place[None, None, None, :] <= query_place[None, None, :, None]
    )
    return (scores, allowed)


def body_any(
    layer_in,
    per_layer_in,
    doc_lengths,
    w_query,
    w_key,
    w_value,
    w_out,
    w_gate,
    w_up,
    w_down,
    laurel_left,
    laurel_right,
    per_gate,
    per_proj,
    norm_gains,
    head_gains,
    out_grad,
):
    seq_count = layer_in.shape[0]
    width_all = layer_in.shape[2] * lax.axis_size("row")
    head_dim = head_gains.shape[1]
    heads_here = w_query.shape[1] // head_dim
    heads_all = heads_here * lax.axis_size("col")
    key_width = w_key.shape[1]
    ff_here = w_gate.shape[1]
    local_len = layer_in.shape[1] * lax.axis_size("col")
    tokens_row = local_len // lax.axis_size("row")
    seq_len = local_len * lax.axis_size("seq")
    col_index = lax.axis_index("col")
    even_col = col_index % 2 == 0
    q_width = heads_here * head_dim
    partner_key, partner_value = swapped((w_key, w_value), "col", 0)
    key_head = jnp.where(
        even_col,
        jnp.concatenate([w_key, partner_key], axis=1),
        jnp.concatenate([partner_key, w_key], axis=1),
    )
    value_head = jnp.where(
        even_col,
        jnp.concatenate([w_value, partner_value], axis=1),
        jnp.concatenate([partner_value, w_value], axis=1),
    )
    w_heads = jnp.concatenate([w_query, key_head, value_head], axis=1)
    w_back = jnp.concatenate([w_query, w_key, w_value], axis=1)
    w_gate_up = jnp.concatenate([w_gate, w_up], axis=1)
    inputs = layer_in.astype(jnp.float32)
    x_norm, x_normed, x_factor = norm_forward(inputs, norm_gains[0], width_all)
    x_low = x_norm.astype(jnp.bfloat16)
    x_rows, head_raw = spread_rows(x_low, lambda gathered: times_right(gathered, w_heads))
    q_raw = head_raw[:, :, :q_width].reshape(seq_count, tokens_row, heads_here, head_dim)
    k_raw = head_raw[:, :, q_width : q_width + head_dim]
    v_raw = head_raw[:, :, q_width + head_dim :]
    query_seg, query_place, query_pos = doc_places(
        doc_lengths, lax.axis_index(("seq", "row")) * tokens_row, tokens_row
    )
    key_seg, unused_place, unused_pos = doc_places(doc_lengths, 0, seq_len)
    cosine_table, sine_table = rotation(query_pos, head_dim)

    def query_prep(raw_part, gain_vec):
        return rotate(
            head_norm(raw_part, gain_vec), cosine_table[:, :, None], sine_table[:, :, None]
        )

    def key_prep(raw_part, gain_vec):
        return rotate(head_norm(raw_part, gain_vec), cosine_table, sine_table)

    def value_prep(raw_part):
        return head_norm(raw_part, 1.0)

    q_rot, query_back = jax.vjp(query_prep, q_raw, head_gains[0])
    k_rot, key_back = jax.vjp(key_prep, k_raw, head_gains[1])
    v_normed, value_back = jax.vjp(value_prep, v_raw)
    q_low = q_rot.astype(jnp.bfloat16)
    keys_all, values_all = (
        lax.all_gather(k_rot.astype(jnp.bfloat16), ("seq", "row"), axis=1, tiled=True),
        lax.all_gather(v_normed.astype(jnp.bfloat16), ("seq", "row"), axis=1, tiled=True),
    )
    block_size = min(512, seq_len)
    block_count = seq_len // block_size
    blocks = jnp.arange(block_count, dtype=jnp.int32)

    def scored(block_index):
        return block_scores(
            q_low, keys_all, block_index * block_size, block_size, query_seg, query_place, key_seg
        )

    def values_at(block_index):
        return lax.dynamic_slice_in_dim(values_all, block_index * block_size, block_size, 1)

    def stats_step(carry, block_index):
        row_top, row_total = carry
        scores, allowed = scored(block_index)
        new_top = jnp.maximum(row_top, jnp.max(jnp.where(allowed, scores, MASK_FILL), axis=3))
        weights = jnp.where(allowed, jnp.exp(scores - new_top[..., None]), 0.0)
        row_total = row_total * jnp.exp(row_top - new_top) + jnp.sum(weights, axis=3)
        return ((new_top, row_total), None)

    start_top = jnp.full((seq_count, heads_here, tokens_row), MASK_FILL, jnp.float32)
    (row_top, row_total), unused = lax.scan(
        stats_step, (start_top, jnp.zeros_like(start_top)), blocks
    )
    log_total = row_top + jnp.log(row_total)

    def probs_at(block_index):
        scores, allowed = scored(block_index)
        return jnp.where(allowed, jnp.exp(scores - log_total[..., None]), 0.0)

    def out_step(total_out, block_index):
        probs_low = probs_at(block_index).astype(jnp.bfloat16)
        total_out = total_out + jnp.einsum(
            "shqk,skd->sqhd", probs_low, values_at(block_index), preferred_element_type=jnp.float32
        )
        return (total_out, None)

    attended, unused = lax.scan(
        out_step, jnp.zeros((seq_count, tokens_row, heads_here, head_dim), jnp.float32), blocks
    )
    o_low = attended.astype(jnp.bfloat16).reshape(seq_count, tokens_row, q_width)
    head_slots = lax.dynamic_update_slice_in_dim(
        jnp.full((heads_all,), MASK_FILL, jnp.float32),
        jnp.max(row_top, axis=(0, 2)),
        col_index * heads_here,
        0,
    )
    logit_top = lax.pmax(head_slots, ("seq", "row", "col"))
    o_rows, attn_val = spread_cols(o_low, lambda gathered: times_right(gathered, w_out))
    attn_norm, attn_normed, attn_factor = norm_forward(attn_val, norm_gains[1], width_all)
    h_one = inputs + attn_norm
    lr_low = width_total(times_right(x_low, laurel_left)).astype(jnp.bfloat16)
    lo_val = times_right(lr_low, laurel_right)
    lo_norm, lo_normed, lo_factor = norm_forward(lo_val, norm_gains[2], width_all)
    h_two = (h_one + (x_norm + lo_norm)) * ROOT_HALF
    f_norm, f_normed, f_factor = norm_forward(h_two, norm_gains[3], width_all)
    f_low = f_norm.astype(jnp.bfloat16)
    f_rows, gate_up = spread_rows(f_low, lambda gathered: times_right(gathered, w_gate_up))
    gate_val = gate_up[:, :, :ff_here]
    up_val = gate_up[:, :, ff_here:]

    def geglu(gate_part, up_part):
        return jax.nn.gelu(gate_part, approximate=True) * up_part

    hidden, geglu_back = jax.vjp(geglu, gate_val, up_val)
    hid_low = hidden.astype(jnp.bfloat16)
    hid_rows, ff_val = spread_cols(hid_low, lambda gathered: times_right(gathered, w_down))
    ff_norm, ff_normed, ff_factor = norm_forward(ff_val, norm_gains[4], width_all)
    h_three = h_two + ff_norm
    h_low = h_three.astype(jnp.bfloat16)
    pg_val = width_total(times_right(h_low, per_gate))
    per_input = per_layer_in.astype(jnp.float32)

    def per_mix(gate_part):
        return jax.nn.gelu(gate_part, approximate=True) * per_input

    gp_val, per_back = jax.vjp(per_mix, pg_val)
    gp_low = gp_val.astype(jnp.bfloat16)
    pp_val = times_right(gp_low, per_proj)
    pp_norm, pp_normed, pp_factor = norm_forward(pp_val, norm_gains[5], width_all)
    layer_out = (h_three + pp_norm).astype(jnp.bfloat16)
    grad_top = out_grad.astype(jnp.float32)
    d_pp, gain_five = norm_backward(grad_top, pp_normed, pp_factor, norm_gains[5], width_all)
    d_pp_low = d_pp.astype(jnp.bfloat16)
    grad_per_proj = outer_sum(gp_low, d_pp_low)
    (d_pg,) = per_back(width_total(times_back(d_pp_low, per_proj)))
    d_pg_low = d_pg.astype(jnp.bfloat16)
    grad_per_gate = outer_sum(h_low, d_pg_low)
    d_three = grad_top + times_back(d_pg_low, per_gate)
    d_ff, gain_four = norm_backward(d_three, ff_normed, ff_factor, norm_gains[4], width_all)
    d_ff_low = d_ff.astype(jnp.bfloat16)
    dff_rows, d_hidden = spread_rows(d_ff_low, lambda gathered: times_back(gathered, w_down))
    grad_down = outer_sum(hid_rows, dff_rows)
    d_gate, d_up = geglu_back(d_hidden)
    d_gate_up = jnp.concatenate([d_gate, d_up], axis=2).astype(jnp.bfloat16)
    dgu_rows, d_f_low = spread_cols(d_gate_up, lambda gathered: times_back(gathered, w_gate_up))
    grad_gate_up = outer_sum(f_rows, dgu_rows)
    d_f, gain_three = norm_backward(d_f_low, f_normed, f_factor, norm_gains[3], width_all)
    d_half = (d_three + d_f) * ROOT_HALF
    d_lo, gain_two = norm_backward(d_half, lo_normed, lo_factor, norm_gains[2], width_all)
    d_lo_low = d_lo.astype(jnp.bfloat16)
    grad_laurel_right = outer_sum(lr_low, d_lo_low)
    d_lr_low = width_total(times_back(d_lo_low, laurel_right)).astype(jnp.bfloat16)
    grad_laurel_left = outer_sum(x_low, d_lr_low)
    d_attn, gain_one = norm_backward(d_half, attn_normed, attn_factor, norm_gains[1], width_all)
    d_attn_low = d_attn.astype(jnp.bfloat16)
    dattn_rows, d_o = spread_rows(d_attn_low, lambda gathered: times_back(gathered, w_out))
    grad_w_out = outer_sum(o_rows, dattn_rows)
    d_o_low = d_o.astype(jnp.bfloat16).reshape(seq_count, tokens_row, heads_here, head_dim)

    def delta_step(total_delta, block_index):
        d_probs = jnp.einsum(
            "sqhd,skd->shqk", d_o_low, values_at(block_index), preferred_element_type=jnp.float32
        )
        return (total_delta + jnp.sum(probs_at(block_index) * d_probs, axis=3), None)

    row_delta, unused = lax.scan(delta_step, jnp.zeros_like(log_total), blocks)

    def grad_step(carry, block_index):
        d_query, d_keys, d_values = carry
        block_start = block_index * block_size
        prob_vals = probs_at(block_index)
        d_probs = jnp.einsum(
            "sqhd,skd->shqk", d_o_low, values_at(block_index), preferred_element_type=jnp.float32
        )
        d_scores = (prob_vals * (d_probs - row_delta[..., None])).astype(jnp.bfloat16)
        keys_part = lax.dynamic_slice_in_dim(keys_all, block_start, block_size, 1)
        d_query = d_query + jnp.einsum(
            "shqk,skd->sqhd", d_scores, keys_part, preferred_element_type=jnp.float32
        )
        key_part = jnp.einsum("shqk,sqhd->skd", d_scores, q_low, preferred_element_type=jnp.float32)
        value_part = jnp.einsum(
            "shqk,sqhd->skd",
            prob_vals.astype(jnp.bfloat16),
            d_o_low,
            preferred_element_type=jnp.float32,
        )
        d_keys = lax.dynamic_update_slice_in_dim(d_keys, key_part, block_start, 1)
        d_values = lax.dynamic_update_slice_in_dim(d_values, value_part, block_start, 1)
        return ((d_query, d_keys, d_values), None)

    zero_keys = jnp.zeros((seq_count, seq_len, head_dim), jnp.float32)
    (d_query, d_keys, d_values), unused = lax.scan(
        grad_step, (jnp.zeros_like(attended), zero_keys, zero_keys), blocks
    )
    own_keys, own_values = (
        lax.psum_scatter(d_keys, ("seq", "row"), scatter_dimension=1, tiled=True),
        lax.psum_scatter(d_values, ("seq", "row"), scatter_dimension=1, tiled=True),
    )
    pair_keys, pair_values = swapped((own_keys, own_values), "col", 0)
    d_q_raw, d_q_gain = query_back(d_query)
    d_k_raw, d_k_gain = key_back(own_keys + pair_keys)
    (d_v_raw,) = value_back(own_values + pair_values)
    key_offset = col_index % 2 * key_width
    d_heads_low = jnp.concatenate(
        [
            d_q_raw.reshape(seq_count, tokens_row, q_width),
            lax.dynamic_slice_in_dim(d_k_raw, key_offset, key_width, 2),
            lax.dynamic_slice_in_dim(d_v_raw, key_offset, key_width, 2),
        ],
        axis=2,
    ).astype(jnp.bfloat16)
    dhead_rows, d_x_heads = spread_cols(d_heads_low, lambda gathered: times_back(gathered, w_back))
    grad_heads = outer_sum(x_rows, dhead_rows)
    d_x_low = d_x_heads + times_back(d_lr_low, laurel_left)
    d_x_part, gain_zero = norm_backward(
        d_half + d_x_low, x_normed, x_factor, norm_gains[0], width_all
    )
    grad_in = (d_half + d_x_part).astype(jnp.bfloat16)
    head_part = width_total(jnp.stack([d_q_gain, d_k_gain * 0.5]))
    sum_heads, sum_out, sum_gate_up, sum_down = lax.psum(
        (grad_heads, grad_w_out, grad_gate_up, grad_down), "seq"
    )
    sum_left, sum_right, sum_per_gate, sum_per_proj, sum_gains, sum_head_gains = lax.psum(
        (
            grad_laurel_left,
            grad_laurel_right,
            grad_per_gate,
            grad_per_proj,
            jnp.stack([gain_zero, gain_one, gain_two, gain_three, gain_four, gain_five]),
            head_part,
        ),
        ("seq", "col"),
    )
    clip_factor = jnp.sqrt(CLIP_LEVEL / jnp.maximum(logit_top, CLIP_LEVEL))
    clipped_gains = jnp.stack(
        [
            clip_factor[:, None] * head_gains[0][None, :],
            clip_factor[:, None] * head_gains[1][None, :],
        ]
    )
    return (
        layer_out,
        grad_in,
        sum_heads[:, :q_width],
        sum_heads[:, q_width : q_width + key_width],
        sum_heads[:, q_width + key_width :],
        sum_out,
        sum_gate_up[:, :ff_here],
        sum_gate_up[:, ff_here:],
        sum_down,
        sum_left,
        sum_right,
        sum_per_gate,
        sum_per_proj,
        sum_gains,
        sum_head_gains,
        clipped_gains,
    )


def group_gather(values):
    return lax.all_gather(values, ("seq", "col"), axis=0, tiled=True)


def group_scatter(partial):
    return lax.psum_scatter(
        partial.astype(jnp.bfloat16), ("seq", "col"), scatter_dimension=0, tiled=True
    ).astype(jnp.float32)


def to_owner(values):
    seq_count, tokens, width = values.shape
    rows = lax.axis_size("row")
    parts = values.reshape(rows, seq_count * tokens // rows, width)
    moved = lax.all_to_all(parts, "row", split_axis=0, concat_axis=0)
    return moved.transpose(1, 0, 2).reshape(parts.shape[1], rows * width)


def from_owner(values, seq_count):
    tokens, width = values.shape
    rows = lax.axis_size("row")
    parts = values.reshape(tokens, rows, width // rows).transpose(1, 0, 2)
    moved = lax.all_to_all(parts, "row", split_axis=0, concat_axis=0)
    return moved.reshape(seq_count, rows * tokens // seq_count, width // rows)


def mm(left_side, right_side):
    return jnp.dot(left_side, right_side, preferred_element_type=jnp.float32)


def mm_nt(left_side, right_side):
    return lax.dot_general(
        left_side, right_side, (((1,), (1,)), ((), ())), preferred_element_type=jnp.float32
    )


def mm_tn(left_side, right_side):
    return lax.dot_general(
        left_side, right_side, (((0,), (0,)), ((), ())), preferred_element_type=jnp.float32
    )


def rms(values):
    factor = lax.rsqrt(jnp.mean(values * values, axis=-1, keepdims=True) + EPSILON)
    return values * factor, factor


def rms_back(grad_values, normed, factor, gain_vec):
    grad_normed = grad_values * gain_vec
    inner = jnp.mean(grad_normed * normed, axis=-1, keepdims=True)
    return (
        factor * (grad_normed - normed * inner),
        jnp.sum(grad_values * normed, axis=0, keepdims=True),
    )


def gather_rows(values, axis):
    return lax.all_gather(values, "row", axis=axis, tiled=True)


def scatter_rows(values, axis):
    return lax.psum_scatter(
        values.astype(jnp.bfloat16), "row", scatter_dimension=axis, tiled=True
    ).astype(jnp.float32)


def both_cores(values, axis):
    return lax.all_gather(values, "seq", axis=axis, tiled=True)


def remote(src, dst, send_sem, recv_sem, device):
    return pltpu.make_async_remote_copy(
        src_ref=src,
        dst_ref=dst,
        send_sem=send_sem,
        recv_sem=recv_sem,
        device_id=device,
        device_id_type=MESH,
    )


def greet(core, row, col):
    barrier = pltpu.get_barrier_semaphore()
    near = [(core, row ^ 1, col), (core, row ^ 2, col), (core, row ^ 3, col), (1 - core, row, col)]
    for device in near:
        pl.semaphore_signal(barrier, inc=1, device_id=device, device_id_type=MESH)

    @pl.when(col > 0)
    def _():
        pl.semaphore_signal(barrier, inc=1, device_id=(core, row, col - 1), device_id_type=MESH)

    @pl.when(col < 3)
    def _():
        pl.semaphore_signal(barrier, inc=1, device_id=(core, row, col + 1), device_id_type=MESH)

    ends = jnp.where((col == 0) | (col == 3), 1, 2)
    pl.semaphore_wait(barrier, 4 + ends)


class Gather:
    def __init__(self, place, buf, rows, sems):
        self.core, self.row, self.col = place
        self.buf, self.rows = buf, rows
        self.send_z, self.recv_z, self.send_s, self.recv_s = sems

    def part(self, core, col, piece):
        rows = self.rows // PIECES
        first = (core * 4 + col) * self.rows + piece * rows
        return self.buf.at[pl.ds(pl.multiple_of(first, rows), rows)]

    def hop(self, dist, right, piece):
        part = self.part(self.core, self.col - dist if right else self.col + dist, piece)
        lane = ((0 if right else 3) + dist) * PIECES + piece
        return remote(
            part,
            part,
            self.send_z.at[lane],
            self.recv_z.at[lane],
            (self.core, self.row, self.col + (1 if right else -1)),
        )

    def came(self, dist, right, piece):
        part = self.part(self.core, self.col - dist if right else self.col + dist, piece)
        lane = ((0 if right else 3) + dist - 1) * PIECES + piece
        return remote(
            part, part, self.send_z.at[lane], self.recv_z.at[lane], (self.core, self.row, self.col)
        )

    def to_sibling(self, col, piece, core=None):
        part = self.part(self.core if core is None else core, col, piece)
        lane = col * PIECES + piece
        return remote(
            part,
            part,
            self.send_s.at[lane],
            self.recv_s.at[lane],
            (1 - self.core, self.row, self.col),
        )

    def start(self):
        col = self.col
        for piece in range(PIECES):

            @pl.when(col < 3)
            def _():
                self.hop(0, True, piece).start()

            @pl.when(col > 0)
            def _():
                self.hop(0, False, piece).start()

        for piece in range(PIECES):
            self.to_sibling(col, piece).start()

    def forward(self, work=()):
        col = self.col
        work = list(work)
        for dist in (1, 2, 3):
            for piece in range(PIECES):

                @pl.when(col >= dist)
                def _():
                    self.came(dist, True, piece).wait_recv()
                    if dist < 3:

                        @pl.when(col < 3)
                        def _():
                            self.hop(dist, True, piece).start()

                    self.to_sibling(col - dist, piece).start()

                @pl.when(col + dist <= 3)
                def _():
                    self.came(dist, False, piece).wait_recv()
                    if dist < 3:

                        @pl.when(col > 0)
                        def _():
                            self.hop(dist, False, piece).start()

                    self.to_sibling(col + dist, piece).start()

            if work:
                work.pop(0)()

    def finish(self):
        for piece in range(PIECES):
            for col in range(4):
                self.to_sibling(col, piece, 1 - self.core).wait_recv()

    def drain(self):
        for piece in range(PIECES):
            for col in range(4):
                self.to_sibling(col, piece).wait_send()
            for dist in (0, 1, 2):

                @pl.when((self.col < 3) & (self.col >= dist))
                def _():
                    self.hop(dist, True, piece).wait_send()

                @pl.when((self.col > 0) & (self.col + dist <= 3))
                def _():
                    self.hop(dist, False, piece).wait_send()


class Scatter:
    def __init__(self, place, rows, bufs, sems):
        self.core, self.row, self.col = place
        self.rows = rows
        self.give, self.keep, self.got, self.sent, self.left, self.right = bufs
        self.send_z, self.recv_z, self.send_s, self.recv_s = sems

    def sibling(self, dest):
        rows = pl.ds(dest * self.rows, self.rows)
        return remote(
            self.give.at[rows],
            self.got.at[rows],
            self.send_s.at[dest],
            self.recv_s.at[dest],
            (1 - self.core, self.row, self.col),
        )

    def start(self):
        for dest in (3, 0, 2, 1):
            self.sibling(dest).start()

    def piece(self, piece):
        rows = self.rows // PIECES
        return pl.ds(piece * rows, rows)

    def mine(self, dest, piece):
        count = self.rows // PIECES
        rows = pl.ds(dest * self.rows + piece * count, count)
        return self.keep[rows].astype(F32) + self.got[rows].astype(F32)

    def inbox(self, dest, right):
        return self.left.at[dest - 1] if right else self.right.at[dest]

    def hop(self, dest, right, piece):
        lane = ((0 if right else 4) + dest) * PIECES + piece
        return remote(
            self.sent.at[dest, self.piece(piece)],
            self.inbox(dest, right).at[self.piece(piece)],
            self.send_z.at[lane],
            self.recv_z.at[lane],
            (self.core, self.row, self.col + (1 if right else -1)),
        )

    def step(self, col, dest, right, piece):
        rows = self.piece(piece)
        if piece == 0:
            self.sibling(dest).wait_recv()
        total = self.mine(dest, piece)
        if col != (0 if right else 3):
            self.hop(dest, right, piece).wait_recv()
            total = total + self.inbox(dest, right)[rows].astype(F32)
        self.sent[dest, rows] = total.astype(BF)
        self.hop(dest, right, piece).start()

    def steps(self, col):
        if col > 1:
            return [
                [(3 - dest, not right, piece) for dest, right, piece in part]
                for part in self.steps(3 - col)
            ]
        full = lambda dest, right: [(dest, right, piece) for piece in range(PIECES)]
        if col == 0:
            return [full(3, True) + full(2, True), full(1, True)]
        near, far = full(3, True) + full(2, True), full(0, False)
        lag, order = PIECES - 1, []
        for index, item in enumerate(near):
            order.append(item)
            if index + 1 >= lag and far:
                order.append(far.pop(0))
        cut = PIECES + 2
        return [order[:cut], order[cut:] + far]

    def run(self, result, work=()):
        work = list(work)
        for part in range(2):
            for col in range(4):

                @pl.when(self.col == col)
                def _():
                    for dest, right, piece in self.steps(col)[part]:
                        self.step(col, dest, right, piece)

            for call in work[part : part + 1]:
                call()
        for call in work[2:]:
            call()
        for dest in range(4):

            @pl.when(self.col == dest)
            def _():
                self.sibling(dest).wait_recv()
                for piece in range(PIECES):
                    rows = self.piece(piece)
                    total = self.mine(dest, piece)
                    for right in (True, False):
                        if dest != (0 if right else 3):
                            self.hop(dest, right, piece).wait_recv()
                            total = total + self.inbox(dest, right)[rows].astype(F32)
                    result[rows] = total

    def drain(self):
        for dest in range(4):
            self.sibling(dest).wait_send()
        for piece in range(PIECES):
            for dest in (1, 2, 3):

                @pl.when(self.col < dest)
                def _():
                    self.hop(dest, True, piece).wait_send()

                @pl.when(self.col > 3 - dest)
                def _():
                    self.hop(3 - dest, False, piece).wait_send()


class RowGather:
    def __init__(self, place, source, block, halves, sems):
        self.core, self.row, self.col = place
        self.source, self.block, self.halves = source, block, halves
        self.sems = sems

    def neighbour(self, mask):
        return (self.core, self.row ^ mask, self.col)

    def own(self):
        return pltpu.make_async_copy(self.source, self.block(self.row), self.sems.at[8])

    def first(self, mask, block=None):
        lane = mask - 1
        return remote(
            self.source,
            self.block(self.row) if block is None else block,
            self.sems.at[lane],
            self.sems.at[4 + lane],
            self.neighbour(mask),
        )

    def second(self, mask):
        part = self.halves(self.row ^ (3 - mask))[mask - 1]
        return remote(
            part, part, self.sems.at[1 + mask], self.sems.at[5 + mask], self.neighbour(mask)
        )

    def start(self):
        self.first(1).start()
        self.first(2).start()
        self.own().start()

    def finish_first(self):
        for mask in (1, 2):
            self.first(mask, self.block(self.row ^ mask)).wait_recv()
            self.first(mask).wait_send()
        self.own().wait()

    def forward(self):
        self.first(1, self.block(self.row ^ 1)).wait_recv()
        self.second(2).start()
        self.first(2, self.block(self.row ^ 2)).wait_recv()
        self.second(1).start()

    def finish(self):
        for mask in (1, 2):
            part = self.halves(self.row ^ 3)[mask - 1]
            remote(
                part, part, self.sems.at[1 + mask], self.sems.at[5 + mask], self.neighbour(mask)
            ).wait_recv()
        self.own().wait()
        self.first(1).wait_send()
        self.first(2).wait_send()
        self.second(1).wait_send()
        self.second(2).wait_send()


def by_rows(buf, block_rows):
    half = block_rows // 2

    def block(index):
        return buf.at[pl.ds(pl.multiple_of(index * block_rows, block_rows), block_rows)]

    def halves(index):
        return [
            buf.at[pl.ds(pl.multiple_of(index * block_rows + part * half, half), half)]
            for part in range(2)
        ]

    return block, halves


def by_core_rows(core):
    def split(buf, block_rows):
        own = block_rows // 2

        def piece(index, part, count):
            first = index * block_rows + core * own + part * (own // count)
            return buf.at[pl.ds(pl.multiple_of(first, own // count), own // count)]

        return (
            lambda index: piece(index, 0, 1),
            lambda index: [piece(index, part, 2) for part in range(2)],
        )

    return split


def by_cols(buf, block_cols):
    rows = buf.shape[0] // 2

    def block(index):
        return buf.at[:, pl.ds(pl.multiple_of(index * block_cols, block_cols), block_cols)]

    def halves(index):
        cols = pl.ds(pl.multiple_of(index * block_cols, block_cols), block_cols)
        return [buf.at[pl.ds(part * rows, rows), cols] for part in range(2)]

    return block, halves


def gelu_both(values):
    inner = 0.7978845608028654 * (values + 0.044715 * values * values * values)
    bend = jnp.tanh(inner)
    slope = 0.7978845608028654 * (1.0 + 3.0 * 0.044715 * values * values)
    return 0.5 * values * (1.0 + bend), 0.5 * (1.0 + bend) + 0.5 * values * (1.0 - bend * bend) * slope


def head_parts(raw, gain, cosine, sine):
    factor = lax.rsqrt(jnp.mean(raw * raw, axis=1, keepdims=True) + EPSILON)
    half = raw.shape[1] // 2
    scaled = raw * factor * gain
    first, second = scaled[:, :half], scaled[:, half:]
    return jnp.concatenate([first * cosine - second * sine, second * cosine + first * sine], axis=1)


def forward_kernel(
    x_in,
    g_in,
    gains_in,
    w_query,
    w_key,
    w_value,
    w_out,
    w_gate,
    w_up,
    w_down,
    laurel_left,
    laurel_right,
    per_gate,
    per_proj,
    cosine,
    sine,
    start,
    head_gains,
    x_own,
    g_own,
    gains,
    raw_q,
    raw_kv,
    q_low,
    kv,
    lse,
    top,
    o_low,
    attn_val,
    lr_low,
    ff_val,
    vll,
    vlr,
    vpg,
    vpp,
    wq_all,
    wkv_all,
    wo_all,
    wg_all,
    wu_all,
    wd_all,
    xg_all,
    fg_all,
    gate_all,
    up_all,
    turned_all,
    w_kv_pair,
    gains_pad,
    vq,
    vkv,
    vo,
    vg,
    vu,
    vd,
    xg,
    fg,
    gate,
    up,
    hid,
    turned,
    give,
    keep,
    got,
    sent,
    left,
    right,
    give2,
    keep2,
    got2,
    sent2,
    left2,
    right2,
    row_sems,
    z_send,
    z_recv,
    s_send,
    s_recv,
    misc_send,
    misc_recv,
    out_sems,
):
    core, row, col = lax.axis_index("seq"), lax.axis_index("row"), lax.axis_index("col")
    place = (core, row, col)
    own_tokens, width = x_own.shape
    block = x_in.shape[2]
    head_dim = head_gains.shape[1]
    tokens = xg.shape[0]
    ff_part = gate.shape[1]
    chunk = 2 * own_tokens
    key_width = w_key.shape[1]
    half = row % 2
    greet(core, row, col)

    my_cols = pl.ds(pl.multiple_of(row * block, block), block)

    def hand_over(mask):
        return remote(
            x_in.at[row ^ mask],
            x_own.at[:, my_cols],
            misc_send.at[mask],
            misc_recv.at[mask],
            (core, row ^ mask, col),
        )

    def hand_grad(mask):
        return remote(
            g_in.at[row ^ mask],
            g_own.at[:, my_cols],
            misc_send.at[11 + mask],
            misc_recv.at[11 + mask],
            (core, row ^ mask, col),
        )

    def hand_gains(mask):
        return remote(
            gains_pad,
            gains.at[:, my_cols],
            misc_send.at[3 + mask],
            misc_recv.at[3 + mask],
            (core, row ^ mask, col),
        )

    for mask in (3, 1, 2):
        hand_over(mask).start()
    gains_pad[pl.ds(0, 6)] = gains_in[...]
    gains_pad[pl.ds(6, 2)] = jnp.zeros((2, block), F32)
    for mask in (3, 1, 2):
        hand_gains(mask).start()
    x_own[:, my_cols] = x_in[row]
    g_own[:, my_cols] = g_in[row]
    gains[:, my_cols] = gains_pad[...]

    pair_cols = pl.ds(pl.multiple_of(col % 2 * key_width, key_width), key_width)
    w_kv_own = w_kv_pair.at[:, pair_cols]
    w_kv_own[...] = jnp.where(core == 0, w_key[...].astype(F32), w_value[...].astype(F32)).astype(BF)
    pair = remote(w_kv_own, w_kv_own, misc_send.at[7], misc_recv.at[7], (core, row, col ^ 1))
    pair.start()

    lanes = iter(range(32))

    def rows_of(source, buf, split=by_rows, size=block):
        block_of, halves_of = split(buf, size)
        return RowGather(place, source, block_of, halves_of, row_sems.at[next(lanes)])

    tile = 256
    core_head = pl.ds(pl.multiple_of(core * head_dim, head_dim), head_dim)

    def core_tile(index):
        return pl.ds(pl.multiple_of(core * ff_part + index * tile, tile), tile)

    get_q = rows_of(w_query.at[:, core_head], vq)
    get_kv = rows_of(w_kv_pair, vkv)
    get_o = rows_of(w_out.at[core_head], vo, by_cols)
    get_laurel = [rows_of(laurel_left, vll), rows_of(laurel_right, vlr, by_cols)]
    per_rows, per_cols = per_gate.shape[0] // 2, per_proj.shape[0] // 2
    own_rows = pl.ds(pl.multiple_of(core * per_rows, per_rows), per_rows)
    own_cols = pl.ds(pl.multiple_of(core * per_cols, per_cols), per_cols)
    get_per = [
        rows_of(per_gate.at[own_rows], vpg, by_core_rows(core)),
        rows_of(per_proj.at[own_cols], vpp.at[own_cols], by_cols),
    ]
    tiles = ff_part // tile
    get_gu = [
        [
            rows_of(whole.at[:, core_tile(index)], buf.at[:, pl.ds(index * tile, tile)])
            for whole, buf in ((w_gate, vg), (w_up, vu))
        ]
        for index in range(tiles)
    ]
    half_ff = ff_part // 2
    get_d = [
        rows_of(
            w_down.at[pl.ds(pl.multiple_of(core * ff_part + part * half_ff, half_ff), half_ff)],
            vd.at[pl.ds(part * half_ff, half_ff)],
            by_cols,
        )
        for part in range(2)
    ]

    def per_parts(which, lane):
        parts = [
            vpg.at[pl.ds(pl.multiple_of(index * block + which * per_rows, per_rows), per_rows)]
            for index in range(4)
        ]
        parts.append(vpp.at[pl.ds(pl.multiple_of(which * per_cols, per_cols), per_cols)])
        return list(enumerate(parts, lane))

    def begin(jobs):
        for job in jobs:
            job.start()

    def push(jobs):
        for job in jobs:
            job.forward()

    def complete(jobs):
        for job in jobs:
            job.finish()

    get_q.start()
    pair.wait_recv()
    get_kv.start()

    for mask in (1, 2, 3):
        remote(
            x_in.at[row],
            x_own.at[:, pl.ds(pl.multiple_of((row ^ mask) * block, block), block)],
            misc_send.at[mask],
            misc_recv.at[mask],
            (core, row, col),
        ).wait_recv()
        remote(
            gains_pad,
            gains.at[:, pl.ds(pl.multiple_of((row ^ mask) * block, block), block)],
            misc_send.at[3 + mask],
            misc_recv.at[3 + mask],
            (core, row, col),
        ).wait_recv()

    def own_norm():
        values = x_own[...].astype(F32)
        factor = lax.rsqrt(jnp.mean(values * values, axis=1, keepdims=True) + EPSILON)
        return values, values * factor * gains[pl.ds(0, 1)]

    mine = pl.ds(pl.multiple_of((core * 4 + col) * own_tokens, own_tokens), own_tokens)
    xg[mine] = own_norm()[1].astype(BF)
    sems = lambda lane: (z_send.at[lane], z_recv.at[lane], s_send.at[lane], s_recv.at[lane])
    gather_x = Gather(place, xg, own_tokens, sems(0))
    gather_x.start()
    gather_x.forward(
        [
            lambda: None,
            lambda: (push([get_q, get_kv]), begin([get_o])),
        ]
    )
    gather_x.finish()
    complete([get_q, get_kv])

    raw_q[...] = mm(xg[...], vq[...])
    raw_kv[...] = mm(xg[...], vkv[...])
    q_low[...] = head_parts(raw_q[...], head_gains[pl.ds(0, 1)], cosine[...], sine[...]).astype(BF)
    is_key = core == 0
    kv_here = head_parts(
        raw_kv[...],
        jnp.where(is_key, head_gains[pl.ds(1, 1)], 1.0),
        jnp.where(is_key, cosine[...], 1.0),
        jnp.where(is_key, sine[...], 0.0),
    ).astype(BF)

    def kv_part(kind, which):
        return kv.at[kind, pl.ds(pl.multiple_of(which * tokens, tokens), tokens)]

    kv[core, pl.ds(pl.multiple_of(half * tokens, tokens), tokens)] = kv_here
    here = kv_part(core, half)
    to_x = remote(here, here, misc_send.at[8], misc_recv.at[8], (core, row ^ 1, col))
    to_s = remote(here, here, misc_send.at[9], misc_recv.at[9], (1 - core, row, col))
    to_x.start()
    to_s.start()
    push([get_o])
    begin(get_gu[0] + get_laurel + get_gu[1])
    came = kv_part(core, half ^ 1)
    remote(here, came, misc_send.at[8], misc_recv.at[8], (core, row, col)).wait_recv()
    on_s = remote(came, came, misc_send.at[10], misc_recv.at[10], (1 - core, row, col))
    on_s.start()
    other = kv_part(1 - core, half)
    remote(other, other, misc_send.at[9], misc_recv.at[9], (core, row, col)).wait_recv()
    other_came = kv_part(1 - core, half ^ 1)
    remote(other_came, other_came, misc_send.at[10], misc_recv.at[10], (core, row, col)).wait_recv()

    q_rows = 128
    key_token = lax.broadcasted_iota(jnp.int32, (1, 2 * tokens), 1)
    in_half = key_token % tokens
    key_place = in_half // own_tokens * chunk + key_token // tokens * own_tokens + in_half % own_tokens
    top[...] = jnp.full(top.shape, MASK_FILL, F32)

    def attend(step, carry):
        first = pl.multiple_of(step * q_rows, q_rows)
        rows = pl.ds(first, q_rows)
        token = first + lax.broadcasted_iota(jnp.int32, (q_rows, 1), 0)
        q_place = token // own_tokens * chunk + half * own_tokens + token % own_tokens
        allowed = (key_place <= q_place) & (key_place >= start[rows])
        scores = jnp.where(allowed, mm_nt(q_low[rows], kv[0]), MASK_FILL)
        row_top = jnp.max(scores, axis=1, keepdims=True)
        weights = jnp.exp(scores - row_top)
        total = jnp.sum(weights, axis=1, keepdims=True)
        probs = (weights * (1.0 / total)).astype(BF)
        o_low[rows] = mm(probs, kv[1]).astype(BF)
        lse[rows] = row_top + jnp.log(total)
        top[...] = jnp.maximum(top[...], jnp.max(row_top))
        return carry

    lax.fori_loop(0, tokens // q_rows, attend, 0)
    get_o.finish()

    away = pl.multiple_of((1 - core) * 4 * own_tokens, 4 * own_tokens)
    home = pl.multiple_of(core * 4 * own_tokens, 4 * own_tokens)
    scatter = Scatter(place, own_tokens, (give, keep, got, sent, left, right), sems(1))

    def project(source, weights, target, first):
        def step(index, carry):
            cols = pl.ds(pl.multiple_of(index * block, block), block)
            value = mm(source[pl.ds(first, 4 * own_tokens)], weights[:, cols])
            target[:, cols] = value.astype(target.dtype)
            return carry

        lax.fori_loop(0, width // block, step, 0)

    project(o_low, vo, give, away)
    scatter.start()
    project(o_low, vo, keep, home)
    scatter.run(
        attn_val,
        [lambda: (push(get_gu[0]), push(get_laurel)), lambda: begin(get_gu[2])],
    )
    push(get_gu[1])
    begin(get_gu[3])

    complete(get_laurel)
    inputs, x_norm = own_norm()
    attn_normed = rms(attn_val[...])[0]
    lr_low[...] = mm(xg[mine], vll[...]).astype(BF)
    lo_normed = rms(mm(lr_low[...], vlr[...]))[0]
    h_two = (
        inputs + attn_normed * gains[pl.ds(1, 1)] + (x_norm + lo_normed * gains[pl.ds(2, 1)])
    ) * ROOT_HALF
    fg[mine] = (rms(h_two)[0] * gains[pl.ds(3, 1)]).astype(BF)
    gather_f = Gather(place, fg, own_tokens, sems(2))
    gather_f.start()
    gather_f.forward(
        [
            lambda: None,
            lambda: push(get_gu[2]),
            lambda: begin(get_d[:1]),
        ]
    )
    gather_f.finish()

    def unit_tile(index):
        complete(get_gu[index])
        cols = pl.ds(index * tile, tile)
        bent, slope = gelu_both(mm(fg[...], vg[:, cols]))
        up_part = mm(fg[...], vu[:, cols])
        gate[:, cols] = (up_part * slope).astype(BF)
        up[:, cols] = bent.astype(BF)
        hid[:, cols] = (bent * up_part).astype(BF)

    for index in range(tiles):
        if index == 1:
            push(get_gu[3])
            begin(get_d[1:])
        unit_tile(index)
    turned[...] = hid[...].T
    for job in get_d:
        job.forward()
    keep_weights = [
        pltpu.make_async_copy(source, target, out_sems.at[lane])
        for lane, (source, target) in enumerate(
            [
                (vq, wq_all),
                (vkv, wkv_all),
                (vo, wo_all),
                (vg, wg_all),
                (vu, wu_all),
                (vd, wd_all),
                (xg, xg_all),
                (fg, fg_all),
                (gate, gate_all),
                (up, up_all),
            ]
        )
    ]
    begin(get_per)
    for mask in (1, 2, 3):
        hand_grad(mask).start()
    complete(get_d)
    for copy in keep_weights:
        copy.start()
    scatter_ff = Scatter(place, own_tokens, (give2, keep2, got2, sent2, left2, right2), sems(3))
    project(hid, vd, give2, away)
    scatter_ff.start()
    project(hid, vd, keep2, home)
    get_turned = rows_of(
        turned.at[pl.ds(0, half_ff)], turned_all.at[pl.ds(0, half_ff)], by_cols, tokens
    )
    rest = pl.ds(half_ff, half_ff)
    keep_rest = pltpu.make_async_copy(
        turned.at[rest],
        turned_all.at[rest, pl.ds(pl.multiple_of(row * tokens, tokens), tokens)],
        out_sems.at[10],
    )
    keep_rest.start()
    scatter_ff.run(ff_val, [lambda: (push(get_per), get_turned.start())])
    complete(get_per)
    share = [
        remote(part, part, misc_send.at[lane], misc_recv.at[lane], (1 - core, row, col))
        for lane, part in per_parts(core, 16)
    ]
    for copy in share:
        copy.start()
    for lane, part in per_parts(1 - core, 16):
        remote(part, part, misc_send.at[lane], misc_recv.at[lane], (core, row, col)).wait_recv()
    for copy in share:
        copy.wait_send()
    get_turned.finish_first()
    keep_rest.wait()

    for mask in (1, 2, 3):
        hand_over(mask).wait_send()
        hand_gains(mask).wait_send()
        hand_grad(mask).wait_send()
        remote(
            g_in.at[row],
            g_own.at[:, pl.ds(pl.multiple_of((row ^ mask) * block, block), block)],
            misc_send.at[11 + mask],
            misc_recv.at[11 + mask],
            (core, row, col),
        ).wait_recv()
    gather_x.drain()
    scatter.drain()
    gather_f.drain()
    scatter_ff.drain()
    pair.wait_send()
    to_x.wait_send()
    to_s.wait_send()
    on_s.wait_send()
    for copy in keep_weights:
        copy.wait()


def run_forward(x_in, g_in, gains_in, weights_in, tables, head_gains):
    cosine, sine, start = tables
    w_gate, laurel_left, per_gate, per_proj = (weights_in[i] for i in (4, 7, 9, 10))
    block = x_in.shape[2]
    own, width = x_in.shape[1], 4 * block
    tokens, head_dim, ff_part = 8 * own, head_gains.shape[1], w_gate.shape[1] // 2
    rank = laurel_left.shape[1]
    vm = pl.BlockSpec(memory_space=pltpu.VMEM)
    hbm = pl.BlockSpec(memory_space=pl.ANY)
    shape = jax.ShapeDtypeStruct
    weights = [
        (width, head_dim),
        (width, head_dim),
        (head_dim, width),
        (width, ff_part),
        (width, ff_part),
        (ff_part, width),
    ]
    acts = [
        (tokens, width),
        (tokens, width),
        (tokens, ff_part),
        (tokens, ff_part),
    ]
    outs = [
        shape((own, width), BF),
        shape((own, width), BF),
        shape((8, width), F32),
        shape((tokens, head_dim), F32),
        shape((tokens, head_dim), F32),
        shape((tokens, head_dim), BF),
        shape((2, 2 * tokens, head_dim), BF),
        shape((tokens, 1), F32),
        shape((8, 128), F32),
        shape((tokens, head_dim), BF),
        shape((own, width), F32),
        shape((own, rank), BF),
        shape((own, width), F32),
        shape((width, rank), BF),
        shape((rank, width), BF),
        shape((width, per_gate.shape[1]), BF),
        shape((per_proj.shape[0], width), BF),
    ] + [shape(size, BF) for size in weights + acts + [(ff_part, 4 * tokens)]]
    scatter_bufs = [
        pltpu.VMEM((4 * own, width), BF),
        pltpu.VMEM((4 * own, width), F32),
        pltpu.VMEM((4 * own, width), BF),
        pltpu.VMEM((4, own, width), BF),
        pltpu.VMEM((3, own, width), BF),
        pltpu.VMEM((3, own, width), BF),
    ]
    dma = pltpu.SemaphoreType.DMA
    return pl.pallas_call(
        forward_kernel,
        out_shape=outs,
        in_specs=[vm, vm, vm, hbm, vm, vm] + [hbm] * 8 + [vm] * 4,
        out_specs=[vm] * 17 + [hbm] * 11,
        scratch_shapes=[pltpu.VMEM((block, head_dim), BF), pltpu.VMEM((8, block), F32)]
        + [pltpu.VMEM(size, BF) for size in weights + acts]
        + [pltpu.VMEM((tokens, ff_part), BF), pltpu.VMEM((ff_part, tokens), BF)]
        + scatter_bufs * 2
        + [
            dma((18, 10)),
            dma((4, 8 * PIECES)),
            dma((4, 8 * PIECES)),
            dma((4, 4 * PIECES)),
            dma((4, 4 * PIECES)),
            dma((24,)),
            dma((24,)),
            dma((11,)),
        ],
        compiler_params=pltpu.CompilerParams(
            collective_id=0, has_side_effects=True, vmem_limit_bytes=VMEM_BYTES
        ),
        cost_estimate=pl.CostEstimate(flops=2 * 10**10, bytes_accessed=5 * 10**7, transcendentals=10**6),
    )(x_in, g_in, gains_in, *weights_in, cosine, sine, start, head_gains)


class RowScatter:
    def __init__(self, place, halves, came, sems, stage=None):
        self.core, self.row, self.col = place
        self.halves, self.came, self.sems = halves, came, sems
        self.stage = stage

    def send(self, lane, index, half, mask):
        return remote(
            self.halves(index)[half],
            self.came.at[lane],
            self.sems.at[lane],
            self.sems.at[6 + lane],
            (self.core, self.row ^ mask, self.col),
        )

    def lane(self, lane):
        index, half, mask = ((1, 0, 1), (3, 0, 1), (2, 1, 2), (3, 1, 2), (2, 0, 2), (1, 1, 1))[lane]
        return self.send(lane, self.row ^ index, half, mask)

    def start(self, lanes=(1, 3, 0, 2)):
        for lane in lanes:
            self.lane(lane).start()

    def load(self, lane):
        slot = {0: 0, 1: 0, 4: 0, 2: 1, 3: 1, 5: 1}[lane]
        return slot, pltpu.make_async_copy(
            self.came.at[lane], self.stage[0].at[slot], self.stage[1].at[slot]
        )

    def fetch(self, *lanes):
        for lane in lanes:
            self.lane(lane).wait_recv()
            if self.stage is not None:
                self.load(lane)[1].start()

    def add(self, lane, index, half):
        if self.stage is None:
            value = self.came[lane]
        else:
            slot, copy = self.load(lane)
            copy.wait()
            value = self.stage[0][slot]
        part = self.halves(self.row ^ index)[half]
        part[...] = (part[...].astype(F32) + value.astype(F32)).astype(BF)

    def middle(self):
        for lane, out, index, half in ((1, 4, 2, 0), (3, 5, 1, 1)):
            self.add(lane, index, half)
            self.lane(out).start()

    def early(self):
        self.add(0, 0, 0)
        self.add(2, 0, 1)

    def finish(self):
        self.add(4, 0, 0)
        self.add(5, 0, 1)

    def drain(self):
        for lane in range(6):
            self.lane(lane).wait_send()


def head_back(grad, raw, gain, cosine, sine):
    factor = lax.rsqrt(jnp.mean(raw * raw, axis=1, keepdims=True) + EPSILON)
    half = raw.shape[1] // 2
    normed = raw * factor
    first, second = grad[:, :half], grad[:, half:]
    back = jnp.concatenate([first * cosine + second * sine, second * cosine - first * sine], axis=1)
    gain_grad = jnp.sum(back * normed, axis=0, keepdims=True)
    inner = back * gain
    return factor * (inner - normed * jnp.mean(inner * normed, axis=1, keepdims=True)), gain_grad


def backward_kernel(
    x_own,
    g_own,
    per_in,
    gains,
    head_gains,
    attn_val,
    lr_low,
    ff_val,
    raw_q,
    raw_kv,
    q_low,
    kv,
    lse,
    top,
    o_low,
    cosine,
    sine,
    start,
    vll,
    vlr,
    vpg,
    vpp,
    xg_in,
    fg_in,
    gate_in,
    up_in,
    turned_in,
    wq_in,
    wkv_in,
    wo_in,
    wg_in,
    wu_in,
    wd_in,
    y_out,
    x_grad,
    g_gain,
    tops,
    small_a,
    gq,
    gkv,
    gout,
    ggate,
    gup,
    gdown,
    came_g,
    came_u,
    turned_far,
    turned_near,
    vq,
    vkv,
    vo,
    vg,
    vu,
    vd,
    fg,
    gate,
    up,
    dff_all,
    down_stage,
    dffg,
    dattng,
    dgate,
    dup,
    give,
    keep,
    got,
    sent,
    left,
    right,
    own_sum,
    h_two_ref,
    d_three_ref,
    low_ref,
    gpart,
    gcame,
    gpart2,
    gcame2,
    small_give,
    small_keep,
    small_got,
    small_row,
    small_z,
    d_o,
    d_kv,
    kv_give,
    kv_got,
    kv_x_got,
    kv_p_got,
    pkv,
    came_q,
    came_kv,
    came_o,
    stage_g,
    stage_sems,
    load_sems,
    row_sems,
    z_send,
    z_recv,
    s_send,
    s_recv,
    misc_send,
    misc_recv,
    gain_send,
    gain_recv,
    done_sems,
    ff_sems,
    down_sems,
    turned_sems,
):
    core, row, col = lax.axis_index("seq"), lax.axis_index("row"), lax.axis_index("col")
    place = (core, row, col)
    own_tokens, width = x_own.shape
    block = width // 4
    tokens, head_dim = raw_q.shape
    ff_part = gate.shape[1]
    chunk = 2 * own_tokens
    key_width = head_dim // 2
    half = row % 2
    rank = lr_low.shape[1]
    my_cols = pl.ds(pl.multiple_of(row * block, block), block)
    mine = pl.ds(pl.multiple_of((core * 4 + col) * own_tokens, own_tokens), own_tokens)
    away = pl.multiple_of((1 - core) * 4 * own_tokens, 4 * own_tokens)
    home = pl.multiple_of(core * 4 * own_tokens, 4 * own_tokens)

    barrier = pltpu.get_barrier_semaphore()
    for mask in (1, 2, 3):
        pl.semaphore_signal(barrier, inc=1, device_id=(core, row ^ mask, col), device_id_type=MESH)
        for other in (0, 1):
            pl.semaphore_signal(
                barrier, inc=1, device_id=(core ^ other, row, col ^ mask), device_id_type=MESH
            )
    pl.semaphore_signal(barrier, inc=1, device_id=(1 - core, row, col), device_id_type=MESH)
    loads = [
        pltpu.make_async_copy(source, target, load_sems.at[lane])
        for lane, (source, target) in enumerate(
            [
                (wd_in, vd),
                (gate_in, gate),
                (up_in, up),
                (wg_in, vg),
                (wu_in, vu),
                (fg_in, fg),
                (wo_in, vo),
                (wq_in, vq),
                (wkv_in, vkv),
            ]
        )
    ]
    for load in loads:
        load.start()
    pl.semaphore_wait(barrier, 10)
    half_ff = ff_part // 2

    def turned_on(part, mask):
        rows = pl.ds(part * half_ff + (mask - 1) * (half_ff // 2), half_ff // 2)
        first = pl.multiple_of((row ^ (3 - mask)) * tokens, tokens)
        if part == 0:
            source = turned_in.at[rows, pl.ds(first, tokens)]
        else:
            source = turned_near.at[2 - mask, pl.ds((mask - 1) * (half_ff // 2), half_ff // 2)]
        lane = part * 2 + mask - 1
        return remote(
            source,
            turned_far.at[rows],
            row_sems.at[0, lane],
            row_sems.at[0, 6 + lane],
            (core, row ^ mask, col),
        )

    def turned_over(mask):
        return remote(
            turned_in.at[
                pl.ds(half_ff, half_ff), pl.ds(pl.multiple_of(row * tokens, tokens), tokens)
            ],
            turned_near.at[mask - 1],
            row_sems.at[0, 3 + mask],
            row_sems.at[0, 9 + mask],
            (core, row ^ mask, col),
        )

    for mask in (1, 2):
        turned_on(0, mask).start()
        turned_over(mask).start()

    def turned_rest():
        for mask in (1, 2):
            turned_over(mask).wait_recv()
        for mask in (1, 2):
            turned_on(1, mask).start()


    def gain(index):
        return gains[pl.ds(index, 1)]

    inputs = x_own[...].astype(F32)
    x_norm = rms(inputs)[0] * gain(0)
    attn_normed = rms(attn_val[...])[0]
    lo_normed = rms(mm(lr_low[...], vlr[...]))[0]
    h_two = (inputs + attn_normed * gain(1) + (x_norm + lo_normed * gain(2))) * ROOT_HALF
    h_two_ref[...] = h_two
    ff_normed, ff_factor = rms(ff_val[...])
    h_three = h_two + ff_normed * gain(4)
    h_low = h_three.astype(BF)
    p_gate, p_proj = vpg[...], vpp[...]
    pg_gelu, pg_slope = gelu_both(mm(h_low, p_gate))
    per_input = per_in[row].astype(F32)
    gp_low = (pg_gelu * per_input).astype(BF)
    pp_normed, pp_factor = rms(mm(gp_low, p_proj))
    low_ref[...] = (h_three + pp_normed * gain(5)).astype(BF)

    def hand_back(source, target, mask, lane):
        return remote(
            source.at[:, pl.ds(pl.multiple_of((row ^ mask) * block, block), block)],
            target.at[row],
            misc_send.at[lane + mask],
            misc_recv.at[lane + mask],
            (core, row ^ mask, col),
        )

    def came_back(target, mask, lane):
        return remote(
            target.at[row ^ mask],
            target.at[row ^ mask],
            misc_send.at[lane + mask],
            misc_recv.at[lane + mask],
            (core, row, col),
        )

    for mask in (1, 2, 3):
        hand_back(low_ref, y_out, mask, 0).start()
    y_out[row] = low_ref[:, my_cols]

    grad_top = g_own[...].astype(F32)
    d_pp, gain_five = rms_back(grad_top, pp_normed, pp_factor, gain(5))
    d_pp_low = d_pp.astype(BF)
    d_pg_low = (mm_nt(d_pp_low, p_proj) * per_input * pg_slope).astype(BF)
    d_three = grad_top + mm_nt(d_pg_low, p_gate)
    d_three_ref[...] = d_three
    d_ff, gain_four = rms_back(d_three, ff_normed, ff_factor, gain(4))
    gpart[...] = jnp.zeros(gpart.shape, F32)
    gpart[pl.ds(5, 1)] = gain_five
    gpart[pl.ds(4, 1)] = gain_four
    dffg[mine] = d_ff.astype(BF)
    sems = lambda lane: (z_send.at[lane], z_recv.at[lane], s_send.at[lane], s_recv.at[lane])
    gather_ff = Gather(place, dffg, own_tokens, sems(0))
    gather_ff.start()

    def small(kind, first, value):
        rows = pl.ds(first, value.shape[0])
        value = value.astype(BF)

        @pl.when(core == kind)
        def _():
            small_keep[rows] = value

        @pl.when(core != kind)
        def _():
            small_give[rows] = value

    small(0, rank, mm_tn(gp_low, d_pp_low))
    small(1, rank, mm_tn(d_pg_low, h_low))
    gather_ff.forward([lambda: None, turned_rest])
    gather_ff.finish()

    part_rows = tokens // 2

    def ff_piece(group, which):
        return dff_all.at[
            pl.ds(pl.multiple_of(group * tokens + which * part_rows, part_rows), part_rows)
        ]

    def ff_over(mask):
        return remote(
            dffg.at[
                pl.ds(pl.multiple_of(core * part_rows, part_rows), part_rows),
                pl.ds(pl.multiple_of((row ^ mask) * block, block), block),
            ],
            ff_piece(row, core),
            ff_sems.at[mask],
            ff_sems.at[4 + mask],
            (core, row ^ mask, col),
        )

    def ff_came(mask):
        part = ff_piece(row ^ mask, core)
        return remote(part, part, ff_sems.at[mask], ff_sems.at[4 + mask], (core, row, col))

    def ff_share(mask, which):
        part = ff_piece(row ^ mask, which)
        return remote(
            part, part, ff_sems.at[8 + mask], ff_sems.at[12 + mask], (1 - core, row, col)
        )

    for mask in (1, 2, 3):
        ff_over(mask).start()
    dff_all[pl.ds(pl.multiple_of(row * tokens, tokens), tokens)] = dffg[:, my_cols]

    tile = 256
    for load in loads[:3]:
        load.wait()

    def units(index, carry):
        cols = pl.ds(pl.multiple_of(index * tile, tile), tile)
        d_hid = mm_nt(dffg[...], vd[cols])
        dgate[:, cols] = (d_hid * gate[:, cols].astype(F32)).astype(BF)
        dup[:, cols] = (d_hid * up[:, cols].astype(F32)).astype(BF)
        return carry

    lax.fori_loop(0, ff_part // tile, units, 0)
    for load in loads[3:5]:
        load.wait()

    def back_ff(target, first):
        rows = pl.ds(first, 4 * own_tokens)

        def step(index, carry):
            cols = pl.ds(pl.multiple_of(index * block, block), block)
            value = mm_nt(dgate[rows], vg[cols]) + mm_nt(dup[rows], vu[cols])
            target[:, cols] = value.astype(target.dtype)
            return carry

        lax.fori_loop(0, width // block, step, 0)

    scatter_f = Scatter(place, own_tokens, (give, keep, got, sent, left, right), sems(1))
    back_ff(give, away)
    scatter_f.start()
    back_ff(keep, home)

    put_g = RowScatter(place, by_rows(vg, block)[1], came_g, row_sems.at[1], (stage_g, stage_sems))
    put_u = RowScatter(place, by_rows(vu, block)[1], came_u, row_sems.at[2], (stage_g, stage_sems))

    def load_turned(lane):
        mask, part = ((0, None), (3, None), (1, 0), (1, 1), (2, 0), (2, 1))[lane]
        cols = pl.ds(pl.multiple_of((row ^ mask) * tokens, tokens), tokens)
        if part is None:
            source = turned_far if mask else turned_in.at[:, cols]
            target = vd.at[:, cols]
        else:
            rows = pl.ds(part * half_ff, half_ff)
            source = turned_near.at[mask - 1] if part else turned_in.at[rows, cols]
            target = vd.at[rows, cols]
        return pltpu.make_async_copy(source, target, turned_sems.at[lane])

    def down_ready():
        for mask in (1, 2):
            for part in range(2):
                turned_on(part, mask).wait_recv()
        for lane in range(6):
            load_turned(lane).start()
        for mask in (1, 2, 3):
            ff_came(mask).wait_recv()
            ff_share(mask, core).start()

    def down_tile(index):
        slot = index % 2
        rows = pl.ds(index * tile, tile)
        target = gdown.at[pl.ds(pl.multiple_of(core * ff_part + index * tile, tile), tile)]
        local = pltpu.make_async_copy(down_stage.at[slot], target, down_sems.at[index])
        over = remote(
            down_stage.at[slot],
            target,
            down_sems.at[4 + index],
            down_sems.at[8 + index],
            (1 - core, row, col),
        )
        return slot, rows, local, over

    def down_grad():
        for lane in range(6):
            load_turned(lane).wait()
        for mask in (1, 2, 3):
            ff_share(mask, 1 - core).wait_recv()
        for index in range(ff_part // tile):
            slot, rows, local, over = down_tile(index)
            if index >= 2:
                before = down_tile(index - 2)
                before[2].wait()
                before[3].wait_send()
            down_stage[slot] = mm(vd[rows], dff_all[...]).astype(BF)
            local.start()
            over.start()

    def gate_grad(target, grad, put):
        def step(index, carry):
            rows = pl.ds(pl.multiple_of(index * tile, tile), tile)
            target[rows] = mm_tn(fg[:, rows], grad[...]).astype(BF)
            return carry

        lax.fori_loop(0, width // tile, step, 0)

    def start_gate():
        loads[5].wait()
        gate_grad(vg, dgate, put_g)
        put_g.start()

    def start_up():
        gate_grad(vu, dup, put_u)
        put_u.start((1, 3))

    scatter_f.run(own_sum, [start_gate, start_up, down_ready])

    gather_ff.drain()
    f_normed, f_factor = rms(h_two_ref[...])
    d_f, gain_three = rms_back(own_sum[...], f_normed, f_factor, gain(3))
    d_half = (d_three_ref[...] + d_f) * ROOT_HALF
    d_three_ref[...] = d_half
    attn_normed, attn_factor = rms(attn_val[...])
    d_attn, gain_one = rms_back(d_half, attn_normed, attn_factor, gain(1))
    dattng[mine] = d_attn.astype(BF)
    gather_a = Gather(place, dattng, own_tokens, sems(2))
    gather_a.start()
    lo_normed, lo_factor = rms(mm(lr_low[...], vlr[...]))
    d_lo, gain_two = rms_back(d_half, lo_normed, lo_factor, gain(2))
    d_lo_low = d_lo.astype(BF)
    d_lr_low = mm_nt(d_lo_low, vlr[...]).astype(BF)
    small(0, 0, mm_tn(lr_low[...], d_lo_low))
    x_low = (rms(x_own[...].astype(F32))[0] * gain(0)).astype(BF)
    small(1, 0, mm_tn(d_lr_low, x_low))
    own_sum[...] = d_half + mm_nt(d_lr_low, vll[...])
    gpart[pl.ds(3, 1)] = gain_three
    gpart[pl.ds(2, 1)] = gain_two
    gpart[pl.ds(1, 1)] = gain_one
    small_swap = remote(
        small_give, small_got, misc_send.at[8], misc_recv.at[8], (1 - core, row, col)
    )
    small_swap.start()
    put_s = RowScatter(place, by_cols(small_keep, block)[1], small_row, row_sems.at[6])

    def small_sum():
        small_swap.wait_recv()
        small_keep[...] = (small_keep[...].astype(F32) + small_got[...].astype(F32)).astype(BF)

    def middle_gate():
        put_g.fetch(1, 3)
        down_grad()
        put_g.middle()

    def more_small():
        small_sum()
        put_g.fetch(0, 2)

    gather_a.forward([middle_gate, more_small, put_g.early])
    gather_a.finish()
    scatter_f.drain()

    loads[6].wait()
    d_o[...] = mm_nt(dattng[...], vo[...]).astype(BF)
    q_rows = 128
    key_token = lax.broadcasted_iota(jnp.int32, (1, 2 * tokens), 1)
    in_half = key_token % tokens
    key_place = in_half // own_tokens * chunk + key_token // tokens * own_tokens + in_half % own_tokens
    d_kv[...] = jnp.zeros(d_kv.shape, F32)

    def attend(step, carry):
        first = pl.multiple_of(step * q_rows, q_rows)
        rows = pl.ds(first, q_rows)
        token = first + lax.broadcasted_iota(jnp.int32, (q_rows, 1), 0)
        q_place = token // own_tokens * chunk + half * own_tokens + token % own_tokens
        allowed = (key_place <= q_place) & (key_place >= start[rows])
        scores = jnp.where(allowed, mm_nt(q_low[rows], kv[0]), MASK_FILL)
        probs = jnp.exp(scores - lse[rows])
        d_probs = mm_nt(d_o[rows], kv[1])
        delta = jnp.sum(probs * d_probs, axis=1, keepdims=True)
        d_scores = (probs * (d_probs - delta)).astype(BF)
        d_kv[0] += mm_tn(d_scores, q_low[rows])
        d_kv[1] += mm_tn(probs.astype(BF), d_o[rows])
        d_raw, gain_part = head_back(
            mm(d_scores, kv[0]), raw_q[rows], head_gains[pl.ds(0, 1)], cosine[rows], sine[rows]
        )
        d_o[rows] = d_raw.astype(BF)
        return carry + gain_part

    gain_q = lax.fori_loop(0, tokens // q_rows, attend, jnp.zeros((1, head_dim), F32))

    kv_give[...] = d_kv[1 - core].astype(BF)
    swap_kv = remote(kv_give, kv_got, misc_send.at[9], misc_recv.at[9], (1 - core, row, col))
    swap_kv.start()

    def out_grad():
        for part in range(2):
            wide = pl.ds(part * (width // 2), width // 2)
            vo[:, wide] = mm_tn(o_low[...], dattng[:, wide]).astype(BF)

    put_o = RowScatter(place, by_cols(vo, block)[1], came_o, row_sems.at[3])
    swap_kv.wait()
    kv_x = kv_give.at[pl.ds(0, tokens)]
    theirs = pl.ds(pl.multiple_of((half ^ 1) * tokens, tokens), tokens)
    ours = pl.ds(pl.multiple_of(half * tokens, tokens), tokens)
    kv_x[...] = (d_kv[core, theirs] + kv_got[theirs].astype(F32)).astype(BF)
    over_x = remote(kv_x, kv_x_got, misc_send.at[10], misc_recv.at[10], (core, row ^ 1, col))
    over_x.start()
    put_u.start((0, 2))
    load_x = pltpu.make_async_copy(xg_in, dffg, load_sems.at[10])
    for mask in (1, 2, 3):
        ff_over(mask).wait_send()
    load_x.start()
    put_u.fetch(1, 3)
    out_grad()
    put_u.middle()
    put_s.start()
    put_o.start()
    loads[7].wait()
    loads[8].wait()
    over_x.wait_recv()
    d_kind = d_kv[core, ours] + kv_got[ours].astype(F32) + kv_x_got[...].astype(F32)
    kv_p = kv_got.at[pl.ds(0, tokens)]
    kv_p[...] = d_kind.astype(BF)
    over_p = remote(kv_p, kv_p_got, misc_send.at[11], misc_recv.at[11], (core, row, col ^ 1))
    over_p.start()
    over_p.wait()
    d_kind = kv_p[...].astype(F32) + kv_p_got[...].astype(F32)
    is_key = core == 0
    d_kind_raw, gain_k = head_back(
        d_kind,
        raw_kv[...],
        jnp.where(is_key, head_gains[pl.ds(1, 1)], 1.0),
        jnp.where(is_key, cosine[...], 1.0),
        jnp.where(is_key, sine[...], 0.0),
    )
    for part in range(4):
        gpart[pl.ds(6, 1), pl.ds(part * block, head_dim)] = gain_q
        gpart[pl.ds(6, 1), pl.ds(part * block + head_dim, head_dim)] = gain_k * jnp.where(
            is_key, 0.5, 0.0
        )
    kv_p[...] = d_kind_raw.astype(BF)
    pair_cols = pl.ds(pl.multiple_of(col % 2 * key_width, key_width), key_width)

    def back_heads(target, first):
        rows = pl.ds(first, 4 * own_tokens)

        def step(index, carry):
            cols = pl.ds(pl.multiple_of(index * block, block), block)
            value = mm_nt(d_o[rows], vq[cols]) + mm_nt(kv_p[rows, pair_cols], vkv[cols, pair_cols])
            target[:, cols] = value.astype(target.dtype)
            return carry

        lax.fori_loop(0, width // block, step, 0)

    scatter_x = Scatter(place, own_tokens, (give, keep, got, sent, left, right), sems(3))
    back_heads(give, away)
    scatter_x.start()
    back_heads(keep, home)
    put_q = RowScatter(place, by_rows(vq, block)[1], came_q, row_sems.at[4])
    put_kv = RowScatter(place, by_rows(pkv, block)[1], came_kv, row_sems.at[5])

    def query_grad():
        load_x.wait()

        def step(index, carry):
            rows = pl.ds(pl.multiple_of(index * tile, tile), tile)
            vq[rows] = mm_tn(dffg[:, rows], d_o[...]).astype(BF)
            pkv[rows] = mm_tn(dffg[:, rows], kv_p[:, pair_cols]).astype(BF)
            return carry

        lax.fori_loop(0, width // tile, step, 0)
        put_q.start()
        put_kv.start()

    def deliver(lane, source, target):
        local = pltpu.make_async_copy(source, target, done_sems.at[lane])
        over = remote(
            source, target, done_sems.at[8 + lane], done_sems.at[16 + lane], (1 - core, row, col)
        )
        local.start()
        over.start()
        done.append((local, over))

    core_ff = pl.ds(pl.multiple_of(core * ff_part, ff_part), ff_part)
    core_head = pl.ds(pl.multiple_of(core * head_dim, head_dim), head_dim)
    sib_ff = pl.ds(pl.multiple_of((1 - core) * ff_part, ff_part), ff_part)
    sib_head = pl.ds(pl.multiple_of((1 - core) * head_dim, head_dim), head_dim)
    row_block = pl.ds(pl.multiple_of(row * block, block), block)
    done = []

    quarter = block // 4

    def small_quarter(mask):
        return remote(
            small_keep.at[
                :, pl.ds(pl.multiple_of(row * block + (col ^ mask) * quarter, quarter), quarter)
            ],
            small_z.at[mask],
            misc_send.at[11 + mask],
            misc_recv.at[11 + mask],
            (core, row, col ^ mask),
        )

    def gate_finish():
        put_g.fetch(4, 5)
        put_g.finish()
        deliver(1, vg.at[row_block], ggate.at[:, core_ff])
        put_u.fetch(0, 2)
        put_u.early()

    d_half_here = d_three_ref
    scatter_x.run(h_two_ref, [query_grad, gate_finish])
    d_xn = own_sum[...] + h_two_ref[...]
    x_normed, x_factor = rms(x_own[...].astype(F32))
    d_in, gain_zero = rms_back(d_xn, x_normed, x_factor, gain(0))
    gpart[pl.ds(0, 1)] = gain_zero
    for mask in (1, 2, 3):
        hand_back(low_ref, y_out, mask, 0).wait_send()
    low_ref[...] = (d_half_here[...] + d_in).astype(BF)
    for mask in (1, 2, 3):
        hand_back(low_ref, x_grad, mask, 4).start()
    x_grad[row] = low_ref[:, my_cols]

    gpart[pl.ds(8, 8)] = jnp.full((8, width), jnp.max(top[...]), F32)

    def gain_row(mask):
        return remote(
            gpart.at[:, pl.ds(pl.multiple_of((row ^ mask) * block, block), block)],
            gcame.at[mask],
            gain_send.at[mask],
            gain_recv.at[mask],
            (core, row ^ mask, col),
        )

    for mask in (1, 2, 3):
        gain_row(mask).start()
    gcame[0] = gpart[:, my_cols]
    for mask in (1, 2, 3):
        gain_row(mask).wait_recv()
    summed = gcame[0] + gcame[1] + gcame[2] + gcame[3]
    largest = jnp.maximum(jnp.maximum(gcame[0], gcame[1]), jnp.maximum(gcame[2], gcame[3]))
    gpart2[pl.ds(0, 8)] = summed[:8]
    gpart2[pl.ds(8, 8)] = largest[8:]
    me = core * 4 + col
    members = [(other, mask) for other in (0, 1) for mask in range(4) if other or mask]

    def gain_group(other, mask):
        lane = 4 + other * 4 + mask
        return remote(
            gpart2,
            gcame2.at[me],
            gain_send.at[lane],
            gain_recv.at[lane],
            (core ^ other, row, col ^ mask),
        )

    for other, mask in members:
        gain_group(other, mask).start()
    gcame2[me] = gpart2[...]
    for put in (put_s, put_o, put_q, put_kv):
        put.fetch(1, 3)
        put.middle()
    put_u.fetch(4, 5)
    put_u.finish()
    deliver(2, vu.at[row_block], gup.at[:, core_ff])
    put_s.fetch(0, 2, 4, 5)
    put_s.early()
    put_s.finish()
    for mask in (1, 2, 3):
        small_quarter(mask).start()

    def small_share(other, mask):
        lane = 16 + other * 4 + mask
        return remote(
            kv_x.at[pl.ds(0, small_keep.shape[0]), pl.ds(0, quarter)],
            small_a.at[core, col],
            misc_send.at[lane],
            misc_recv.at[lane],
            (core ^ other, row, col ^ mask),
        )

    for mask in (1, 2, 3):
        small_quarter(mask).wait_recv()
    small_total = small_keep[
        :, pl.ds(pl.multiple_of(row * block + col * quarter, quarter), quarter)
    ].astype(F32)
    for mask in (1, 2, 3):
        small_total = small_total + small_z[mask].astype(F32)
    over_x.wait_send()
    kv_x[pl.ds(0, small_keep.shape[0]), pl.ds(0, quarter)] = small_total.astype(BF)
    for other, mask in members:
        small_share(other, mask).start()
    small_a[core, col] = small_total.astype(BF)
    for put, lane, source, target in (
        (put_o, 4, vo.at[:, row_block], gout.at[core_head]),
        (put_kv, 3, pkv.at[row_block], gkv.at[core]),
        (put_q, 5, vq.at[row_block], gq.at[:, core_head]),
    ):
        put.fetch(0, 2, 4, 5)
        put.early()
        put.finish()
        deliver(lane, source, target)

    for other, mask in members:
        who = (core ^ other) * 4 + (col ^ mask)
        lane = 4 + other * 4 + mask
        remote(
            gpart2, gcame2.at[who], gain_send.at[lane], gain_recv.at[lane], (core, row, col)
        ).wait_recv()
    total = gcame2[0]
    for who in range(1, 8):
        total = total + gcame2[who]
    g_gain[...] = total[:8]
    for who in range(8):
        head = 2 * (who % 4) + who // 4
        tops[pl.ds(head, 1)] = gcame2[who, pl.ds(8, 1), pl.ds(0, 128)]

    gather_a.drain()
    scatter_x.drain()
    for other, mask in members:
        part = small_a.at[core ^ other, col ^ mask]
        lane = 16 + other * 4 + mask
        remote(part, part, misc_send.at[lane], misc_recv.at[lane], (core, row, col)).wait_recv()
        small_share(other, mask).wait_send()
        gain_group(other, mask).wait_send()
    for mask in (1, 2, 3):
        came_back(y_out, mask, 0).wait_recv()
        came_back(x_grad, mask, 4).wait_recv()
        hand_back(low_ref, x_grad, mask, 4).wait_send()
        gain_row(mask).wait_send()
        small_quarter(mask).wait_send()
    small_swap.wait_send()
    for put in (put_g, put_u, put_o, put_q, put_kv, put_s):
        put.drain()
    for mask in (1, 2):
        turned_over(mask).wait_send()
        for part in range(2):
            turned_on(part, mask).wait_send()
    for mask in (1, 2, 3):
        ff_share(mask, core).wait_send()
    for index in range(ff_part // tile):
        slot, rows, local, over = down_tile(index)
        if index >= 2:
            local.wait()
            over.wait_send()
        target = gdown.at[pl.ds(pl.multiple_of((1 - core) * ff_part + index * tile, tile), tile)]
        remote(
            target, target, down_sems.at[4 + index], down_sems.at[8 + index], (core, row, col)
        ).wait_recv()
    theirs_at = {
        1: ggate.at[:, sib_ff],
        2: gup.at[:, sib_ff],
        3: gkv.at[1 - core],
        4: gout.at[sib_head],
        5: gq.at[:, sib_head],
    }
    for lane, (local, over) in zip((1, 2, 4, 3, 5), done):
        local.wait()
        over.wait_send()
        target = theirs_at[lane]
        remote(
            target, target, done_sems.at[8 + lane], done_sems.at[16 + lane], (core, row, col)
        ).wait_recv()


def run_backward(small_args, big_args):
    x_own, per_in, head_gains = small_args[0], small_args[2], small_args[4]
    own, width = x_own.shape
    block = width // 4
    gate = big_args[2]
    tokens, ff_part = gate.shape
    head_dim = head_gains.shape[1]
    rank = small_args[6].shape[1]
    small_rows = sum(small_args[lane].shape[0] for lane in (19, 21))
    vm = pl.BlockSpec(memory_space=pltpu.VMEM)
    hbm = pl.BlockSpec(memory_space=pl.ANY)
    shape = jax.ShapeDtypeStruct
    vmem = pltpu.VMEM
    dma = pltpu.SemaphoreType.DMA
    outs = [
        shape((4, own, block), BF),
        shape((4, own, block), BF),
        shape((8, block), F32),
        shape((8, 128), F32),
        shape((2, 4, small_rows, block // 4), BF),
        shape((block, 2 * head_dim), BF),
        shape((2, block, head_dim // 2), BF),
        shape((2 * head_dim, block), BF),
        shape((block, 2 * ff_part), BF),
        shape((block, 2 * ff_part), BF),
        shape((2 * ff_part, block), BF),
        shape((6, block // 2, ff_part), BF),
        shape((6, block // 2, ff_part), BF),
        shape((ff_part, tokens), BF),
        shape((2, ff_part // 2, tokens), BF),
    ]
    scratch = [
        vmem((width, head_dim), BF),
        vmem((width, head_dim), BF),
        vmem((head_dim, width), BF),
        vmem((width, ff_part), BF),
        vmem((width, ff_part), BF),
        vmem((ff_part, width), BF),
        vmem((tokens, width), BF),
        vmem((tokens, ff_part), BF),
        vmem((tokens, ff_part), BF),
        vmem((4 * tokens, block), BF),
        vmem((2, 256, block), BF),
        vmem((tokens, width), BF),
        vmem((tokens, width), BF),
        vmem((tokens, ff_part), BF),
        vmem((tokens, ff_part), BF),
        vmem((4 * own, width), BF),
        vmem((4 * own, width), F32),
        vmem((4 * own, width), BF),
        vmem((4, own, width), BF),
        vmem((3, own, width), BF),
        vmem((3, own, width), BF),
        vmem((own, width), F32),
        vmem((own, width), F32),
        vmem((own, width), F32),
        vmem((own, width), BF),
        vmem((16, width), F32),
        vmem((4, 16, block), F32),
        vmem((16, block), F32),
        vmem((8, 16, block), F32),
        vmem((small_rows, width), BF),
        vmem((small_rows, width), BF),
        vmem((small_rows, width), BF),
        vmem((6, small_rows // 2, block), BF),
        vmem((4, small_rows, block // 4), BF),
        vmem((tokens, head_dim), BF),
        vmem((2, 2 * tokens, head_dim), F32),
        vmem((2 * tokens, head_dim), BF),
        vmem((2 * tokens, head_dim), BF),
        vmem((tokens, head_dim), BF),
        vmem((tokens, head_dim), BF),
        vmem((width, head_dim // 2), BF),
        vmem((6, block // 2, head_dim), BF),
        vmem((6, block // 2, head_dim // 2), BF),
        vmem((6, head_dim // 2, block), BF),
        vmem((2, block // 2, ff_part), BF),
        dma((2,)),
        dma((11,)),
        dma((7, 12)),
        dma((4, 8 * PIECES)),
        dma((4, 8 * PIECES)),
        dma((4, 4 * PIECES)),
        dma((4, 4 * PIECES)),
        dma((24,)),
        dma((24,)),
        dma((12,)),
        dma((12,)),
        dma((24,)),
        dma((16,)),
        dma((12,)),
        dma((6,)),
    ]
    return pl.pallas_call(
        backward_kernel,
        out_shape=outs,
        in_specs=[vm] * 22 + [hbm] * 11,
        out_specs=[vm] * 5 + [hbm] * 10,
        scratch_shapes=scratch,
        compiler_params=pltpu.CompilerParams(
            collective_id=1, has_side_effects=True, vmem_limit_bytes=VMEM_BYTES
        ),
        cost_estimate=pl.CostEstimate(
            flops=4 * 10**10, bytes_accessed=10**8, transcendentals=2 * 10**6
        ),
    )(*small_args, *big_args)


def finish_kernel(
    y_in,
    x_in,
    gains,
    tops,
    small,
    gq,
    gkv,
    gout,
    ggate,
    gup,
    gdown,
    head_gains,
    y_out,
    x_out,
    o_query,
    o_key,
    o_value,
    o_out,
    o_gate,
    o_up,
    o_down,
    o_left,
    o_right,
    o_per_gate,
    o_per_proj,
    o_gains,
    o_head,
    o_clip,
):
    o_query[...] = gq[...].astype(F32)
    o_key[...] = gkv[0].astype(F32)
    o_value[...] = gkv[1].astype(F32)
    o_out[...] = gout[...].astype(F32)
    o_gate[...] = ggate[...].astype(F32)
    o_up[...] = gup[...].astype(F32)
    o_down[...] = gdown[...].astype(F32)
    head_dim = head_gains.shape[1]
    quarter = small.shape[3]
    rank = o_right.shape[0]

    @pl.when(pl.program_id(0) == 0)
    def _():
        own = y_in.shape[1]
        for part in range(4):
            rows = pl.ds(part % 2 * own, own)
            y_out[part // 2, rows] = y_in[part]
            x_out[part // 2, rows] = x_in[part]

    @pl.when(pl.program_id(0) == 1)
    def _():
        for part in range(4):
            cols = pl.ds(part * quarter, quarter)
            first = small[0, part].astype(F32)
            o_right[:, cols] = first[:rank]
            o_per_proj[:, cols] = first[rank:]
            second = small[1, part].astype(F32)
            o_left[cols] = second[:rank].T
            o_per_gate[cols] = second[rank:].T

    @pl.when(pl.program_id(0) == 2)
    def _():
        o_gains[...] = gains[pl.ds(0, 6)]
        o_head[pl.ds(0, 1)] = gains[pl.ds(6, 1), pl.ds(0, head_dim)]
        o_head[pl.ds(1, 1)] = gains[pl.ds(6, 1), pl.ds(head_dim, head_dim)]
        factor = jnp.sqrt(CLIP_LEVEL / jnp.maximum(tops[...], CLIP_LEVEL))[:, :1]
        o_clip[0] = factor * head_gains[pl.ds(0, 1)]
        o_clip[1] = factor * head_gains[pl.ds(1, 1)]


def run_finish(results, head_gains, rank):
    y_out, x_grad, g_gain, tops, small, gq, gkv, gout, ggate, gup, gdown = results
    steps = 8
    shape = jax.ShapeDtypeStruct

    def whole(array):
        dims = len(array.shape)
        return pl.BlockSpec(array.shape, lambda step: (0,) * dims)

    def rows(array):
        size = (array.shape[0] // steps, array.shape[1])
        return pl.BlockSpec(size, lambda step: (step, 0))

    own, block = y_out.shape[1:]
    key_width = gkv.shape[2]
    proj = small.shape[2] - rank
    tokens_shape = shape((2, 2 * own, block), BF)
    by_rows_out = [
        shape(gq.shape, F32),
        shape(gkv.shape[1:], F32),
        shape(gkv.shape[1:], F32),
        shape(gout.shape, F32),
        shape(ggate.shape, F32),
        shape(gup.shape, F32),
        shape(gdown.shape, F32),
    ]
    whole_out = [
        shape((block, rank), F32),
        shape((rank, block), F32),
        shape((block, proj), F32),
        shape((proj, block), F32),
        shape((6, block), F32),
        shape(head_gains.shape, F32),
        shape((2, tops.shape[0], head_gains.shape[1]), F32),
    ]
    kv_spec = pl.BlockSpec((2, block // steps, key_width), lambda step: (0, step, 0))
    return pl.pallas_call(
        finish_kernel,
        grid=(steps,),
        out_shape=[tokens_shape, tokens_shape] + by_rows_out + whole_out,
        in_specs=[whole(y_out), whole(x_grad), whole(g_gain), whole(tops), whole(small), rows(gq), kv_spec]
        + [rows(array) for array in (gout, ggate, gup, gdown)]
        + [whole(head_gains)],
        out_specs=[whole(tokens_shape)] * 2
        + [rows(array) for array in by_rows_out]
        + [whole(array) for array in whole_out],
        compiler_params=pltpu.CompilerParams(vmem_limit_bytes=VMEM_BYTES),
        cost_estimate=pl.CostEstimate(flops=10**7, bytes_accessed=3 * 10**7, transcendentals=0),
    )(*results, head_gains)


def body_pair(
    layer_in,
    per_layer_in,
    doc_lengths,
    w_query,
    w_key,
    w_value,
    w_out,
    w_gate,
    w_up,
    w_down,
    laurel_left,
    laurel_right,
    per_gate,
    per_proj,
    norm_gains,
    head_gains,
    out_grad,
):
    core, row, col = lax.axis_index("seq"), lax.axis_index("row"), lax.axis_index("col")
    rows, cols, cores = lax.axis_size("row"), lax.axis_size("col"), lax.axis_size("seq")
    seq_count = layer_in.shape[0]
    head_dim = head_gains.shape[1]
    key_width = w_key.shape[1]
    ff_part = w_gate.shape[1] // cores
    chunk = layer_in.shape[1]
    halves = rows // seq_count
    own_tokens = chunk // halves
    group_tokens = own_tokens * cores * cols
    even_col = col % 2 == 0

    lengths = doc_lengths[row // halves]
    count = doc_lengths.shape[1]
    upto = jnp.tril(jnp.ones((count, count), jnp.int32))
    doc_ends = jnp.sum(lengths[None, :] * upto, axis=1)

    def places_of(half):
        token = jnp.arange(group_tokens, dtype=jnp.int32)
        place = token // own_tokens * chunk + half * own_tokens + token % own_tokens
        before = (doc_ends[None, :] <= place[:, None]).astype(jnp.int32)
        start = jnp.sum(before * lengths[None, :], axis=1)
        return place, start

    half = row % halves
    place, start = places_of(half)
    other_place, other_start = places_of(half ^ 1)
    key_place = jnp.stack([place, other_place])[jnp.array([0, 1]) ^ half].reshape(-1)
    allowed = (key_place[None, :] <= place[:, None]) & (key_place[None, :] >= start[:, None])
    cosine_table, sine_table = rotation(place - start, head_dim)

    rank = laurel_left.shape[1]
    saved = run_forward(
        layer_in.reshape(rows, own_tokens, -1),
        out_grad.reshape(rows, own_tokens, -1),
        norm_gains,
        (
            w_query,
            w_key,
            w_value,
            w_out,
            w_gate,
            w_up,
            w_down,
            laurel_left,
            laurel_right,
            per_gate,
            per_proj,
        ),
        (
            cosine_table[:, : head_dim // 2],
            sine_table[:, : head_dim // 2],
            start[:, None],
        ),
        head_gains,
    )
    (x_own, g_own, gains, raw_q, raw_kv, q_low, kv, lse, top_tile, o_low, attn_val, lr_low, ff_val) = saved[
        :13
    ]
    l_left, l_right, p_gate, p_proj = saved[13:17]
    w_q, w_kv_all, w_o, w_g, w_u, w_d, x_all, f_all, gate_val, up_val, turned = saved[17:]
    half_table = head_dim // 2
    results = run_backward(
        (
            x_own,
            g_own,
            per_layer_in.reshape(rows, own_tokens, -1),
            gains,
            head_gains,
            attn_val,
            lr_low,
            ff_val,
            raw_q,
            raw_kv,
            q_low,
            kv,
            lse,
            top_tile,
            o_low,
            cosine_table[:, :half_table],
            sine_table[:, :half_table],
            start[:, None],
            l_left,
            l_right,
            p_gate,
            p_proj,
        ),
        (x_all, f_all, gate_val, up_val, turned, w_q, w_kv_all, w_o, w_g, w_u, w_d),
    )
    return tuple(run_finish(results[:11], head_gains, rank))


def solution(mesh):
    sizes = tuple(mesh.shape[axis] for axis in ("seq", "row", "col"))
    body = body_pair if sizes == (2, 4, 4) else body_any
    return jax.shard_map(
        body,
        mesh=mesh,
        in_specs=(
            P(None, ("seq", "col"), "row"),
            P(None, ("seq", "col"), None),
            P(),
            P("row", "col"),
            P("row", "col"),
            P("row", "col"),
            P("col", "row"),
            P("row", "col"),
            P("row", "col"),
            P("col", "row"),
            P("row", None),
            P(None, "row"),
            P("row", None),
            P(None, "row"),
            P(None, "row"),
            P(),
            P(None, ("seq", "col"), "row"),
        ),
        out_specs=(
            P(None, ("seq", "col"), "row"),
            P(None, ("seq", "col"), "row"),
            P("row", "col"),
            P("row", "col"),
            P("row", "col"),
            P("col", "row"),
            P("row", "col"),
            P("row", "col"),
            P("col", "row"),
            P("row", None),
            P(None, "row"),
            P("row", None),
            P(None, "row"),
            P(None, "row"),
            P(),
            P(),
        ),
        check_vma=False,
    )
```

```python
import functools

import jax
import jax.numpy as jnp
from jax import lax
from jax.experimental import pallas as pl
from jax.experimental.pallas import tpu as pltpu
from jax.sharding import PartitionSpec as P

EPSILON = 1e-06
CLIP_LEVEL = 3.0
ROPE_BASE = 1000000.0
ROOT_HALF = 0.7071067811865476
MASK_FILL = -1e30
MESH = pl.DeviceIdType.MESH
BF = jnp.bfloat16
F32 = jnp.float32
VMEM_BYTES = 63 * 2**20
PIECES = 4


def swapped(value, axis, apart):
    mask = 2**apart
    pairs = [(source, source ^ mask) for source in range(lax.axis_size(axis))]
    return lax.ppermute(value, axis, pairs)


def width_total(values):
    return lax.psum(values, "row")


def gather_tokens(values):
    return lax.all_gather(values, "col", axis=1, tiled=True)


def spread_rows(values, project):
    gathered = gather_tokens(values)
    return (gathered, lax.psum_scatter(project(gathered), "row", scatter_dimension=1, tiled=True))


def spread_cols(values, project):
    gathered = lax.all_gather(values, "row", axis=1, tiled=True)
    return (gathered, lax.psum_scatter(project(gathered), "col", scatter_dimension=1, tiled=True))


def times_right(left_side, right_side):
    return jnp.einsum("std,dn->stn", left_side, right_side, preferred_element_type=jnp.float32)


def times_back(left_side, right_side):
    return jnp.einsum("stn,dn->std", left_side, right_side, preferred_element_type=jnp.float32)


def outer_sum(left_side, right_side):
    return jnp.einsum("std,stn->dn", left_side, right_side, preferred_element_type=jnp.float32)


def norm_forward(values, gain_vec, width_all):
    square_sum = width_total(jnp.sum(values * values, axis=-1, keepdims=True))
    factor = lax.rsqrt(square_sum / width_all + EPSILON)
    normed = values * factor
    return (normed * gain_vec, normed, factor)


def norm_backward(grad_values, normed, factor, gain_vec, width_all):
    grad_normed = grad_values * gain_vec
    inner_sum = width_total(jnp.sum(grad_normed * normed, axis=-1, keepdims=True))
    result = factor * (grad_normed - normed * (inner_sum / width_all))
    return (result, jnp.sum(grad_values * normed, axis=(0, 1)))


def head_norm(values, gain_vec):
    return (
        values * lax.rsqrt(jnp.mean(values * values, axis=-1, keepdims=True) + EPSILON) * gain_vec
    )


def rotation(position, width_all):
    half_width = width_all // 2
    frequency = ROPE_BASE ** (-2.0 * jnp.arange(half_width, dtype=jnp.float32) / width_all)
    angles = position.astype(jnp.float32)[..., None] * frequency
    cosine_table = jnp.concatenate([jnp.cos(angles), jnp.cos(angles)], axis=-1)
    sine_table = jnp.concatenate([jnp.sin(angles), jnp.sin(angles)], axis=-1)
    return (cosine_table, sine_table)


def rotate(values, cosine_table, sine_table):
    half_width = values.shape[-1] // 2
    turned = jnp.concatenate([-values[..., half_width:], values[..., :half_width]], axis=-1)
    return values * cosine_table + turned * sine_table


def doc_places(doc_lengths, first_place, place_count):
    upto = jnp.tril(jnp.ones((doc_lengths.shape[1], doc_lengths.shape[1]), jnp.int32))
    doc_ends = jnp.sum(doc_lengths[:, None, :] * upto[None], axis=2)
    places = first_place + jnp.arange(place_count, dtype=jnp.int32)
    before = (doc_ends[:, None, :] <= places[None, :, None]).astype(jnp.int32)
    segment = jnp.sum(before, axis=2)
    doc_start = jnp.sum(before * doc_lengths[:, None, :], axis=2)
    return (segment, places, places[None, :] - doc_start)


def block_scores(queries, keys_all, block_start, block_size, query_seg, query_place, key_seg):
    keys_part = lax.dynamic_slice_in_dim(keys_all, block_start, block_size, 1)
    scores = jnp.einsum("sqhd,skd->shqk", queries, keys_part, preferred_element_type=jnp.float32)
    seg_part = lax.dynamic_slice_in_dim(key_seg, block_start, block_size, 1)
    key_place = block_start + jnp.arange(block_size, dtype=jnp.int32)
    allowed = (query_seg[:, None, :, None] == seg_part[:, None, None, :]) & (
        key_place[None, None, None, :] <= query_place[None, None, :, None]
    )
    return (scores, allowed)


def body_any(
    layer_in,
    per_layer_in,
    doc_lengths,
    w_query,
    w_key,
    w_value,
    w_out,
    w_gate,
    w_up,
    w_down,
    laurel_left,
    laurel_right,
    per_gate,
    per_proj,
    norm_gains,
    head_gains,
    out_grad,
):
    seq_count = layer_in.shape[0]
    width_all = layer_in.shape[2] * lax.axis_size("row")
    head_dim = head_gains.shape[1]
    heads_here = w_query.shape[1] // head_dim
    heads_all = heads_here * lax.axis_size("col")
    key_width = w_key.shape[1]
    ff_here = w_gate.shape[1]
    local_len = layer_in.shape[1] * lax.axis_size("col")
    tokens_row = local_len // lax.axis_size("row")
    seq_len = local_len * lax.axis_size("seq")
    col_index = lax.axis_index("col")
    even_col = col_index % 2 == 0
    q_width = heads_here * head_dim
    partner_key, partner_value = swapped((w_key, w_value), "col", 0)
    key_head = jnp.where(
        even_col,
        jnp.concatenate([w_key, partner_key], axis=1),
        jnp.concatenate([partner_key, w_key], axis=1),
    )
    value_head = jnp.where(
        even_col,
        jnp.concatenate([w_value, partner_value], axis=1),
        jnp.concatenate([partner_value, w_value], axis=1),
    )
    w_heads = jnp.concatenate([w_query, key_head, value_head], axis=1)
    w_back = jnp.concatenate([w_query, w_key, w_value], axis=1)
    w_gate_up = jnp.concatenate([w_gate, w_up], axis=1)
    inputs = layer_in.astype(jnp.float32)
    x_norm, x_normed, x_factor = norm_forward(inputs, norm_gains[0], width_all)
    x_low = x_norm.astype(jnp.bfloat16)
    x_rows, head_raw = spread_rows(x_low, lambda gathered: times_right(gathered, w_heads))
    q_raw = head_raw[:, :, :q_width].reshape(seq_count, tokens_row, heads_here, head_dim)
    k_raw = head_raw[:, :, q_width : q_width + head_dim]
    v_raw = head_raw[:, :, q_width + head_dim :]
    query_seg, query_place, query_pos = doc_places(
        doc_lengths, lax.axis_index(("seq", "row")) * tokens_row, tokens_row
    )
    key_seg, unused_place, unused_pos = doc_places(doc_lengths, 0, seq_len)
    cosine_table, sine_table = rotation(query_pos, head_dim)

    def query_prep(raw_part, gain_vec):
        return rotate(
            head_norm(raw_part, gain_vec), cosine_table[:, :, None], sine_table[:, :, None]
        )

    def key_prep(raw_part, gain_vec):
        return rotate(head_norm(raw_part, gain_vec), cosine_table, sine_table)

    def value_prep(raw_part):
        return head_norm(raw_part, 1.0)

    q_rot, query_back = jax.vjp(query_prep, q_raw, head_gains[0])
    k_rot, key_back = jax.vjp(key_prep, k_raw, head_gains[1])
    v_normed, value_back = jax.vjp(value_prep, v_raw)
    q_low = q_rot.astype(jnp.bfloat16)
    keys_all, values_all = (
        lax.all_gather(k_rot.astype(jnp.bfloat16), ("seq", "row"), axis=1, tiled=True),
        lax.all_gather(v_normed.astype(jnp.bfloat16), ("seq", "row"), axis=1, tiled=True),
    )
    block_size = min(512, seq_len)
    block_count = seq_len // block_size
    blocks = jnp.arange(block_count, dtype=jnp.int32)

    def scored(block_index):
        return block_scores(
            q_low, keys_all, block_index * block_size, block_size, query_seg, query_place, key_seg
        )

    def values_at(block_index):
        return lax.dynamic_slice_in_dim(values_all, block_index * block_size, block_size, 1)

    def stats_step(carry, block_index):
        row_top, row_total = carry
        scores, allowed = scored(block_index)
        new_top = jnp.maximum(row_top, jnp.max(jnp.where(allowed, scores, MASK_FILL), axis=3))
        weights = jnp.where(allowed, jnp.exp(scores - new_top[..., None]), 0.0)
        row_total = row_total * jnp.exp(row_top - new_top) + jnp.sum(weights, axis=3)
        return ((new_top, row_total), None)

    start_top = jnp.full((seq_count, heads_here, tokens_row), MASK_FILL, jnp.float32)
    (row_top, row_total), unused = lax.scan(
        stats_step, (start_top, jnp.zeros_like(start_top)), blocks
    )
    log_total = row_top + jnp.log(row_total)

    def probs_at(block_index):
        scores, allowed = scored(block_index)
        return jnp.where(allowed, jnp.exp(scores - log_total[..., None]), 0.0)

    def out_step(total_out, block_index):
        probs_low = probs_at(block_index).astype(jnp.bfloat16)
        total_out = total_out + jnp.einsum(
            "shqk,skd->sqhd", probs_low, values_at(block_index), preferred_element_type=jnp.float32
        )
        return (total_out, None)

    attended, unused = lax.scan(
        out_step, jnp.zeros((seq_count, tokens_row, heads_here, head_dim), jnp.float32), blocks
    )
    o_low = attended.astype(jnp.bfloat16).reshape(seq_count, tokens_row, q_width)
    head_slots = lax.dynamic_update_slice_in_dim(
        jnp.full((heads_all,), MASK_FILL, jnp.float32),
        jnp.max(row_top, axis=(0, 2)),
        col_index * heads_here,
        0,
    )
    logit_top = lax.pmax(head_slots, ("seq", "row", "col"))
    o_rows, attn_val = spread_cols(o_low, lambda gathered: times_right(gathered, w_out))
    attn_norm, attn_normed, attn_factor = norm_forward(attn_val, norm_gains[1], width_all)
    h_one = inputs + attn_norm
    lr_low = width_total(times_right(x_low, laurel_left)).astype(jnp.bfloat16)
    lo_val = times_right(lr_low, laurel_right)
    lo_norm, lo_normed, lo_factor = norm_forward(lo_val, norm_gains[2], width_all)
    h_two = (h_one + (x_norm + lo_norm)) * ROOT_HALF
    f_norm, f_normed, f_factor = norm_forward(h_two, norm_gains[3], width_all)
    f_low = f_norm.astype(jnp.bfloat16)
    f_rows, gate_up = spread_rows(f_low, lambda gathered: times_right(gathered, w_gate_up))
    gate_val = gate_up[:, :, :ff_here]
    up_val = gate_up[:, :, ff_here:]

    def geglu(gate_part, up_part):
        return jax.nn.gelu(gate_part, approximate=True) * up_part

    hidden, geglu_back = jax.vjp(geglu, gate_val, up_val)
    hid_low = hidden.astype(jnp.bfloat16)
    hid_rows, ff_val = spread_cols(hid_low, lambda gathered: times_right(gathered, w_down))
    ff_norm, ff_normed, ff_factor = norm_forward(ff_val, norm_gains[4], width_all)
    h_three = h_two + ff_norm
    h_low = h_three.astype(jnp.bfloat16)
    pg_val = width_total(times_right(h_low, per_gate))
    per_input = per_layer_in.astype(jnp.float32)

    def per_mix(gate_part):
        return jax.nn.gelu(gate_part, approximate=True) * per_input

    gp_val, per_back = jax.vjp(per_mix, pg_val)
    gp_low = gp_val.astype(jnp.bfloat16)
    pp_val = times_right(gp_low, per_proj)
    pp_norm, pp_normed, pp_factor = norm_forward(pp_val, norm_gains[5], width_all)
    layer_out = (h_three + pp_norm).astype(jnp.bfloat16)
    grad_top = out_grad.astype(jnp.float32)
    d_pp, gain_five = norm_backward(grad_top, pp_normed, pp_factor, norm_gains[5], width_all)
    d_pp_low = d_pp.astype(jnp.bfloat16)
    grad_per_proj = outer_sum(gp_low, d_pp_low)
    (d_pg,) = per_back(width_total(times_back(d_pp_low, per_proj)))
    d_pg_low = d_pg.astype(jnp.bfloat16)
    grad_per_gate = outer_sum(h_low, d_pg_low)
    d_three = grad_top + times_back(d_pg_low, per_gate)
    d_ff, gain_four = norm_backward(d_three, ff_normed, ff_factor, norm_gains[4], width_all)
    d_ff_low = d_ff.astype(jnp.bfloat16)
    dff_rows, d_hidden = spread_rows(d_ff_low, lambda gathered: times_back(gathered, w_down))
    grad_down = outer_sum(hid_rows, dff_rows)
    d_gate, d_up = geglu_back(d_hidden)
    d_gate_up = jnp.concatenate([d_gate, d_up], axis=2).astype(jnp.bfloat16)
    dgu_rows, d_f_low = spread_cols(d_gate_up, lambda gathered: times_back(gathered, w_gate_up))
    grad_gate_up = outer_sum(f_rows, dgu_rows)
    d_f, gain_three = norm_backward(d_f_low, f_normed, f_factor, norm_gains[3], width_all)
    d_half = (d_three + d_f) * ROOT_HALF
    d_lo, gain_two = norm_backward(d_half, lo_normed, lo_factor, norm_gains[2], width_all)
    d_lo_low = d_lo.astype(jnp.bfloat16)
    grad_laurel_right = outer_sum(lr_low, d_lo_low)
    d_lr_low = width_total(times_back(d_lo_low, laurel_right)).astype(jnp.bfloat16)
    grad_laurel_left = outer_sum(x_low, d_lr_low)
    d_attn, gain_one = norm_backward(d_half, attn_normed, attn_factor, norm_gains[1], width_all)
    d_attn_low = d_attn.astype(jnp.bfloat16)
    dattn_rows, d_o = spread_rows(d_attn_low, lambda gathered: times_back(gathered, w_out))
    grad_w_out = outer_sum(o_rows, dattn_rows)
    d_o_low = d_o.astype(jnp.bfloat16).reshape(seq_count, tokens_row, heads_here, head_dim)

    def delta_step(total_delta, block_index):
        d_probs = jnp.einsum(
            "sqhd,skd->shqk", d_o_low, values_at(block_index), preferred_element_type=jnp.float32
        )
        return (total_delta + jnp.sum(probs_at(block_index) * d_probs, axis=3), None)

    row_delta, unused = lax.scan(delta_step, jnp.zeros_like(log_total), blocks)

    def grad_step(carry, block_index):
        d_query, d_keys, d_values = carry
        block_start = block_index * block_size
        prob_vals = probs_at(block_index)
        d_probs = jnp.einsum(
            "sqhd,skd->shqk", d_o_low, values_at(block_index), preferred_element_type=jnp.float32
        )
        d_scores = (prob_vals * (d_probs - row_delta[..., None])).astype(jnp.bfloat16)
        keys_part = lax.dynamic_slice_in_dim(keys_all, block_start, block_size, 1)
        d_query = d_query + jnp.einsum(
            "shqk,skd->sqhd", d_scores, keys_part, preferred_element_type=jnp.float32
        )
        key_part = jnp.einsum("shqk,sqhd->skd", d_scores, q_low, preferred_element_type=jnp.float32)
        value_part = jnp.einsum(
            "shqk,sqhd->skd",
            prob_vals.astype(jnp.bfloat16),
            d_o_low,
            preferred_element_type=jnp.float32,
        )
        d_keys = lax.dynamic_update_slice_in_dim(d_keys, key_part, block_start, 1)
        d_values = lax.dynamic_update_slice_in_dim(d_values, value_part, block_start, 1)
        return ((d_query, d_keys, d_values), None)

    zero_keys = jnp.zeros((seq_count, seq_len, head_dim), jnp.float32)
    (d_query, d_keys, d_values), unused = lax.scan(
        grad_step, (jnp.zeros_like(attended), zero_keys, zero_keys), blocks
    )
    own_keys, own_values = (
        lax.psum_scatter(d_keys, ("seq", "row"), scatter_dimension=1, tiled=True),
        lax.psum_scatter(d_values, ("seq", "row"), scatter_dimension=1, tiled=True),
    )
    pair_keys, pair_values = swapped((own_keys, own_values), "col", 0)
    d_q_raw, d_q_gain = query_back(d_query)
    d_k_raw, d_k_gain = key_back(own_keys + pair_keys)
    (d_v_raw,) = value_back(own_values + pair_values)
    key_offset = col_index % 2 * key_width
    d_heads_low = jnp.concatenate(
        [
            d_q_raw.reshape(seq_count, tokens_row, q_width),
            lax.dynamic_slice_in_dim(d_k_raw, key_offset, key_width, 2),
            lax.dynamic_slice_in_dim(d_v_raw, key_offset, key_width, 2),
        ],
        axis=2,
    ).astype(jnp.bfloat16)
    dhead_rows, d_x_heads = spread_cols(d_heads_low, lambda gathered: times_back(gathered, w_back))
    grad_heads = outer_sum(x_rows, dhead_rows)
    d_x_low = d_x_heads + times_back(d_lr_low, laurel_left)
    d_x_part, gain_zero = norm_backward(
        d_half + d_x_low, x_normed, x_factor, norm_gains[0], width_all
    )
    grad_in = (d_half + d_x_part).astype(jnp.bfloat16)
    head_part = width_total(jnp.stack([d_q_gain, d_k_gain * 0.5]))
    sum_heads, sum_out, sum_gate_up, sum_down = lax.psum(
        (grad_heads, grad_w_out, grad_gate_up, grad_down), "seq"
    )
    sum_left, sum_right, sum_per_gate, sum_per_proj, sum_gains, sum_head_gains = lax.psum(
        (
            grad_laurel_left,
            grad_laurel_right,
            grad_per_gate,
            grad_per_proj,
            jnp.stack([gain_zero, gain_one, gain_two, gain_three, gain_four, gain_five]),
            head_part,
        ),
        ("seq", "col"),
    )
    clip_factor = jnp.sqrt(CLIP_LEVEL / jnp.maximum(logit_top, CLIP_LEVEL))
    clipped_gains = jnp.stack(
        [
            clip_factor[:, None] * head_gains[0][None, :],
            clip_factor[:, None] * head_gains[1][None, :],
        ]
    )
    return (
        layer_out,
        grad_in,
        sum_heads[:, :q_width],
        sum_heads[:, q_width : q_width + key_width],
        sum_heads[:, q_width + key_width :],
        sum_out,
        sum_gate_up[:, :ff_here],
        sum_gate_up[:, ff_here:],
        sum_down,
        sum_left,
        sum_right,
        sum_per_gate,
        sum_per_proj,
        sum_gains,
        sum_head_gains,
        clipped_gains,
    )


def group_gather(values):
    return lax.all_gather(values, ("seq", "col"), axis=0, tiled=True)


def group_scatter(partial):
    return lax.psum_scatter(
        partial.astype(jnp.bfloat16), ("seq", "col"), scatter_dimension=0, tiled=True
    ).astype(jnp.float32)


def to_owner(values):
    seq_count, tokens, width = values.shape
    rows = lax.axis_size("row")
    parts = values.reshape(rows, seq_count * tokens // rows, width)
    moved = lax.all_to_all(parts, "row", split_axis=0, concat_axis=0)
    return moved.transpose(1, 0, 2).reshape(parts.shape[1], rows * width)


def from_owner(values, seq_count):
    tokens, width = values.shape
    rows = lax.axis_size("row")
    parts = values.reshape(tokens, rows, width // rows).transpose(1, 0, 2)
    moved = lax.all_to_all(parts, "row", split_axis=0, concat_axis=0)
    return moved.reshape(seq_count, rows * tokens // seq_count, width // rows)


def mm(left_side, right_side):
    return jnp.dot(left_side, right_side, preferred_element_type=jnp.float32)


def mm_nt(left_side, right_side):
    return lax.dot_general(
        left_side, right_side, (((1,), (1,)), ((), ())), preferred_element_type=jnp.float32
    )


def mm_tn(left_side, right_side):
    return lax.dot_general(
        left_side, right_side, (((0,), (0,)), ((), ())), preferred_element_type=jnp.float32
    )


def rms(values):
    factor = lax.rsqrt(jnp.mean(values * values, axis=-1, keepdims=True) + EPSILON)
    return values * factor, factor


def rms_back(grad_values, normed, factor, gain_vec):
    grad_normed = grad_values * gain_vec
    inner = jnp.mean(grad_normed * normed, axis=-1, keepdims=True)
    return (
        factor * (grad_normed - normed * inner),
        jnp.sum(grad_values * normed, axis=0, keepdims=True),
    )


def gather_rows(values, axis):
    return lax.all_gather(values, "row", axis=axis, tiled=True)


def scatter_rows(values, axis):
    return lax.psum_scatter(
        values.astype(jnp.bfloat16), "row", scatter_dimension=axis, tiled=True
    ).astype(jnp.float32)


def both_cores(values, axis):
    return lax.all_gather(values, "seq", axis=axis, tiled=True)


def remote(src, dst, send_sem, recv_sem, device):
    return pltpu.make_async_remote_copy(
        src_ref=src,
        dst_ref=dst,
        send_sem=send_sem,
        recv_sem=recv_sem,
        device_id=device,
        device_id_type=MESH,
    )


def greet(core, row, col):
    barrier = pltpu.get_barrier_semaphore()
    near = [(core, row ^ 1, col), (core, row ^ 2, col), (core, row ^ 3, col), (1 - core, row, col)]
    for device in near:
        pl.semaphore_signal(barrier, inc=1, device_id=device, device_id_type=MESH)

    @pl.when(col > 0)
    def _():
        pl.semaphore_signal(barrier, inc=1, device_id=(core, row, col - 1), device_id_type=MESH)

    @pl.when(col < 3)
    def _():
        pl.semaphore_signal(barrier, inc=1, device_id=(core, row, col + 1), device_id_type=MESH)

    ends = jnp.where((col == 0) | (col == 3), 1, 2)
    pl.semaphore_wait(barrier, 4 + ends)


class Gather:
    def __init__(self, place, buf, rows, sems):
        self.core, self.row, self.col = place
        self.buf, self.rows = buf, rows
        self.send_z, self.recv_z, self.send_s, self.recv_s = sems

    def part(self, core, col, piece):
        rows = self.rows // PIECES
        first = (core * 4 + col) * self.rows + piece * rows
        return self.buf.at[pl.ds(pl.multiple_of(first, rows), rows)]

    def hop(self, dist, right, piece):
        part = self.part(self.core, self.col - dist if right else self.col + dist, piece)
        lane = ((0 if right else 3) + dist) * PIECES + piece
        return remote(
            part,
            part,
            self.send_z.at[lane],
            self.recv_z.at[lane],
            (self.core, self.row, self.col + (1 if right else -1)),
        )

    def came(self, dist, right, piece):
        part = self.part(self.core, self.col - dist if right else self.col + dist, piece)
        lane = ((0 if right else 3) + dist - 1) * PIECES + piece
        return remote(
            part, part, self.send_z.at[lane], self.recv_z.at[lane], (self.core, self.row, self.col)
        )

    def to_sibling(self, col, piece, core=None):
        part = self.part(self.core if core is None else core, col, piece)
        lane = col * PIECES + piece
        return remote(
            part,
            part,
            self.send_s.at[lane],
            self.recv_s.at[lane],
            (1 - self.core, self.row, self.col),
        )

    def start(self):
        col = self.col
        for piece in range(PIECES):

            @pl.when(col < 3)
            def _():
                self.hop(0, True, piece).start()

            @pl.when(col > 0)
            def _():
                self.hop(0, False, piece).start()

        for piece in range(PIECES):
            self.to_sibling(col, piece).start()

    def forward(self, work=()):
        col = self.col
        work = list(work)
        for dist in (1, 2, 3):
            for piece in range(PIECES):

                @pl.when(col >= dist)
                def _():
                    self.came(dist, True, piece).wait_recv()
                    if dist < 3:

                        @pl.when(col < 3)
                        def _():
                            self.hop(dist, True, piece).start()

                    self.to_sibling(col - dist, piece).start()

                @pl.when(col + dist <= 3)
                def _():
                    self.came(dist, False, piece).wait_recv()
                    if dist < 3:

                        @pl.when(col > 0)
                        def _():
                            self.hop(dist, False, piece).start()

                    self.to_sibling(col + dist, piece).start()

            if work:
                work.pop(0)()

    def finish(self):
        for piece in range(PIECES):
            for col in range(4):
                self.to_sibling(col, piece, 1 - self.core).wait_recv()

    def drain(self):
        for piece in range(PIECES):
            for col in range(4):
                self.to_sibling(col, piece).wait_send()
            for dist in (0, 1, 2):

                @pl.when((self.col < 3) & (self.col >= dist))
                def _():
                    self.hop(dist, True, piece).wait_send()

                @pl.when((self.col > 0) & (self.col + dist <= 3))
                def _():
                    self.hop(dist, False, piece).wait_send()


class Scatter:
    def __init__(self, place, rows, bufs, sems):
        self.core, self.row, self.col = place
        self.rows = rows
        self.give, self.keep, self.got, self.sent, self.left, self.right = bufs
        self.send_z, self.recv_z, self.send_s, self.recv_s = sems

    def sibling(self, dest):
        rows = pl.ds(dest * self.rows, self.rows)
        return remote(
            self.give.at[rows],
            self.got.at[rows],
            self.send_s.at[dest],
            self.recv_s.at[dest],
            (1 - self.core, self.row, self.col),
        )

    def start(self):
        for dest in (3, 0, 2, 1):
            self.sibling(dest).start()

    def piece(self, piece):
        rows = self.rows // PIECES
        return pl.ds(piece * rows, rows)

    def mine(self, dest, piece):
        count = self.rows // PIECES
        rows = pl.ds(dest * self.rows + piece * count, count)
        return self.keep[rows].astype(F32) + self.got[rows].astype(F32)

    def inbox(self, dest, right):
        return self.left.at[dest - 1] if right else self.right.at[dest]

    def hop(self, dest, right, piece):
        lane = ((0 if right else 4) + dest) * PIECES + piece
        return remote(
            self.sent.at[dest, self.piece(piece)],
            self.inbox(dest, right).at[self.piece(piece)],
            self.send_z.at[lane],
            self.recv_z.at[lane],
            (self.core, self.row, self.col + (1 if right else -1)),
        )

    def step(self, col, dest, right, piece):
        rows = self.piece(piece)
        if piece == 0:
            self.sibling(dest).wait_recv()
        total = self.mine(dest, piece)
        if col != (0 if right else 3):
            self.hop(dest, right, piece).wait_recv()
            total = total + self.inbox(dest, right)[rows].astype(F32)
        self.sent[dest, rows] = total.astype(BF)
        self.hop(dest, right, piece).start()

    def steps(self, col):
        if col > 1:
            return [
                [(3 - dest, not right, piece) for dest, right, piece in part]
                for part in self.steps(3 - col)
            ]
        full = lambda dest, right: [(dest, right, piece) for piece in range(PIECES)]
        if col == 0:
            return [full(3, True) + full(2, True), full(1, True)]
        near, far = full(3, True) + full(2, True), full(0, False)
        lag, order = PIECES - 1, []
        for index, item in enumerate(near):
            order.append(item)
            if index + 1 >= lag and far:
                order.append(far.pop(0))
        cut = PIECES + 2
        return [order[:cut], order[cut:] + far]

    def run(self, result, work=()):
        work = list(work)
        for part in range(2):
            for col in range(4):

                @pl.when(self.col == col)
                def _():
                    for dest, right, piece in self.steps(col)[part]:
                        self.step(col, dest, right, piece)

            for call in work[part : part + 1]:
                call()
        for call in work[2:]:
            call()
        for dest in range(4):

            @pl.when(self.col == dest)
            def _():
                self.sibling(dest).wait_recv()
                for piece in range(PIECES):
                    rows = self.piece(piece)
                    total = self.mine(dest, piece)
                    for right in (True, False):
                        if dest != (0 if right else 3):
                            self.hop(dest, right, piece).wait_recv()
                            total = total + self.inbox(dest, right)[rows].astype(F32)
                    result[rows] = total

    def drain(self):
        for dest in range(4):
            self.sibling(dest).wait_send()
        for piece in range(PIECES):
            for dest in (1, 2, 3):

                @pl.when(self.col < dest)
                def _():
                    self.hop(dest, True, piece).wait_send()

                @pl.when(self.col > 3 - dest)
                def _():
                    self.hop(3 - dest, False, piece).wait_send()


class RowGather:
    def __init__(self, place, source, block, halves, sems):
        self.core, self.row, self.col = place
        self.source, self.block, self.halves = source, block, halves
        self.sems = sems

    def neighbour(self, mask):
        return (self.core, self.row ^ mask, self.col)

    def own(self):
        return pltpu.make_async_copy(self.source, self.block(self.row), self.sems.at[8])

    def first(self, mask, block=None):
        lane = mask - 1
        return remote(
            self.source,
            self.block(self.row) if block is None else block,
            self.sems.at[lane],
            self.sems.at[4 + lane],
            self.neighbour(mask),
        )

    def second(self, mask):
        part = self.halves(self.row ^ (3 - mask))[mask - 1]
        return remote(
            part, part, self.sems.at[1 + mask], self.sems.at[5 + mask], self.neighbour(mask)
        )

    def start(self):
        self.first(1).start()
        self.first(2).start()
        self.own().start()

    def finish_first(self):
        for mask in (1, 2):
            self.first(mask, self.block(self.row ^ mask)).wait_recv()
            self.first(mask).wait_send()
        self.own().wait()

    def forward(self):
        self.first(1, self.block(self.row ^ 1)).wait_recv()
        self.second(2).start()
        self.first(2, self.block(self.row ^ 2)).wait_recv()
        self.second(1).start()

    def finish(self):
        for mask in (1, 2):
            part = self.halves(self.row ^ 3)[mask - 1]
            remote(
                part, part, self.sems.at[1 + mask], self.sems.at[5 + mask], self.neighbour(mask)
            ).wait_recv()
        self.own().wait()
        self.first(1).wait_send()
        self.first(2).wait_send()
        self.second(1).wait_send()
        self.second(2).wait_send()


def by_rows(buf, block_rows):
    half = block_rows // 2

    def block(index):
        return buf.at[pl.ds(pl.multiple_of(index * block_rows, block_rows), block_rows)]

    def halves(index):
        return [
            buf.at[pl.ds(pl.multiple_of(index * block_rows + part * half, half), half)]
            for part in range(2)
        ]

    return block, halves


def by_core_rows(core):
    def split(buf, block_rows):
        own = block_rows // 2

        def piece(index, part, count):
            first = index * block_rows + core * own + part * (own // count)
            return buf.at[pl.ds(pl.multiple_of(first, own // count), own // count)]

        return (
            lambda index: piece(index, 0, 1),
            lambda index: [piece(index, part, 2) for part in range(2)],
        )

    return split


def by_half_cols(part):
    def split(buf, block_cols):
        own, rows = block_cols // 2, buf.shape[0] // 2

        def cols(index):
            return pl.ds(pl.multiple_of(index * block_cols + part * own, own), own)

        return (
            lambda index: buf.at[:, cols(index)],
            lambda index: [buf.at[pl.ds(piece * rows, rows), cols(index)] for piece in range(2)],
        )

    return split


def by_cols(buf, block_cols):
    rows = buf.shape[0] // 2

    def block(index):
        return buf.at[:, pl.ds(pl.multiple_of(index * block_cols, block_cols), block_cols)]

    def halves(index):
        cols = pl.ds(pl.multiple_of(index * block_cols, block_cols), block_cols)
        return [buf.at[pl.ds(part * rows, rows), cols] for part in range(2)]

    return block, halves


def gelu_both(values):
    inner = 0.7978845608028654 * (values + 0.044715 * values * values * values)
    bend = jnp.tanh(inner)
    slope = 0.7978845608028654 * (1.0 + 3.0 * 0.044715 * values * values)
    return 0.5 * values * (1.0 + bend), 0.5 * (1.0 + bend) + 0.5 * values * (1.0 - bend * bend) * slope


def head_parts(raw, gain, cosine, sine):
    factor = lax.rsqrt(jnp.mean(raw * raw, axis=1, keepdims=True) + EPSILON)
    half = raw.shape[1] // 2
    scaled = raw * factor * gain
    first, second = scaled[:, :half], scaled[:, half:]
    return jnp.concatenate([first * cosine - second * sine, second * cosine + first * sine], axis=1)


def forward_kernel(
    x_in,
    g_in,
    gains_in,
    w_query,
    w_key,
    w_value,
    w_out,
    w_gate,
    w_up,
    w_down,
    laurel_left,
    laurel_right,
    per_gate,
    per_proj,
    cosine,
    sine,
    start,
    head_gains,
    x_own,
    g_own,
    gains,
    raw_q,
    raw_kv,
    q_low,
    kv,
    lse,
    top,
    o_low,
    attn_val,
    lr_low,
    ff_val,
    laurels,
    vpg,
    vpp,
    wq_all,
    wkv_all,
    wo_all,
    wg_all,
    wu_all,
    wd_all,
    xg_all,
    fg_all,
    gate_all,
    up_all,
    turned_all,
    w_kv_pair,
    laurel_own,
    gains_pad,
    vq,
    vkv,
    vo,
    vg,
    vu,
    vd,
    xg,
    fg,
    gate,
    up,
    hid,
    turned,
    give,
    keep,
    got,
    sent,
    left,
    right,
    give2,
    keep2,
    got2,
    sent2,
    left2,
    right2,
    half_sum,
    row_sems,
    z_send,
    z_recv,
    s_send,
    s_recv,
    misc_send,
    misc_recv,
    out_sems,
):
    core, row, col = lax.axis_index("seq"), lax.axis_index("row"), lax.axis_index("col")
    place = (core, row, col)
    own_tokens, width = x_own.shape
    block = x_in.shape[2]
    head_dim = head_gains.shape[1]
    tokens = xg.shape[0]
    ff_part = gate.shape[1]
    chunk = 2 * own_tokens
    key_width = w_key.shape[1]
    half = row % 2
    half_block = block // 2
    halves2 = (give2, keep2, got2, sent2, left2, right2)
    greet(core, row, col)

    my_cols = pl.ds(pl.multiple_of(row * block, block), block)

    def hand_over(mask):
        return remote(
            x_in.at[row ^ mask],
            x_own.at[:, my_cols],
            misc_send.at[mask],
            misc_recv.at[mask],
            (core, row ^ mask, col),
        )

    def hand_grad(mask):
        return remote(
            g_in.at[row ^ mask],
            g_own.at[:, my_cols],
            misc_send.at[11 + mask],
            misc_recv.at[11 + mask],
            (core, row ^ mask, col),
        )

    def hand_gains(mask):
        return remote(
            gains_pad,
            gains.at[:, my_cols],
            misc_send.at[3 + mask],
            misc_recv.at[3 + mask],
            (core, row ^ mask, col),
        )

    for mask in (3, 1, 2):
        hand_over(mask).start()
    gains_pad[pl.ds(0, 6)] = gains_in[...]
    gains_pad[pl.ds(6, 2)] = jnp.zeros((2, block), F32)
    for mask in (3, 1, 2):
        hand_gains(mask).start()
    x_own[:, my_cols] = x_in[row]
    g_own[:, my_cols] = g_in[row]
    gains[:, my_cols] = gains_pad[...]

    pair_cols = pl.ds(pl.multiple_of(col % 2 * key_width, key_width), key_width)
    w_kv_own = w_kv_pair.at[:, pair_cols]
    w_kv_own[...] = jnp.where(core == 0, w_key[...].astype(F32), w_value[...].astype(F32)).astype(BF)
    pair = remote(w_kv_own, w_kv_own, misc_send.at[7], misc_recv.at[7], (core, row, col ^ 1))
    pair.start()

    lanes = iter(range(32))

    def rows_of(source, buf, split=by_rows, size=block):
        block_of, halves_of = split(buf, size)
        return RowGather(place, source, block_of, halves_of, row_sems.at[next(lanes)])

    tile = 256
    core_head = pl.ds(pl.multiple_of(core * head_dim, head_dim), head_dim)

    def core_tile(index):
        return pl.ds(pl.multiple_of(core * ff_part + index * tile, tile), tile)

    get_q = rows_of(w_query.at[:, core_head], vq)
    get_kv = rows_of(w_kv_pair, vkv)
    get_o = rows_of(w_out.at[core_head], vo, by_cols)
    laurel_own[...] = jnp.where(
        core == 0, laurel_left[...].astype(F32), laurel_right[...].astype(F32)
    ).astype(BF)
    get_laurel = [rows_of(laurel_own, laurels.at[core], by_cols)]
    per_rows, per_cols = per_gate.shape[0] // 2, per_proj.shape[0] // 2
    own_rows = pl.ds(pl.multiple_of(core * per_rows, per_rows), per_rows)
    own_cols = pl.ds(pl.multiple_of(core * per_cols, per_cols), per_cols)
    get_per = [
        rows_of(per_gate.at[own_rows], vpg, by_core_rows(core)),
        rows_of(per_proj.at[own_cols], vpp.at[own_cols], by_cols),
    ]
    tiles = ff_part // tile
    get_gu = [
        [
            rows_of(whole.at[:, core_tile(index)], buf.at[:, pl.ds(index * tile, tile)])
            for whole, buf in ((w_gate, vg), (w_up, vu))
        ]
        for index in range(tiles)
    ]
    half_ff = ff_part // 2
    core_ff = pl.ds(pl.multiple_of(core * ff_part, ff_part), ff_part)
    get_d = [
        rows_of(w_down.at[core_ff, pl.ds(part * (block // 2), block // 2)], vd, by_half_cols(part))
        for part in range(2)
    ]

    def per_parts(which, lane):
        parts = [
            vpg.at[pl.ds(pl.multiple_of(index * block + which * per_rows, per_rows), per_rows)]
            for index in range(4)
        ]
        parts.append(vpp.at[pl.ds(pl.multiple_of(which * per_cols, per_cols), per_cols)])
        return list(enumerate(parts, lane))

    def begin(jobs):
        for job in jobs:
            job.start()

    def push(jobs):
        for job in jobs:
            job.forward()

    def complete(jobs):
        for job in jobs:
            job.finish()

    get_q.start()
    pair.wait_recv()
    get_kv.start()

    for mask in (1, 2, 3):
        remote(
            x_in.at[row],
            x_own.at[:, pl.ds(pl.multiple_of((row ^ mask) * block, block), block)],
            misc_send.at[mask],
            misc_recv.at[mask],
            (core, row, col),
        ).wait_recv()
        remote(
            gains_pad,
            gains.at[:, pl.ds(pl.multiple_of((row ^ mask) * block, block), block)],
            misc_send.at[3 + mask],
            misc_recv.at[3 + mask],
            (core, row, col),
        ).wait_recv()

    def own_norm():
        values = x_own[...].astype(F32)
        factor = lax.rsqrt(jnp.mean(values * values, axis=1, keepdims=True) + EPSILON)
        return values, values * factor * gains[pl.ds(0, 1)]

    mine = pl.ds(pl.multiple_of((core * 4 + col) * own_tokens, own_tokens), own_tokens)
    xg[mine] = own_norm()[1].astype(BF)
    sems = lambda lane: (z_send.at[lane], z_recv.at[lane], s_send.at[lane], s_recv.at[lane])
    gather_x = Gather(place, xg, own_tokens, sems(0))
    gather_x.start()
    gather_x.forward(
        [
            lambda: None,
            lambda: (push([get_q, get_kv]), begin([get_o])),
        ]
    )
    gather_x.finish()
    complete([get_q, get_kv])

    raw_q[...] = mm(xg[...], vq[...])
    raw_kv[...] = mm(xg[...], vkv[...])
    q_low[...] = head_parts(raw_q[...], head_gains[pl.ds(0, 1)], cosine[...], sine[...]).astype(BF)
    is_key = core == 0
    kv_here = head_parts(
        raw_kv[...],
        jnp.where(is_key, head_gains[pl.ds(1, 1)], 1.0),
        jnp.where(is_key, cosine[...], 1.0),
        jnp.where(is_key, sine[...], 0.0),
    ).astype(BF)

    def kv_part(kind, which):
        return kv.at[kind, pl.ds(pl.multiple_of(which * tokens, tokens), tokens)]

    kv[core, pl.ds(pl.multiple_of(half * tokens, tokens), tokens)] = kv_here
    here = kv_part(core, half)
    to_x = remote(here, here, misc_send.at[8], misc_recv.at[8], (core, row ^ 1, col))
    to_s = remote(here, here, misc_send.at[9], misc_recv.at[9], (1 - core, row, col))
    to_x.start()
    to_s.start()
    push([get_o])
    begin(get_gu[0] + get_laurel + get_gu[1])
    came = kv_part(core, half ^ 1)
    remote(here, came, misc_send.at[8], misc_recv.at[8], (core, row, col)).wait_recv()
    on_s = remote(came, came, misc_send.at[10], misc_recv.at[10], (1 - core, row, col))
    on_s.start()
    other = kv_part(1 - core, half)
    remote(other, other, misc_send.at[9], misc_recv.at[9], (core, row, col)).wait_recv()
    other_came = kv_part(1 - core, half ^ 1)
    remote(other_came, other_came, misc_send.at[10], misc_recv.at[10], (core, row, col)).wait_recv()

    q_rows = 128
    key_token = lax.broadcasted_iota(jnp.int32, (1, 2 * tokens), 1)
    in_half = key_token % tokens
    key_place = in_half // own_tokens * chunk + key_token // tokens * own_tokens + in_half % own_tokens
    top[...] = jnp.full(top.shape, MASK_FILL, F32)

    def attend(step, carry):
        first = pl.multiple_of(step * q_rows, q_rows)
        rows = pl.ds(first, q_rows)
        token = first + lax.broadcasted_iota(jnp.int32, (q_rows, 1), 0)
        q_place = token // own_tokens * chunk + half * own_tokens + token % own_tokens
        allowed = (key_place <= q_place) & (key_place >= start[rows])
        scores = jnp.where(allowed, mm_nt(q_low[rows], kv[0]), MASK_FILL)
        row_top = jnp.max(scores, axis=1, keepdims=True)
        weights = jnp.exp(scores - row_top)
        total = jnp.sum(weights, axis=1, keepdims=True)
        probs = (weights * (1.0 / total)).astype(BF)
        o_low[rows] = mm(probs, kv[1]).astype(BF)
        lse[rows] = row_top + jnp.log(total)
        top[...] = jnp.maximum(top[...], jnp.max(row_top))
        return carry

    lax.fori_loop(0, tokens // q_rows, attend, 0)
    get_o.finish()

    away = pl.multiple_of((1 - core) * 4 * own_tokens, 4 * own_tokens)
    home = pl.multiple_of(core * 4 * own_tokens, 4 * own_tokens)
    scatter = Scatter(place, own_tokens, (give, keep, got, sent, left, right), sems(1))

    def project(source, weights, target, first):
        def step(index, carry):
            cols = pl.ds(pl.multiple_of(index * block, block), block)
            value = mm(source[pl.ds(first, 4 * own_tokens)], weights[:, cols])
            target[:, cols] = value.astype(target.dtype)
            return carry

        lax.fori_loop(0, width // block, step, 0)

    project(o_low, vo, give, away)
    scatter.start()
    project(o_low, vo, keep, home)
    scatter.run(
        attn_val,
        [lambda: (push(get_gu[0]), push(get_laurel)), lambda: begin(get_gu[2])],
    )
    push(get_gu[1])
    begin(get_gu[3])

    complete(get_laurel)
    laurel_here = laurels.at[core]
    laurel_share = remote(
        laurel_here, laurel_here, misc_send.at[22], misc_recv.at[22], (1 - core, row, col)
    )
    laurel_share.start()
    inputs, x_norm = own_norm()
    attn_normed = rms(attn_val[...])[0]
    laurel_there = laurels.at[1 - core]
    remote(
        laurel_there, laurel_there, misc_send.at[22], misc_recv.at[22], (core, row, col)
    ).wait_recv()
    lr_low[...] = mm_nt(xg[mine], laurels[0]).astype(BF)
    lo_normed = rms(mm(lr_low[...], laurels[1]))[0]
    h_two = (
        inputs + attn_normed * gains[pl.ds(1, 1)] + (x_norm + lo_normed * gains[pl.ds(2, 1)])
    ) * ROOT_HALF
    fg[mine] = (rms(h_two)[0] * gains[pl.ds(3, 1)]).astype(BF)
    gather_f = Gather(place, fg, own_tokens, sems(2))
    gather_f.start()
    gather_f.forward(
        [
            lambda: None,
            lambda: push(get_gu[2]),
            lambda: begin(get_d[:1]),
        ]
    )
    gather_f.finish()

    def unit_tile(index):
        complete(get_gu[index])
        cols = pl.ds(index * tile, tile)
        bent, slope = gelu_both(mm(fg[...], vg[:, cols]))
        up_part = mm(fg[...], vu[:, cols])
        gate[:, cols] = (up_part * slope).astype(BF)
        up[:, cols] = bent.astype(BF)
        hid[:, cols] = (bent * up_part).astype(BF)

    for index in range(tiles):
        if index == 1:
            push(get_gu[3])
        if index == 3:
            push(get_d[:1])
            begin(get_d[1:])
        unit_tile(index)
    turned[...] = hid[...].T
    scatter_ff = [
        Scatter(place, own_tokens, tuple(buf.at[part] for buf in halves2), sems(3 + part))
        for part in range(2)
    ]

    def project_half(part, target, first):
        def step(index, carry):
            cols = pl.ds(pl.multiple_of(index * block + part * half_block, half_block), half_block)
            here = pl.ds(pl.multiple_of(index * half_block, half_block), half_block)
            value = mm(hid[pl.ds(first, 4 * own_tokens)], vd[:, cols])
            target[:, here] = value.astype(target.dtype)
            return carry

        lax.fori_loop(0, width // block, step, 0)

    def down_half(part):
        complete(get_d[part : part + 1])
        project_half(part, give2.at[part], away)
        scatter_ff[part].start()
        project_half(part, keep2.at[part], home)

    def spread_half(part):
        for index in range(width // block):
            ff_val[:, pl.ds(index * block + part * half_block, half_block)] = half_sum[
                :, pl.ds(index * half_block, half_block)
            ]

    def late():
        push(get_d[1:])
        begin(get_per)
        for mask in (1, 2, 3):
            hand_grad(mask).start()

    down_half(0)
    scatter_ff[0].run(half_sum, [lambda: None, late])
    spread_half(0)
    down_half(1)
    keep_weights = [
        pltpu.make_async_copy(source, target, out_sems.at[lane])
        for lane, (source, target) in enumerate(
            [
                (vq, wq_all),
                (vkv, wkv_all),
                (vo, wo_all),
                (vg, wg_all),
                (vu, wu_all),
                (vd, wd_all),
                (xg, xg_all),
                (fg, fg_all),
                (gate, gate_all),
                (up, up_all),
            ]
        )
    ]
    for copy in keep_weights:
        copy.start()
    get_turned = rows_of(
        turned.at[pl.ds(0, half_ff)], turned_all.at[pl.ds(0, half_ff)], by_cols, tokens
    )
    rest = pl.ds(half_ff, half_ff)
    keep_rest = pltpu.make_async_copy(
        turned.at[rest],
        turned_all.at[rest, pl.ds(pl.multiple_of(row * tokens, tokens), tokens)],
        out_sems.at[10],
    )
    keep_rest.start()
    scatter_ff[1].run(half_sum, [lambda: (push(get_per), get_turned.start())])
    spread_half(1)
    complete(get_per)
    share = [
        remote(part, part, misc_send.at[lane], misc_recv.at[lane], (1 - core, row, col))
        for lane, part in per_parts(core, 16)
    ]
    for copy in share:
        copy.start()
    for lane, part in per_parts(1 - core, 16):
        remote(part, part, misc_send.at[lane], misc_recv.at[lane], (core, row, col)).wait_recv()
    for copy in share:
        copy.wait_send()
    get_turned.finish_first()
    keep_rest.wait()

    for mask in (1, 2, 3):
        hand_over(mask).wait_send()
        hand_gains(mask).wait_send()
        hand_grad(mask).wait_send()
        remote(
            g_in.at[row],
            g_own.at[:, pl.ds(pl.multiple_of((row ^ mask) * block, block), block)],
            misc_send.at[11 + mask],
            misc_recv.at[11 + mask],
            (core, row, col),
        ).wait_recv()
    gather_x.drain()
    scatter.drain()
    gather_f.drain()
    scatter_ff[0].drain()
    scatter_ff[1].drain()
    laurel_share.wait_send()
    pair.wait_send()
    to_x.wait_send()
    to_s.wait_send()
    on_s.wait_send()
    for copy in keep_weights:
        copy.wait()


def run_forward(x_in, g_in, gains_in, weights_in, tables, head_gains):
    cosine, sine, start = tables
    w_gate, laurel_left, per_gate, per_proj = (weights_in[i] for i in (4, 7, 9, 10))
    block = x_in.shape[2]
    own, width = x_in.shape[1], 4 * block
    tokens, head_dim, ff_part = 8 * own, head_gains.shape[1], w_gate.shape[1] // 2
    rank = laurel_left.shape[0]
    vm = pl.BlockSpec(memory_space=pltpu.VMEM)
    hbm = pl.BlockSpec(memory_space=pl.ANY)
    shape = jax.ShapeDtypeStruct
    weights = [
        (width, head_dim),
        (width, head_dim),
        (head_dim, width),
        (width, ff_part),
        (width, ff_part),
        (ff_part, width),
    ]
    acts = [
        (tokens, width),
        (tokens, width),
        (tokens, ff_part),
        (tokens, ff_part),
    ]
    outs = [
        shape((own, width), BF),
        shape((own, width), BF),
        shape((8, width), F32),
        shape((tokens, head_dim), F32),
        shape((tokens, head_dim), F32),
        shape((tokens, head_dim), BF),
        shape((2, 2 * tokens, head_dim), BF),
        shape((tokens, 1), F32),
        shape((8, 128), F32),
        shape((tokens, head_dim), BF),
        shape((own, width), F32),
        shape((own, rank), BF),
        shape((own, width), F32),
        shape((2, rank, width), BF),
        shape((width, per_gate.shape[1]), BF),
        shape((per_proj.shape[0], width), BF),
    ] + [shape(size, BF) for size in weights + acts + [(ff_part, 4 * tokens)]]
    scatter_bufs = [
        pltpu.VMEM((4 * own, width), BF),
        pltpu.VMEM((4 * own, width), F32),
        pltpu.VMEM((4 * own, width), BF),
        pltpu.VMEM((4, own, width), BF),
        pltpu.VMEM((3, own, width), BF),
        pltpu.VMEM((3, own, width), BF),
    ]
    dma = pltpu.SemaphoreType.DMA
    return pl.pallas_call(
        forward_kernel,
        out_shape=outs,
        in_specs=[vm, vm, vm, hbm, vm, vm] + [hbm] * 4 + [vm] * 2 + [hbm] * 2 + [vm] * 4,
        out_specs=[vm] * 16 + [hbm] * 11,
        scratch_shapes=[
            pltpu.VMEM((block, head_dim), BF),
            pltpu.VMEM((rank, block), BF),
            pltpu.VMEM((8, block), F32),
        ]
        + [pltpu.VMEM(size, BF) for size in weights + acts]
        + [pltpu.VMEM((tokens, ff_part), BF), pltpu.VMEM((ff_part, tokens), BF)]
        + scatter_bufs
        + [pltpu.VMEM((2,) + buf.shape[:-1] + (width // 2,), buf.dtype) for buf in scatter_bufs]
        + [pltpu.VMEM((own, width // 2), F32)]
        + [
            dma((18, 10)),
            dma((5, 8 * PIECES)),
            dma((5, 8 * PIECES)),
            dma((5, 4 * PIECES)),
            dma((5, 4 * PIECES)),
            dma((24,)),
            dma((24,)),
            dma((11,)),
        ],
        compiler_params=pltpu.CompilerParams(
            collective_id=0, has_side_effects=True, vmem_limit_bytes=VMEM_BYTES
        ),
        cost_estimate=pl.CostEstimate(flops=2 * 10**10, bytes_accessed=5 * 10**7, transcendentals=10**6),
    )(x_in, g_in, gains_in, *weights_in, cosine, sine, start, head_gains)


class RowScatter:
    def __init__(self, place, halves, came, sems, stage=None):
        self.core, self.row, self.col = place
        self.halves, self.came, self.sems = halves, came, sems
        self.stage = stage

    def send(self, lane, index, half, mask):
        return remote(
            self.halves(index)[half],
            self.came.at[lane],
            self.sems.at[lane],
            self.sems.at[6 + lane],
            (self.core, self.row ^ mask, self.col),
        )

    def lane(self, lane):
        index, half, mask = ((1, 0, 1), (3, 0, 1), (2, 1, 2), (3, 1, 2), (2, 0, 2), (1, 1, 1))[lane]
        return self.send(lane, self.row ^ index, half, mask)

    def start(self, lanes=(1, 3, 0, 2)):
        for lane in lanes:
            self.lane(lane).start()

    def load(self, lane):
        slot = {0: 0, 1: 0, 4: 0, 2: 1, 3: 1, 5: 1}[lane]
        return slot, pltpu.make_async_copy(
            self.came.at[lane], self.stage[0].at[slot], self.stage[1].at[slot]
        )

    def fetch(self, *lanes):
        for lane in lanes:
            self.lane(lane).wait_recv()
            if self.stage is not None:
                self.load(lane)[1].start()

    def add(self, lane, index, half):
        if self.stage is None:
            value = self.came[lane]
        else:
            slot, copy = self.load(lane)
            copy.wait()
            value = self.stage[0][slot]
        part = self.halves(self.row ^ index)[half]
        part[...] = (part[...].astype(F32) + value.astype(F32)).astype(BF)

    def middle(self):
        for lane, out, index, half in ((1, 4, 2, 0), (3, 5, 1, 1)):
            self.add(lane, index, half)
            self.lane(out).start()

    def early(self):
        self.add(0, 0, 0)
        self.add(2, 0, 1)

    def finish(self):
        self.add(4, 0, 0)
        self.add(5, 0, 1)

    def drain(self):
        for lane in range(6):
            self.lane(lane).wait_send()


def head_back(grad, raw, gain, cosine, sine):
    factor = lax.rsqrt(jnp.mean(raw * raw, axis=1, keepdims=True) + EPSILON)
    half = raw.shape[1] // 2
    normed = raw * factor
    first, second = grad[:, :half], grad[:, half:]
    back = jnp.concatenate([first * cosine + second * sine, second * cosine - first * sine], axis=1)
    gain_grad = jnp.sum(back * normed, axis=0, keepdims=True)
    inner = back * gain
    return factor * (inner - normed * jnp.mean(inner * normed, axis=1, keepdims=True)), gain_grad


def backward_kernel(
    x_own,
    g_own,
    per_in,
    gains,
    head_gains,
    attn_val,
    lr_low,
    ff_val,
    raw_q,
    raw_kv,
    q_low,
    kv,
    lse,
    top,
    o_low,
    cosine,
    sine,
    start,
    laurels,
    vpg,
    vpp,
    xg_in,
    fg_in,
    gate_in,
    up_in,
    turned_in,
    wq_in,
    wkv_in,
    wo_in,
    wg_in,
    wu_in,
    wd_in,
    y_out,
    x_grad,
    g_gain,
    tops,
    small_a,
    gq,
    gkv,
    gout,
    ggate,
    gup,
    gdown,
    came_g,
    came_u,
    turned_far,
    turned_near,
    vq,
    vkv,
    vo,
    vg,
    vu,
    vd,
    fg,
    gate,
    up,
    dff_all,
    down_stage,
    dffg,
    dattng,
    dgate,
    dup,
    give,
    keep,
    got,
    sent,
    left,
    right,
    own_sum,
    h_two_ref,
    d_three_ref,
    low_ref,
    gpart,
    gcame,
    gpart2,
    gcame2,
    small_give,
    small_keep,
    small_got,
    small_row,
    small_z,
    d_o,
    d_kv,
    kv_give,
    kv_got,
    kv_x_got,
    kv_p_got,
    pkv,
    came_q,
    came_kv,
    came_o,
    stage_g,
    stage_sems,
    load_sems,
    row_sems,
    z_send,
    z_recv,
    s_send,
    s_recv,
    misc_send,
    misc_recv,
    gain_send,
    gain_recv,
    done_sems,
    ff_sems,
    down_sems,
    turned_sems,
):
    core, row, col = lax.axis_index("seq"), lax.axis_index("row"), lax.axis_index("col")
    place = (core, row, col)
    own_tokens, width = x_own.shape
    block = width // 4
    tokens, head_dim = raw_q.shape
    ff_part = gate.shape[1]
    chunk = 2 * own_tokens
    key_width = head_dim // 2
    half = row % 2
    rank = lr_low.shape[1]
    my_cols = pl.ds(pl.multiple_of(row * block, block), block)
    mine = pl.ds(pl.multiple_of((core * 4 + col) * own_tokens, own_tokens), own_tokens)
    away = pl.multiple_of((1 - core) * 4 * own_tokens, 4 * own_tokens)
    home = pl.multiple_of(core * 4 * own_tokens, 4 * own_tokens)

    barrier = pltpu.get_barrier_semaphore()
    for mask in (1, 2, 3):
        pl.semaphore_signal(barrier, inc=1, device_id=(core, row ^ mask, col), device_id_type=MESH)
        for other in (0, 1):
            pl.semaphore_signal(
                barrier, inc=1, device_id=(core ^ other, row, col ^ mask), device_id_type=MESH
            )
    pl.semaphore_signal(barrier, inc=1, device_id=(1 - core, row, col), device_id_type=MESH)
    loads = [
        pltpu.make_async_copy(source, target, load_sems.at[lane])
        for lane, (source, target) in enumerate(
            [
                (wd_in, vd),
                (gate_in, gate),
                (up_in, up),
                (wg_in, vg),
                (wu_in, vu),
                (fg_in, fg),
                (wo_in, vo),
                (wq_in, vq),
                (wkv_in, vkv),
            ]
        )
    ]
    for load in loads:
        load.start()
    pl.semaphore_wait(barrier, 10)
    half_ff = ff_part // 2

    def turned_on(part, mask):
        rows = pl.ds(part * half_ff + (mask - 1) * (half_ff // 2), half_ff // 2)
        first = pl.multiple_of((row ^ (3 - mask)) * tokens, tokens)
        if part == 0:
            source = turned_in.at[rows, pl.ds(first, tokens)]
        else:
            source = turned_near.at[2 - mask, pl.ds((mask - 1) * (half_ff // 2), half_ff // 2)]
        lane = part * 2 + mask - 1
        return remote(
            source,
            turned_far.at[rows],
            row_sems.at[0, lane],
            row_sems.at[0, 6 + lane],
            (core, row ^ mask, col),
        )

    def turned_over(mask):
        return remote(
            turned_in.at[
                pl.ds(half_ff, half_ff), pl.ds(pl.multiple_of(row * tokens, tokens), tokens)
            ],
            turned_near.at[mask - 1],
            row_sems.at[0, 3 + mask],
            row_sems.at[0, 9 + mask],
            (core, row ^ mask, col),
        )

    for mask in (1, 2):
        turned_on(0, mask).start()
        turned_over(mask).start()

    def turned_rest():
        for mask in (1, 2):
            turned_over(mask).wait_recv()
        for mask in (1, 2):
            turned_on(1, mask).start()


    def gain(index):
        return gains[pl.ds(index, 1)]

    inputs = x_own[...].astype(F32)
    x_norm = rms(inputs)[0] * gain(0)
    attn_normed = rms(attn_val[...])[0]
    lo_normed = rms(mm(lr_low[...], laurels[1]))[0]
    h_two = (inputs + attn_normed * gain(1) + (x_norm + lo_normed * gain(2))) * ROOT_HALF
    h_two_ref[...] = h_two
    ff_normed, ff_factor = rms(ff_val[...])
    h_three = h_two + ff_normed * gain(4)
    h_low = h_three.astype(BF)
    p_gate, p_proj = vpg[...], vpp[...]
    pg_gelu, pg_slope = gelu_both(mm(h_low, p_gate))
    per_input = per_in[row].astype(F32)
    gp_low = (pg_gelu * per_input).astype(BF)
    pp_normed, pp_factor = rms(mm(gp_low, p_proj))
    low_ref[...] = (h_three + pp_normed * gain(5)).astype(BF)

    def hand_back(source, target, mask, lane):
        return remote(
            source.at[:, pl.ds(pl.multiple_of((row ^ mask) * block, block), block)],
            target.at[row],
            misc_send.at[lane + mask],
            misc_recv.at[lane + mask],
            (core, row ^ mask, col),
        )

    def came_back(target, mask, lane):
        return remote(
            target.at[row ^ mask],
            target.at[row ^ mask],
            misc_send.at[lane + mask],
            misc_recv.at[lane + mask],
            (core, row, col),
        )

    for mask in (1, 2, 3):
        hand_back(low_ref, y_out, mask, 0).start()
    y_out[row] = low_ref[:, my_cols]

    grad_top = g_own[...].astype(F32)
    d_pp, gain_five = rms_back(grad_top, pp_normed, pp_factor, gain(5))
    d_pp_low = d_pp.astype(BF)
    d_pg_low = (mm_nt(d_pp_low, p_proj) * per_input * pg_slope).astype(BF)
    d_three = grad_top + mm_nt(d_pg_low, p_gate)
    d_three_ref[...] = d_three
    d_ff, gain_four = rms_back(d_three, ff_normed, ff_factor, gain(4))
    gpart[...] = jnp.zeros(gpart.shape, F32)
    gpart[pl.ds(5, 1)] = gain_five
    gpart[pl.ds(4, 1)] = gain_four
    dffg[mine] = d_ff.astype(BF)
    sems = lambda lane: (z_send.at[lane], z_recv.at[lane], s_send.at[lane], s_recv.at[lane])
    gather_ff = Gather(place, dffg, own_tokens, sems(0))
    gather_ff.start()

    def small(kind, first, value):
        rows = pl.ds(first, value.shape[0])
        value = value.astype(BF)

        @pl.when(core == kind)
        def _():
            small_keep[rows] = value

        @pl.when(core != kind)
        def _():
            small_give[rows] = value

    small(0, rank, mm_tn(gp_low, d_pp_low))
    small(1, rank, mm_tn(d_pg_low, h_low))
    gather_ff.forward([lambda: None, turned_rest])
    gather_ff.finish()

    part_rows = tokens // 2

    def ff_piece(group, which):
        return dff_all.at[
            pl.ds(pl.multiple_of(group * tokens + which * part_rows, part_rows), part_rows)
        ]

    def ff_over(mask):
        return remote(
            dffg.at[
                pl.ds(pl.multiple_of(core * part_rows, part_rows), part_rows),
                pl.ds(pl.multiple_of((row ^ mask) * block, block), block),
            ],
            ff_piece(row, core),
            ff_sems.at[mask],
            ff_sems.at[4 + mask],
            (core, row ^ mask, col),
        )

    def ff_came(mask):
        part = ff_piece(row ^ mask, core)
        return remote(part, part, ff_sems.at[mask], ff_sems.at[4 + mask], (core, row, col))

    def ff_share(mask, which):
        part = ff_piece(row ^ mask, which)
        return remote(
            part, part, ff_sems.at[8 + mask], ff_sems.at[12 + mask], (1 - core, row, col)
        )

    for mask in (1, 2, 3):
        ff_over(mask).start()
    dff_all[pl.ds(pl.multiple_of(row * tokens, tokens), tokens)] = dffg[:, my_cols]

    tile = 256
    for load in loads[:3]:
        load.wait()

    def units(index, carry):
        cols = pl.ds(pl.multiple_of(index * tile, tile), tile)
        d_hid = mm_nt(dffg[...], vd[cols])
        dgate[:, cols] = (d_hid * gate[:, cols].astype(F32)).astype(BF)
        dup[:, cols] = (d_hid * up[:, cols].astype(F32)).astype(BF)
        return carry

    lax.fori_loop(0, ff_part // tile, units, 0)
    for load in loads[3:5]:
        load.wait()

    def back_ff(target, first):
        rows = pl.ds(first, 4 * own_tokens)

        def step(index, carry):
            cols = pl.ds(pl.multiple_of(index * block, block), block)
            value = mm_nt(dgate[rows], vg[cols]) + mm_nt(dup[rows], vu[cols])
            target[:, cols] = value.astype(target.dtype)
            return carry

        lax.fori_loop(0, width // block, step, 0)

    scatter_f = Scatter(place, own_tokens, (give, keep, got, sent, left, right), sems(1))
    back_ff(give, away)
    scatter_f.start()
    back_ff(keep, home)

    put_g = RowScatter(place, by_rows(vg, block)[1], came_g, row_sems.at[1], (stage_g, stage_sems))
    put_u = RowScatter(place, by_rows(vu, block)[1], came_u, row_sems.at[2], (stage_g, stage_sems))

    def load_turned(lane):
        mask, part = ((0, None), (3, None), (1, 0), (1, 1), (2, 0), (2, 1))[lane]
        cols = pl.ds(pl.multiple_of((row ^ mask) * tokens, tokens), tokens)
        if part is None:
            source = turned_far if mask else turned_in.at[:, cols]
            target = vd.at[:, cols]
        else:
            rows = pl.ds(part * half_ff, half_ff)
            source = turned_near.at[mask - 1] if part else turned_in.at[rows, cols]
            target = vd.at[rows, cols]
        return pltpu.make_async_copy(source, target, turned_sems.at[lane])

    def down_ready():
        for mask in (1, 2):
            for part in range(2):
                turned_on(part, mask).wait_recv()
        for lane in range(6):
            load_turned(lane).start()
        for mask in (1, 2, 3):
            ff_came(mask).wait_recv()
            ff_share(mask, core).start()

    def down_tile(index):
        slot = index % 2
        rows = pl.ds(index * tile, tile)
        target = gdown.at[pl.ds(pl.multiple_of(core * ff_part + index * tile, tile), tile)]
        local = pltpu.make_async_copy(down_stage.at[slot], target, down_sems.at[index])
        over = remote(
            down_stage.at[slot],
            target,
            down_sems.at[4 + index],
            down_sems.at[8 + index],
            (1 - core, row, col),
        )
        return slot, rows, local, over

    def down_grad():
        for lane in range(6):
            load_turned(lane).wait()
        for mask in (1, 2, 3):
            ff_share(mask, 1 - core).wait_recv()
        for index in range(ff_part // tile):
            slot, rows, local, over = down_tile(index)
            if index >= 2:
                before = down_tile(index - 2)
                before[2].wait()
                before[3].wait_send()
            down_stage[slot] = mm(vd[rows], dff_all[...]).astype(BF)
            local.start()
            over.start()

    def gate_grad(target, grad, put):
        def step(index, carry):
            rows = pl.ds(pl.multiple_of(index * tile, tile), tile)
            target[rows] = mm_tn(fg[:, rows], grad[...]).astype(BF)
            return carry

        lax.fori_loop(0, width // tile, step, 0)

    def start_gate():
        loads[5].wait()
        gate_grad(vg, dgate, put_g)
        put_g.start()

    def start_up():
        gate_grad(vu, dup, put_u)
        put_u.start((1, 3))

    start_gate()
    scatter_f.run(own_sum, [start_up, down_ready])

    gather_ff.drain()
    f_normed, f_factor = rms(h_two_ref[...])
    d_f, gain_three = rms_back(own_sum[...], f_normed, f_factor, gain(3))
    d_half = (d_three_ref[...] + d_f) * ROOT_HALF
    d_three_ref[...] = d_half
    attn_normed, attn_factor = rms(attn_val[...])
    d_attn, gain_one = rms_back(d_half, attn_normed, attn_factor, gain(1))
    dattng[mine] = d_attn.astype(BF)
    gather_a = Gather(place, dattng, own_tokens, sems(2))
    gather_a.start()
    lo_normed, lo_factor = rms(mm(lr_low[...], laurels[1]))
    d_lo, gain_two = rms_back(d_half, lo_normed, lo_factor, gain(2))
    d_lo_low = d_lo.astype(BF)
    d_lr_low = mm_nt(d_lo_low, laurels[1]).astype(BF)
    small(0, 0, mm_tn(lr_low[...], d_lo_low))
    x_low = (rms(x_own[...].astype(F32))[0] * gain(0)).astype(BF)
    small(1, 0, mm_tn(d_lr_low, x_low))
    own_sum[...] = d_half + mm(d_lr_low, laurels[0])
    gpart[pl.ds(3, 1)] = gain_three
    gpart[pl.ds(2, 1)] = gain_two
    gpart[pl.ds(1, 1)] = gain_one
    small_swap = remote(
        small_give, small_got, misc_send.at[8], misc_recv.at[8], (1 - core, row, col)
    )
    small_swap.start()
    put_s = RowScatter(place, by_cols(small_keep, block)[1], small_row, row_sems.at[6])

    def small_sum():
        small_swap.wait_recv()
        small_keep[...] = (small_keep[...].astype(F32) + small_got[...].astype(F32)).astype(BF)

    def middle_gate():
        put_g.fetch(1, 3)
        down_grad()
        put_g.middle()

    def more_small():
        small_sum()
        put_g.fetch(0, 2)

    gather_a.forward([middle_gate, more_small, put_g.early])
    gather_a.finish()
    scatter_f.drain()

    loads[6].wait()
    d_o[...] = mm_nt(dattng[...], vo[...]).astype(BF)
    q_rows = 128
    key_token = lax.broadcasted_iota(jnp.int32, (1, 2 * tokens), 1)
    in_half = key_token % tokens
    key_place = in_half // own_tokens * chunk + key_token // tokens * own_tokens + in_half % own_tokens
    d_kv[...] = jnp.zeros(d_kv.shape, F32)

    def attend(step, carry):
        first = pl.multiple_of(step * q_rows, q_rows)
        rows = pl.ds(first, q_rows)
        token = first + lax.broadcasted_iota(jnp.int32, (q_rows, 1), 0)
        q_place = token // own_tokens * chunk + half * own_tokens + token % own_tokens
        allowed = (key_place <= q_place) & (key_place >= start[rows])
        scores = jnp.where(allowed, mm_nt(q_low[rows], kv[0]), MASK_FILL)
        probs = jnp.exp(scores - lse[rows])
        d_probs = mm_nt(d_o[rows], kv[1])
        delta = jnp.sum(probs * d_probs, axis=1, keepdims=True)
        d_scores = (probs * (d_probs - delta)).astype(BF)
        d_kv[0] += mm_tn(d_scores, q_low[rows])
        d_kv[1] += mm_tn(probs.astype(BF), d_o[rows])
        d_raw, gain_part = head_back(
            mm(d_scores, kv[0]), raw_q[rows], head_gains[pl.ds(0, 1)], cosine[rows], sine[rows]
        )
        d_o[rows] = d_raw.astype(BF)
        return carry + gain_part

    gain_q = lax.fori_loop(0, tokens // q_rows, attend, jnp.zeros((1, head_dim), F32))

    kv_give[...] = d_kv[1 - core].astype(BF)
    swap_kv = remote(kv_give, kv_got, misc_send.at[9], misc_recv.at[9], (1 - core, row, col))
    swap_kv.start()

    def out_grad():
        for part in range(2):
            wide = pl.ds(part * (width // 2), width // 2)
            vo[:, wide] = mm_tn(o_low[...], dattng[:, wide]).astype(BF)

    put_o = RowScatter(place, by_cols(vo, block)[1], came_o, row_sems.at[3])
    swap_kv.wait()
    kv_x = kv_give.at[pl.ds(0, tokens)]
    theirs = pl.ds(pl.multiple_of((half ^ 1) * tokens, tokens), tokens)
    ours = pl.ds(pl.multiple_of(half * tokens, tokens), tokens)
    kv_x[...] = (d_kv[core, theirs] + kv_got[theirs].astype(F32)).astype(BF)
    over_x = remote(kv_x, kv_x_got, misc_send.at[10], misc_recv.at[10], (core, row ^ 1, col))
    over_x.start()
    put_u.start((0, 2))
    load_x = pltpu.make_async_copy(xg_in, dffg, load_sems.at[10])
    for mask in (1, 2, 3):
        ff_over(mask).wait_send()
    load_x.start()
    put_u.fetch(1, 3)
    out_grad()
    put_u.middle()
    put_s.start()
    put_o.start()
    loads[7].wait()
    loads[8].wait()
    over_x.wait_recv()
    d_kind = d_kv[core, ours] + kv_got[ours].astype(F32) + kv_x_got[...].astype(F32)
    kv_p = kv_got.at[pl.ds(0, tokens)]
    kv_p[...] = d_kind.astype(BF)
    over_p = remote(kv_p, kv_p_got, misc_send.at[11], misc_recv.at[11], (core, row, col ^ 1))
    over_p.start()
    over_p.wait()
    d_kind = kv_p[...].astype(F32) + kv_p_got[...].astype(F32)
    is_key = core == 0
    d_kind_raw, gain_k = head_back(
        d_kind,
        raw_kv[...],
        jnp.where(is_key, head_gains[pl.ds(1, 1)], 1.0),
        jnp.where(is_key, cosine[...], 1.0),
        jnp.where(is_key, sine[...], 0.0),
    )
    for part in range(4):
        gpart[pl.ds(6, 1), pl.ds(part * block, head_dim)] = gain_q
        gpart[pl.ds(6, 1), pl.ds(part * block + head_dim, head_dim)] = gain_k * jnp.where(
            is_key, 0.5, 0.0
        )
    kv_p[...] = d_kind_raw.astype(BF)
    pair_cols = pl.ds(pl.multiple_of(col % 2 * key_width, key_width), key_width)

    def back_heads(target, first):
        rows = pl.ds(first, 4 * own_tokens)

        def step(index, carry):
            cols = pl.ds(pl.multiple_of(index * block, block), block)
            value = mm_nt(d_o[rows], vq[cols]) + mm_nt(kv_p[rows, pair_cols], vkv[cols, pair_cols])
            target[:, cols] = value.astype(target.dtype)
            return carry

        lax.fori_loop(0, width // block, step, 0)

    scatter_x = Scatter(place, own_tokens, (give, keep, got, sent, left, right), sems(3))
    back_heads(give, away)
    scatter_x.start()
    back_heads(keep, home)
    put_q = RowScatter(place, by_rows(vq, block)[1], came_q, row_sems.at[4])
    put_kv = RowScatter(place, by_rows(pkv, block)[1], came_kv, row_sems.at[5])

    def query_grad():
        load_x.wait()

        def step(index, carry):
            rows = pl.ds(pl.multiple_of(index * tile, tile), tile)
            vq[rows] = mm_tn(dffg[:, rows], d_o[...]).astype(BF)
            pkv[rows] = mm_tn(dffg[:, rows], kv_p[:, pair_cols]).astype(BF)
            return carry

        lax.fori_loop(0, width // tile, step, 0)
        put_q.start()
        put_kv.start()

    def deliver(lane, source, target):
        local = pltpu.make_async_copy(source, target, done_sems.at[lane])
        over = remote(
            source, target, done_sems.at[8 + lane], done_sems.at[16 + lane], (1 - core, row, col)
        )
        local.start()
        over.start()
        done.append((local, over))

    core_ff = pl.ds(pl.multiple_of(core * ff_part, ff_part), ff_part)
    core_head = pl.ds(pl.multiple_of(core * head_dim, head_dim), head_dim)
    sib_ff = pl.ds(pl.multiple_of((1 - core) * ff_part, ff_part), ff_part)
    sib_head = pl.ds(pl.multiple_of((1 - core) * head_dim, head_dim), head_dim)
    row_block = pl.ds(pl.multiple_of(row * block, block), block)
    done = []

    quarter = block // 4

    def small_quarter(mask):
        return remote(
            small_keep.at[
                :, pl.ds(pl.multiple_of(row * block + (col ^ mask) * quarter, quarter), quarter)
            ],
            small_z.at[mask],
            misc_send.at[11 + mask],
            misc_recv.at[11 + mask],
            (core, row, col ^ mask),
        )

    def gate_finish():
        put_g.fetch(4, 5)
        put_g.finish()
        deliver(1, vg.at[row_block], ggate.at[:, core_ff])
        put_u.fetch(0, 2)
        put_u.early()

    d_half_here = d_three_ref
    scatter_x.run(h_two_ref, [query_grad, gate_finish])
    d_xn = own_sum[...] + h_two_ref[...]
    x_normed, x_factor = rms(x_own[...].astype(F32))
    d_in, gain_zero = rms_back(d_xn, x_normed, x_factor, gain(0))
    gpart[pl.ds(0, 1)] = gain_zero
    for mask in (1, 2, 3):
        hand_back(low_ref, y_out, mask, 0).wait_send()
    low_ref[...] = (d_half_here[...] + d_in).astype(BF)
    for mask in (1, 2, 3):
        hand_back(low_ref, x_grad, mask, 4).start()
    x_grad[row] = low_ref[:, my_cols]

    gpart[pl.ds(8, 8)] = jnp.full((8, width), jnp.max(top[...]), F32)

    def gain_row(mask):
        return remote(
            gpart.at[:, pl.ds(pl.multiple_of((row ^ mask) * block, block), block)],
            gcame.at[mask],
            gain_send.at[mask],
            gain_recv.at[mask],
            (core, row ^ mask, col),
        )

    for mask in (1, 2, 3):
        gain_row(mask).start()
    gcame[0] = gpart[:, my_cols]
    for put in (put_s, put_o, put_q, put_kv):
        put.fetch(1, 3)
        put.middle()
    for mask in (1, 2, 3):
        gain_row(mask).wait_recv()
    summed = gcame[0] + gcame[1] + gcame[2] + gcame[3]
    largest = jnp.maximum(jnp.maximum(gcame[0], gcame[1]), jnp.maximum(gcame[2], gcame[3]))
    gpart2[pl.ds(0, 8)] = summed[:8]
    gpart2[pl.ds(8, 8)] = largest[8:]
    me = core * 4 + col
    members = [(other, mask) for other in (0, 1) for mask in range(4) if other or mask]

    def gain_group(other, mask):
        lane = 4 + other * 4 + mask
        return remote(
            gpart2,
            gcame2.at[me],
            gain_send.at[lane],
            gain_recv.at[lane],
            (core ^ other, row, col ^ mask),
        )

    for other, mask in members:
        gain_group(other, mask).start()
    gcame2[me] = gpart2[...]
    put_s.fetch(0, 2, 4, 5)
    put_s.early()
    put_s.finish()
    for mask in (1, 2, 3):
        small_quarter(mask).start()
    put_u.fetch(4, 5)
    put_u.finish()
    deliver(2, vu.at[row_block], gup.at[:, core_ff])

    def small_share(other, mask):
        lane = 16 + other * 4 + mask
        return remote(
            kv_x.at[pl.ds(0, small_keep.shape[0]), pl.ds(0, quarter)],
            small_a.at[core, col],
            misc_send.at[lane],
            misc_recv.at[lane],
            (core ^ other, row, col ^ mask),
        )

    for mask in (1, 2, 3):
        small_quarter(mask).wait_recv()
    small_total = small_keep[
        :, pl.ds(pl.multiple_of(row * block + col * quarter, quarter), quarter)
    ].astype(F32)
    for mask in (1, 2, 3):
        small_total = small_total + small_z[mask].astype(F32)
    over_x.wait_send()
    kv_x[pl.ds(0, small_keep.shape[0]), pl.ds(0, quarter)] = small_total.astype(BF)
    for other, mask in members:
        small_share(other, mask).start()
    small_a[core, col] = small_total.astype(BF)
    for put, lane, source, target in (
        (put_o, 4, vo.at[:, row_block], gout.at[core_head]),
        (put_kv, 3, pkv.at[row_block], gkv.at[core]),
        (put_q, 5, vq.at[row_block], gq.at[:, core_head]),
    ):
        put.fetch(0, 2, 4, 5)
        put.early()
        put.finish()
        deliver(lane, source, target)

    for other, mask in members:
        who = (core ^ other) * 4 + (col ^ mask)
        lane = 4 + other * 4 + mask
        remote(
            gpart2, gcame2.at[who], gain_send.at[lane], gain_recv.at[lane], (core, row, col)
        ).wait_recv()
    total = gcame2[0]
    for who in range(1, 8):
        total = total + gcame2[who]
    g_gain[...] = total[:8]
    for who in range(8):
        head = 2 * (who % 4) + who // 4
        tops[pl.ds(head, 1)] = gcame2[who, pl.ds(8, 1), pl.ds(0, 128)]

    gather_a.drain()
    scatter_x.drain()
    for other, mask in members:
        part = small_a.at[core ^ other, col ^ mask]
        lane = 16 + other * 4 + mask
        remote(part, part, misc_send.at[lane], misc_recv.at[lane], (core, row, col)).wait_recv()
        small_share(other, mask).wait_send()
        gain_group(other, mask).wait_send()
    for mask in (1, 2, 3):
        came_back(y_out, mask, 0).wait_recv()
        came_back(x_grad, mask, 4).wait_recv()
        hand_back(low_ref, x_grad, mask, 4).wait_send()
        gain_row(mask).wait_send()
        small_quarter(mask).wait_send()
    small_swap.wait_send()
    for put in (put_g, put_u, put_o, put_q, put_kv, put_s):
        put.drain()
    for mask in (1, 2):
        turned_over(mask).wait_send()
        for part in range(2):
            turned_on(part, mask).wait_send()
    for mask in (1, 2, 3):
        ff_share(mask, core).wait_send()
    for index in range(ff_part // tile):
        slot, rows, local, over = down_tile(index)
        if index >= 2:
            local.wait()
            over.wait_send()
        target = gdown.at[pl.ds(pl.multiple_of((1 - core) * ff_part + index * tile, tile), tile)]
        remote(
            target, target, down_sems.at[4 + index], down_sems.at[8 + index], (core, row, col)
        ).wait_recv()
    theirs_at = {
        1: ggate.at[:, sib_ff],
        2: gup.at[:, sib_ff],
        3: gkv.at[1 - core],
        4: gout.at[sib_head],
        5: gq.at[:, sib_head],
    }
    for lane, (local, over) in zip((1, 2, 4, 3, 5), done):
        local.wait()
        over.wait_send()
        target = theirs_at[lane]
        remote(
            target, target, done_sems.at[8 + lane], done_sems.at[16 + lane], (core, row, col)
        ).wait_recv()


def run_backward(small_args, big_args):
    x_own, per_in, head_gains = small_args[0], small_args[2], small_args[4]
    own, width = x_own.shape
    block = width // 4
    gate = big_args[2]
    tokens, ff_part = gate.shape
    head_dim = head_gains.shape[1]
    rank = small_args[6].shape[1]
    small_rows = small_args[18].shape[1] + small_args[20].shape[0]
    vm = pl.BlockSpec(memory_space=pltpu.VMEM)
    hbm = pl.BlockSpec(memory_space=pl.ANY)
    shape = jax.ShapeDtypeStruct
    vmem = pltpu.VMEM
    dma = pltpu.SemaphoreType.DMA
    outs = [
        shape((4, own, block), BF),
        shape((4, own, block), BF),
        shape((8, block), F32),
        shape((8, 128), F32),
        shape((2, 4, small_rows, block // 4), BF),
        shape((block, 2 * head_dim), BF),
        shape((2, block, head_dim // 2), BF),
        shape((2 * head_dim, block), BF),
        shape((block, 2 * ff_part), BF),
        shape((block, 2 * ff_part), BF),
        shape((2 * ff_part, block), BF),
        shape((6, block // 2, ff_part), BF),
        shape((6, block // 2, ff_part), BF),
        shape((ff_part, tokens), BF),
        shape((2, ff_part // 2, tokens), BF),
    ]
    scratch = [
        vmem((width, head_dim), BF),
        vmem((width, head_dim), BF),
        vmem((head_dim, width), BF),
        vmem((width, ff_part), BF),
        vmem((width, ff_part), BF),
        vmem((ff_part, width), BF),
        vmem((tokens, width), BF),
        vmem((tokens, ff_part), BF),
        vmem((tokens, ff_part), BF),
        vmem((4 * tokens, block), BF),
        vmem((2, 256, block), BF),
        vmem((tokens, width), BF),
        vmem((tokens, width), BF),
        vmem((tokens, ff_part), BF),
        vmem((tokens, ff_part), BF),
        vmem((4 * own, width), BF),
        vmem((4 * own, width), F32),
        vmem((4 * own, width), BF),
        vmem((4, own, width), BF),
        vmem((3, own, width), BF),
        vmem((3, own, width), BF),
        vmem((own, width), F32),
        vmem((own, width), F32),
        vmem((own, width), F32),
        vmem((own, width), BF),
        vmem((16, width), F32),
        vmem((4, 16, block), F32),
        vmem((16, block), F32),
        vmem((8, 16, block), F32),
        vmem((small_rows, width), BF),
        vmem((small_rows, width), BF),
        vmem((small_rows, width), BF),
        vmem((6, small_rows // 2, block), BF),
        vmem((4, small_rows, block // 4), BF),
        vmem((tokens, head_dim), BF),
        vmem((2, 2 * tokens, head_dim), F32),
        vmem((2 * tokens, head_dim), BF),
        vmem((2 * tokens, head_dim), BF),
        vmem((tokens, head_dim), BF),
        vmem((tokens, head_dim), BF),
        vmem((width, head_dim // 2), BF),
        vmem((6, block // 2, head_dim), BF),
        vmem((6, block // 2, head_dim // 2), BF),
        vmem((6, head_dim // 2, block), BF),
        vmem((2, block // 2, ff_part), BF),
        dma((2,)),
        dma((11,)),
        dma((7, 12)),
        dma((4, 8 * PIECES)),
        dma((4, 8 * PIECES)),
        dma((4, 4 * PIECES)),
        dma((4, 4 * PIECES)),
        dma((24,)),
        dma((24,)),
        dma((12,)),
        dma((12,)),
        dma((24,)),
        dma((16,)),
        dma((12,)),
        dma((6,)),
    ]
    return pl.pallas_call(
        backward_kernel,
        out_shape=outs,
        in_specs=[vm] * 21 + [hbm] * 11,
        out_specs=[vm] * 5 + [hbm] * 10,
        scratch_shapes=scratch,
        compiler_params=pltpu.CompilerParams(
            collective_id=1, has_side_effects=True, vmem_limit_bytes=VMEM_BYTES
        ),
        cost_estimate=pl.CostEstimate(
            flops=4 * 10**10, bytes_accessed=10**8, transcendentals=2 * 10**6
        ),
    )(*small_args, *big_args)


def finish_kernel(
    y_in,
    x_in,
    gains,
    tops,
    small,
    gq,
    gkv,
    gout,
    ggate,
    gup,
    gdown,
    head_gains,
    y_out,
    x_out,
    o_query,
    o_key,
    o_value,
    o_out,
    o_gate,
    o_up,
    o_down,
    o_left,
    o_right,
    o_per_gate,
    o_per_proj,
    o_gains,
    o_head,
    o_clip,
):
    o_query[...] = gq[...].astype(F32)
    o_key[...] = gkv[0].astype(F32)
    o_value[...] = gkv[1].astype(F32)
    o_out[...] = gout[...].astype(F32)
    o_gate[...] = ggate[...].astype(F32)
    o_up[...] = gup[...].astype(F32)
    o_down[...] = gdown[...].astype(F32)
    head_dim = head_gains.shape[1]
    quarter = small.shape[3]
    rank = o_right.shape[0]

    @pl.when(pl.program_id(0) == 0)
    def _():
        own = y_in.shape[1]
        for part in range(4):
            rows = pl.ds(part % 2 * own, own)
            y_out[part // 2, rows] = y_in[part]
            x_out[part // 2, rows] = x_in[part]

    @pl.when(pl.program_id(0) == 1)
    def _():
        for part in range(4):
            cols = pl.ds(part * quarter, quarter)
            first = small[0, part].astype(F32)
            o_right[:, cols] = first[:rank]
            o_per_proj[:, cols] = first[rank:]
            second = small[1, part].astype(F32)
            o_left[:, cols] = second[:rank]
            o_per_gate[cols] = second[rank:].T

    @pl.when(pl.program_id(0) == 2)
    def _():
        o_gains[...] = gains[pl.ds(0, 6)]
        o_head[pl.ds(0, 1)] = gains[pl.ds(6, 1), pl.ds(0, head_dim)]
        o_head[pl.ds(1, 1)] = gains[pl.ds(6, 1), pl.ds(head_dim, head_dim)]
        factor = jnp.sqrt(CLIP_LEVEL / jnp.maximum(tops[...], CLIP_LEVEL))[:, :1]
        o_clip[0] = factor * head_gains[pl.ds(0, 1)]
        o_clip[1] = factor * head_gains[pl.ds(1, 1)]


def run_finish(results, head_gains, rank):
    y_out, x_grad, g_gain, tops, small, gq, gkv, gout, ggate, gup, gdown = results
    steps = 8
    shape = jax.ShapeDtypeStruct

    def whole(array):
        dims = len(array.shape)
        return pl.BlockSpec(array.shape, lambda step: (0,) * dims)

    def rows(array):
        size = (array.shape[0] // steps, array.shape[1])
        return pl.BlockSpec(size, lambda step: (step, 0))

    own, block = y_out.shape[1:]
    key_width = gkv.shape[2]
    proj = small.shape[2] - rank
    tokens_shape = shape((2, 2 * own, block), BF)
    by_rows_out = [
        shape(gq.shape, F32),
        shape(gkv.shape[1:], F32),
        shape(gkv.shape[1:], F32),
        shape(gout.shape, F32),
        shape(ggate.shape, F32),
        shape(gup.shape, F32),
        shape(gdown.shape, F32),
    ]
    whole_out = [
        shape((rank, block), F32),
        shape((rank, block), F32),
        shape((block, proj), F32),
        shape((proj, block), F32),
        shape((6, block), F32),
        shape(head_gains.shape, F32),
        shape((2, tops.shape[0], head_gains.shape[1]), F32),
    ]
    kv_spec = pl.BlockSpec((2, block // steps, key_width), lambda step: (0, step, 0))
    return pl.pallas_call(
        finish_kernel,
        grid=(steps,),
        out_shape=[tokens_shape, tokens_shape] + by_rows_out + whole_out,
        in_specs=[whole(y_out), whole(x_grad), whole(g_gain), whole(tops), whole(small), rows(gq), kv_spec]
        + [rows(array) for array in (gout, ggate, gup, gdown)]
        + [whole(head_gains)],
        out_specs=[whole(tokens_shape)] * 2
        + [rows(array) for array in by_rows_out]
        + [whole(array) for array in whole_out],
        compiler_params=pltpu.CompilerParams(vmem_limit_bytes=VMEM_BYTES),
        cost_estimate=pl.CostEstimate(flops=10**7, bytes_accessed=3 * 10**7, transcendentals=0),
    )(*results, head_gains)


def body_pair(
    layer_in,
    per_layer_in,
    doc_lengths,
    w_query,
    w_key,
    w_value,
    w_out,
    w_gate,
    w_up,
    w_down,
    laurel_left,
    laurel_right,
    per_gate,
    per_proj,
    norm_gains,
    head_gains,
    out_grad,
):
    core, row, col = lax.axis_index("seq"), lax.axis_index("row"), lax.axis_index("col")
    rows, cols, cores = lax.axis_size("row"), lax.axis_size("col"), lax.axis_size("seq")
    seq_count = layer_in.shape[0]
    head_dim = head_gains.shape[1]
    key_width = w_key.shape[1]
    ff_part = w_gate.shape[1] // cores
    chunk = layer_in.shape[1]
    halves = rows // seq_count
    own_tokens = chunk // halves
    group_tokens = own_tokens * cores * cols
    even_col = col % 2 == 0

    lengths = doc_lengths[row // halves]
    count = doc_lengths.shape[1]
    upto = jnp.tril(jnp.ones((count, count), jnp.int32))
    doc_ends = jnp.sum(lengths[None, :] * upto, axis=1)

    def places_of(half):
        token = jnp.arange(group_tokens, dtype=jnp.int32)
        place = token // own_tokens * chunk + half * own_tokens + token % own_tokens
        before = (doc_ends[None, :] <= place[:, None]).astype(jnp.int32)
        start = jnp.sum(before * lengths[None, :], axis=1)
        return place, start

    half = row % halves
    place, start = places_of(half)
    other_place, other_start = places_of(half ^ 1)
    key_place = jnp.stack([place, other_place])[jnp.array([0, 1]) ^ half].reshape(-1)
    allowed = (key_place[None, :] <= place[:, None]) & (key_place[None, :] >= start[:, None])
    cosine_table, sine_table = rotation(place - start, head_dim)

    rank = laurel_left.shape[1]
    saved = run_forward(
        layer_in.reshape(rows, own_tokens, -1),
        out_grad.reshape(rows, own_tokens, -1),
        norm_gains,
        (
            w_query,
            w_key,
            w_value,
            w_out,
            w_gate,
            w_up,
            w_down,
            laurel_left.T,
            laurel_right,
            per_gate,
            per_proj,
        ),
        (
            cosine_table[:, : head_dim // 2],
            sine_table[:, : head_dim // 2],
            start[:, None],
        ),
        head_gains,
    )
    (x_own, g_own, gains, raw_q, raw_kv, q_low, kv, lse, top_tile, o_low, attn_val, lr_low, ff_val) = saved[
        :13
    ]
    laurels, p_gate, p_proj = saved[13:16]
    w_q, w_kv_all, w_o, w_g, w_u, w_d, x_all, f_all, gate_val, up_val, turned = saved[16:]
    half_table = head_dim // 2
    results = run_backward(
        (
            x_own,
            g_own,
            per_layer_in.reshape(rows, own_tokens, -1),
            gains,
            head_gains,
            attn_val,
            lr_low,
            ff_val,
            raw_q,
            raw_kv,
            q_low,
            kv,
            lse,
            top_tile,
            o_low,
            cosine_table[:, :half_table],
            sine_table[:, :half_table],
            start[:, None],
            laurels,
            p_gate,
            p_proj,
        ),
        (x_all, f_all, gate_val, up_val, turned, w_q, w_kv_all, w_o, w_g, w_u, w_d),
    )
    finished = list(run_finish(results[:11], head_gains, rank))
    finished[9] = finished[9].T
    return tuple(finished)


def solution(mesh):
    sizes = tuple(mesh.shape[axis] for axis in ("seq", "row", "col"))
    body = body_pair if sizes == (2, 4, 4) else body_any
    return jax.shard_map(
        body,
        mesh=mesh,
        in_specs=(
            P(None, ("seq", "col"), "row"),
            P(None, ("seq", "col"), None),
            P(),
            P("row", "col"),
            P("row", "col"),
            P("row", "col"),
            P("col", "row"),
            P("row", "col"),
            P("row", "col"),
            P("col", "row"),
            P("row", None),
            P(None, "row"),
            P("row", None),
            P(None, "row"),
            P(None, "row"),
            P(),
            P(None, ("seq", "col"), "row"),
        ),
        out_specs=(
            P(None, ("seq", "col"), "row"),
            P(None, ("seq", "col"), "row"),
            P("row", "col"),
            P("row", "col"),
            P("row", "col"),
            P("col", "row"),
            P("row", "col"),
            P("row", "col"),
            P("col", "row"),
            P("row", None),
            P(None, "row"),
            P("row", None),
            P(None, "row"),
            P(None, "row"),
            P(),
            P(),
        ),
        check_vma=False,
    )
```

```python
import math

import jax
import jax.numpy as jnp
from jax import lax
from jax.experimental import pallas as pl
from jax.experimental.pallas import tpu as pltpu
from jax.sharding import PartitionSpec as P

EPSILON = 1e-06
CLIP_LEVEL = 3.0
ROPE_BASE = 1000000.0
ROOT_HALF = 0.7071067811865476
MASK_FILL = -1e30
MESH = pl.DeviceIdType.MESH
BF = jnp.bfloat16
F32 = jnp.float32
VMEM_BYTES = 63 * 2**20
PIECES = 4


def swapped(value, axis, apart):
    mask = 2**apart
    pairs = [(source, source ^ mask) for source in range(lax.axis_size(axis))]
    return lax.ppermute(value, axis, pairs)


def width_total(values):
    return lax.psum(values, "row")


def gather_tokens(values):
    return lax.all_gather(values, "col", axis=1, tiled=True)


def spread_rows(values, project):
    gathered = gather_tokens(values)
    return (gathered, lax.psum_scatter(project(gathered), "row", scatter_dimension=1, tiled=True))


def spread_cols(values, project):
    gathered = lax.all_gather(values, "row", axis=1, tiled=True)
    return (gathered, lax.psum_scatter(project(gathered), "col", scatter_dimension=1, tiled=True))


def times_right(left_side, right_side):
    return jnp.einsum("std,dn->stn", left_side, right_side, preferred_element_type=jnp.float32)


def times_back(left_side, right_side):
    return jnp.einsum("stn,dn->std", left_side, right_side, preferred_element_type=jnp.float32)


def outer_sum(left_side, right_side):
    return jnp.einsum("std,stn->dn", left_side, right_side, preferred_element_type=jnp.float32)


def norm_forward(values, gain_vec, width_all):
    square_sum = width_total(jnp.sum(values * values, axis=-1, keepdims=True))
    factor = lax.rsqrt(square_sum / width_all + EPSILON)
    normed = values * factor
    return (normed * gain_vec, normed, factor)


def norm_backward(grad_values, normed, factor, gain_vec, width_all):
    grad_normed = grad_values * gain_vec
    inner_sum = width_total(jnp.sum(grad_normed * normed, axis=-1, keepdims=True))
    result = factor * (grad_normed - normed * (inner_sum / width_all))
    return (result, jnp.sum(grad_values * normed, axis=(0, 1)))


def head_norm(values, gain_vec):
    return (
        values * lax.rsqrt(jnp.mean(values * values, axis=-1, keepdims=True) + EPSILON) * gain_vec
    )


def rotation(position, width_all):
    half_width = width_all // 2
    frequency = ROPE_BASE ** (-2.0 * jnp.arange(half_width, dtype=jnp.float32) / width_all)
    angles = position.astype(jnp.float32)[..., None] * frequency
    cosine_table = jnp.concatenate([jnp.cos(angles), jnp.cos(angles)], axis=-1)
    sine_table = jnp.concatenate([jnp.sin(angles), jnp.sin(angles)], axis=-1)
    return (cosine_table, sine_table)


def rotate(values, cosine_table, sine_table):
    half_width = values.shape[-1] // 2
    turned = jnp.concatenate([-values[..., half_width:], values[..., :half_width]], axis=-1)
    return values * cosine_table + turned * sine_table


def doc_places(doc_lengths, first_place, place_count):
    upto = jnp.tril(jnp.ones((doc_lengths.shape[1], doc_lengths.shape[1]), jnp.int32))
    doc_ends = jnp.sum(doc_lengths[:, None, :] * upto[None], axis=2)
    places = first_place + jnp.arange(place_count, dtype=jnp.int32)
    before = (doc_ends[:, None, :] <= places[None, :, None]).astype(jnp.int32)
    segment = jnp.sum(before, axis=2)
    doc_start = jnp.sum(before * doc_lengths[:, None, :], axis=2)
    return (segment, places, places[None, :] - doc_start)


def block_scores(queries, keys_all, block_start, block_size, query_seg, query_place, key_seg):
    keys_part = lax.dynamic_slice_in_dim(keys_all, block_start, block_size, 1)
    scores = jnp.einsum("sqhd,skd->shqk", queries, keys_part, preferred_element_type=jnp.float32)
    seg_part = lax.dynamic_slice_in_dim(key_seg, block_start, block_size, 1)
    key_place = block_start + jnp.arange(block_size, dtype=jnp.int32)
    allowed = (query_seg[:, None, :, None] == seg_part[:, None, None, :]) & (
        key_place[None, None, None, :] <= query_place[None, None, :, None]
    )
    return (scores, allowed)


def body_any(
    layer_in,
    per_layer_in,
    doc_lengths,
    w_query,
    w_key,
    w_value,
    w_out,
    w_gate,
    w_up,
    w_down,
    laurel_left,
    laurel_right,
    per_gate,
    per_proj,
    norm_gains,
    head_gains,
    out_grad,
):
    seq_count = layer_in.shape[0]
    width_all = layer_in.shape[2] * lax.axis_size("row")
    head_dim = head_gains.shape[1]
    heads_here = w_query.shape[1] // head_dim
    heads_all = heads_here * lax.axis_size("col")
    key_width = w_key.shape[1]
    ff_here = w_gate.shape[1]
    local_len = layer_in.shape[1] * lax.axis_size("col")
    tokens_row = local_len // lax.axis_size("row")
    seq_len = local_len * lax.axis_size("seq")
    col_index = lax.axis_index("col")
    even_col = col_index % 2 == 0
    q_width = heads_here * head_dim
    partner_key, partner_value = swapped((w_key, w_value), "col", 0)
    key_head = jnp.where(
        even_col,
        jnp.concatenate([w_key, partner_key], axis=1),
        jnp.concatenate([partner_key, w_key], axis=1),
    )
    value_head = jnp.where(
        even_col,
        jnp.concatenate([w_value, partner_value], axis=1),
        jnp.concatenate([partner_value, w_value], axis=1),
    )
    w_heads = jnp.concatenate([w_query, key_head, value_head], axis=1)
    w_back = jnp.concatenate([w_query, w_key, w_value], axis=1)
    w_gate_up = jnp.concatenate([w_gate, w_up], axis=1)
    inputs = layer_in.astype(jnp.float32)
    x_norm, x_normed, x_factor = norm_forward(inputs, norm_gains[0], width_all)
    x_low = x_norm.astype(jnp.bfloat16)
    x_rows, head_raw = spread_rows(x_low, lambda gathered: times_right(gathered, w_heads))
    q_raw = head_raw[:, :, :q_width].reshape(seq_count, tokens_row, heads_here, head_dim)
    k_raw = head_raw[:, :, q_width : q_width + head_dim]
    v_raw = head_raw[:, :, q_width + head_dim :]
    query_seg, query_place, query_pos = doc_places(
        doc_lengths, lax.axis_index(("seq", "row")) * tokens_row, tokens_row
    )
    key_seg, unused_place, unused_pos = doc_places(doc_lengths, 0, seq_len)
    cosine_table, sine_table = rotation(query_pos, head_dim)

    def query_prep(raw_part, gain_vec):
        return rotate(
            head_norm(raw_part, gain_vec), cosine_table[:, :, None], sine_table[:, :, None]
        )

    def key_prep(raw_part, gain_vec):
        return rotate(head_norm(raw_part, gain_vec), cosine_table, sine_table)

    def value_prep(raw_part):
        return head_norm(raw_part, 1.0)

    q_rot, query_back = jax.vjp(query_prep, q_raw, head_gains[0])
    k_rot, key_back = jax.vjp(key_prep, k_raw, head_gains[1])
    v_normed, value_back = jax.vjp(value_prep, v_raw)
    q_low = q_rot.astype(jnp.bfloat16)
    keys_all, values_all = (
        lax.all_gather(k_rot.astype(jnp.bfloat16), ("seq", "row"), axis=1, tiled=True),
        lax.all_gather(v_normed.astype(jnp.bfloat16), ("seq", "row"), axis=1, tiled=True),
    )
    block_size = min(512, seq_len)
    block_count = seq_len // block_size
    blocks = jnp.arange(block_count, dtype=jnp.int32)

    def scored(block_index):
        return block_scores(
            q_low, keys_all, block_index * block_size, block_size, query_seg, query_place, key_seg
        )

    def values_at(block_index):
        return lax.dynamic_slice_in_dim(values_all, block_index * block_size, block_size, 1)

    def stats_step(carry, block_index):
        row_top, row_total = carry
        scores, allowed = scored(block_index)
        new_top = jnp.maximum(row_top, jnp.max(jnp.where(allowed, scores, MASK_FILL), axis=3))
        weights = jnp.where(allowed, jnp.exp(scores - new_top[..., None]), 0.0)
        row_total = row_total * jnp.exp(row_top - new_top) + jnp.sum(weights, axis=3)
        return ((new_top, row_total), None)

    start_top = jnp.full((seq_count, heads_here, tokens_row), MASK_FILL, jnp.float32)
    (row_top, row_total), unused = lax.scan(
        stats_step, (start_top, jnp.zeros_like(start_top)), blocks
    )
    log_total = row_top + jnp.log(row_total)

    def probs_at(block_index):
        scores, allowed = scored(block_index)
        return jnp.where(allowed, jnp.exp(scores - log_total[..., None]), 0.0)

    def out_step(total_out, block_index):
        probs_low = probs_at(block_index).astype(jnp.bfloat16)
        total_out = total_out + jnp.einsum(
            "shqk,skd->sqhd", probs_low, values_at(block_index), preferred_element_type=jnp.float32
        )
        return (total_out, None)

    attended, unused = lax.scan(
        out_step, jnp.zeros((seq_count, tokens_row, heads_here, head_dim), jnp.float32), blocks
    )
    o_low = attended.astype(jnp.bfloat16).reshape(seq_count, tokens_row, q_width)
    head_slots = lax.dynamic_update_slice_in_dim(
        jnp.full((heads_all,), MASK_FILL, jnp.float32),
        jnp.max(row_top, axis=(0, 2)),
        col_index * heads_here,
        0,
    )
    logit_top = lax.pmax(head_slots, ("seq", "row", "col"))
    o_rows, attn_val = spread_cols(o_low, lambda gathered: times_right(gathered, w_out))
    attn_norm, attn_normed, attn_factor = norm_forward(attn_val, norm_gains[1], width_all)
    h_one = inputs + attn_norm
    lr_low = width_total(times_right(x_low, laurel_left)).astype(jnp.bfloat16)
    lo_val = times_right(lr_low, laurel_right)
    lo_norm, lo_normed, lo_factor = norm_forward(lo_val, norm_gains[2], width_all)
    h_two = (h_one + (x_norm + lo_norm)) * ROOT_HALF
    f_norm, f_normed, f_factor = norm_forward(h_two, norm_gains[3], width_all)
    f_low = f_norm.astype(jnp.bfloat16)
    f_rows, gate_up = spread_rows(f_low, lambda gathered: times_right(gathered, w_gate_up))
    gate_val = gate_up[:, :, :ff_here]
    up_val = gate_up[:, :, ff_here:]

    def geglu(gate_part, up_part):
        return jax.nn.gelu(gate_part, approximate=True) * up_part

    hidden, geglu_back = jax.vjp(geglu, gate_val, up_val)
    hid_low = hidden.astype(jnp.bfloat16)
    hid_rows, ff_val = spread_cols(hid_low, lambda gathered: times_right(gathered, w_down))
    ff_norm, ff_normed, ff_factor = norm_forward(ff_val, norm_gains[4], width_all)
    h_three = h_two + ff_norm
    h_low = h_three.astype(jnp.bfloat16)
    pg_val = width_total(times_right(h_low, per_gate))
    per_input = per_layer_in.astype(jnp.float32)

    def per_mix(gate_part):
        return jax.nn.gelu(gate_part, approximate=True) * per_input

    gp_val, per_back = jax.vjp(per_mix, pg_val)
    gp_low = gp_val.astype(jnp.bfloat16)
    pp_val = times_right(gp_low, per_proj)
    pp_norm, pp_normed, pp_factor = norm_forward(pp_val, norm_gains[5], width_all)
    layer_out = (h_three + pp_norm).astype(jnp.bfloat16)
    grad_top = out_grad.astype(jnp.float32)
    d_pp, gain_five = norm_backward(grad_top, pp_normed, pp_factor, norm_gains[5], width_all)
    d_pp_low = d_pp.astype(jnp.bfloat16)
    grad_per_proj = outer_sum(gp_low, d_pp_low)
    (d_pg,) = per_back(width_total(times_back(d_pp_low, per_proj)))
    d_pg_low = d_pg.astype(jnp.bfloat16)
    grad_per_gate = outer_sum(h_low, d_pg_low)
    d_three = grad_top + times_back(d_pg_low, per_gate)
    d_ff, gain_four = norm_backward(d_three, ff_normed, ff_factor, norm_gains[4], width_all)
    d_ff_low = d_ff.astype(jnp.bfloat16)
    dff_rows, d_hidden = spread_rows(d_ff_low, lambda gathered: times_back(gathered, w_down))
    grad_down = outer_sum(hid_rows, dff_rows)
    d_gate, d_up = geglu_back(d_hidden)
    d_gate_up = jnp.concatenate([d_gate, d_up], axis=2).astype(jnp.bfloat16)
    dgu_rows, d_f_low = spread_cols(d_gate_up, lambda gathered: times_back(gathered, w_gate_up))
    grad_gate_up = outer_sum(f_rows, dgu_rows)
    d_f, gain_three = norm_backward(d_f_low, f_normed, f_factor, norm_gains[3], width_all)
    d_half = (d_three + d_f) * ROOT_HALF
    d_lo, gain_two = norm_backward(d_half, lo_normed, lo_factor, norm_gains[2], width_all)
    d_lo_low = d_lo.astype(jnp.bfloat16)
    grad_laurel_right = outer_sum(lr_low, d_lo_low)
    d_lr_low = width_total(times_back(d_lo_low, laurel_right)).astype(jnp.bfloat16)
    grad_laurel_left = outer_sum(x_low, d_lr_low)
    d_attn, gain_one = norm_backward(d_half, attn_normed, attn_factor, norm_gains[1], width_all)
    d_attn_low = d_attn.astype(jnp.bfloat16)
    dattn_rows, d_o = spread_rows(d_attn_low, lambda gathered: times_back(gathered, w_out))
    grad_w_out = outer_sum(o_rows, dattn_rows)
    d_o_low = d_o.astype(jnp.bfloat16).reshape(seq_count, tokens_row, heads_here, head_dim)

    def delta_step(total_delta, block_index):
        d_probs = jnp.einsum(
            "sqhd,skd->shqk", d_o_low, values_at(block_index), preferred_element_type=jnp.float32
        )
        return (total_delta + jnp.sum(probs_at(block_index) * d_probs, axis=3), None)

    row_delta, unused = lax.scan(delta_step, jnp.zeros_like(log_total), blocks)

    def grad_step(carry, block_index):
        d_query, d_keys, d_values = carry
        block_start = block_index * block_size
        prob_vals = probs_at(block_index)
        d_probs = jnp.einsum(
            "sqhd,skd->shqk", d_o_low, values_at(block_index), preferred_element_type=jnp.float32
        )
        d_scores = (prob_vals * (d_probs - row_delta[..., None])).astype(jnp.bfloat16)
        keys_part = lax.dynamic_slice_in_dim(keys_all, block_start, block_size, 1)
        d_query = d_query + jnp.einsum(
            "shqk,skd->sqhd", d_scores, keys_part, preferred_element_type=jnp.float32
        )
        key_part = jnp.einsum("shqk,sqhd->skd", d_scores, q_low, preferred_element_type=jnp.float32)
        value_part = jnp.einsum(
            "shqk,sqhd->skd",
            prob_vals.astype(jnp.bfloat16),
            d_o_low,
            preferred_element_type=jnp.float32,
        )
        d_keys = lax.dynamic_update_slice_in_dim(d_keys, key_part, block_start, 1)
        d_values = lax.dynamic_update_slice_in_dim(d_values, value_part, block_start, 1)
        return ((d_query, d_keys, d_values), None)

    zero_keys = jnp.zeros((seq_count, seq_len, head_dim), jnp.float32)
    (d_query, d_keys, d_values), unused = lax.scan(
        grad_step, (jnp.zeros_like(attended), zero_keys, zero_keys), blocks
    )
    own_keys, own_values = (
        lax.psum_scatter(d_keys, ("seq", "row"), scatter_dimension=1, tiled=True),
        lax.psum_scatter(d_values, ("seq", "row"), scatter_dimension=1, tiled=True),
    )
    pair_keys, pair_values = swapped((own_keys, own_values), "col", 0)
    d_q_raw, d_q_gain = query_back(d_query)
    d_k_raw, d_k_gain = key_back(own_keys + pair_keys)
    (d_v_raw,) = value_back(own_values + pair_values)
    key_offset = col_index % 2 * key_width
    d_heads_low = jnp.concatenate(
        [
            d_q_raw.reshape(seq_count, tokens_row, q_width),
            lax.dynamic_slice_in_dim(d_k_raw, key_offset, key_width, 2),
            lax.dynamic_slice_in_dim(d_v_raw, key_offset, key_width, 2),
        ],
        axis=2,
    ).astype(jnp.bfloat16)
    dhead_rows, d_x_heads = spread_cols(d_heads_low, lambda gathered: times_back(gathered, w_back))
    grad_heads = outer_sum(x_rows, dhead_rows)
    d_x_low = d_x_heads + times_back(d_lr_low, laurel_left)
    d_x_part, gain_zero = norm_backward(
        d_half + d_x_low, x_normed, x_factor, norm_gains[0], width_all
    )
    grad_in = (d_half + d_x_part).astype(jnp.bfloat16)
    head_part = width_total(jnp.stack([d_q_gain, d_k_gain * 0.5]))
    sum_heads, sum_out, sum_gate_up, sum_down = lax.psum(
        (grad_heads, grad_w_out, grad_gate_up, grad_down), "seq"
    )
    sum_left, sum_right, sum_per_gate, sum_per_proj, sum_gains, sum_head_gains = lax.psum(
        (
            grad_laurel_left,
            grad_laurel_right,
            grad_per_gate,
            grad_per_proj,
            jnp.stack([gain_zero, gain_one, gain_two, gain_three, gain_four, gain_five]),
            head_part,
        ),
        ("seq", "col"),
    )
    clip_factor = jnp.sqrt(CLIP_LEVEL / jnp.maximum(logit_top, CLIP_LEVEL))
    clipped_gains = jnp.stack(
        [
            clip_factor[:, None] * head_gains[0][None, :],
            clip_factor[:, None] * head_gains[1][None, :],
        ]
    )
    return (
        layer_out,
        grad_in,
        sum_heads[:, :q_width],
        sum_heads[:, q_width : q_width + key_width],
        sum_heads[:, q_width + key_width :],
        sum_out,
        sum_gate_up[:, :ff_here],
        sum_gate_up[:, ff_here:],
        sum_down,
        sum_left,
        sum_right,
        sum_per_gate,
        sum_per_proj,
        sum_gains,
        sum_head_gains,
        clipped_gains,
    )


def group_gather(values):
    return lax.all_gather(values, ("seq", "col"), axis=0, tiled=True)


def group_scatter(partial):
    return lax.psum_scatter(
        partial.astype(jnp.bfloat16), ("seq", "col"), scatter_dimension=0, tiled=True
    ).astype(jnp.float32)


def to_owner(values):
    seq_count, tokens, width = values.shape
    rows = lax.axis_size("row")
    parts = values.reshape(rows, seq_count * tokens // rows, width)
    moved = lax.all_to_all(parts, "row", split_axis=0, concat_axis=0)
    return moved.transpose(1, 0, 2).reshape(parts.shape[1], rows * width)


def from_owner(values, seq_count):
    tokens, width = values.shape
    rows = lax.axis_size("row")
    parts = values.reshape(tokens, rows, width // rows).transpose(1, 0, 2)
    moved = lax.all_to_all(parts, "row", split_axis=0, concat_axis=0)
    return moved.reshape(seq_count, rows * tokens // seq_count, width // rows)


def mm(left_side, right_side):
    return jnp.dot(left_side, right_side, preferred_element_type=jnp.float32)


def mm_nt(left_side, right_side):
    return lax.dot_general(
        left_side, right_side, (((1,), (1,)), ((), ())), preferred_element_type=jnp.float32
    )


def mm_tn(left_side, right_side):
    return lax.dot_general(
        left_side, right_side, (((0,), (0,)), ((), ())), preferred_element_type=jnp.float32
    )


def rms(values):
    factor = lax.rsqrt(jnp.mean(values * values, axis=-1, keepdims=True) + EPSILON)
    return values * factor, factor


def rms_back(grad_values, normed, factor, gain_vec):
    grad_normed = grad_values * gain_vec
    inner = jnp.mean(grad_normed * normed, axis=-1, keepdims=True)
    return (
        factor * (grad_normed - normed * inner),
        jnp.sum(grad_values * normed, axis=0, keepdims=True),
    )


def gather_rows(values, axis):
    return lax.all_gather(values, "row", axis=axis, tiled=True)


def scatter_rows(values, axis):
    return lax.psum_scatter(
        values.astype(jnp.bfloat16), "row", scatter_dimension=axis, tiled=True
    ).astype(jnp.float32)


def both_cores(values, axis):
    return lax.all_gather(values, "seq", axis=axis, tiled=True)


def remote(src, dst, send_sem, recv_sem, device):
    return pltpu.make_async_remote_copy(
        src_ref=src,
        dst_ref=dst,
        send_sem=send_sem,
        recv_sem=recv_sem,
        device_id=device,
        device_id_type=MESH,
    )


def greet(core, row, col):
    barrier = pltpu.get_barrier_semaphore()
    near = [(core, row ^ 1, col), (core, row ^ 2, col), (core, row ^ 3, col), (1 - core, row, col)]
    for device in near:
        pl.semaphore_signal(barrier, inc=1, device_id=device, device_id_type=MESH)

    @pl.when(col > 0)
    def _():
        pl.semaphore_signal(barrier, inc=1, device_id=(core, row, col - 1), device_id_type=MESH)

    @pl.when(col < 3)
    def _():
        pl.semaphore_signal(barrier, inc=1, device_id=(core, row, col + 1), device_id_type=MESH)

    ends = jnp.where((col == 0) | (col == 3), 1, 2)
    pl.semaphore_wait(barrier, 4 + ends)


class Gather:
    def __init__(self, place, buf, rows, sems):
        self.core, self.row, self.col = place
        self.buf, self.rows = buf, rows
        self.send_z, self.recv_z, self.send_s, self.recv_s = sems

    def part(self, core, col, piece):
        rows = self.rows // PIECES
        first = (core * 4 + col) * self.rows + piece * rows
        return self.buf.at[pl.ds(pl.multiple_of(first, rows), rows)]

    def hop(self, dist, right, piece):
        part = self.part(self.core, self.col - dist if right else self.col + dist, piece)
        lane = ((0 if right else 3) + dist) * PIECES + piece
        return remote(
            part,
            part,
            self.send_z.at[lane],
            self.recv_z.at[lane],
            (self.core, self.row, self.col + (1 if right else -1)),
        )

    def came(self, dist, right, piece):
        part = self.part(self.core, self.col - dist if right else self.col + dist, piece)
        lane = ((0 if right else 3) + dist - 1) * PIECES + piece
        return remote(
            part, part, self.send_z.at[lane], self.recv_z.at[lane], (self.core, self.row, self.col)
        )

    def to_sibling(self, col, piece, core=None):
        part = self.part(self.core if core is None else core, col, piece)
        lane = col * PIECES + piece
        return remote(
            part,
            part,
            self.send_s.at[lane],
            self.recv_s.at[lane],
            (1 - self.core, self.row, self.col),
        )

    def start(self):
        col = self.col
        for piece in range(PIECES):

            @pl.when(col < 3)
            def _():
                self.hop(0, True, piece).start()

            @pl.when(col > 0)
            def _():
                self.hop(0, False, piece).start()

        for piece in range(PIECES):
            self.to_sibling(col, piece).start()

    def forward(self, work=()):
        col = self.col
        work = list(work)
        for dist in (1, 2, 3):
            for piece in range(PIECES):

                @pl.when(col >= dist)
                def _():
                    self.came(dist, True, piece).wait_recv()
                    if dist < 3:

                        @pl.when(col < 3)
                        def _():
                            self.hop(dist, True, piece).start()

                    self.to_sibling(col - dist, piece).start()

                @pl.when(col + dist <= 3)
                def _():
                    self.came(dist, False, piece).wait_recv()
                    if dist < 3:

                        @pl.when(col > 0)
                        def _():
                            self.hop(dist, False, piece).start()

                    self.to_sibling(col + dist, piece).start()

            if work:
                work.pop(0)()

    def finish(self):
        for piece in range(PIECES):
            for col in range(4):
                self.to_sibling(col, piece, 1 - self.core).wait_recv()

    def drain(self):
        for piece in range(PIECES):
            for col in range(4):
                self.to_sibling(col, piece).wait_send()
            for dist in (0, 1, 2):

                @pl.when((self.col < 3) & (self.col >= dist))
                def _():
                    self.hop(dist, True, piece).wait_send()

                @pl.when((self.col > 0) & (self.col + dist <= 3))
                def _():
                    self.hop(dist, False, piece).wait_send()


class Scatter:
    def __init__(self, place, rows, bufs, sems):
        self.core, self.row, self.col = place
        self.rows = rows
        self.give, self.keep, self.got, self.sent, self.left, self.right = bufs
        self.send_z, self.recv_z, self.send_s, self.recv_s = sems

    def sibling(self, dest):
        rows = pl.ds(dest * self.rows, self.rows)
        return remote(
            self.give.at[rows],
            self.got.at[rows],
            self.send_s.at[dest],
            self.recv_s.at[dest],
            (1 - self.core, self.row, self.col),
        )

    def start(self):
        for dest in (3, 0, 2, 1):
            self.sibling(dest).start()

    def piece(self, piece):
        rows = self.rows // PIECES
        return pl.ds(piece * rows, rows)

    def mine(self, dest, piece):
        count = self.rows // PIECES
        rows = pl.ds(dest * self.rows + piece * count, count)
        return self.keep[rows].astype(F32) + self.got[rows].astype(F32)

    def inbox(self, dest, right):
        return self.left.at[dest - 1] if right else self.right.at[dest]

    def hop(self, dest, right, piece):
        lane = ((0 if right else 4) + dest) * PIECES + piece
        return remote(
            self.sent.at[dest, self.piece(piece)],
            self.inbox(dest, right).at[self.piece(piece)],
            self.send_z.at[lane],
            self.recv_z.at[lane],
            (self.core, self.row, self.col + (1 if right else -1)),
        )

    def step(self, col, dest, right, piece):
        rows = self.piece(piece)
        if piece == 0:
            self.sibling(dest).wait_recv()
        total = self.mine(dest, piece)
        if col != (0 if right else 3):
            self.hop(dest, right, piece).wait_recv()
            total = total + self.inbox(dest, right)[rows].astype(F32)
        self.sent[dest, rows] = total.astype(BF)
        self.hop(dest, right, piece).start()

    def steps(self, col):
        if col > 1:
            return [
                [(3 - dest, not right, piece) for dest, right, piece in part]
                for part in self.steps(3 - col)
            ]
        full = lambda dest, right: [(dest, right, piece) for piece in range(PIECES)]
        if col == 0:
            return [full(3, True) + full(2, True), full(1, True)]
        near, far = full(3, True) + full(2, True), full(0, False)
        lag, order = PIECES - 1, []
        for index, item in enumerate(near):
            order.append(item)
            if index + 1 >= lag and far:
                order.append(far.pop(0))
        cut = PIECES + 2
        return [order[:cut], order[cut:] + far]

    def run(self, result, work=()):
        work = list(work)
        for part in range(2):
            for col in range(4):

                @pl.when(self.col == col)
                def _():
                    for dest, right, piece in self.steps(col)[part]:
                        self.step(col, dest, right, piece)

            for call in work[part : part + 1]:
                call()
        for call in work[2:]:
            call()
        for dest in range(4):

            @pl.when(self.col == dest)
            def _():
                self.sibling(dest).wait_recv()
                for piece in range(PIECES):
                    rows = self.piece(piece)
                    total = self.mine(dest, piece)
                    for right in (True, False):
                        if dest != (0 if right else 3):
                            self.hop(dest, right, piece).wait_recv()
                            total = total + self.inbox(dest, right)[rows].astype(F32)
                    result[rows] = total

    def drain(self):
        for dest in range(4):
            self.sibling(dest).wait_send()
        for piece in range(PIECES):
            for dest in (1, 2, 3):

                @pl.when(self.col < dest)
                def _():
                    self.hop(dest, True, piece).wait_send()

                @pl.when(self.col > 3 - dest)
                def _():
                    self.hop(3 - dest, False, piece).wait_send()


class RowGather:
    def __init__(self, place, source, block, halves, sems, ways=(1, 2)):
        self.core, self.row, self.col = place
        self.source, self.block, self.halves = source, block, halves
        self.ways = ways
        self.sems = sems

    def neighbour(self, mask):
        return (self.core, self.row ^ mask, self.col)

    def own(self):
        return pltpu.make_async_copy(self.source, self.block(self.row), self.sems.at[8])

    def first(self, mask, block=None):
        lane = mask - 1
        return remote(
            self.source,
            self.block(self.row) if block is None else block,
            self.sems.at[lane],
            self.sems.at[4 + lane],
            self.neighbour(mask),
        )

    def across(self, index, mask):
        return self.block(index) if len(self.ways) == 1 else self.halves(index)[mask - 1]

    def second(self, mask):
        part = self.across(self.row ^ (3 - mask), mask)
        return remote(
            part, part, self.sems.at[1 + mask], self.sems.at[5 + mask], self.neighbour(mask)
        )

    def start(self):
        self.first(1).start()
        self.first(2).start()
        self.own().start()

    def finish_first(self):
        for mask in (1, 2):
            self.first(mask, self.block(self.row ^ mask)).wait_recv()
            self.first(mask).wait_send()
        self.own().wait()

    def forward(self):
        for mask in (1, 2):
            self.first(mask, self.block(self.row ^ mask)).wait_recv()
            if 3 - mask in self.ways:
                self.second(3 - mask).start()

    def finish(self):
        for mask in self.ways:
            part = self.across(self.row ^ 3, mask)
            remote(
                part, part, self.sems.at[1 + mask], self.sems.at[5 + mask], self.neighbour(mask)
            ).wait_recv()
        self.own().wait()
        for mask in (1, 2):
            self.first(mask).wait_send()
        for mask in self.ways:
            self.second(mask).wait_send()


def by_rows(buf, block_rows):
    half = block_rows // 2

    def block(index):
        return buf.at[pl.ds(pl.multiple_of(index * block_rows, block_rows), block_rows)]

    def halves(index):
        return [
            buf.at[pl.ds(pl.multiple_of(index * block_rows + part * half, half), half)]
            for part in range(2)
        ]

    return block, halves


def by_core_rows(core):
    def split(buf, block_rows):
        own = block_rows // 2

        def piece(index, part, count):
            first = index * block_rows + core * own + part * (own // count)
            return buf.at[pl.ds(pl.multiple_of(first, own // count), own // count)]

        return (
            lambda index: piece(index, 0, 1),
            lambda index: [piece(index, part, 2) for part in range(2)],
        )

    return split


def by_half_cols(part):
    def split(buf, block_cols):
        own, rows = block_cols // 2, buf.shape[0] // 2

        def cols(index):
            return pl.ds(pl.multiple_of(index * block_cols + part * own, own), own)

        return (
            lambda index: buf.at[:, cols(index)],
            lambda index: [buf.at[pl.ds(piece * rows, rows), cols(index)] for piece in range(2)],
        )

    return split


def by_cols(buf, block_cols):
    rows = buf.shape[0] // 2

    def block(index):
        return buf.at[:, pl.ds(pl.multiple_of(index * block_cols, block_cols), block_cols)]

    def halves(index):
        cols = pl.ds(pl.multiple_of(index * block_cols, block_cols), block_cols)
        return [buf.at[pl.ds(part * rows, rows), cols] for part in range(2)]

    return block, halves


def gelu_both(values):
    inner = 0.7978845608028654 * (values + 0.044715 * values * values * values)
    bend = jnp.tanh(inner)
    slope = 0.7978845608028654 * (1.0 + 3.0 * 0.044715 * values * values)
    return 0.5 * values * (1.0 + bend), 0.5 * (1.0 + bend) + 0.5 * values * (1.0 - bend * bend) * slope


def head_parts(raw, gain, cosine, sine):
    factor = lax.rsqrt(jnp.mean(raw * raw, axis=1, keepdims=True) + EPSILON)
    half = raw.shape[1] // 2
    scaled = raw * factor * gain
    first, second = scaled[:, :half], scaled[:, half:]
    return jnp.concatenate([first * cosine - second * sine, second * cosine + first * sine], axis=1)


def forward_kernel(
    x_in,
    g_in,
    gains_in,
    w_query,
    w_key,
    w_value,
    w_out,
    w_gate,
    w_up,
    w_down,
    laurel_left,
    laurel_right,
    per_gate,
    per_proj,
    lengths,
    head_gains,
    x_own,
    g_own,
    gains,
    raw_q,
    raw_kv,
    q_low,
    kv,
    lse,
    top,
    o_low,
    attn_val,
    lr_low,
    ff_val,
    laurels,
    vpg,
    vpp,
    cosine,
    sine,
    start,
    wq_all,
    wkv_all,
    wo_all,
    wg_all,
    wu_all,
    wd_all,
    xg_all,
    fg_all,
    gate_all,
    up_all,
    turned_all,
    w_kv_pair,
    laurel_own,
    gains_pad,
    vq,
    vkv,
    vo,
    vg,
    vu,
    vd,
    xg,
    fg,
    gate,
    up,
    hid,
    turned,
    give,
    keep,
    got,
    sent,
    left,
    right,
    give2,
    keep2,
    got2,
    sent2,
    left2,
    right2,
    half_sum,
    row_sems,
    z_send,
    z_recv,
    s_send,
    s_recv,
    misc_send,
    misc_recv,
    out_sems,
):
    core, row, col = lax.axis_index("seq"), lax.axis_index("row"), lax.axis_index("col")
    place = (core, row, col)
    own_tokens, width = x_own.shape
    block = x_in.shape[2]
    head_dim = head_gains.shape[1]
    tokens = xg.shape[0]
    ff_part = gate.shape[1]
    chunk = 2 * own_tokens
    key_width = w_key.shape[1]
    half = row % 2
    half_block = block // 2
    halves2 = (give2, keep2, got2, sent2, left2, right2)
    greet(core, row, col)

    my_cols = pl.ds(pl.multiple_of(row * block, block), block)

    def hand_over(mask):
        return remote(
            x_in.at[row ^ mask],
            x_own.at[:, my_cols],
            misc_send.at[mask],
            misc_recv.at[mask],
            (core, row ^ mask, col),
        )

    def hand_grad(mask):
        return remote(
            g_in.at[row ^ mask],
            g_own.at[:, my_cols],
            misc_send.at[11 + mask],
            misc_recv.at[11 + mask],
            (core, row ^ mask, col),
        )

    def hand_gains(mask):
        return remote(
            gains_pad,
            gains.at[:, my_cols],
            misc_send.at[3 + mask],
            misc_recv.at[3 + mask],
            (core, row ^ mask, col),
        )

    for mask in (3, 1, 2):
        hand_over(mask).start()
    gains_pad[pl.ds(0, 6)] = gains_in[...]
    gains_pad[pl.ds(6, 2)] = jnp.zeros((2, block), F32)
    for mask in (3, 1, 2):
        hand_gains(mask).start()
    x_own[:, my_cols] = x_in[row]
    g_own[:, my_cols] = g_in[row]
    gains[:, my_cols] = gains_pad[...]

    pair_cols = pl.ds(pl.multiple_of(col % 2 * key_width, key_width), key_width)
    w_kv_own = w_kv_pair.at[:, pair_cols]
    w_kv_own[...] = jnp.where(core == 0, w_key[...].astype(F32), w_value[...].astype(F32)).astype(BF)
    pair = remote(w_kv_own, w_kv_own, misc_send.at[7], misc_recv.at[7], (core, row, col ^ 1))
    pair.start()

    lanes = iter(range(32))

    def rows_of(source, buf, split=by_rows, size=block, ways=(1, 2)):
        block_of, halves_of = split(buf, size)
        return RowGather(place, source, block_of, halves_of, row_sems.at[next(lanes)], ways)

    tile = 256
    core_head = pl.ds(pl.multiple_of(core * head_dim, head_dim), head_dim)

    def core_tile(index):
        return pl.ds(pl.multiple_of(core * ff_part + index * tile, tile), tile)

    get_q = rows_of(w_query.at[:, core_head], vq)
    get_kv = rows_of(w_kv_pair, vkv)
    get_o = rows_of(w_out.at[core_head], vo, by_cols, ways=(2,))
    laurel_own[...] = jnp.where(
        core == 0, laurel_left[...].astype(F32), laurel_right[...].astype(F32)
    ).astype(BF)
    get_laurel = [rows_of(laurel_own, laurels.at[core], by_cols)]
    per_rows, per_cols = per_gate.shape[0] // 2, per_proj.shape[0] // 2
    own_rows = pl.ds(pl.multiple_of(core * per_rows, per_rows), per_rows)
    own_cols = pl.ds(pl.multiple_of(core * per_cols, per_cols), per_cols)
    get_per = [
        rows_of(per_gate.at[own_rows], vpg, by_core_rows(core)),
        rows_of(per_proj.at[own_cols], vpp.at[own_cols], by_cols),
    ]
    tiles = ff_part // tile
    get_gu = [
        [
            rows_of(whole.at[:, core_tile(index)], buf.at[:, pl.ds(index * tile, tile)])
            for whole, buf in ((w_gate, vg), (w_up, vu))
        ]
        for index in range(tiles)
    ]
    half_ff = ff_part // 2
    core_ff = pl.ds(pl.multiple_of(core * ff_part, ff_part), ff_part)
    get_d = [
        rows_of(w_down.at[core_ff, pl.ds(part * (block // 2), block // 2)], vd, by_half_cols(part))
        for part in range(2)
    ]

    def per_parts(which, lane):
        parts = [
            vpg.at[pl.ds(pl.multiple_of(index * block + which * per_rows, per_rows), per_rows)]
            for index in range(4)
        ]
        parts.append(vpp.at[pl.ds(pl.multiple_of(which * per_cols, per_cols), per_cols)])
        return list(enumerate(parts, lane))

    def begin(jobs):
        for job in jobs:
            job.start()

    def push(jobs):
        for job in jobs:
            job.forward()

    def complete(jobs):
        for job in jobs:
            job.finish()

    get_q.start()
    pair.wait_recv()
    get_kv.start()

    for mask in (1, 2, 3):
        remote(
            x_in.at[row],
            x_own.at[:, pl.ds(pl.multiple_of((row ^ mask) * block, block), block)],
            misc_send.at[mask],
            misc_recv.at[mask],
            (core, row, col),
        ).wait_recv()
        remote(
            gains_pad,
            gains.at[:, pl.ds(pl.multiple_of((row ^ mask) * block, block), block)],
            misc_send.at[3 + mask],
            misc_recv.at[3 + mask],
            (core, row, col),
        ).wait_recv()

    def own_norm():
        values = x_own[...].astype(F32)
        factor = lax.rsqrt(jnp.mean(values * values, axis=1, keepdims=True) + EPSILON)
        return values, values * factor * gains[pl.ds(0, 1)]

    mine = pl.ds(pl.multiple_of((core * 4 + col) * own_tokens, own_tokens), own_tokens)
    xg[mine] = own_norm()[1].astype(BF)
    sems = lambda lane: (z_send.at[lane], z_recv.at[lane], s_send.at[lane], s_recv.at[lane])
    gather_x = Gather(place, xg, own_tokens, sems(0))
    gather_x.start()

    def doc_tables():
        token = lax.broadcasted_iota(jnp.int32, (tokens, 1), 0)
        token_place = token // own_tokens * chunk + half * own_tokens + token % own_tokens
        doc_start, doc_end = jnp.zeros((tokens, 1), jnp.int32), 0
        for doc in range(lengths.shape[1]):
            length = lengths[row // 2, doc]
            doc_end = doc_end + length
            doc_start = doc_start + jnp.where(token_place >= doc_end, length, 0)
        start[...] = doc_start
        pair_index = lax.broadcasted_iota(jnp.int32, (1, head_dim // 2), 1).astype(F32)
        frequency = jnp.exp(pair_index * (-2.0 * math.log(ROPE_BASE) / head_dim))
        angles = (token_place - doc_start).astype(F32) * frequency
        sine[...] = angles
        cosine[...] = jnp.cos(angles)

    gather_x.forward(
        [
            doc_tables,
            lambda: (push([get_q, get_kv]), begin([get_o])),
        ]
    )
    gather_x.finish()
    sine[...] = jnp.sin(sine[...])
    complete([get_q, get_kv])

    raw_q[...] = mm(xg[...], vq[...])
    raw_kv[...] = mm(xg[...], vkv[...])
    q_low[...] = head_parts(raw_q[...], head_gains[pl.ds(0, 1)], cosine[...], sine[...]).astype(BF)
    is_key = core == 0
    kv_here = head_parts(
        raw_kv[...],
        jnp.where(is_key, head_gains[pl.ds(1, 1)], 1.0),
        jnp.where(is_key, cosine[...], 1.0),
        jnp.where(is_key, sine[...], 0.0),
    ).astype(BF)

    def kv_part(kind, which):
        return kv.at[kind, pl.ds(pl.multiple_of(which * tokens, tokens), tokens)]

    kv[core, pl.ds(pl.multiple_of(half * tokens, tokens), tokens)] = kv_here
    here = kv_part(core, half)
    to_x = remote(here, here, misc_send.at[8], misc_recv.at[8], (core, row ^ 1, col))
    to_s = remote(here, here, misc_send.at[9], misc_recv.at[9], (1 - core, row, col))
    to_x.start()
    to_s.start()
    push([get_o])
    begin(get_gu[0] + get_laurel + get_gu[1])
    came = kv_part(core, half ^ 1)
    remote(here, came, misc_send.at[8], misc_recv.at[8], (core, row, col)).wait_recv()
    on_s = remote(came, came, misc_send.at[10], misc_recv.at[10], (1 - core, row, col))
    on_s.start()
    other = kv_part(1 - core, half)
    remote(other, other, misc_send.at[9], misc_recv.at[9], (core, row, col)).wait_recv()
    other_came = kv_part(1 - core, half ^ 1)
    remote(other_came, other_came, misc_send.at[10], misc_recv.at[10], (core, row, col)).wait_recv()

    q_rows = 128
    key_token = lax.broadcasted_iota(jnp.int32, (1, 2 * tokens), 1)
    in_half = key_token % tokens
    key_place = in_half // own_tokens * chunk + key_token // tokens * own_tokens + in_half % own_tokens
    top[...] = jnp.full(top.shape, MASK_FILL, F32)

    def attend(step, carry):
        first = pl.multiple_of(step * q_rows, q_rows)
        rows = pl.ds(first, q_rows)
        token = first + lax.broadcasted_iota(jnp.int32, (q_rows, 1), 0)
        q_place = token // own_tokens * chunk + half * own_tokens + token % own_tokens
        allowed = (key_place <= q_place) & (key_place >= start[rows])
        scores = jnp.where(allowed, mm_nt(q_low[rows], kv[0]), MASK_FILL)
        row_top = jnp.max(scores, axis=1, keepdims=True)
        weights = jnp.exp(scores - row_top)
        total = jnp.sum(weights, axis=1, keepdims=True)
        probs = (weights * (1.0 / total)).astype(BF)
        o_low[rows] = mm(probs, kv[1]).astype(BF)
        lse[rows] = row_top + jnp.log(total)
        top[...] = jnp.maximum(top[...], jnp.max(row_top))
        return carry

    lax.fori_loop(0, tokens // q_rows, attend, 0)
    get_o.finish()

    away = pl.multiple_of((1 - core) * 4 * own_tokens, 4 * own_tokens)
    home = pl.multiple_of(core * 4 * own_tokens, 4 * own_tokens)
    scatter = Scatter(place, own_tokens, (give, keep, got, sent, left, right), sems(1))

    def project(source, weights, target, first):
        def step(index, carry):
            cols = pl.ds(pl.multiple_of(index * block, block), block)
            value = mm(source[pl.ds(first, 4 * own_tokens)], weights[:, cols])
            target[:, cols] = value.astype(target.dtype)
            return carry

        lax.fori_loop(0, width // block, step, 0)

    project(o_low, vo, give, away)
    scatter.start()
    project(o_low, vo, keep, home)
    scatter.run(
        attn_val,
        [lambda: (push(get_gu[0]), push(get_laurel)), lambda: begin(get_gu[2])],
    )
    push(get_gu[1])
    begin(get_gu[3])

    complete(get_laurel)
    laurel_here = laurels.at[core]
    laurel_share = remote(
        laurel_here, laurel_here, misc_send.at[22], misc_recv.at[22], (1 - core, row, col)
    )
    laurel_share.start()
    inputs, x_norm = own_norm()
    attn_normed = rms(attn_val[...])[0]
    laurel_there = laurels.at[1 - core]
    remote(
        laurel_there, laurel_there, misc_send.at[22], misc_recv.at[22], (core, row, col)
    ).wait_recv()
    lr_low[...] = mm_nt(xg[mine], laurels[0]).astype(BF)
    lo_normed = rms(mm(lr_low[...], laurels[1]))[0]
    h_two = (
        inputs + attn_normed * gains[pl.ds(1, 1)] + (x_norm + lo_normed * gains[pl.ds(2, 1)])
    ) * ROOT_HALF
    fg[mine] = (rms(h_two)[0] * gains[pl.ds(3, 1)]).astype(BF)
    gather_f = Gather(place, fg, own_tokens, sems(2))
    gather_f.start()
    gather_f.forward(
        [
            lambda: None,
            lambda: push(get_gu[2]),
            lambda: begin(get_d[:1]),
        ]
    )
    gather_f.finish()

    def unit_tile(index):
        complete(get_gu[index])
        cols = pl.ds(index * tile, tile)
        bent, slope = gelu_both(mm(fg[...], vg[:, cols]))
        up_part = mm(fg[...], vu[:, cols])
        gate[:, cols] = (up_part * slope).astype(BF)
        up[:, cols] = bent.astype(BF)
        hid[:, cols] = (bent * up_part).astype(BF)

    for index in range(tiles):
        if index == 1:
            push(get_gu[3])
        if index == 3:
            push(get_d[:1])
            begin(get_d[1:])
        unit_tile(index)
    turned[...] = hid[...].T
    scatter_ff = [
        Scatter(place, own_tokens, tuple(buf.at[part] for buf in halves2), sems(3 + part))
        for part in range(2)
    ]

    def project_half(part, target, first):
        def step(index, carry):
            cols = pl.ds(pl.multiple_of(index * block + part * half_block, half_block), half_block)
            here = pl.ds(pl.multiple_of(index * half_block, half_block), half_block)
            value = mm(hid[pl.ds(first, 4 * own_tokens)], vd[:, cols])
            target[:, here] = value.astype(target.dtype)
            return carry

        lax.fori_loop(0, width // block, step, 0)

    def down_half(part):
        complete(get_d[part : part + 1])
        project_half(part, give2.at[part], away)
        scatter_ff[part].start()
        project_half(part, keep2.at[part], home)

    def spread_half(part):
        for index in range(width // block):
            ff_val[:, pl.ds(index * block + part * half_block, half_block)] = half_sum[
                :, pl.ds(index * half_block, half_block)
            ]

    def late():
        push(get_d[1:])
        begin(get_per)
        for mask in (1, 2, 3):
            hand_grad(mask).start()

    down_half(0)
    scatter_ff[0].run(half_sum, [lambda: None, late])
    spread_half(0)
    down_half(1)
    keep_weights = [
        pltpu.make_async_copy(source, target, out_sems.at[lane])
        for lane, (source, target) in enumerate(
            [
                (vq, wq_all),
                (vkv, wkv_all),
                (vo, wo_all),
                (vg, wg_all),
                (vu, wu_all),
                (vd, wd_all),
                (xg, xg_all),
                (fg, fg_all),
                (gate, gate_all),
                (up, up_all),
            ]
        )
    ]
    for copy in keep_weights:
        copy.start()
    get_turned = rows_of(
        turned.at[pl.ds(0, half_ff)], turned_all.at[pl.ds(0, half_ff)], by_cols, tokens
    )
    rest = pl.ds(half_ff, half_ff)
    keep_rest = pltpu.make_async_copy(
        turned.at[rest],
        turned_all.at[rest, pl.ds(pl.multiple_of(row * tokens, tokens), tokens)],
        out_sems.at[10],
    )
    keep_rest.start()
    scatter_ff[1].run(half_sum, [lambda: (push(get_per), get_turned.start())])
    spread_half(1)
    complete(get_per)
    share = [
        remote(part, part, misc_send.at[lane], misc_recv.at[lane], (1 - core, row, col))
        for lane, part in per_parts(core, 16)
    ]
    for copy in share:
        copy.start()
    for lane, part in per_parts(1 - core, 16):
        remote(part, part, misc_send.at[lane], misc_recv.at[lane], (core, row, col)).wait_recv()
    for copy in share:
        copy.wait_send()
    get_turned.finish_first()
    keep_rest.wait()

    for mask in (1, 2, 3):
        hand_over(mask).wait_send()
        hand_gains(mask).wait_send()
        hand_grad(mask).wait_send()
        remote(
            g_in.at[row],
            g_own.at[:, pl.ds(pl.multiple_of((row ^ mask) * block, block), block)],
            misc_send.at[11 + mask],
            misc_recv.at[11 + mask],
            (core, row, col),
        ).wait_recv()
    gather_x.drain()
    scatter.drain()
    gather_f.drain()
    scatter_ff[0].drain()
    scatter_ff[1].drain()
    laurel_share.wait_send()
    pair.wait_send()
    to_x.wait_send()
    to_s.wait_send()
    on_s.wait_send()
    for copy in keep_weights:
        copy.wait()


def run_forward(x_in, g_in, gains_in, weights_in, lengths, head_gains):
    w_gate, laurel_left, per_gate, per_proj = (weights_in[i] for i in (4, 7, 9, 10))
    block = x_in.shape[2]
    own, width = x_in.shape[1], 4 * block
    tokens, head_dim, ff_part = 8 * own, head_gains.shape[1], w_gate.shape[1] // 2
    rank = laurel_left.shape[0]
    vm = pl.BlockSpec(memory_space=pltpu.VMEM)
    hbm = pl.BlockSpec(memory_space=pl.ANY)
    shape = jax.ShapeDtypeStruct
    weights = [
        (width, head_dim),
        (width, head_dim),
        (head_dim, width),
        (width, ff_part),
        (width, ff_part),
        (ff_part, width),
    ]
    acts = [
        (tokens, width),
        (tokens, width),
        (tokens, ff_part),
        (tokens, ff_part),
    ]
    outs = [
        shape((own, width), BF),
        shape((own, width), BF),
        shape((8, width), F32),
        shape((tokens, head_dim), F32),
        shape((tokens, head_dim), F32),
        shape((tokens, head_dim), BF),
        shape((2, 2 * tokens, head_dim), BF),
        shape((tokens, 1), F32),
        shape((8, 128), F32),
        shape((tokens, head_dim), BF),
        shape((own, width), F32),
        shape((own, rank), BF),
        shape((own, width), F32),
        shape((2, rank, width), BF),
        shape((width, per_gate.shape[1]), BF),
        shape((per_proj.shape[0], width), BF),
        shape((tokens, head_dim // 2), F32),
        shape((tokens, head_dim // 2), F32),
        shape((tokens, 1), jnp.int32),
    ] + [shape(size, BF) for size in weights + acts + [(ff_part, 4 * tokens)]]
    scatter_bufs = [
        pltpu.VMEM((4 * own, width), BF),
        pltpu.VMEM((4 * own, width), F32),
        pltpu.VMEM((4 * own, width), BF),
        pltpu.VMEM((4, own, width), BF),
        pltpu.VMEM((3, own, width), BF),
        pltpu.VMEM((3, own, width), BF),
    ]
    dma = pltpu.SemaphoreType.DMA
    return pl.pallas_call(
        forward_kernel,
        out_shape=outs,
        in_specs=[vm, vm, vm, hbm, vm, vm] + [hbm] * 4 + [vm] * 2
        + [hbm] * 2
        + [pl.BlockSpec(memory_space=pltpu.SMEM), vm],
        out_specs=[vm] * 19 + [hbm] * 11,
        scratch_shapes=[
            pltpu.VMEM((block, head_dim), BF),
            pltpu.VMEM((rank, block), BF),
            pltpu.VMEM((8, block), F32),
        ]
        + [pltpu.VMEM(size, BF) for size in weights + acts]
        + [pltpu.VMEM((tokens, ff_part), BF), pltpu.VMEM((ff_part, tokens), BF)]
        + scatter_bufs
        + [pltpu.VMEM((2,) + buf.shape[:-1] + (width // 2,), buf.dtype) for buf in scatter_bufs]
        + [pltpu.VMEM((own, width // 2), F32)]
        + [
            dma((18, 10)),
            dma((5, 8 * PIECES)),
            dma((5, 8 * PIECES)),
            dma((5, 4 * PIECES)),
            dma((5, 4 * PIECES)),
            dma((24,)),
            dma((24,)),
            dma((11,)),
        ],
        compiler_params=pltpu.CompilerParams(
            collective_id=0, has_side_effects=True, vmem_limit_bytes=VMEM_BYTES
        ),
        cost_estimate=pl.CostEstimate(flops=2 * 10**10, bytes_accessed=5 * 10**7, transcendentals=10**6),
    )(x_in, g_in, gains_in, *weights_in, lengths, head_gains)


class RowScatter:
    def __init__(self, place, halves, came, sems, stage=None):
        self.core, self.row, self.col = place
        self.halves, self.came, self.sems = halves, came, sems
        self.stage = stage

    def send(self, lane, index, half, mask):
        return remote(
            self.halves(index)[half],
            self.came.at[lane],
            self.sems.at[lane],
            self.sems.at[6 + lane],
            (self.core, self.row ^ mask, self.col),
        )

    def lane(self, lane):
        index, half, mask = ((1, 0, 1), (3, 0, 1), (2, 1, 2), (3, 1, 2), (2, 0, 2), (1, 1, 1))[lane]
        return self.send(lane, self.row ^ index, half, mask)

    def start(self, lanes=(1, 3, 0, 2)):
        for lane in lanes:
            self.lane(lane).start()

    def load(self, lane):
        slot = {0: 0, 1: 0, 4: 0, 2: 1, 3: 1, 5: 1}[lane]
        return slot, pltpu.make_async_copy(
            self.came.at[lane], self.stage[0].at[slot], self.stage[1].at[slot]
        )

    def fetch(self, *lanes):
        for lane in lanes:
            self.lane(lane).wait_recv()
            if self.stage is not None:
                self.load(lane)[1].start()

    def add(self, lane, index, half):
        if self.stage is None:
            value = self.came[lane]
        else:
            slot, copy = self.load(lane)
            copy.wait()
            value = self.stage[0][slot]
        part = self.halves(self.row ^ index)[half]
        part[...] = (part[...].astype(F32) + value.astype(F32)).astype(BF)

    def middle(self):
        for lane, out, index, half in ((1, 4, 2, 0), (3, 5, 1, 1)):
            self.add(lane, index, half)
            self.lane(out).start()

    def early(self):
        self.add(0, 0, 0)
        self.add(2, 0, 1)

    def finish(self):
        self.add(4, 0, 0)
        self.add(5, 0, 1)

    def drain(self):
        for lane in range(6):
            self.lane(lane).wait_send()


def head_back(grad, raw, gain, cosine, sine):
    factor = lax.rsqrt(jnp.mean(raw * raw, axis=1, keepdims=True) + EPSILON)
    half = raw.shape[1] // 2
    normed = raw * factor
    first, second = grad[:, :half], grad[:, half:]
    back = jnp.concatenate([first * cosine + second * sine, second * cosine - first * sine], axis=1)
    gain_grad = jnp.sum(back * normed, axis=0, keepdims=True)
    inner = back * gain
    return factor * (inner - normed * jnp.mean(inner * normed, axis=1, keepdims=True)), gain_grad


def backward_kernel(
    x_own,
    g_own,
    per_in,
    gains,
    head_gains,
    attn_val,
    lr_low,
    ff_val,
    raw_q,
    raw_kv,
    q_low,
    kv,
    lse,
    top,
    o_low,
    cosine,
    sine,
    start,
    laurels,
    vpg,
    vpp,
    xg_in,
    fg_in,
    gate_in,
    up_in,
    turned_in,
    wq_in,
    wkv_in,
    wo_in,
    wg_in,
    wu_in,
    wd_in,
    y_out,
    x_grad,
    g_gain,
    tops,
    small_a,
    gq,
    gkv,
    gout,
    ggate,
    gup,
    gdown,
    came_g,
    came_u,
    turned_far,
    turned_near,
    vq,
    vkv,
    vo,
    vg,
    vu,
    vd,
    fg,
    gate,
    up,
    dff_all,
    down_stage,
    dffg,
    dattng,
    dgate,
    dup,
    give,
    keep,
    got,
    sent,
    left,
    right,
    own_sum,
    h_two_ref,
    d_three_ref,
    low_ref,
    gpart,
    gcame,
    gpart2,
    gcame2,
    small_give,
    small_keep,
    small_got,
    small_row,
    small_z,
    d_o,
    d_kv,
    kv_give,
    kv_got,
    kv_x_got,
    kv_p_got,
    pkv,
    came_q,
    came_kv,
    came_o,
    stage_g,
    stage_sems,
    load_sems,
    row_sems,
    z_send,
    z_recv,
    s_send,
    s_recv,
    misc_send,
    misc_recv,
    gain_send,
    gain_recv,
    done_sems,
    ff_sems,
    down_sems,
    turned_sems,
    kv_sems,
):
    core, row, col = lax.axis_index("seq"), lax.axis_index("row"), lax.axis_index("col")
    place = (core, row, col)
    own_tokens, width = x_own.shape
    block = width // 4
    tokens, head_dim = raw_q.shape
    ff_part = gate.shape[1]
    chunk = 2 * own_tokens
    key_width = head_dim // 2
    half = row % 2
    rank = lr_low.shape[1]
    my_cols = pl.ds(pl.multiple_of(row * block, block), block)
    mine = pl.ds(pl.multiple_of((core * 4 + col) * own_tokens, own_tokens), own_tokens)
    away = pl.multiple_of((1 - core) * 4 * own_tokens, 4 * own_tokens)
    home = pl.multiple_of(core * 4 * own_tokens, 4 * own_tokens)

    barrier = pltpu.get_barrier_semaphore()
    for mask in (1, 2, 3):
        pl.semaphore_signal(barrier, inc=1, device_id=(core, row ^ mask, col), device_id_type=MESH)
        for other in (0, 1):
            pl.semaphore_signal(
                barrier, inc=1, device_id=(core ^ other, row, col ^ mask), device_id_type=MESH
            )
    pl.semaphore_signal(barrier, inc=1, device_id=(1 - core, row, col), device_id_type=MESH)
    loads = [
        pltpu.make_async_copy(source, target, load_sems.at[lane])
        for lane, (source, target) in enumerate(
            [
                (wd_in, vd),
                (gate_in, gate),
                (up_in, up),
                (wg_in, vg),
                (wu_in, vu),
                (fg_in, fg),
                (wo_in, vo),
                (wq_in, vq),
                (wkv_in, vkv),
            ]
        )
    ]
    for load in loads:
        load.start()
    pl.semaphore_wait(barrier, 10)
    half_ff = ff_part // 2

    def turned_on(part, mask):
        rows = pl.ds(part * half_ff + (mask - 1) * (half_ff // 2), half_ff // 2)
        first = pl.multiple_of((row ^ (3 - mask)) * tokens, tokens)
        if part == 0:
            source = turned_in.at[rows, pl.ds(first, tokens)]
        else:
            source = turned_near.at[2 - mask, pl.ds((mask - 1) * (half_ff // 2), half_ff // 2)]
        lane = part * 2 + mask - 1
        return remote(
            source,
            turned_far.at[rows],
            row_sems.at[0, lane],
            row_sems.at[0, 6 + lane],
            (core, row ^ mask, col),
        )

    def turned_over(mask):
        return remote(
            turned_in.at[
                pl.ds(half_ff, half_ff), pl.ds(pl.multiple_of(row * tokens, tokens), tokens)
            ],
            turned_near.at[mask - 1],
            row_sems.at[0, 3 + mask],
            row_sems.at[0, 9 + mask],
            (core, row ^ mask, col),
        )

    for mask in (1, 2):
        turned_on(0, mask).start()
        turned_over(mask).start()

    def turned_rest():
        for mask in (1, 2):
            turned_over(mask).wait_recv()
        for mask in (1, 2):
            turned_on(1, mask).start()


    def gain(index):
        return gains[pl.ds(index, 1)]

    inputs = x_own[...].astype(F32)
    x_norm = rms(inputs)[0] * gain(0)
    attn_normed = rms(attn_val[...])[0]
    lo_normed = rms(mm(lr_low[...], laurels[1]))[0]
    h_two = (inputs + attn_normed * gain(1) + (x_norm + lo_normed * gain(2))) * ROOT_HALF
    h_two_ref[...] = h_two
    ff_normed, ff_factor = rms(ff_val[...])
    h_three = h_two + ff_normed * gain(4)
    h_low = h_three.astype(BF)
    p_gate, p_proj = vpg[...], vpp[...]
    pg_gelu, pg_slope = gelu_both(mm(h_low, p_gate))
    per_input = per_in[row].astype(F32)
    gp_low = (pg_gelu * per_input).astype(BF)
    pp_normed, pp_factor = rms(mm(gp_low, p_proj))
    low_ref[...] = (h_three + pp_normed * gain(5)).astype(BF)

    def hand_back(source, target, mask, lane):
        return remote(
            source.at[:, pl.ds(pl.multiple_of((row ^ mask) * block, block), block)],
            target.at[row],
            misc_send.at[lane + mask],
            misc_recv.at[lane + mask],
            (core, row ^ mask, col),
        )

    def came_back(target, mask, lane):
        return remote(
            target.at[row ^ mask],
            target.at[row ^ mask],
            misc_send.at[lane + mask],
            misc_recv.at[lane + mask],
            (core, row, col),
        )

    for mask in (1, 2, 3):
        hand_back(low_ref, y_out, mask, 0).start()
    y_out[row] = low_ref[:, my_cols]

    grad_top = g_own[...].astype(F32)
    d_pp, gain_five = rms_back(grad_top, pp_normed, pp_factor, gain(5))
    d_pp_low = d_pp.astype(BF)
    d_pg_low = (mm_nt(d_pp_low, p_proj) * per_input * pg_slope).astype(BF)
    d_three = grad_top + mm_nt(d_pg_low, p_gate)
    d_three_ref[...] = d_three
    d_ff, gain_four = rms_back(d_three, ff_normed, ff_factor, gain(4))
    gpart[...] = jnp.zeros(gpart.shape, F32)
    gpart[pl.ds(5, 1)] = gain_five
    gpart[pl.ds(4, 1)] = gain_four
    dffg[mine] = d_ff.astype(BF)
    sems = lambda lane: (z_send.at[lane], z_recv.at[lane], s_send.at[lane], s_recv.at[lane])
    gather_ff = Gather(place, dffg, own_tokens, sems(0))
    gather_ff.start()

    def small(kind, first, value):
        rows = pl.ds(first, value.shape[0])
        value = value.astype(BF)

        @pl.when(core == kind)
        def _():
            small_keep[rows] = value

        @pl.when(core != kind)
        def _():
            small_give[rows] = value

    small(0, rank, mm_tn(gp_low, d_pp_low))
    small(1, rank, mm_tn(d_pg_low, h_low))
    gather_ff.forward([lambda: None, turned_rest])
    gather_ff.finish()

    part_rows = tokens // 2

    def ff_piece(group, which):
        return dff_all.at[
            pl.ds(pl.multiple_of(group * tokens + which * part_rows, part_rows), part_rows)
        ]

    def ff_over(mask):
        return remote(
            dffg.at[
                pl.ds(pl.multiple_of(core * part_rows, part_rows), part_rows),
                pl.ds(pl.multiple_of((row ^ mask) * block, block), block),
            ],
            ff_piece(row, core),
            ff_sems.at[mask],
            ff_sems.at[4 + mask],
            (core, row ^ mask, col),
        )

    def ff_came(mask):
        part = ff_piece(row ^ mask, core)
        return remote(part, part, ff_sems.at[mask], ff_sems.at[4 + mask], (core, row, col))

    def ff_share(mask, which):
        part = ff_piece(row ^ mask, which)
        return remote(
            part, part, ff_sems.at[8 + mask], ff_sems.at[12 + mask], (1 - core, row, col)
        )

    for mask in (1, 2, 3):
        ff_over(mask).start()
    dff_all[pl.ds(pl.multiple_of(row * tokens, tokens), tokens)] = dffg[:, my_cols]

    tile = 256
    for load in loads[:3]:
        load.wait()

    def units(index, carry):
        cols = pl.ds(pl.multiple_of(index * tile, tile), tile)
        d_hid = mm_nt(dffg[...], vd[cols])
        dgate[:, cols] = (d_hid * gate[:, cols].astype(F32)).astype(BF)
        dup[:, cols] = (d_hid * up[:, cols].astype(F32)).astype(BF)
        return carry

    lax.fori_loop(0, ff_part // tile, units, 0)
    for load in loads[3:5]:
        load.wait()

    def back_ff(target, first):
        rows = pl.ds(first, 4 * own_tokens)

        def step(index, carry):
            cols = pl.ds(pl.multiple_of(index * block, block), block)
            value = mm_nt(dgate[rows], vg[cols]) + mm_nt(dup[rows], vu[cols])
            target[:, cols] = value.astype(target.dtype)
            return carry

        lax.fori_loop(0, width // block, step, 0)

    scatter_f = Scatter(place, own_tokens, (give, keep, got, sent, left, right), sems(1))
    back_ff(give, away)
    scatter_f.start()
    back_ff(keep, home)

    put_g = RowScatter(place, by_rows(vg, block)[1], came_g, row_sems.at[1], (stage_g, stage_sems))
    put_u = RowScatter(place, by_rows(vu, block)[1], came_u, row_sems.at[2], (stage_g, stage_sems))

    def load_turned(lane):
        mask, part = ((0, None), (3, None), (1, 0), (1, 1), (2, 0), (2, 1))[lane]
        cols = pl.ds(pl.multiple_of((row ^ mask) * tokens, tokens), tokens)
        if part is None:
            source = turned_far if mask else turned_in.at[:, cols]
            target = vd.at[:, cols]
        else:
            rows = pl.ds(part * half_ff, half_ff)
            source = turned_near.at[mask - 1] if part else turned_in.at[rows, cols]
            target = vd.at[rows, cols]
        return pltpu.make_async_copy(source, target, turned_sems.at[lane])

    def down_ready():
        for mask in (1, 2):
            for part in range(2):
                turned_on(part, mask).wait_recv()
        for lane in range(6):
            load_turned(lane).start()
        for mask in (1, 2, 3):
            ff_came(mask).wait_recv()
            ff_share(mask, core).start()

    def down_tile(index):
        slot = index % 2
        rows = pl.ds(index * tile, tile)
        target = gdown.at[pl.ds(pl.multiple_of(core * ff_part + index * tile, tile), tile)]
        local = pltpu.make_async_copy(down_stage.at[slot], target, down_sems.at[index])
        over = remote(
            down_stage.at[slot],
            target,
            down_sems.at[4 + index],
            down_sems.at[8 + index],
            (1 - core, row, col),
        )
        return slot, rows, local, over

    def down_grad():
        for lane in range(6):
            load_turned(lane).wait()
        for mask in (1, 2, 3):
            ff_share(mask, 1 - core).wait_recv()
        for index in range(ff_part // tile):
            slot, rows, local, over = down_tile(index)
            if index >= 2:
                before = down_tile(index - 2)
                before[2].wait()
                before[3].wait_send()
            down_stage[slot] = mm(vd[rows], dff_all[...]).astype(BF)
            local.start()
            over.start()

    def gate_grad(target, grad, put):
        def step(index, carry):
            rows = pl.ds(pl.multiple_of(index * tile, tile), tile)
            target[rows] = mm_tn(fg[:, rows], grad[...]).astype(BF)
            return carry

        lax.fori_loop(0, width // tile, step, 0)

    def start_gate():
        loads[5].wait()
        gate_grad(vg, dgate, put_g)
        put_g.start()

    def start_up():
        gate_grad(vu, dup, put_u)
        put_u.start((1, 3))

    start_gate()
    scatter_f.run(own_sum, [start_up, down_ready])

    gather_ff.drain()
    f_normed, f_factor = rms(h_two_ref[...])
    d_f, gain_three = rms_back(own_sum[...], f_normed, f_factor, gain(3))
    d_half = (d_three_ref[...] + d_f) * ROOT_HALF
    d_three_ref[...] = d_half
    attn_normed, attn_factor = rms(attn_val[...])
    d_attn, gain_one = rms_back(d_half, attn_normed, attn_factor, gain(1))
    dattng[mine] = d_attn.astype(BF)
    gather_a = Gather(place, dattng, own_tokens, sems(2))
    gather_a.start()
    lo_normed, lo_factor = rms(mm(lr_low[...], laurels[1]))
    d_lo, gain_two = rms_back(d_half, lo_normed, lo_factor, gain(2))
    d_lo_low = d_lo.astype(BF)
    d_lr_low = mm_nt(d_lo_low, laurels[1]).astype(BF)
    small(0, 0, mm_tn(lr_low[...], d_lo_low))
    x_low = (rms(x_own[...].astype(F32))[0] * gain(0)).astype(BF)
    small(1, 0, mm_tn(d_lr_low, x_low))
    own_sum[...] = d_half + mm(d_lr_low, laurels[0])
    gpart[pl.ds(3, 1)] = gain_three
    gpart[pl.ds(2, 1)] = gain_two
    gpart[pl.ds(1, 1)] = gain_one
    small_swap = remote(
        small_give, small_got, misc_send.at[8], misc_recv.at[8], (1 - core, row, col)
    )
    small_swap.start()
    put_s = RowScatter(place, by_cols(small_keep, block)[1], small_row, row_sems.at[6])

    def small_sum():
        small_swap.wait_recv()
        small_keep[...] = (small_keep[...].astype(F32) + small_got[...].astype(F32)).astype(BF)

    def middle_gate():
        put_g.fetch(1, 3)
        down_grad()
        put_g.middle()

    def more_small():
        small_sum()
        put_g.fetch(0, 2)

    gather_a.forward([middle_gate, more_small, put_g.early])
    gather_a.finish()
    scatter_f.drain()

    loads[6].wait()
    d_o[...] = mm_nt(dattng[...], vo[...]).astype(BF)
    q_rows = 128
    key_token = lax.broadcasted_iota(jnp.int32, (1, 2 * tokens), 1)
    in_half = key_token % tokens
    key_place = in_half // own_tokens * chunk + key_token // tokens * own_tokens + in_half % own_tokens
    d_kv[...] = jnp.zeros(d_kv.shape, F32)

    def attend(step, carry):
        first = pl.multiple_of(step * q_rows, q_rows)
        rows = pl.ds(first, q_rows)
        token = first + lax.broadcasted_iota(jnp.int32, (q_rows, 1), 0)
        q_place = token // own_tokens * chunk + half * own_tokens + token % own_tokens
        allowed = (key_place <= q_place) & (key_place >= start[rows])
        scores = jnp.where(allowed, mm_nt(q_low[rows], kv[0]), MASK_FILL)
        probs = jnp.exp(scores - lse[rows])
        d_probs = mm_nt(d_o[rows], kv[1])
        delta = jnp.sum(probs * d_probs, axis=1, keepdims=True)
        d_scores = (probs * (d_probs - delta)).astype(BF)
        d_kv[0] += mm_tn(d_scores, q_low[rows])
        d_kv[1] += mm_tn(probs.astype(BF), d_o[rows])
        d_raw, gain_part = head_back(
            mm(d_scores, kv[0]), raw_q[rows], head_gains[pl.ds(0, 1)], cosine[rows], sine[rows]
        )
        d_o[rows] = d_raw.astype(BF)
        return carry + gain_part

    gain_q = lax.fori_loop(0, tokens // q_rows, attend, jnp.zeros((1, head_dim), F32))

    kv_give[...] = d_kv[1 - core].astype(BF)
    swap_kv = remote(kv_give, kv_got, misc_send.at[9], misc_recv.at[9], (1 - core, row, col))
    swap_kv.start()

    def out_grad():
        for part in range(2):
            wide = pl.ds(part * (width // 2), width // 2)
            vo[:, wide] = mm_tn(o_low[...], dattng[:, wide]).astype(BF)

    put_o = RowScatter(place, by_cols(vo, block)[1], came_o, row_sems.at[3])
    swap_kv.wait()
    kv_x = kv_give.at[pl.ds(0, tokens)]
    theirs = pl.ds(pl.multiple_of((half ^ 1) * tokens, tokens), tokens)
    ours = pl.ds(pl.multiple_of(half * tokens, tokens), tokens)
    kv_x[...] = (d_kv[core, theirs] + kv_got[theirs].astype(F32)).astype(BF)
    kv_half = tokens // 2

    def over_x(piece):
        rows = pl.ds(piece * kv_half, kv_half)
        return remote(
            kv_x.at[rows],
            kv_x_got.at[rows],
            kv_sems.at[piece],
            kv_sems.at[2 + piece],
            (core, row ^ 1, col),
        )

    def over_p(piece):
        rows = pl.ds(piece * kv_half, kv_half)
        return remote(
            kv_p.at[rows],
            kv_p_got.at[rows],
            kv_sems.at[4 + piece],
            kv_sems.at[6 + piece],
            (core, row, col ^ 1),
        )

    for piece in range(2):
        over_x(piece).start()
    put_u.start((0, 2))
    load_x = pltpu.make_async_copy(xg_in, dffg, load_sems.at[10])
    for mask in (1, 2, 3):
        ff_over(mask).wait_send()
    load_x.start()
    put_u.fetch(1, 3)
    out_grad()
    put_u.middle()
    put_s.start()
    put_o.start()
    loads[7].wait()
    loads[8].wait()
    kv_p = kv_got.at[pl.ds(0, tokens)]
    d_kind = d_kv[core, ours] + kv_got[ours].astype(F32)
    for piece in range(2):
        rows = pl.ds(piece * kv_half, kv_half)
        over_x(piece).wait_recv()
        part = d_kind[piece * kv_half : (piece + 1) * kv_half] + kv_x_got[rows].astype(F32)
        kv_p[rows] = part.astype(BF)
        over_p(piece).start()
    for piece in range(2):
        over_p(piece).wait()
    d_kind = kv_p[...].astype(F32) + kv_p_got[...].astype(F32)
    is_key = core == 0
    d_kind_raw, gain_k = head_back(
        d_kind,
        raw_kv[...],
        jnp.where(is_key, head_gains[pl.ds(1, 1)], 1.0),
        jnp.where(is_key, cosine[...], 1.0),
        jnp.where(is_key, sine[...], 0.0),
    )
    for part in range(4):
        gpart[pl.ds(6, 1), pl.ds(part * block, head_dim)] = gain_q
        gpart[pl.ds(6, 1), pl.ds(part * block + head_dim, head_dim)] = gain_k * jnp.where(
            is_key, 0.5, 0.0
        )
    kv_p[...] = d_kind_raw.astype(BF)
    pair_cols = pl.ds(pl.multiple_of(col % 2 * key_width, key_width), key_width)

    def back_heads(target, first):
        rows = pl.ds(first, 4 * own_tokens)

        def step(index, carry):
            cols = pl.ds(pl.multiple_of(index * block, block), block)
            value = mm_nt(d_o[rows], vq[cols]) + mm_nt(kv_p[rows, pair_cols], vkv[cols, pair_cols])
            target[:, cols] = value.astype(target.dtype)
            return carry

        lax.fori_loop(0, width // block, step, 0)

    scatter_x = Scatter(place, own_tokens, (give, keep, got, sent, left, right), sems(3))
    back_heads(give, away)
    scatter_x.start()
    back_heads(keep, home)
    put_q = RowScatter(place, by_rows(vq, block)[1], came_q, row_sems.at[4])
    put_kv = RowScatter(place, by_rows(pkv, block)[1], came_kv, row_sems.at[5])

    def query_grad():
        load_x.wait()

        def step(index, carry):
            rows = pl.ds(pl.multiple_of(index * tile, tile), tile)
            vq[rows] = mm_tn(dffg[:, rows], d_o[...]).astype(BF)
            pkv[rows] = mm_tn(dffg[:, rows], kv_p[:, pair_cols]).astype(BF)
            return carry

        lax.fori_loop(0, width // tile, step, 0)
        put_q.start()
        put_kv.start()

    def deliver(lane, source, target):
        local = pltpu.make_async_copy(source, target, done_sems.at[lane])
        over = remote(
            source, target, done_sems.at[8 + lane], done_sems.at[16 + lane], (1 - core, row, col)
        )
        local.start()
        over.start()
        done.append((local, over))

    core_ff = pl.ds(pl.multiple_of(core * ff_part, ff_part), ff_part)
    core_head = pl.ds(pl.multiple_of(core * head_dim, head_dim), head_dim)
    sib_ff = pl.ds(pl.multiple_of((1 - core) * ff_part, ff_part), ff_part)
    sib_head = pl.ds(pl.multiple_of((1 - core) * head_dim, head_dim), head_dim)
    row_block = pl.ds(pl.multiple_of(row * block, block), block)
    done = []

    quarter = block // 4

    def small_quarter(mask):
        return remote(
            small_keep.at[
                :, pl.ds(pl.multiple_of(row * block + (col ^ mask) * quarter, quarter), quarter)
            ],
            small_z.at[mask],
            misc_send.at[11 + mask],
            misc_recv.at[11 + mask],
            (core, row, col ^ mask),
        )

    def gate_finish():
        put_g.fetch(4, 5)
        put_g.finish()
        deliver(1, vg.at[row_block], ggate.at[:, core_ff])
        put_u.fetch(0, 2)
        put_u.early()

    d_half_here = d_three_ref
    scatter_x.run(h_two_ref, [query_grad, gate_finish])
    d_xn = own_sum[...] + h_two_ref[...]
    x_normed, x_factor = rms(x_own[...].astype(F32))
    d_in, gain_zero = rms_back(d_xn, x_normed, x_factor, gain(0))
    gpart[pl.ds(0, 1)] = gain_zero
    for mask in (1, 2, 3):
        hand_back(low_ref, y_out, mask, 0).wait_send()
    low_ref[...] = (d_half_here[...] + d_in).astype(BF)
    for mask in (1, 2, 3):
        hand_back(low_ref, x_grad, mask, 4).start()
    x_grad[row] = low_ref[:, my_cols]

    gpart[pl.ds(8, 8)] = jnp.full((8, width), jnp.max(top[...]), F32)

    def gain_row(mask):
        return remote(
            gpart.at[:, pl.ds(pl.multiple_of((row ^ mask) * block, block), block)],
            gcame.at[mask],
            gain_send.at[mask],
            gain_recv.at[mask],
            (core, row ^ mask, col),
        )

    for mask in (1, 2, 3):
        gain_row(mask).start()
    gcame[0] = gpart[:, my_cols]
    for put in (put_s, put_o, put_q, put_kv):
        put.fetch(1, 3)
        put.middle()
    for mask in (1, 2, 3):
        gain_row(mask).wait_recv()
    summed = gcame[0] + gcame[1] + gcame[2] + gcame[3]
    largest = jnp.maximum(jnp.maximum(gcame[0], gcame[1]), jnp.maximum(gcame[2], gcame[3]))
    gpart2[pl.ds(0, 8)] = summed[:8]
    gpart2[pl.ds(8, 8)] = largest[8:]
    me = core * 4 + col
    members = [(other, mask) for other in (0, 1) for mask in range(4) if other or mask]

    def gain_group(other, mask):
        lane = 4 + other * 4 + mask
        return remote(
            gpart2,
            gcame2.at[me],
            gain_send.at[lane],
            gain_recv.at[lane],
            (core ^ other, row, col ^ mask),
        )

    for other, mask in members:
        gain_group(other, mask).start()
    gcame2[me] = gpart2[...]
    put_s.fetch(0, 2, 4, 5)
    put_s.early()
    put_s.finish()
    for mask in (1, 2, 3):
        small_quarter(mask).start()
    put_u.fetch(4, 5)
    put_u.finish()
    deliver(2, vu.at[row_block], gup.at[:, core_ff])

    def small_share(other, mask):
        lane = 16 + other * 4 + mask
        return remote(
            kv_x.at[pl.ds(0, small_keep.shape[0]), pl.ds(0, quarter)],
            small_a.at[core, col],
            misc_send.at[lane],
            misc_recv.at[lane],
            (core ^ other, row, col ^ mask),
        )

    for mask in (1, 2, 3):
        small_quarter(mask).wait_recv()
    small_total = small_keep[
        :, pl.ds(pl.multiple_of(row * block + col * quarter, quarter), quarter)
    ].astype(F32)
    for mask in (1, 2, 3):
        small_total = small_total + small_z[mask].astype(F32)
    for piece in range(2):
        over_x(piece).wait_send()
    kv_x[pl.ds(0, small_keep.shape[0]), pl.ds(0, quarter)] = small_total.astype(BF)
    for other, mask in members:
        small_share(other, mask).start()
    small_a[core, col] = small_total.astype(BF)
    for put, lane, source, target in (
        (put_o, 4, vo.at[:, row_block], gout.at[core_head]),
        (put_kv, 3, pkv.at[row_block], gkv.at[core]),
        (put_q, 5, vq.at[row_block], gq.at[:, core_head]),
    ):
        put.fetch(0, 2, 4, 5)
        put.early()
        put.finish()
        deliver(lane, source, target)

    for other, mask in members:
        who = (core ^ other) * 4 + (col ^ mask)
        lane = 4 + other * 4 + mask
        remote(
            gpart2, gcame2.at[who], gain_send.at[lane], gain_recv.at[lane], (core, row, col)
        ).wait_recv()
    total = gcame2[0]
    for who in range(1, 8):
        total = total + gcame2[who]
    g_gain[...] = total[:8]
    for who in range(8):
        head = 2 * (who % 4) + who // 4
        tops[pl.ds(head, 1)] = gcame2[who, pl.ds(8, 1), pl.ds(0, 128)]

    gather_a.drain()
    scatter_x.drain()
    for other, mask in members:
        part = small_a.at[core ^ other, col ^ mask]
        lane = 16 + other * 4 + mask
        remote(part, part, misc_send.at[lane], misc_recv.at[lane], (core, row, col)).wait_recv()
        small_share(other, mask).wait_send()
        gain_group(other, mask).wait_send()
    for mask in (1, 2, 3):
        came_back(y_out, mask, 0).wait_recv()
        came_back(x_grad, mask, 4).wait_recv()
        hand_back(low_ref, x_grad, mask, 4).wait_send()
        gain_row(mask).wait_send()
        small_quarter(mask).wait_send()
    small_swap.wait_send()
    for put in (put_g, put_u, put_o, put_q, put_kv, put_s):
        put.drain()
    for mask in (1, 2):
        turned_over(mask).wait_send()
        for part in range(2):
            turned_on(part, mask).wait_send()
    for mask in (1, 2, 3):
        ff_share(mask, core).wait_send()
    for index in range(ff_part // tile):
        slot, rows, local, over = down_tile(index)
        if index >= 2:
            local.wait()
            over.wait_send()
        target = gdown.at[pl.ds(pl.multiple_of((1 - core) * ff_part + index * tile, tile), tile)]
        remote(
            target, target, down_sems.at[4 + index], down_sems.at[8 + index], (core, row, col)
        ).wait_recv()
    theirs_at = {
        1: ggate.at[:, sib_ff],
        2: gup.at[:, sib_ff],
        3: gkv.at[1 - core],
        4: gout.at[sib_head],
        5: gq.at[:, sib_head],
    }
    for lane, (local, over) in zip((1, 2, 4, 3, 5), done):
        local.wait()
        over.wait_send()
        target = theirs_at[lane]
        remote(
            target, target, done_sems.at[8 + lane], done_sems.at[16 + lane], (core, row, col)
        ).wait_recv()


def run_backward(small_args, big_args):
    x_own, per_in, head_gains = small_args[0], small_args[2], small_args[4]
    own, width = x_own.shape
    block = width // 4
    gate = big_args[2]
    tokens, ff_part = gate.shape
    head_dim = head_gains.shape[1]
    rank = small_args[6].shape[1]
    small_rows = small_args[18].shape[1] + small_args[20].shape[0]
    vm = pl.BlockSpec(memory_space=pltpu.VMEM)
    hbm = pl.BlockSpec(memory_space=pl.ANY)
    shape = jax.ShapeDtypeStruct
    vmem = pltpu.VMEM
    dma = pltpu.SemaphoreType.DMA
    outs = [
        shape((4, own, block), BF),
        shape((4, own, block), BF),
        shape((8, block), F32),
        shape((8, 128), F32),
        shape((2, 4, small_rows, block // 4), BF),
        shape((block, 2 * head_dim), BF),
        shape((2, block, head_dim // 2), BF),
        shape((2 * head_dim, block), BF),
        shape((block, 2 * ff_part), BF),
        shape((block, 2 * ff_part), BF),
        shape((2 * ff_part, block), BF),
        shape((6, block // 2, ff_part), BF),
        shape((6, block // 2, ff_part), BF),
        shape((ff_part, tokens), BF),
        shape((2, ff_part // 2, tokens), BF),
    ]
    scratch = [
        vmem((width, head_dim), BF),
        vmem((width, head_dim), BF),
        vmem((head_dim, width), BF),
        vmem((width, ff_part), BF),
        vmem((width, ff_part), BF),
        vmem((ff_part, width), BF),
        vmem((tokens, width), BF),
        vmem((tokens, ff_part), BF),
        vmem((tokens, ff_part), BF),
        vmem((4 * tokens, block), BF),
        vmem((2, 256, block), BF),
        vmem((tokens, width), BF),
        vmem((tokens, width), BF),
        vmem((tokens, ff_part), BF),
        vmem((tokens, ff_part), BF),
        vmem((4 * own, width), BF),
        vmem((4 * own, width), F32),
        vmem((4 * own, width), BF),
        vmem((4, own, width), BF),
        vmem((3, own, width), BF),
        vmem((3, own, width), BF),
        vmem((own, width), F32),
        vmem((own, width), F32),
        vmem((own, width), F32),
        vmem((own, width), BF),
        vmem((16, width), F32),
        vmem((4, 16, block), F32),
        vmem((16, block), F32),
        vmem((8, 16, block), F32),
        vmem((small_rows, width), BF),
        vmem((small_rows, width), BF),
        vmem((small_rows, width), BF),
        vmem((6, small_rows // 2, block), BF),
        vmem((4, small_rows, block // 4), BF),
        vmem((tokens, head_dim), BF),
        vmem((2, 2 * tokens, head_dim), F32),
        vmem((2 * tokens, head_dim), BF),
        vmem((2 * tokens, head_dim), BF),
        vmem((tokens, head_dim), BF),
        vmem((tokens, head_dim), BF),
        vmem((width, head_dim // 2), BF),
        vmem((6, block // 2, head_dim), BF),
        vmem((6, block // 2, head_dim // 2), BF),
        vmem((6, head_dim // 2, block), BF),
        vmem((2, block // 2, ff_part), BF),
        dma((2,)),
        dma((11,)),
        dma((7, 12)),
        dma((4, 8 * PIECES)),
        dma((4, 8 * PIECES)),
        dma((4, 4 * PIECES)),
        dma((4, 4 * PIECES)),
        dma((24,)),
        dma((24,)),
        dma((12,)),
        dma((12,)),
        dma((24,)),
        dma((16,)),
        dma((12,)),
        dma((6,)),
        dma((8,)),
    ]
    return pl.pallas_call(
        backward_kernel,
        out_shape=outs,
        in_specs=[vm] * 21 + [hbm] * 11,
        out_specs=[vm] * 5 + [hbm] * 10,
        scratch_shapes=scratch,
        compiler_params=pltpu.CompilerParams(
            collective_id=1, has_side_effects=True, vmem_limit_bytes=VMEM_BYTES
        ),
        cost_estimate=pl.CostEstimate(
            flops=4 * 10**10, bytes_accessed=10**8, transcendentals=2 * 10**6
        ),
    )(*small_args, *big_args)


def finish_kernel(
    y_in,
    x_in,
    gains,
    tops,
    small,
    gq,
    gkv,
    gout,
    ggate,
    gup,
    gdown,
    head_gains,
    y_out,
    x_out,
    o_query,
    o_key,
    o_value,
    o_out,
    o_gate,
    o_up,
    o_down,
    o_left,
    o_right,
    o_per_gate,
    o_per_proj,
    o_gains,
    o_head,
    o_clip,
):
    o_query[...] = gq[...].astype(F32)
    o_key[...] = gkv[0].astype(F32)
    o_value[...] = gkv[1].astype(F32)
    o_out[...] = gout[...].astype(F32)
    o_gate[...] = ggate[...].astype(F32)
    o_up[...] = gup[...].astype(F32)
    o_down[...] = gdown[...].astype(F32)
    head_dim = head_gains.shape[1]
    quarter = small.shape[3]
    rank = o_right.shape[0]

    @pl.when(pl.program_id(0) == 0)
    def _():
        own = y_in.shape[1]
        for part in range(4):
            rows = pl.ds(part % 2 * own, own)
            y_out[part // 2, rows] = y_in[part]
            x_out[part // 2, rows] = x_in[part]

    @pl.when(pl.program_id(0) == 1)
    def _():
        for part in range(4):
            cols = pl.ds(part * quarter, quarter)
            first = small[0, part].astype(F32)
            o_right[:, cols] = first[:rank]
            o_per_proj[:, cols] = first[rank:]
            second = small[1, part].astype(F32)
            o_left[:, cols] = second[:rank]
            o_per_gate[cols] = second[rank:].T

    @pl.when(pl.program_id(0) == 1)
    def _():
        o_gains[...] = gains[pl.ds(0, 6)]
        o_head[pl.ds(0, 1)] = gains[pl.ds(6, 1), pl.ds(0, head_dim)]
        o_head[pl.ds(1, 1)] = gains[pl.ds(6, 1), pl.ds(head_dim, head_dim)]
        factor = jnp.sqrt(CLIP_LEVEL / jnp.maximum(tops[...], CLIP_LEVEL))[:, :1]
        o_clip[0] = factor * head_gains[pl.ds(0, 1)]
        o_clip[1] = factor * head_gains[pl.ds(1, 1)]


def run_finish(results, head_gains, rank):
    y_out, x_grad, g_gain, tops, small, gq, gkv, gout, ggate, gup, gdown = results
    steps = 2
    shape = jax.ShapeDtypeStruct

    def whole(array):
        dims = len(array.shape)
        return pl.BlockSpec(array.shape, lambda step: (0,) * dims)

    def rows(array):
        size = (array.shape[0] // steps, array.shape[1])
        return pl.BlockSpec(size, lambda step: (step, 0))

    own, block = y_out.shape[1:]
    key_width = gkv.shape[2]
    proj = small.shape[2] - rank
    tokens_shape = shape((2, 2 * own, block), BF)
    by_rows_out = [
        shape(gq.shape, F32),
        shape(gkv.shape[1:], F32),
        shape(gkv.shape[1:], F32),
        shape(gout.shape, F32),
        shape(ggate.shape, F32),
        shape(gup.shape, F32),
        shape(gdown.shape, F32),
    ]
    whole_out = [
        shape((rank, block), F32),
        shape((rank, block), F32),
        shape((block, proj), F32),
        shape((proj, block), F32),
        shape((6, block), F32),
        shape(head_gains.shape, F32),
        shape((2, tops.shape[0], head_gains.shape[1]), F32),
    ]
    kv_spec = pl.BlockSpec((2, block // steps, key_width), lambda step: (0, step, 0))
    return pl.pallas_call(
        finish_kernel,
        grid=(steps,),
        out_shape=[tokens_shape, tokens_shape] + by_rows_out + whole_out,
        in_specs=[whole(y_out), whole(x_grad), whole(g_gain), whole(tops), whole(small), rows(gq), kv_spec]
        + [rows(array) for array in (gout, ggate, gup, gdown)]
        + [whole(head_gains)],
        out_specs=[whole(tokens_shape)] * 2
        + [rows(array) for array in by_rows_out]
        + [whole(array) for array in whole_out],
        compiler_params=pltpu.CompilerParams(vmem_limit_bytes=VMEM_BYTES),
        cost_estimate=pl.CostEstimate(flops=10**7, bytes_accessed=3 * 10**7, transcendentals=0),
    )(*results, head_gains)


def body_pair(
    layer_in,
    per_layer_in,
    doc_lengths,
    w_query,
    w_key,
    w_value,
    w_out,
    w_gate,
    w_up,
    w_down,
    laurel_left,
    laurel_right,
    per_gate,
    per_proj,
    norm_gains,
    head_gains,
    out_grad,
):
    core, row, col = lax.axis_index("seq"), lax.axis_index("row"), lax.axis_index("col")
    rows, cols, cores = lax.axis_size("row"), lax.axis_size("col"), lax.axis_size("seq")
    seq_count = layer_in.shape[0]
    head_dim = head_gains.shape[1]
    key_width = w_key.shape[1]
    ff_part = w_gate.shape[1] // cores
    chunk = layer_in.shape[1]
    halves = rows // seq_count
    own_tokens = chunk // halves
    group_tokens = own_tokens * cores * cols
    even_col = col % 2 == 0

    rank = laurel_left.shape[1]
    saved = run_forward(
        layer_in.reshape(rows, own_tokens, -1),
        out_grad.reshape(rows, own_tokens, -1),
        norm_gains,
        (
            w_query,
            w_key,
            w_value,
            w_out,
            w_gate,
            w_up,
            w_down,
            laurel_left.T,
            laurel_right,
            per_gate,
            per_proj,
        ),
        doc_lengths,
        head_gains,
    )
    (x_own, g_own, gains, raw_q, raw_kv, q_low, kv, lse, top_tile, o_low, attn_val, lr_low, ff_val) = saved[
        :13
    ]
    laurels, p_gate, p_proj, cosine, sine, start = saved[13:19]
    w_q, w_kv_all, w_o, w_g, w_u, w_d, x_all, f_all, gate_val, up_val, turned = saved[19:]
    results = run_backward(
        (
            x_own,
            g_own,
            per_layer_in.reshape(rows, own_tokens, -1),
            gains,
            head_gains,
            attn_val,
            lr_low,
            ff_val,
            raw_q,
            raw_kv,
            q_low,
            kv,
            lse,
            top_tile,
            o_low,
            cosine,
            sine,
            start,
            laurels,
            p_gate,
            p_proj,
        ),
        (x_all, f_all, gate_val, up_val, turned, w_q, w_kv_all, w_o, w_g, w_u, w_d),
    )
    finished = list(run_finish(results[:11], head_gains, rank))
    finished[9] = finished[9].T
    return tuple(finished)


def solution(mesh):
    sizes = tuple(mesh.shape[axis] for axis in ("seq", "row", "col"))
    body = body_pair if sizes == (2, 4, 4) else body_any
    return jax.shard_map(
        body,
        mesh=mesh,
        in_specs=(
            P(None, ("seq", "col"), "row"),
            P(None, ("seq", "col"), None),
            P(),
            P("row", "col"),
            P("row", "col"),
            P("row", "col"),
            P("col", "row"),
            P("row", "col"),
            P("row", "col"),
            P("col", "row"),
            P("row", None),
            P(None, "row"),
            P("row", None),
            P(None, "row"),
            P(None, "row"),
            P(),
            P(None, ("seq", "col"), "row"),
        ),
        out_specs=(
            P(None, ("seq", "col"), "row"),
            P(None, ("seq", "col"), "row"),
            P("row", "col"),
            P("row", "col"),
            P("row", "col"),
            P("col", "row"),
            P("row", "col"),
            P("row", "col"),
            P("col", "row"),
            P("row", None),
            P(None, "row"),
            P("row", None),
            P(None, "row"),
            P(None, "row"),
            P(),
            P(),
        ),
        check_vma=False,
    )
```

```python
import math

import jax
import jax.numpy as jnp
from jax import lax
from jax.experimental import pallas as pl
from jax.experimental.pallas import tpu as pltpu
from jax.sharding import PartitionSpec as P

EPSILON = 1e-06
CLIP_LEVEL = 3.0
ROPE_BASE = 1000000.0
ROOT_HALF = 0.7071067811865476
MASK_FILL = -1e30
MESH = pl.DeviceIdType.MESH
BF = jnp.bfloat16
F32 = jnp.float32
VMEM_BYTES = 63 * 2**20
PIECES = 4
TURNED_PART = 4


def swapped(value, axis, apart):
    mask = 2**apart
    pairs = [(source, source ^ mask) for source in range(lax.axis_size(axis))]
    return lax.ppermute(value, axis, pairs)


def width_total(values):
    return lax.psum(values, "row")


def gather_tokens(values):
    return lax.all_gather(values, "col", axis=1, tiled=True)


def spread_rows(values, project):
    gathered = gather_tokens(values)
    return (gathered, lax.psum_scatter(project(gathered), "row", scatter_dimension=1, tiled=True))


def spread_cols(values, project):
    gathered = lax.all_gather(values, "row", axis=1, tiled=True)
    return (gathered, lax.psum_scatter(project(gathered), "col", scatter_dimension=1, tiled=True))


def times_right(left_side, right_side):
    return jnp.einsum("std,dn->stn", left_side, right_side, preferred_element_type=jnp.float32)


def times_back(left_side, right_side):
    return jnp.einsum("stn,dn->std", left_side, right_side, preferred_element_type=jnp.float32)


def outer_sum(left_side, right_side):
    return jnp.einsum("std,stn->dn", left_side, right_side, preferred_element_type=jnp.float32)


def norm_forward(values, gain_vec, width_all):
    square_sum = width_total(jnp.sum(values * values, axis=-1, keepdims=True))
    factor = lax.rsqrt(square_sum / width_all + EPSILON)
    normed = values * factor
    return (normed * gain_vec, normed, factor)


def norm_backward(grad_values, normed, factor, gain_vec, width_all):
    grad_normed = grad_values * gain_vec
    inner_sum = width_total(jnp.sum(grad_normed * normed, axis=-1, keepdims=True))
    result = factor * (grad_normed - normed * (inner_sum / width_all))
    return (result, jnp.sum(grad_values * normed, axis=(0, 1)))


def head_norm(values, gain_vec):
    return (
        values * lax.rsqrt(jnp.mean(values * values, axis=-1, keepdims=True) + EPSILON) * gain_vec
    )


def rotation(position, width_all):
    half_width = width_all // 2
    frequency = ROPE_BASE ** (-2.0 * jnp.arange(half_width, dtype=jnp.float32) / width_all)
    angles = position.astype(jnp.float32)[..., None] * frequency
    cosine_table = jnp.concatenate([jnp.cos(angles), jnp.cos(angles)], axis=-1)
    sine_table = jnp.concatenate([jnp.sin(angles), jnp.sin(angles)], axis=-1)
    return (cosine_table, sine_table)


def rotate(values, cosine_table, sine_table):
    half_width = values.shape[-1] // 2
    turned = jnp.concatenate([-values[..., half_width:], values[..., :half_width]], axis=-1)
    return values * cosine_table + turned * sine_table


def doc_places(doc_lengths, first_place, place_count):
    upto = jnp.tril(jnp.ones((doc_lengths.shape[1], doc_lengths.shape[1]), jnp.int32))
    doc_ends = jnp.sum(doc_lengths[:, None, :] * upto[None], axis=2)
    places = first_place + jnp.arange(place_count, dtype=jnp.int32)
    before = (doc_ends[:, None, :] <= places[None, :, None]).astype(jnp.int32)
    segment = jnp.sum(before, axis=2)
    doc_start = jnp.sum(before * doc_lengths[:, None, :], axis=2)
    return (segment, places, places[None, :] - doc_start)


def block_scores(queries, keys_all, block_start, block_size, query_seg, query_place, key_seg):
    keys_part = lax.dynamic_slice_in_dim(keys_all, block_start, block_size, 1)
    scores = jnp.einsum("sqhd,skd->shqk", queries, keys_part, preferred_element_type=jnp.float32)
    seg_part = lax.dynamic_slice_in_dim(key_seg, block_start, block_size, 1)
    key_place = block_start + jnp.arange(block_size, dtype=jnp.int32)
    allowed = (query_seg[:, None, :, None] == seg_part[:, None, None, :]) & (
        key_place[None, None, None, :] <= query_place[None, None, :, None]
    )
    return (scores, allowed)


def body_any(
    layer_in,
    per_layer_in,
    doc_lengths,
    w_query,
    w_key,
    w_value,
    w_out,
    w_gate,
    w_up,
    w_down,
    laurel_left,
    laurel_right,
    per_gate,
    per_proj,
    norm_gains,
    head_gains,
    out_grad,
):
    seq_count = layer_in.shape[0]
    width_all = layer_in.shape[2] * lax.axis_size("row")
    head_dim = head_gains.shape[1]
    heads_here = w_query.shape[1] // head_dim
    heads_all = heads_here * lax.axis_size("col")
    key_width = w_key.shape[1]
    ff_here = w_gate.shape[1]
    local_len = layer_in.shape[1] * lax.axis_size("col")
    tokens_row = local_len // lax.axis_size("row")
    seq_len = local_len * lax.axis_size("seq")
    col_index = lax.axis_index("col")
    even_col = col_index % 2 == 0
    q_width = heads_here * head_dim
    partner_key, partner_value = swapped((w_key, w_value), "col", 0)
    key_head = jnp.where(
        even_col,
        jnp.concatenate([w_key, partner_key], axis=1),
        jnp.concatenate([partner_key, w_key], axis=1),
    )
    value_head = jnp.where(
        even_col,
        jnp.concatenate([w_value, partner_value], axis=1),
        jnp.concatenate([partner_value, w_value], axis=1),
    )
    w_heads = jnp.concatenate([w_query, key_head, value_head], axis=1)
    w_back = jnp.concatenate([w_query, w_key, w_value], axis=1)
    w_gate_up = jnp.concatenate([w_gate, w_up], axis=1)
    inputs = layer_in.astype(jnp.float32)
    x_norm, x_normed, x_factor = norm_forward(inputs, norm_gains[0], width_all)
    x_low = x_norm.astype(jnp.bfloat16)
    x_rows, head_raw = spread_rows(x_low, lambda gathered: times_right(gathered, w_heads))
    q_raw = head_raw[:, :, :q_width].reshape(seq_count, tokens_row, heads_here, head_dim)
    k_raw = head_raw[:, :, q_width : q_width + head_dim]
    v_raw = head_raw[:, :, q_width + head_dim :]
    query_seg, query_place, query_pos = doc_places(
        doc_lengths, lax.axis_index(("seq", "row")) * tokens_row, tokens_row
    )
    key_seg, unused_place, unused_pos = doc_places(doc_lengths, 0, seq_len)
    cosine_table, sine_table = rotation(query_pos, head_dim)

    def query_prep(raw_part, gain_vec):
        return rotate(
            head_norm(raw_part, gain_vec), cosine_table[:, :, None], sine_table[:, :, None]
        )

    def key_prep(raw_part, gain_vec):
        return rotate(head_norm(raw_part, gain_vec), cosine_table, sine_table)

    def value_prep(raw_part):
        return head_norm(raw_part, 1.0)

    q_rot, query_back = jax.vjp(query_prep, q_raw, head_gains[0])
    k_rot, key_back = jax.vjp(key_prep, k_raw, head_gains[1])
    v_normed, value_back = jax.vjp(value_prep, v_raw)
    q_low = q_rot.astype(jnp.bfloat16)
    keys_all, values_all = (
        lax.all_gather(k_rot.astype(jnp.bfloat16), ("seq", "row"), axis=1, tiled=True),
        lax.all_gather(v_normed.astype(jnp.bfloat16), ("seq", "row"), axis=1, tiled=True),
    )
    block_size = min(512, seq_len)
    block_count = seq_len // block_size
    blocks = jnp.arange(block_count, dtype=jnp.int32)

    def scored(block_index):
        return block_scores(
            q_low, keys_all, block_index * block_size, block_size, query_seg, query_place, key_seg
        )

    def values_at(block_index):
        return lax.dynamic_slice_in_dim(values_all, block_index * block_size, block_size, 1)

    def stats_step(carry, block_index):
        row_top, row_total = carry
        scores, allowed = scored(block_index)
        new_top = jnp.maximum(row_top, jnp.max(jnp.where(allowed, scores, MASK_FILL), axis=3))
        weights = jnp.where(allowed, jnp.exp(scores - new_top[..., None]), 0.0)
        row_total = row_total * jnp.exp(row_top - new_top) + jnp.sum(weights, axis=3)
        return ((new_top, row_total), None)

    start_top = jnp.full((seq_count, heads_here, tokens_row), MASK_FILL, jnp.float32)
    (row_top, row_total), unused = lax.scan(
        stats_step, (start_top, jnp.zeros_like(start_top)), blocks
    )
    log_total = row_top + jnp.log(row_total)

    def probs_at(block_index):
        scores, allowed = scored(block_index)
        return jnp.where(allowed, jnp.exp(scores - log_total[..., None]), 0.0)

    def out_step(total_out, block_index):
        probs_low = probs_at(block_index).astype(jnp.bfloat16)
        total_out = total_out + jnp.einsum(
            "shqk,skd->sqhd", probs_low, values_at(block_index), preferred_element_type=jnp.float32
        )
        return (total_out, None)

    attended, unused = lax.scan(
        out_step, jnp.zeros((seq_count, tokens_row, heads_here, head_dim), jnp.float32), blocks
    )
    o_low = attended.astype(jnp.bfloat16).reshape(seq_count, tokens_row, q_width)
    head_slots = lax.dynamic_update_slice_in_dim(
        jnp.full((heads_all,), MASK_FILL, jnp.float32),
        jnp.max(row_top, axis=(0, 2)),
        col_index * heads_here,
        0,
    )
    logit_top = lax.pmax(head_slots, ("seq", "row", "col"))
    o_rows, attn_val = spread_cols(o_low, lambda gathered: times_right(gathered, w_out))
    attn_norm, attn_normed, attn_factor = norm_forward(attn_val, norm_gains[1], width_all)
    h_one = inputs + attn_norm
    lr_low = width_total(times_right(x_low, laurel_left)).astype(jnp.bfloat16)
    lo_val = times_right(lr_low, laurel_right)
    lo_norm, lo_normed, lo_factor = norm_forward(lo_val, norm_gains[2], width_all)
    h_two = (h_one + (x_norm + lo_norm)) * ROOT_HALF
    f_norm, f_normed, f_factor = norm_forward(h_two, norm_gains[3], width_all)
    f_low = f_norm.astype(jnp.bfloat16)
    f_rows, gate_up = spread_rows(f_low, lambda gathered: times_right(gathered, w_gate_up))
    gate_val = gate_up[:, :, :ff_here]
    up_val = gate_up[:, :, ff_here:]

    def geglu(gate_part, up_part):
        return jax.nn.gelu(gate_part, approximate=True) * up_part

    hidden, geglu_back = jax.vjp(geglu, gate_val, up_val)
    hid_low = hidden.astype(jnp.bfloat16)
    hid_rows, ff_val = spread_cols(hid_low, lambda gathered: times_right(gathered, w_down))
    ff_norm, ff_normed, ff_factor = norm_forward(ff_val, norm_gains[4], width_all)
    h_three = h_two + ff_norm
    h_low = h_three.astype(jnp.bfloat16)
    pg_val = width_total(times_right(h_low, per_gate))
    per_input = per_layer_in.astype(jnp.float32)

    def per_mix(gate_part):
        return jax.nn.gelu(gate_part, approximate=True) * per_input

    gp_val, per_back = jax.vjp(per_mix, pg_val)
    gp_low = gp_val.astype(jnp.bfloat16)
    pp_val = times_right(gp_low, per_proj)
    pp_norm, pp_normed, pp_factor = norm_forward(pp_val, norm_gains[5], width_all)
    layer_out = (h_three + pp_norm).astype(jnp.bfloat16)
    grad_top = out_grad.astype(jnp.float32)
    d_pp, gain_five = norm_backward(grad_top, pp_normed, pp_factor, norm_gains[5], width_all)
    d_pp_low = d_pp.astype(jnp.bfloat16)
    grad_per_proj = outer_sum(gp_low, d_pp_low)
    (d_pg,) = per_back(width_total(times_back(d_pp_low, per_proj)))
    d_pg_low = d_pg.astype(jnp.bfloat16)
    grad_per_gate = outer_sum(h_low, d_pg_low)
    d_three = grad_top + times_back(d_pg_low, per_gate)
    d_ff, gain_four = norm_backward(d_three, ff_normed, ff_factor, norm_gains[4], width_all)
    d_ff_low = d_ff.astype(jnp.bfloat16)
    dff_rows, d_hidden = spread_rows(d_ff_low, lambda gathered: times_back(gathered, w_down))
    grad_down = outer_sum(hid_rows, dff_rows)
    d_gate, d_up = geglu_back(d_hidden)
    d_gate_up = jnp.concatenate([d_gate, d_up], axis=2).astype(jnp.bfloat16)
    dgu_rows, d_f_low = spread_cols(d_gate_up, lambda gathered: times_back(gathered, w_gate_up))
    grad_gate_up = outer_sum(f_rows, dgu_rows)
    d_f, gain_three = norm_backward(d_f_low, f_normed, f_factor, norm_gains[3], width_all)
    d_half = (d_three + d_f) * ROOT_HALF
    d_lo, gain_two = norm_backward(d_half, lo_normed, lo_factor, norm_gains[2], width_all)
    d_lo_low = d_lo.astype(jnp.bfloat16)
    grad_laurel_right = outer_sum(lr_low, d_lo_low)
    d_lr_low = width_total(times_back(d_lo_low, laurel_right)).astype(jnp.bfloat16)
    grad_laurel_left = outer_sum(x_low, d_lr_low)
    d_attn, gain_one = norm_backward(d_half, attn_normed, attn_factor, norm_gains[1], width_all)
    d_attn_low = d_attn.astype(jnp.bfloat16)
    dattn_rows, d_o = spread_rows(d_attn_low, lambda gathered: times_back(gathered, w_out))
    grad_w_out = outer_sum(o_rows, dattn_rows)
    d_o_low = d_o.astype(jnp.bfloat16).reshape(seq_count, tokens_row, heads_here, head_dim)

    def delta_step(total_delta, block_index):
        d_probs = jnp.einsum(
            "sqhd,skd->shqk", d_o_low, values_at(block_index), preferred_element_type=jnp.float32
        )
        return (total_delta + jnp.sum(probs_at(block_index) * d_probs, axis=3), None)

    row_delta, unused = lax.scan(delta_step, jnp.zeros_like(log_total), blocks)

    def grad_step(carry, block_index):
        d_query, d_keys, d_values = carry
        block_start = block_index * block_size
        prob_vals = probs_at(block_index)
        d_probs = jnp.einsum(
            "sqhd,skd->shqk", d_o_low, values_at(block_index), preferred_element_type=jnp.float32
        )
        d_scores = (prob_vals * (d_probs - row_delta[..., None])).astype(jnp.bfloat16)
        keys_part = lax.dynamic_slice_in_dim(keys_all, block_start, block_size, 1)
        d_query = d_query + jnp.einsum(
            "shqk,skd->sqhd", d_scores, keys_part, preferred_element_type=jnp.float32
        )
        key_part = jnp.einsum("shqk,sqhd->skd", d_scores, q_low, preferred_element_type=jnp.float32)
        value_part = jnp.einsum(
            "shqk,sqhd->skd",
            prob_vals.astype(jnp.bfloat16),
            d_o_low,
            preferred_element_type=jnp.float32,
        )
        d_keys = lax.dynamic_update_slice_in_dim(d_keys, key_part, block_start, 1)
        d_values = lax.dynamic_update_slice_in_dim(d_values, value_part, block_start, 1)
        return ((d_query, d_keys, d_values), None)

    zero_keys = jnp.zeros((seq_count, seq_len, head_dim), jnp.float32)
    (d_query, d_keys, d_values), unused = lax.scan(
        grad_step, (jnp.zeros_like(attended), zero_keys, zero_keys), blocks
    )
    own_keys, own_values = (
        lax.psum_scatter(d_keys, ("seq", "row"), scatter_dimension=1, tiled=True),
        lax.psum_scatter(d_values, ("seq", "row"), scatter_dimension=1, tiled=True),
    )
    pair_keys, pair_values = swapped((own_keys, own_values), "col", 0)
    d_q_raw, d_q_gain = query_back(d_query)
    d_k_raw, d_k_gain = key_back(own_keys + pair_keys)
    (d_v_raw,) = value_back(own_values + pair_values)
    key_offset = col_index % 2 * key_width
    d_heads_low = jnp.concatenate(
        [
            d_q_raw.reshape(seq_count, tokens_row, q_width),
            lax.dynamic_slice_in_dim(d_k_raw, key_offset, key_width, 2),
            lax.dynamic_slice_in_dim(d_v_raw, key_offset, key_width, 2),
        ],
        axis=2,
    ).astype(jnp.bfloat16)
    dhead_rows, d_x_heads = spread_cols(d_heads_low, lambda gathered: times_back(gathered, w_back))
    grad_heads = outer_sum(x_rows, dhead_rows)
    d_x_low = d_x_heads + times_back(d_lr_low, laurel_left)
    d_x_part, gain_zero = norm_backward(
        d_half + d_x_low, x_normed, x_factor, norm_gains[0], width_all
    )
    grad_in = (d_half + d_x_part).astype(jnp.bfloat16)
    head_part = width_total(jnp.stack([d_q_gain, d_k_gain * 0.5]))
    sum_heads, sum_out, sum_gate_up, sum_down = lax.psum(
        (grad_heads, grad_w_out, grad_gate_up, grad_down), "seq"
    )
    sum_left, sum_right, sum_per_gate, sum_per_proj, sum_gains, sum_head_gains = lax.psum(
        (
            grad_laurel_left,
            grad_laurel_right,
            grad_per_gate,
            grad_per_proj,
            jnp.stack([gain_zero, gain_one, gain_two, gain_three, gain_four, gain_five]),
            head_part,
        ),
        ("seq", "col"),
    )
    clip_factor = jnp.sqrt(CLIP_LEVEL / jnp.maximum(logit_top, CLIP_LEVEL))
    clipped_gains = jnp.stack(
        [
            clip_factor[:, None] * head_gains[0][None, :],
            clip_factor[:, None] * head_gains[1][None, :],
        ]
    )
    return (
        layer_out,
        grad_in,
        sum_heads[:, :q_width],
        sum_heads[:, q_width : q_width + key_width],
        sum_heads[:, q_width + key_width :],
        sum_out,
        sum_gate_up[:, :ff_here],
        sum_gate_up[:, ff_here:],
        sum_down,
        sum_left,
        sum_right,
        sum_per_gate,
        sum_per_proj,
        sum_gains,
        sum_head_gains,
        clipped_gains,
    )


def group_gather(values):
    return lax.all_gather(values, ("seq", "col"), axis=0, tiled=True)


def group_scatter(partial):
    return lax.psum_scatter(
        partial.astype(jnp.bfloat16), ("seq", "col"), scatter_dimension=0, tiled=True
    ).astype(jnp.float32)


def to_owner(values):
    seq_count, tokens, width = values.shape
    rows = lax.axis_size("row")
    parts = values.reshape(rows, seq_count * tokens // rows, width)
    moved = lax.all_to_all(parts, "row", split_axis=0, concat_axis=0)
    return moved.transpose(1, 0, 2).reshape(parts.shape[1], rows * width)


def from_owner(values, seq_count):
    tokens, width = values.shape
    rows = lax.axis_size("row")
    parts = values.reshape(tokens, rows, width // rows).transpose(1, 0, 2)
    moved = lax.all_to_all(parts, "row", split_axis=0, concat_axis=0)
    return moved.reshape(seq_count, rows * tokens // seq_count, width // rows)


def mm(left_side, right_side):
    return jnp.dot(left_side, right_side, preferred_element_type=jnp.float32)


def mm_nt(left_side, right_side):
    return lax.dot_general(
        left_side, right_side, (((1,), (1,)), ((), ())), preferred_element_type=jnp.float32
    )


def mm_tn(left_side, right_side):
    return lax.dot_general(
        left_side, right_side, (((0,), (0,)), ((), ())), preferred_element_type=jnp.float32
    )


def rms(values):
    factor = lax.rsqrt(jnp.mean(values * values, axis=-1, keepdims=True) + EPSILON)
    return values * factor, factor


def rms_back(grad_values, normed, factor, gain_vec):
    grad_normed = grad_values * gain_vec
    inner = jnp.mean(grad_normed * normed, axis=-1, keepdims=True)
    return (
        factor * (grad_normed - normed * inner),
        jnp.sum(grad_values * normed, axis=0, keepdims=True),
    )


def gather_rows(values, axis):
    return lax.all_gather(values, "row", axis=axis, tiled=True)


def scatter_rows(values, axis):
    return lax.psum_scatter(
        values.astype(jnp.bfloat16), "row", scatter_dimension=axis, tiled=True
    ).astype(jnp.float32)


def both_cores(values, axis):
    return lax.all_gather(values, "seq", axis=axis, tiled=True)


def remote(src, dst, send_sem, recv_sem, device):
    return pltpu.make_async_remote_copy(
        src_ref=src,
        dst_ref=dst,
        send_sem=send_sem,
        recv_sem=recv_sem,
        device_id=device,
        device_id_type=MESH,
    )


def greet(core, row, col):
    barrier = pltpu.get_barrier_semaphore()
    near = [(core, row ^ 1, col), (core, row ^ 2, col), (core, row ^ 3, col), (1 - core, row, col)]
    for device in near:
        pl.semaphore_signal(barrier, inc=1, device_id=device, device_id_type=MESH)

    @pl.when(col > 0)
    def _():
        pl.semaphore_signal(barrier, inc=1, device_id=(core, row, col - 1), device_id_type=MESH)

    @pl.when(col < 3)
    def _():
        pl.semaphore_signal(barrier, inc=1, device_id=(core, row, col + 1), device_id_type=MESH)

    ends = jnp.where((col == 0) | (col == 3), 1, 2)
    pl.semaphore_wait(barrier, 4 + ends)


class Gather:
    def __init__(self, place, buf, rows, sems):
        self.core, self.row, self.col = place
        self.buf, self.rows = buf, rows
        self.send_z, self.recv_z, self.send_s, self.recv_s = sems

    def part(self, core, col, piece):
        rows = self.rows // PIECES
        first = (core * 4 + col) * self.rows + piece * rows
        return self.buf.at[pl.ds(pl.multiple_of(first, rows), rows)]

    def hop(self, dist, right, piece):
        part = self.part(self.core, self.col - dist if right else self.col + dist, piece)
        lane = ((0 if right else 3) + dist) * PIECES + piece
        return remote(
            part,
            part,
            self.send_z.at[lane],
            self.recv_z.at[lane],
            (self.core, self.row, self.col + (1 if right else -1)),
        )

    def came(self, dist, right, piece):
        part = self.part(self.core, self.col - dist if right else self.col + dist, piece)
        lane = ((0 if right else 3) + dist - 1) * PIECES + piece
        return remote(
            part, part, self.send_z.at[lane], self.recv_z.at[lane], (self.core, self.row, self.col)
        )

    def to_sibling(self, col, piece, core=None):
        part = self.part(self.core if core is None else core, col, piece)
        lane = col * PIECES + piece
        return remote(
            part,
            part,
            self.send_s.at[lane],
            self.recv_s.at[lane],
            (1 - self.core, self.row, self.col),
        )

    def start(self):
        col = self.col
        for piece in range(PIECES):

            @pl.when(col < 3)
            def _():
                self.hop(0, True, piece).start()

            @pl.when(col > 0)
            def _():
                self.hop(0, False, piece).start()

        for piece in range(PIECES):
            self.to_sibling(col, piece).start()

    def forward(self, work=()):
        col = self.col
        work = list(work)
        for dist in (1, 2, 3):
            for piece in range(PIECES):

                @pl.when(col >= dist)
                def _():
                    self.came(dist, True, piece).wait_recv()
                    if dist < 3:

                        @pl.when(col < 3)
                        def _():
                            self.hop(dist, True, piece).start()

                    self.to_sibling(col - dist, piece).start()

                @pl.when(col + dist <= 3)
                def _():
                    self.came(dist, False, piece).wait_recv()
                    if dist < 3:

                        @pl.when(col > 0)
                        def _():
                            self.hop(dist, False, piece).start()

                    self.to_sibling(col + dist, piece).start()

            if work:
                work.pop(0)()

    def finish(self):
        for piece in range(PIECES):
            for col in range(4):
                self.to_sibling(col, piece, 1 - self.core).wait_recv()

    def drain(self):
        for piece in range(PIECES):
            for col in range(4):
                self.to_sibling(col, piece).wait_send()
            for dist in (0, 1, 2):

                @pl.when((self.col < 3) & (self.col >= dist))
                def _():
                    self.hop(dist, True, piece).wait_send()

                @pl.when((self.col > 0) & (self.col + dist <= 3))
                def _():
                    self.hop(dist, False, piece).wait_send()


class Scatter:
    def __init__(self, place, rows, bufs, sems):
        self.core, self.row, self.col = place
        self.rows = rows
        self.give, self.keep, self.got, self.sent, self.left, self.right = bufs
        self.send_z, self.recv_z, self.send_s, self.recv_s = sems

    def sibling(self, dest):
        rows = pl.ds(dest * self.rows, self.rows)
        return remote(
            self.give.at[rows],
            self.got.at[rows],
            self.send_s.at[dest],
            self.recv_s.at[dest],
            (1 - self.core, self.row, self.col),
        )

    def start(self):
        for dest in (3, 0, 2, 1):
            self.sibling(dest).start()

    def piece(self, piece):
        rows = self.rows // PIECES
        return pl.ds(piece * rows, rows)

    def mine(self, dest, piece):
        count = self.rows // PIECES
        rows = pl.ds(dest * self.rows + piece * count, count)
        return self.keep[rows].astype(F32) + self.got[rows].astype(F32)

    def inbox(self, dest, right):
        return self.left.at[dest - 1] if right else self.right.at[dest]

    def hop(self, dest, right, piece):
        lane = ((0 if right else 4) + dest) * PIECES + piece
        return remote(
            self.sent.at[dest, self.piece(piece)],
            self.inbox(dest, right).at[self.piece(piece)],
            self.send_z.at[lane],
            self.recv_z.at[lane],
            (self.core, self.row, self.col + (1 if right else -1)),
        )

    def step(self, col, dest, right, piece):
        rows = self.piece(piece)
        if piece == 0:
            self.sibling(dest).wait_recv()
        total = self.mine(dest, piece)
        if col != (0 if right else 3):
            self.hop(dest, right, piece).wait_recv()
            total = total + self.inbox(dest, right)[rows].astype(F32)
        self.sent[dest, rows] = total.astype(BF)
        self.hop(dest, right, piece).start()

    def steps(self, col):
        if col > 1:
            return [
                [(3 - dest, not right, piece) for dest, right, piece in part]
                for part in self.steps(3 - col)
            ]
        full = lambda dest, right: [(dest, right, piece) for piece in range(PIECES)]
        if col == 0:
            return [full(3, True) + full(2, True), full(1, True)]
        near, far = full(3, True) + full(2, True), full(0, False)
        lag, order = PIECES - 1, []
        for index, item in enumerate(near):
            order.append(item)
            if index + 1 >= lag and far:
                order.append(far.pop(0))
        cut = PIECES + 2
        return [order[:cut], order[cut:] + far]

    def run(self, result, work=()):
        work = list(work)
        for part in range(2):
            for col in range(4):

                @pl.when(self.col == col)
                def _():
                    for dest, right, piece in self.steps(col)[part]:
                        self.step(col, dest, right, piece)

            for call in work[part : part + 1]:
                call()
        for call in work[2:]:
            call()
        for dest in range(4):

            @pl.when(self.col == dest)
            def _():
                self.sibling(dest).wait_recv()
                for piece in range(PIECES):
                    rows = self.piece(piece)
                    total = self.mine(dest, piece)
                    for right in (True, False):
                        if dest != (0 if right else 3):
                            self.hop(dest, right, piece).wait_recv()
                            total = total + self.inbox(dest, right)[rows].astype(F32)
                    result[rows] = total

    def drain(self):
        for dest in range(4):
            self.sibling(dest).wait_send()
        for piece in range(PIECES):
            for dest in (1, 2, 3):

                @pl.when(self.col < dest)
                def _():
                    self.hop(dest, True, piece).wait_send()

                @pl.when(self.col > 3 - dest)
                def _():
                    self.hop(3 - dest, False, piece).wait_send()


class RowGather:
    def __init__(self, place, source, block, halves, sems, ways=(1, 2)):
        self.core, self.row, self.col = place
        self.source, self.block, self.halves = source, block, halves
        self.ways = ways
        self.sems = sems

    def neighbour(self, mask):
        return (self.core, self.row ^ mask, self.col)

    def own(self):
        return pltpu.make_async_copy(self.source, self.block(self.row), self.sems.at[8])

    def first(self, mask, block=None):
        lane = mask - 1
        return remote(
            self.source,
            self.block(self.row) if block is None else block,
            self.sems.at[lane],
            self.sems.at[4 + lane],
            self.neighbour(mask),
        )

    def across(self, index, mask):
        return self.block(index) if len(self.ways) == 1 else self.halves(index)[mask - 1]

    def second(self, mask):
        part = self.across(self.row ^ (3 - mask), mask)
        return remote(
            part, part, self.sems.at[1 + mask], self.sems.at[5 + mask], self.neighbour(mask)
        )

    def start(self):
        self.first(1).start()
        self.first(2).start()
        self.own().start()

    def finish_first(self):
        for mask in (1, 2):
            self.first(mask, self.block(self.row ^ mask)).wait_recv()
            self.first(mask).wait_send()
        self.own().wait()

    def forward(self):
        for mask in (1, 2):
            self.first(mask, self.block(self.row ^ mask)).wait_recv()
            if 3 - mask in self.ways:
                self.second(3 - mask).start()

    def finish(self):
        for mask in self.ways:
            part = self.across(self.row ^ 3, mask)
            remote(
                part, part, self.sems.at[1 + mask], self.sems.at[5 + mask], self.neighbour(mask)
            ).wait_recv()
        self.own().wait()
        for mask in (1, 2):
            self.first(mask).wait_send()
        for mask in self.ways:
            self.second(mask).wait_send()


def by_rows(buf, block_rows):
    half = block_rows // 2

    def block(index):
        return buf.at[pl.ds(pl.multiple_of(index * block_rows, block_rows), block_rows)]

    def halves(index):
        return [
            buf.at[pl.ds(pl.multiple_of(index * block_rows + part * half, half), half)]
            for part in range(2)
        ]

    return block, halves


def by_core_rows(core):
    def split(buf, block_rows):
        own = block_rows // 2

        def piece(index, part, count):
            first = index * block_rows + core * own + part * (own // count)
            return buf.at[pl.ds(pl.multiple_of(first, own // count), own // count)]

        return (
            lambda index: piece(index, 0, 1),
            lambda index: [piece(index, part, 2) for part in range(2)],
        )

    return split


def by_half_cols(part):
    def split(buf, block_cols):
        own, rows = block_cols // 2, buf.shape[0] // 2

        def cols(index):
            return pl.ds(pl.multiple_of(index * block_cols + part * own, own), own)

        return (
            lambda index: buf.at[:, cols(index)],
            lambda index: [buf.at[pl.ds(piece * rows, rows), cols(index)] for piece in range(2)],
        )

    return split


def by_cols(buf, block_cols):
    rows = buf.shape[0] // 2

    def block(index):
        return buf.at[:, pl.ds(pl.multiple_of(index * block_cols, block_cols), block_cols)]

    def halves(index):
        cols = pl.ds(pl.multiple_of(index * block_cols, block_cols), block_cols)
        return [buf.at[pl.ds(part * rows, rows), cols] for part in range(2)]

    return block, halves


def gelu_both(values):
    inner = 0.7978845608028654 * (values + 0.044715 * values * values * values)
    bend = jnp.tanh(inner)
    slope = 0.7978845608028654 * (1.0 + 3.0 * 0.044715 * values * values)
    return 0.5 * values * (1.0 + bend), 0.5 * (1.0 + bend) + 0.5 * values * (1.0 - bend * bend) * slope


def head_parts(raw, gain, cosine, sine):
    factor = lax.rsqrt(jnp.mean(raw * raw, axis=1, keepdims=True) + EPSILON)
    half = raw.shape[1] // 2
    scaled = raw * factor * gain
    first, second = scaled[:, :half], scaled[:, half:]
    return jnp.concatenate([first * cosine - second * sine, second * cosine + first * sine], axis=1)


def forward_kernel(
    x_in,
    g_in,
    gains_in,
    w_query,
    w_key,
    w_value,
    w_out,
    w_gate,
    w_up,
    w_down,
    laurel_left,
    laurel_right,
    per_gate,
    per_proj,
    lengths,
    head_gains,
    x_own,
    g_own,
    gains,
    raw_q,
    raw_kv,
    q_low,
    kv,
    lse,
    top,
    o_low,
    attn_val,
    lr_low,
    ff_val,
    laurels,
    vpg,
    vpp,
    cosine,
    sine,
    start,
    wq_all,
    wkv_all,
    wo_all,
    wg_all,
    wu_all,
    wd_all,
    xg_all,
    fg_all,
    gate_all,
    up_all,
    turned_all,
    w_kv_pair,
    laurel_own,
    gains_pad,
    vq,
    vkv,
    vo,
    vg,
    vu,
    vd,
    xg,
    fg,
    gate,
    up,
    hid,
    turned,
    give,
    keep,
    got,
    sent,
    left,
    right,
    give2,
    keep2,
    got2,
    sent2,
    left2,
    right2,
    half_sum,
    row_sems,
    z_send,
    z_recv,
    s_send,
    s_recv,
    misc_send,
    misc_recv,
    out_sems,
):
    core, row, col = lax.axis_index("seq"), lax.axis_index("row"), lax.axis_index("col")
    place = (core, row, col)
    own_tokens, width = x_own.shape
    block = x_in.shape[2]
    head_dim = head_gains.shape[1]
    tokens = xg.shape[0]
    ff_part = gate.shape[1]
    chunk = 2 * own_tokens
    key_width = w_key.shape[1]
    half = row % 2
    half_block = block // 2
    halves2 = (give2, keep2, got2, sent2, left2, right2)
    greet(core, row, col)

    my_cols = pl.ds(pl.multiple_of(row * block, block), block)

    def hand_over(mask):
        return remote(
            x_in.at[row ^ mask],
            x_own.at[:, my_cols],
            misc_send.at[mask],
            misc_recv.at[mask],
            (core, row ^ mask, col),
        )

    def hand_grad(mask):
        return remote(
            g_in.at[row ^ mask],
            g_own.at[:, my_cols],
            misc_send.at[11 + mask],
            misc_recv.at[11 + mask],
            (core, row ^ mask, col),
        )

    def hand_gains(mask):
        return remote(
            gains_pad,
            gains.at[:, my_cols],
            misc_send.at[3 + mask],
            misc_recv.at[3 + mask],
            (core, row ^ mask, col),
        )

    for mask in (3, 1, 2):
        hand_over(mask).start()
    gains_pad[pl.ds(0, 6)] = gains_in[...]
    gains_pad[pl.ds(6, 2)] = jnp.zeros((2, block), F32)
    for mask in (3, 1, 2):
        hand_gains(mask).start()
    x_own[:, my_cols] = x_in[row]
    g_own[:, my_cols] = g_in[row]
    gains[:, my_cols] = gains_pad[...]

    pair_cols = pl.ds(pl.multiple_of(col % 2 * key_width, key_width), key_width)
    w_kv_own = w_kv_pair.at[:, pair_cols]
    w_kv_own[...] = jnp.where(core == 0, w_key[...].astype(F32), w_value[...].astype(F32)).astype(BF)
    pair = remote(w_kv_own, w_kv_own, misc_send.at[7], misc_recv.at[7], (core, row, col ^ 1))
    pair.start()

    lanes = iter(range(32))

    def rows_of(source, buf, split=by_rows, size=block, ways=(1, 2)):
        block_of, halves_of = split(buf, size)
        return RowGather(place, source, block_of, halves_of, row_sems.at[next(lanes)], ways)

    tile = 256
    core_head = pl.ds(pl.multiple_of(core * head_dim, head_dim), head_dim)

    def core_tile(index):
        return pl.ds(pl.multiple_of(core * ff_part + index * tile, tile), tile)

    get_q = rows_of(w_query.at[:, core_head], vq)
    get_kv = rows_of(w_kv_pair, vkv)
    get_o = rows_of(w_out.at[core_head], vo, by_cols, ways=(2,))
    laurel_own[...] = jnp.where(
        core == 0, laurel_left[...].astype(F32), laurel_right[...].astype(F32)
    ).astype(BF)
    get_laurel = [rows_of(laurel_own, laurels.at[core], by_cols)]
    per_rows, per_cols = per_gate.shape[0] // 2, per_proj.shape[0] // 2
    own_rows = pl.ds(pl.multiple_of(core * per_rows, per_rows), per_rows)
    own_cols = pl.ds(pl.multiple_of(core * per_cols, per_cols), per_cols)
    get_per = [
        rows_of(per_gate.at[own_rows], vpg, by_core_rows(core)),
        rows_of(per_proj.at[own_cols], vpp.at[own_cols], by_cols),
    ]
    tiles = ff_part // tile
    get_gu = [
        [
            rows_of(whole.at[:, core_tile(index)], buf.at[:, pl.ds(index * tile, tile)])
            for whole, buf in ((w_gate, vg), (w_up, vu))
        ]
        for index in range(tiles)
    ]
    half_ff = ff_part // 2
    core_ff = pl.ds(pl.multiple_of(core * ff_part, ff_part), ff_part)
    get_d = [
        rows_of(w_down.at[core_ff, pl.ds(part * (block // 2), block // 2)], vd, by_half_cols(part))
        for part in range(2)
    ]

    def per_parts(which, lane):
        parts = [
            vpg.at[pl.ds(pl.multiple_of(index * block + which * per_rows, per_rows), per_rows)]
            for index in range(4)
        ]
        parts.append(vpp.at[pl.ds(pl.multiple_of(which * per_cols, per_cols), per_cols)])
        return list(enumerate(parts, lane))

    def begin(jobs):
        for job in jobs:
            job.start()

    def push(jobs):
        for job in jobs:
            job.forward()

    def complete(jobs):
        for job in jobs:
            job.finish()

    get_q.start()
    pair.wait_recv()
    get_kv.start()

    for mask in (1, 2, 3):
        remote(
            x_in.at[row],
            x_own.at[:, pl.ds(pl.multiple_of((row ^ mask) * block, block), block)],
            misc_send.at[mask],
            misc_recv.at[mask],
            (core, row, col),
        ).wait_recv()
        remote(
            gains_pad,
            gains.at[:, pl.ds(pl.multiple_of((row ^ mask) * block, block), block)],
            misc_send.at[3 + mask],
            misc_recv.at[3 + mask],
            (core, row, col),
        ).wait_recv()

    def own_norm():
        values = x_own[...].astype(F32)
        factor = lax.rsqrt(jnp.mean(values * values, axis=1, keepdims=True) + EPSILON)
        return values, values * factor * gains[pl.ds(0, 1)]

    mine = pl.ds(pl.multiple_of((core * 4 + col) * own_tokens, own_tokens), own_tokens)
    xg[mine] = own_norm()[1].astype(BF)
    sems = lambda lane: (z_send.at[lane], z_recv.at[lane], s_send.at[lane], s_recv.at[lane])
    gather_x = Gather(place, xg, own_tokens, sems(0))
    gather_x.start()

    def doc_tables():
        token = lax.broadcasted_iota(jnp.int32, (tokens, 1), 0)
        token_place = token // own_tokens * chunk + half * own_tokens + token % own_tokens
        doc_start, doc_end = jnp.zeros((tokens, 1), jnp.int32), 0
        for doc in range(lengths.shape[1]):
            length = lengths[row // 2, doc]
            doc_end = doc_end + length
            doc_start = doc_start + jnp.where(token_place >= doc_end, length, 0)
        start[...] = doc_start
        pair_index = lax.broadcasted_iota(jnp.int32, (1, head_dim // 2), 1).astype(F32)
        frequency = jnp.exp(pair_index * (-2.0 * math.log(ROPE_BASE) / head_dim))
        angles = (token_place - doc_start).astype(F32) * frequency
        sine[...] = angles
        cosine[...] = jnp.cos(angles)

    gather_x.forward(
        [
            doc_tables,
            lambda: (push([get_q, get_kv]), begin([get_o])),
        ]
    )
    gather_x.finish()
    sine[...] = jnp.sin(sine[...])
    complete([get_q, get_kv])

    raw_q[...] = mm(xg[...], vq[...])
    raw_kv[...] = mm(xg[...], vkv[...])
    q_low[...] = head_parts(raw_q[...], head_gains[pl.ds(0, 1)], cosine[...], sine[...]).astype(BF)
    is_key = core == 0
    kv_here = head_parts(
        raw_kv[...],
        jnp.where(is_key, head_gains[pl.ds(1, 1)], 1.0),
        jnp.where(is_key, cosine[...], 1.0),
        jnp.where(is_key, sine[...], 0.0),
    ).astype(BF)

    def kv_part(kind, which):
        return kv.at[kind, pl.ds(pl.multiple_of(which * tokens, tokens), tokens)]

    kv[core, pl.ds(pl.multiple_of(half * tokens, tokens), tokens)] = kv_here
    here = kv_part(core, half)
    to_x = remote(here, here, misc_send.at[8], misc_recv.at[8], (core, row ^ 1, col))
    to_s = remote(here, here, misc_send.at[9], misc_recv.at[9], (1 - core, row, col))
    to_x.start()
    to_s.start()
    push([get_o])
    begin(get_gu[0] + get_laurel + get_gu[1])
    came = kv_part(core, half ^ 1)
    remote(here, came, misc_send.at[8], misc_recv.at[8], (core, row, col)).wait_recv()
    on_s = remote(came, came, misc_send.at[10], misc_recv.at[10], (1 - core, row, col))
    on_s.start()
    other = kv_part(1 - core, half)
    remote(other, other, misc_send.at[9], misc_recv.at[9], (core, row, col)).wait_recv()
    other_came = kv_part(1 - core, half ^ 1)
    remote(other_came, other_came, misc_send.at[10], misc_recv.at[10], (core, row, col)).wait_recv()

    q_rows = 128
    key_token = lax.broadcasted_iota(jnp.int32, (1, 2 * tokens), 1)
    in_half = key_token % tokens
    key_place = in_half // own_tokens * chunk + key_token // tokens * own_tokens + in_half % own_tokens
    top[...] = jnp.full(top.shape, MASK_FILL, F32)

    def attend(step, carry):
        first = pl.multiple_of(step * q_rows, q_rows)
        rows = pl.ds(first, q_rows)
        token = first + lax.broadcasted_iota(jnp.int32, (q_rows, 1), 0)
        q_place = token // own_tokens * chunk + half * own_tokens + token % own_tokens
        allowed = (key_place <= q_place) & (key_place >= start[rows])
        scores = jnp.where(allowed, mm_nt(q_low[rows], kv[0]), MASK_FILL)
        row_top = jnp.max(scores, axis=1, keepdims=True)
        weights = jnp.exp(scores - row_top)
        total = jnp.sum(weights, axis=1, keepdims=True)
        probs = (weights * (1.0 / total)).astype(BF)
        o_low[rows] = mm(probs, kv[1]).astype(BF)
        lse[rows] = row_top + jnp.log(total)
        top[...] = jnp.maximum(top[...], jnp.max(row_top))
        return carry

    lax.fori_loop(0, tokens // q_rows, attend, 0)
    get_o.finish()

    away = pl.multiple_of((1 - core) * 4 * own_tokens, 4 * own_tokens)
    home = pl.multiple_of(core * 4 * own_tokens, 4 * own_tokens)
    scatter = Scatter(place, own_tokens, (give, keep, got, sent, left, right), sems(1))

    def project(source, weights, target, first):
        def step(index, carry):
            cols = pl.ds(pl.multiple_of(index * block, block), block)
            value = mm(source[pl.ds(first, 4 * own_tokens)], weights[:, cols])
            target[:, cols] = value.astype(target.dtype)
            return carry

        lax.fori_loop(0, width // block, step, 0)

    project(o_low, vo, give, away)
    scatter.start()
    project(o_low, vo, keep, home)
    scatter.run(
        attn_val,
        [lambda: (push(get_gu[0]), push(get_laurel)), lambda: begin(get_gu[2])],
    )
    push(get_gu[1])
    begin(get_gu[3])

    complete(get_laurel)
    laurel_here = laurels.at[core]
    laurel_share = remote(
        laurel_here, laurel_here, misc_send.at[22], misc_recv.at[22], (1 - core, row, col)
    )
    laurel_share.start()
    inputs, x_norm = own_norm()
    attn_normed = rms(attn_val[...])[0]
    laurel_there = laurels.at[1 - core]
    remote(
        laurel_there, laurel_there, misc_send.at[22], misc_recv.at[22], (core, row, col)
    ).wait_recv()
    lr_low[...] = mm_nt(xg[mine], laurels[0]).astype(BF)
    lo_normed = rms(mm(lr_low[...], laurels[1]))[0]
    h_two = (
        inputs + attn_normed * gains[pl.ds(1, 1)] + (x_norm + lo_normed * gains[pl.ds(2, 1)])
    ) * ROOT_HALF
    fg[mine] = (rms(h_two)[0] * gains[pl.ds(3, 1)]).astype(BF)
    gather_f = Gather(place, fg, own_tokens, sems(2))
    gather_f.start()
    gather_f.forward(
        [
            lambda: None,
            lambda: push(get_gu[2]),
            lambda: begin(get_d[:1]),
        ]
    )
    gather_f.finish()

    def unit_tile(index):
        complete(get_gu[index])
        cols = pl.ds(index * tile, tile)
        bent, slope = gelu_both(mm(fg[...], vg[:, cols]))
        up_part = mm(fg[...], vu[:, cols])
        gate[:, cols] = (up_part * slope).astype(BF)
        up[:, cols] = bent.astype(BF)
        hid[:, cols] = (bent * up_part).astype(BF)

    for index in range(tiles):
        if index == 1:
            push(get_gu[3])
        if index == 3:
            push(get_d[:1])
            begin(get_d[1:])
        unit_tile(index)
    turned[...] = hid[...].T
    scatter_ff = [
        Scatter(place, own_tokens, tuple(buf.at[part] for buf in halves2), sems(3 + part))
        for part in range(2)
    ]

    def project_half(part, target, first):
        def step(index, carry):
            cols = pl.ds(pl.multiple_of(index * block + part * half_block, half_block), half_block)
            here = pl.ds(pl.multiple_of(index * half_block, half_block), half_block)
            value = mm(hid[pl.ds(first, 4 * own_tokens)], vd[:, cols])
            target[:, here] = value.astype(target.dtype)
            return carry

        lax.fori_loop(0, width // block, step, 0)

    def down_half(part):
        complete(get_d[part : part + 1])
        project_half(part, give2.at[part], away)
        scatter_ff[part].start()
        project_half(part, keep2.at[part], home)

    def spread_half(part):
        for index in range(width // block):
            ff_val[:, pl.ds(index * block + part * half_block, half_block)] = half_sum[
                :, pl.ds(index * half_block, half_block)
            ]

    def late():
        push(get_d[1:])
        begin(get_per)
        for mask in (1, 2, 3):
            hand_grad(mask).start()

    down_half(0)
    scatter_ff[0].run(half_sum, [lambda: None, late])
    spread_half(0)
    down_half(1)
    keep_weights = [
        pltpu.make_async_copy(source, target, out_sems.at[lane])
        for lane, (source, target) in enumerate(
            [
                (vq, wq_all),
                (vkv, wkv_all),
                (vo, wo_all),
                (vg, wg_all),
                (vu, wu_all),
                (vd, wd_all),
                (xg, xg_all),
                (fg, fg_all),
                (gate, gate_all),
                (up, up_all),
            ]
        )
    ]
    for copy in keep_weights:
        copy.start()
    cut = ff_part // TURNED_PART
    get_turned = rows_of(
        turned.at[pl.ds(0, cut)], turned_all.at[pl.ds(0, cut)], by_cols, tokens
    )
    rest = pl.ds(cut, ff_part - cut)
    keep_rest = pltpu.make_async_copy(
        turned.at[rest],
        turned_all.at[rest, pl.ds(pl.multiple_of(row * tokens, tokens), tokens)],
        out_sems.at[10],
    )
    keep_rest.start()
    scatter_ff[1].run(half_sum, [lambda: (push(get_per), get_turned.start())])
    spread_half(1)
    complete(get_per)
    share = [
        remote(part, part, misc_send.at[lane], misc_recv.at[lane], (1 - core, row, col))
        for lane, part in per_parts(core, 16)
    ]
    for copy in share:
        copy.start()
    for lane, part in per_parts(1 - core, 16):
        remote(part, part, misc_send.at[lane], misc_recv.at[lane], (core, row, col)).wait_recv()
    for copy in share:
        copy.wait_send()
    get_turned.finish_first()
    keep_rest.wait()

    for mask in (1, 2, 3):
        hand_over(mask).wait_send()
        hand_gains(mask).wait_send()
        hand_grad(mask).wait_send()
        remote(
            g_in.at[row],
            g_own.at[:, pl.ds(pl.multiple_of((row ^ mask) * block, block), block)],
            misc_send.at[11 + mask],
            misc_recv.at[11 + mask],
            (core, row, col),
        ).wait_recv()
    gather_x.drain()
    scatter.drain()
    gather_f.drain()
    scatter_ff[0].drain()
    scatter_ff[1].drain()
    laurel_share.wait_send()
    pair.wait_send()
    to_x.wait_send()
    to_s.wait_send()
    on_s.wait_send()
    for copy in keep_weights:
        copy.wait()


def run_forward(x_in, g_in, gains_in, weights_in, lengths, head_gains):
    w_gate, laurel_left, per_gate, per_proj = (weights_in[i] for i in (4, 7, 9, 10))
    block = x_in.shape[2]
    own, width = x_in.shape[1], 4 * block
    tokens, head_dim, ff_part = 8 * own, head_gains.shape[1], w_gate.shape[1] // 2
    rank = laurel_left.shape[0]
    vm = pl.BlockSpec(memory_space=pltpu.VMEM)
    hbm = pl.BlockSpec(memory_space=pl.ANY)
    shape = jax.ShapeDtypeStruct
    weights = [
        (width, head_dim),
        (width, head_dim),
        (head_dim, width),
        (width, ff_part),
        (width, ff_part),
        (ff_part, width),
    ]
    acts = [
        (tokens, width),
        (tokens, width),
        (tokens, ff_part),
        (tokens, ff_part),
    ]
    outs = [
        shape((own, width), BF),
        shape((own, width), BF),
        shape((8, width), F32),
        shape((tokens, head_dim), F32),
        shape((tokens, head_dim), F32),
        shape((tokens, head_dim), BF),
        shape((2, 2 * tokens, head_dim), BF),
        shape((tokens, 1), F32),
        shape((8, 128), F32),
        shape((tokens, head_dim), BF),
        shape((own, width), F32),
        shape((own, rank), BF),
        shape((own, width), F32),
        shape((2, rank, width), BF),
        shape((width, per_gate.shape[1]), BF),
        shape((per_proj.shape[0], width), BF),
        shape((tokens, head_dim // 2), F32),
        shape((tokens, head_dim // 2), F32),
        shape((tokens, 1), jnp.int32),
    ] + [shape(size, BF) for size in weights + acts + [(ff_part, 4 * tokens)]]
    scatter_bufs = [
        pltpu.VMEM((4 * own, width), BF),
        pltpu.VMEM((4 * own, width), F32),
        pltpu.VMEM((4 * own, width), BF),
        pltpu.VMEM((4, own, width), BF),
        pltpu.VMEM((3, own, width), BF),
        pltpu.VMEM((3, own, width), BF),
    ]
    dma = pltpu.SemaphoreType.DMA
    return pl.pallas_call(
        forward_kernel,
        out_shape=outs,
        in_specs=[vm, vm, vm, hbm, vm, vm] + [hbm] * 4 + [vm] * 2
        + [hbm] * 2
        + [pl.BlockSpec(memory_space=pltpu.SMEM), vm],
        out_specs=[vm] * 19 + [hbm] * 11,
        scratch_shapes=[
            pltpu.VMEM((block, head_dim), BF),
            pltpu.VMEM((rank, block), BF),
            pltpu.VMEM((8, block), F32),
        ]
        + [pltpu.VMEM(size, BF) for size in weights + acts]
        + [pltpu.VMEM((tokens, ff_part), BF), pltpu.VMEM((ff_part, tokens), BF)]
        + scatter_bufs
        + [pltpu.VMEM((2,) + buf.shape[:-1] + (width // 2,), buf.dtype) for buf in scatter_bufs]
        + [pltpu.VMEM((own, width // 2), F32)]
        + [
            dma((18, 10)),
            dma((5, 8 * PIECES)),
            dma((5, 8 * PIECES)),
            dma((5, 4 * PIECES)),
            dma((5, 4 * PIECES)),
            dma((24,)),
            dma((24,)),
            dma((11,)),
        ],
        compiler_params=pltpu.CompilerParams(
            collective_id=0, has_side_effects=True, vmem_limit_bytes=VMEM_BYTES
        ),
        cost_estimate=pl.CostEstimate(flops=2 * 10**10, bytes_accessed=5 * 10**7, transcendentals=10**6),
    )(x_in, g_in, gains_in, *weights_in, lengths, head_gains)


class RowScatter:
    def __init__(self, place, halves, came, sems, stage=None):
        self.core, self.row, self.col = place
        self.halves, self.came, self.sems = halves, came, sems
        self.stage = stage

    def send(self, lane, index, half, mask):
        return remote(
            self.halves(index)[half],
            self.came.at[lane],
            self.sems.at[lane],
            self.sems.at[6 + lane],
            (self.core, self.row ^ mask, self.col),
        )

    def lane(self, lane):
        index, half, mask = ((1, 0, 1), (3, 0, 1), (2, 1, 2), (3, 1, 2), (2, 0, 2), (1, 1, 1))[lane]
        return self.send(lane, self.row ^ index, half, mask)

    def start(self, lanes=(1, 3, 0, 2)):
        for lane in lanes:
            self.lane(lane).start()

    def load(self, lane):
        slot = {0: 0, 1: 0, 4: 0, 2: 1, 3: 1, 5: 1}[lane]
        return slot, pltpu.make_async_copy(
            self.came.at[lane], self.stage[0].at[slot], self.stage[1].at[slot]
        )

    def fetch(self, *lanes):
        for lane in lanes:
            self.lane(lane).wait_recv()
            if self.stage is not None:
                self.load(lane)[1].start()

    def add(self, lane, index, half):
        if self.stage is None:
            value = self.came[lane]
        else:
            slot, copy = self.load(lane)
            copy.wait()
            value = self.stage[0][slot]
        part = self.halves(self.row ^ index)[half]
        part[...] = (part[...].astype(F32) + value.astype(F32)).astype(BF)

    def middle(self):
        for lane, out, index, half in ((1, 4, 2, 0), (3, 5, 1, 1)):
            self.add(lane, index, half)
            self.lane(out).start()

    def early(self):
        self.add(0, 0, 0)
        self.add(2, 0, 1)

    def finish(self):
        self.add(4, 0, 0)
        self.add(5, 0, 1)

    def drain(self):
        for lane in range(6):
            self.lane(lane).wait_send()


def head_back(grad, raw, gain, cosine, sine):
    factor = lax.rsqrt(jnp.mean(raw * raw, axis=1, keepdims=True) + EPSILON)
    half = raw.shape[1] // 2
    normed = raw * factor
    first, second = grad[:, :half], grad[:, half:]
    back = jnp.concatenate([first * cosine + second * sine, second * cosine - first * sine], axis=1)
    gain_grad = jnp.sum(back * normed, axis=0, keepdims=True)
    inner = back * gain
    return factor * (inner - normed * jnp.mean(inner * normed, axis=1, keepdims=True)), gain_grad


def backward_kernel(
    x_own,
    g_own,
    per_in,
    gains,
    head_gains,
    attn_val,
    lr_low,
    ff_val,
    raw_q,
    raw_kv,
    q_low,
    kv,
    lse,
    top,
    o_low,
    cosine,
    sine,
    start,
    laurels,
    vpg,
    vpp,
    xg_in,
    fg_in,
    gate_in,
    up_in,
    turned_in,
    wq_in,
    wkv_in,
    wo_in,
    wg_in,
    wu_in,
    wd_in,
    y_out,
    x_grad,
    g_gain,
    tops,
    small_a,
    gq,
    gkv,
    gout,
    ggate,
    gup,
    gdown,
    came_g,
    came_u,
    turned_far,
    turned_near,
    vq,
    vkv,
    vo,
    vg,
    vu,
    vd,
    fg,
    gate,
    up,
    dff_all,
    down_stage,
    dffg,
    dattng,
    dgate,
    dup,
    give,
    keep,
    got,
    sent,
    left,
    right,
    own_sum,
    h_two_ref,
    d_three_ref,
    low_ref,
    gpart,
    gcame,
    gpart2,
    gcame2,
    small_give,
    small_keep,
    small_got,
    small_row,
    small_z,
    d_o,
    d_kv,
    kv_give,
    kv_got,
    kv_x_got,
    kv_p_got,
    pkv,
    came_q,
    came_kv,
    came_o,
    stage_g,
    stage_sems,
    load_sems,
    row_sems,
    z_send,
    z_recv,
    s_send,
    s_recv,
    misc_send,
    misc_recv,
    gain_send,
    gain_recv,
    done_sems,
    ff_sems,
    down_sems,
    turned_sems,
    kv_sems,
):
    core, row, col = lax.axis_index("seq"), lax.axis_index("row"), lax.axis_index("col")
    place = (core, row, col)
    own_tokens, width = x_own.shape
    block = width // 4
    tokens, head_dim = raw_q.shape
    ff_part = gate.shape[1]
    chunk = 2 * own_tokens
    key_width = head_dim // 2
    half = row % 2
    rank = lr_low.shape[1]
    my_cols = pl.ds(pl.multiple_of(row * block, block), block)
    mine = pl.ds(pl.multiple_of((core * 4 + col) * own_tokens, own_tokens), own_tokens)
    away = pl.multiple_of((1 - core) * 4 * own_tokens, 4 * own_tokens)
    home = pl.multiple_of(core * 4 * own_tokens, 4 * own_tokens)

    barrier = pltpu.get_barrier_semaphore()
    for mask in (1, 2, 3):
        pl.semaphore_signal(barrier, inc=1, device_id=(core, row ^ mask, col), device_id_type=MESH)
        for other in (0, 1):
            pl.semaphore_signal(
                barrier, inc=1, device_id=(core ^ other, row, col ^ mask), device_id_type=MESH
            )
    pl.semaphore_signal(barrier, inc=1, device_id=(1 - core, row, col), device_id_type=MESH)
    loads = [
        pltpu.make_async_copy(source, target, load_sems.at[lane])
        for lane, (source, target) in enumerate(
            [
                (wd_in, vd),
                (gate_in, gate),
                (up_in, up),
                (wg_in, vg),
                (wu_in, vu),
                (fg_in, fg),
                (wo_in, vo),
                (wq_in, vq),
                (wkv_in, vkv),
            ]
        )
    ]
    for load in loads:
        load.start()
    pl.semaphore_wait(barrier, 10)
    cut = ff_part // TURNED_PART
    spans = ((0, cut), (cut, ff_part - cut))

    def turned_on(part, mask):
        begin, size = spans[part][0], spans[part][1] // 2
        rows = pl.ds(begin + (mask - 1) * size, size)
        first = pl.multiple_of((row ^ (3 - mask)) * tokens, tokens)
        if part == 0:
            source = turned_in.at[rows, pl.ds(first, tokens)]
        else:
            source = turned_near.at[2 - mask, pl.ds((mask - 1) * size, size)]
        lane = part * 2 + mask - 1
        return remote(
            source,
            turned_far.at[rows],
            row_sems.at[0, lane],
            row_sems.at[0, 6 + lane],
            (core, row ^ mask, col),
        )

    def turned_over(mask):
        return remote(
            turned_in.at[
                pl.ds(*spans[1]), pl.ds(pl.multiple_of(row * tokens, tokens), tokens)
            ],
            turned_near.at[mask - 1],
            row_sems.at[0, 3 + mask],
            row_sems.at[0, 9 + mask],
            (core, row ^ mask, col),
        )

    for mask in (1, 2):
        turned_on(0, mask).start()
        turned_over(mask).start()

    def turned_rest():
        for mask in (1, 2):
            turned_over(mask).wait_recv()
        for mask in (1, 2):
            turned_on(1, mask).start()


    def gain(index):
        return gains[pl.ds(index, 1)]

    inputs = x_own[...].astype(F32)
    x_norm = rms(inputs)[0] * gain(0)
    attn_normed = rms(attn_val[...])[0]
    lo_normed = rms(mm(lr_low[...], laurels[1]))[0]
    h_two = (inputs + attn_normed * gain(1) + (x_norm + lo_normed * gain(2))) * ROOT_HALF
    h_two_ref[...] = h_two
    ff_normed, ff_factor = rms(ff_val[...])
    h_three = h_two + ff_normed * gain(4)
    h_low = h_three.astype(BF)
    p_gate, p_proj = vpg[...], vpp[...]
    pg_gelu, pg_slope = gelu_both(mm(h_low, p_gate))
    per_input = per_in[row].astype(F32)
    gp_low = (pg_gelu * per_input).astype(BF)
    pp_normed, pp_factor = rms(mm(gp_low, p_proj))
    low_ref[...] = (h_three + pp_normed * gain(5)).astype(BF)

    def hand_back(source, target, mask, lane):
        return remote(
            source.at[:, pl.ds(pl.multiple_of((row ^ mask) * block, block), block)],
            target.at[row],
            misc_send.at[lane + mask],
            misc_recv.at[lane + mask],
            (core, row ^ mask, col),
        )

    def came_back(target, mask, lane):
        return remote(
            target.at[row ^ mask],
            target.at[row ^ mask],
            misc_send.at[lane + mask],
            misc_recv.at[lane + mask],
            (core, row, col),
        )

    for mask in (1, 2, 3):
        hand_back(low_ref, y_out, mask, 0).start()
    y_out[row] = low_ref[:, my_cols]

    grad_top = g_own[...].astype(F32)
    d_pp, gain_five = rms_back(grad_top, pp_normed, pp_factor, gain(5))
    d_pp_low = d_pp.astype(BF)
    d_pg_low = (mm_nt(d_pp_low, p_proj) * per_input * pg_slope).astype(BF)
    d_three = grad_top + mm_nt(d_pg_low, p_gate)
    d_three_ref[...] = d_three
    d_ff, gain_four = rms_back(d_three, ff_normed, ff_factor, gain(4))
    gpart[...] = jnp.zeros(gpart.shape, F32)
    gpart[pl.ds(5, 1)] = gain_five
    gpart[pl.ds(4, 1)] = gain_four
    dffg[mine] = d_ff.astype(BF)
    sems = lambda lane: (z_send.at[lane], z_recv.at[lane], s_send.at[lane], s_recv.at[lane])
    gather_ff = Gather(place, dffg, own_tokens, sems(0))
    gather_ff.start()

    def small(kind, first, value):
        rows = pl.ds(first, value.shape[0])
        value = value.astype(BF)

        @pl.when(core == kind)
        def _():
            small_keep[rows] = value

        @pl.when(core != kind)
        def _():
            small_give[rows] = value

    small(0, rank, mm_tn(gp_low, d_pp_low))
    small(1, rank, mm_tn(d_pg_low, h_low))
    gather_ff.forward([lambda: None, lambda: None, turned_rest])
    gather_ff.finish()

    part_rows = tokens // 2

    def ff_piece(group, which):
        return dff_all.at[
            pl.ds(pl.multiple_of(group * tokens + which * part_rows, part_rows), part_rows)
        ]

    def ff_over(mask):
        return remote(
            dffg.at[
                pl.ds(pl.multiple_of(core * part_rows, part_rows), part_rows),
                pl.ds(pl.multiple_of((row ^ mask) * block, block), block),
            ],
            ff_piece(row, core),
            ff_sems.at[mask],
            ff_sems.at[4 + mask],
            (core, row ^ mask, col),
        )

    def ff_came(mask):
        part = ff_piece(row ^ mask, core)
        return remote(part, part, ff_sems.at[mask], ff_sems.at[4 + mask], (core, row, col))

    def ff_share(mask, which):
        part = ff_piece(row ^ mask, which)
        return remote(
            part, part, ff_sems.at[8 + mask], ff_sems.at[12 + mask], (1 - core, row, col)
        )

    for mask in (1, 2, 3):
        ff_over(mask).start()
    dff_all[pl.ds(pl.multiple_of(row * tokens, tokens), tokens)] = dffg[:, my_cols]

    tile = 256
    for load in loads[:3]:
        load.wait()

    def units(index, carry):
        cols = pl.ds(pl.multiple_of(index * tile, tile), tile)
        d_hid = mm_nt(dffg[...], vd[cols])
        dgate[:, cols] = (d_hid * gate[:, cols].astype(F32)).astype(BF)
        dup[:, cols] = (d_hid * up[:, cols].astype(F32)).astype(BF)
        return carry

    lax.fori_loop(0, ff_part // tile, units, 0)
    for load in loads[3:5]:
        load.wait()

    def back_ff(target, first):
        rows = pl.ds(first, 4 * own_tokens)

        def step(index, carry):
            cols = pl.ds(pl.multiple_of(index * block, block), block)
            value = mm_nt(dgate[rows], vg[cols]) + mm_nt(dup[rows], vu[cols])
            target[:, cols] = value.astype(target.dtype)
            return carry

        lax.fori_loop(0, width // block, step, 0)

    scatter_f = Scatter(place, own_tokens, (give, keep, got, sent, left, right), sems(1))
    back_ff(give, away)
    scatter_f.start()
    back_ff(keep, home)

    put_g = RowScatter(place, by_rows(vg, block)[1], came_g, row_sems.at[1], (stage_g, stage_sems))
    put_u = RowScatter(place, by_rows(vu, block)[1], came_u, row_sems.at[2], (stage_g, stage_sems))

    def load_turned(lane):
        mask, part = ((0, None), (3, None), (1, 0), (1, 1), (2, 0), (2, 1))[lane]
        cols = pl.ds(pl.multiple_of((row ^ mask) * tokens, tokens), tokens)
        if part is None:
            source = turned_far if mask else turned_in.at[:, cols]
            target = vd.at[:, cols]
        else:
            rows = pl.ds(*spans[part])
            source = turned_near.at[mask - 1] if part else turned_in.at[rows, cols]
            target = vd.at[rows, cols]
        return pltpu.make_async_copy(source, target, turned_sems.at[lane])

    def down_ready():
        for mask in (1, 2):
            for part in range(2):
                turned_on(part, mask).wait_recv()
        for lane in range(6):
            load_turned(lane).start()
        for mask in (1, 2, 3):
            ff_came(mask).wait_recv()
            ff_share(mask, core).start()

    def down_tile(index):
        slot = index % 2
        rows = pl.ds(index * tile, tile)
        target = gdown.at[pl.ds(pl.multiple_of(core * ff_part + index * tile, tile), tile)]
        local = pltpu.make_async_copy(down_stage.at[slot], target, down_sems.at[index])
        over = remote(
            down_stage.at[slot],
            target,
            down_sems.at[4 + index],
            down_sems.at[8 + index],
            (1 - core, row, col),
        )
        return slot, rows, local, over

    def down_grad():
        for lane in range(6):
            load_turned(lane).wait()
        for mask in (1, 2, 3):
            ff_share(mask, 1 - core).wait_recv()
        for index in range(ff_part // tile):
            slot, rows, local, over = down_tile(index)
            if index >= 2:
                before = down_tile(index - 2)
                before[2].wait()
                before[3].wait_send()
            down_stage[slot] = mm(vd[rows], dff_all[...]).astype(BF)
            local.start()
            over.start()

    def gate_grad(target, grad, put):
        def step(index, carry):
            rows = pl.ds(pl.multiple_of(index * tile, tile), tile)
            target[rows] = mm_tn(fg[:, rows], grad[...]).astype(BF)
            return carry

        lax.fori_loop(0, width // tile, step, 0)

    def start_gate():
        loads[5].wait()
        gate_grad(vg, dgate, put_g)
        put_g.start()

    def start_up():
        gate_grad(vu, dup, put_u)
        put_u.start((1, 3))

    start_gate()
    scatter_f.run(own_sum, [start_up, down_ready])

    gather_ff.drain()
    f_normed, f_factor = rms(h_two_ref[...])
    d_f, gain_three = rms_back(own_sum[...], f_normed, f_factor, gain(3))
    d_half = (d_three_ref[...] + d_f) * ROOT_HALF
    d_three_ref[...] = d_half
    attn_normed, attn_factor = rms(attn_val[...])
    d_attn, gain_one = rms_back(d_half, attn_normed, attn_factor, gain(1))
    dattng[mine] = d_attn.astype(BF)
    gather_a = Gather(place, dattng, own_tokens, sems(2))
    gather_a.start()
    lo_normed, lo_factor = rms(mm(lr_low[...], laurels[1]))
    d_lo, gain_two = rms_back(d_half, lo_normed, lo_factor, gain(2))
    d_lo_low = d_lo.astype(BF)
    d_lr_low = mm_nt(d_lo_low, laurels[1]).astype(BF)
    small(0, 0, mm_tn(lr_low[...], d_lo_low))
    x_low = (rms(x_own[...].astype(F32))[0] * gain(0)).astype(BF)
    small(1, 0, mm_tn(d_lr_low, x_low))
    own_sum[...] = d_half + mm(d_lr_low, laurels[0])
    gpart[pl.ds(3, 1)] = gain_three
    gpart[pl.ds(2, 1)] = gain_two
    gpart[pl.ds(1, 1)] = gain_one
    small_swap = remote(
        small_give, small_got, misc_send.at[8], misc_recv.at[8], (1 - core, row, col)
    )
    small_swap.start()
    put_s = RowScatter(place, by_cols(small_keep, block)[1], small_row, row_sems.at[6])

    def small_sum():
        small_swap.wait_recv()
        small_keep[...] = (small_keep[...].astype(F32) + small_got[...].astype(F32)).astype(BF)

    def middle_gate():
        put_g.fetch(1, 3)
        down_grad()
        put_g.middle()

    def more_small():
        small_sum()
        put_g.fetch(0, 2)

    gather_a.forward([middle_gate, more_small, put_g.early])
    gather_a.finish()
    scatter_f.drain()

    loads[6].wait()
    d_o[...] = mm_nt(dattng[...], vo[...]).astype(BF)
    q_rows = 128
    key_token = lax.broadcasted_iota(jnp.int32, (1, 2 * tokens), 1)
    in_half = key_token % tokens
    key_place = in_half // own_tokens * chunk + key_token // tokens * own_tokens + in_half % own_tokens
    d_kv[...] = jnp.zeros(d_kv.shape, F32)

    def attend(step, carry):
        first = pl.multiple_of(step * q_rows, q_rows)
        rows = pl.ds(first, q_rows)
        token = first + lax.broadcasted_iota(jnp.int32, (q_rows, 1), 0)
        q_place = token // own_tokens * chunk + half * own_tokens + token % own_tokens
        allowed = (key_place <= q_place) & (key_place >= start[rows])
        scores = jnp.where(allowed, mm_nt(q_low[rows], kv[0]), MASK_FILL)
        probs = jnp.exp(scores - lse[rows])
        d_probs = mm_nt(d_o[rows], kv[1])
        delta = jnp.sum(probs * d_probs, axis=1, keepdims=True)
        d_scores = (probs * (d_probs - delta)).astype(BF)
        d_kv[0] += mm_tn(d_scores, q_low[rows])
        d_kv[1] += mm_tn(probs.astype(BF), d_o[rows])
        d_raw, gain_part = head_back(
            mm(d_scores, kv[0]), raw_q[rows], head_gains[pl.ds(0, 1)], cosine[rows], sine[rows]
        )
        d_o[rows] = d_raw.astype(BF)
        return carry + gain_part

    gain_q = lax.fori_loop(0, tokens // q_rows, attend, jnp.zeros((1, head_dim), F32))

    kv_give[...] = d_kv[1 - core].astype(BF)
    swap_kv = remote(kv_give, kv_got, misc_send.at[9], misc_recv.at[9], (1 - core, row, col))
    swap_kv.start()

    def out_grad():
        for part in range(2):
            wide = pl.ds(part * (width // 2), width // 2)
            vo[:, wide] = mm_tn(o_low[...], dattng[:, wide]).astype(BF)

    put_o = RowScatter(place, by_cols(vo, block)[1], came_o, row_sems.at[3])
    swap_kv.wait()
    kv_x = kv_give.at[pl.ds(0, tokens)]
    theirs = pl.ds(pl.multiple_of((half ^ 1) * tokens, tokens), tokens)
    ours = pl.ds(pl.multiple_of(half * tokens, tokens), tokens)
    kv_x[...] = (d_kv[core, theirs] + kv_got[theirs].astype(F32)).astype(BF)
    kv_half = tokens // 2

    def over_x(piece):
        rows = pl.ds(piece * kv_half, kv_half)
        return remote(
            kv_x.at[rows],
            kv_x_got.at[rows],
            kv_sems.at[piece],
            kv_sems.at[2 + piece],
            (core, row ^ 1, col),
        )

    def over_p(piece):
        rows = pl.ds(piece * kv_half, kv_half)
        return remote(
            kv_p.at[rows],
            kv_p_got.at[rows],
            kv_sems.at[4 + piece],
            kv_sems.at[6 + piece],
            (core, row, col ^ 1),
        )

    for piece in range(2):
        over_x(piece).start()
    put_u.start((0, 2))
    load_x = pltpu.make_async_copy(xg_in, dffg, load_sems.at[10])
    for mask in (1, 2, 3):
        ff_over(mask).wait_send()
    load_x.start()
    put_u.fetch(1, 3)
    out_grad()
    put_u.middle()
    put_s.start()
    put_o.start()
    loads[7].wait()
    loads[8].wait()
    kv_p = kv_got.at[pl.ds(0, tokens)]
    d_kind = d_kv[core, ours] + kv_got[ours].astype(F32)
    for piece in range(2):
        rows = pl.ds(piece * kv_half, kv_half)
        over_x(piece).wait_recv()
        part = d_kind[piece * kv_half : (piece + 1) * kv_half] + kv_x_got[rows].astype(F32)
        kv_p[rows] = part.astype(BF)
        over_p(piece).start()
    for piece in range(2):
        over_p(piece).wait()
    d_kind = kv_p[...].astype(F32) + kv_p_got[...].astype(F32)
    is_key = core == 0
    d_kind_raw, gain_k = head_back(
        d_kind,
        raw_kv[...],
        jnp.where(is_key, head_gains[pl.ds(1, 1)], 1.0),
        jnp.where(is_key, cosine[...], 1.0),
        jnp.where(is_key, sine[...], 0.0),
    )
    for part in range(4):
        gpart[pl.ds(6, 1), pl.ds(part * block, head_dim)] = gain_q
        gpart[pl.ds(6, 1), pl.ds(part * block + head_dim, head_dim)] = gain_k * jnp.where(
            is_key, 0.5, 0.0
        )
    kv_p[...] = d_kind_raw.astype(BF)
    pair_cols = pl.ds(pl.multiple_of(col % 2 * key_width, key_width), key_width)

    def back_heads(target, first):
        rows = pl.ds(first, 4 * own_tokens)

        def step(index, carry):
            cols = pl.ds(pl.multiple_of(index * block, block), block)
            value = mm_nt(d_o[rows], vq[cols]) + mm_nt(kv_p[rows, pair_cols], vkv[cols, pair_cols])
            target[:, cols] = value.astype(target.dtype)
            return carry

        lax.fori_loop(0, width // block, step, 0)

    scatter_x = Scatter(place, own_tokens, (give, keep, got, sent, left, right), sems(3))
    back_heads(give, away)
    scatter_x.start()
    back_heads(keep, home)
    put_q = RowScatter(place, by_rows(vq, block)[1], came_q, row_sems.at[4])
    put_kv = RowScatter(place, by_rows(pkv, block)[1], came_kv, row_sems.at[5])

    def query_grad():
        load_x.wait()

        def step(index, carry):
            rows = pl.ds(pl.multiple_of(index * tile, tile), tile)
            vq[rows] = mm_tn(dffg[:, rows], d_o[...]).astype(BF)
            pkv[rows] = mm_tn(dffg[:, rows], kv_p[:, pair_cols]).astype(BF)
            return carry

        lax.fori_loop(0, width // tile, step, 0)
        put_q.start()
        put_kv.start()

    def deliver(lane, source, target):
        local = pltpu.make_async_copy(source, target, done_sems.at[lane])
        over = remote(
            source, target, done_sems.at[8 + lane], done_sems.at[16 + lane], (1 - core, row, col)
        )
        local.start()
        over.start()
        done.append((local, over))

    core_ff = pl.ds(pl.multiple_of(core * ff_part, ff_part), ff_part)
    core_head = pl.ds(pl.multiple_of(core * head_dim, head_dim), head_dim)
    sib_ff = pl.ds(pl.multiple_of((1 - core) * ff_part, ff_part), ff_part)
    sib_head = pl.ds(pl.multiple_of((1 - core) * head_dim, head_dim), head_dim)
    row_block = pl.ds(pl.multiple_of(row * block, block), block)
    done = []

    quarter = block // 4

    def small_quarter(mask):
        return remote(
            small_keep.at[
                :, pl.ds(pl.multiple_of(row * block + (col ^ mask) * quarter, quarter), quarter)
            ],
            small_z.at[mask],
            misc_send.at[11 + mask],
            misc_recv.at[11 + mask],
            (core, row, col ^ mask),
        )

    def gate_finish():
        put_g.fetch(4, 5)
        put_g.finish()
        deliver(1, vg.at[row_block], ggate.at[:, core_ff])
        put_u.fetch(0, 2)
        put_u.early()

    d_half_here = d_three_ref
    scatter_x.run(h_two_ref, [query_grad, gate_finish])
    d_xn = own_sum[...] + h_two_ref[...]
    x_normed, x_factor = rms(x_own[...].astype(F32))
    d_in, gain_zero = rms_back(d_xn, x_normed, x_factor, gain(0))
    gpart[pl.ds(0, 1)] = gain_zero
    for mask in (1, 2, 3):
        hand_back(low_ref, y_out, mask, 0).wait_send()
    low_ref[...] = (d_half_here[...] + d_in).astype(BF)
    for mask in (1, 2, 3):
        hand_back(low_ref, x_grad, mask, 4).start()
    x_grad[row] = low_ref[:, my_cols]

    gpart[pl.ds(8, 8)] = jnp.full((8, width), jnp.max(top[...]), F32)

    def gain_row(mask):
        return remote(
            gpart.at[:, pl.ds(pl.multiple_of((row ^ mask) * block, block), block)],
            gcame.at[mask],
            gain_send.at[mask],
            gain_recv.at[mask],
            (core, row ^ mask, col),
        )

    for mask in (1, 2, 3):
        gain_row(mask).start()
    gcame[0] = gpart[:, my_cols]
    for put in (put_s, put_o, put_q, put_kv):
        put.fetch(1, 3)
        put.middle()
    for mask in (1, 2, 3):
        gain_row(mask).wait_recv()
    summed = gcame[0] + gcame[1] + gcame[2] + gcame[3]
    largest = jnp.maximum(jnp.maximum(gcame[0], gcame[1]), jnp.maximum(gcame[2], gcame[3]))
    gpart2[pl.ds(0, 8)] = summed[:8]
    gpart2[pl.ds(8, 8)] = largest[8:]
    me = core * 4 + col
    members = [(other, mask) for other in (0, 1) for mask in range(4) if other or mask]

    def gain_group(other, mask):
        lane = 4 + other * 4 + mask
        return remote(
            gpart2,
            gcame2.at[me],
            gain_send.at[lane],
            gain_recv.at[lane],
            (core ^ other, row, col ^ mask),
        )

    for other, mask in members:
        gain_group(other, mask).start()
    gcame2[me] = gpart2[...]
    put_s.fetch(0, 2, 4, 5)
    put_s.early()
    put_s.finish()
    for mask in (1, 2, 3):
        small_quarter(mask).start()
    put_u.fetch(4, 5)
    put_u.finish()
    deliver(2, vu.at[row_block], gup.at[:, core_ff])

    def small_share(other, mask):
        lane = 16 + other * 4 + mask
        return remote(
            kv_x.at[pl.ds(0, small_keep.shape[0]), pl.ds(0, quarter)],
            small_a.at[core, col],
            misc_send.at[lane],
            misc_recv.at[lane],
            (core ^ other, row, col ^ mask),
        )

    for mask in (1, 2, 3):
        small_quarter(mask).wait_recv()
    small_total = small_keep[
        :, pl.ds(pl.multiple_of(row * block + col * quarter, quarter), quarter)
    ].astype(F32)
    for mask in (1, 2, 3):
        small_total = small_total + small_z[mask].astype(F32)
    for piece in range(2):
        over_x(piece).wait_send()
    kv_x[pl.ds(0, small_keep.shape[0]), pl.ds(0, quarter)] = small_total.astype(BF)
    for other, mask in members:
        small_share(other, mask).start()
    small_a[core, col] = small_total.astype(BF)
    for put, lane, source, target in (
        (put_o, 4, vo.at[:, row_block], gout.at[core_head]),
        (put_kv, 3, pkv.at[row_block], gkv.at[core]),
        (put_q, 5, vq.at[row_block], gq.at[:, core_head]),
    ):
        put.fetch(0, 2, 4, 5)
        put.early()
        put.finish()
        deliver(lane, source, target)

    for other, mask in members:
        who = (core ^ other) * 4 + (col ^ mask)
        lane = 4 + other * 4 + mask
        remote(
            gpart2, gcame2.at[who], gain_send.at[lane], gain_recv.at[lane], (core, row, col)
        ).wait_recv()
    total = gcame2[0]
    for who in range(1, 8):
        total = total + gcame2[who]
    g_gain[...] = total[:8]
    for who in range(8):
        head = 2 * (who % 4) + who // 4
        tops[pl.ds(head, 1)] = gcame2[who, pl.ds(8, 1), pl.ds(0, 128)]

    gather_a.drain()
    scatter_x.drain()
    for other, mask in members:
        part = small_a.at[core ^ other, col ^ mask]
        lane = 16 + other * 4 + mask
        remote(part, part, misc_send.at[lane], misc_recv.at[lane], (core, row, col)).wait_recv()
        small_share(other, mask).wait_send()
        gain_group(other, mask).wait_send()
    for mask in (1, 2, 3):
        came_back(y_out, mask, 0).wait_recv()
        came_back(x_grad, mask, 4).wait_recv()
        hand_back(low_ref, x_grad, mask, 4).wait_send()
        gain_row(mask).wait_send()
        small_quarter(mask).wait_send()
    small_swap.wait_send()
    for put in (put_g, put_u, put_o, put_q, put_kv, put_s):
        put.drain()
    for mask in (1, 2):
        turned_over(mask).wait_send()
        for part in range(2):
            turned_on(part, mask).wait_send()
    for mask in (1, 2, 3):
        ff_share(mask, core).wait_send()
    for index in range(ff_part // tile):
        slot, rows, local, over = down_tile(index)
        if index >= 2:
            local.wait()
            over.wait_send()
        target = gdown.at[pl.ds(pl.multiple_of((1 - core) * ff_part + index * tile, tile), tile)]
        remote(
            target, target, down_sems.at[4 + index], down_sems.at[8 + index], (core, row, col)
        ).wait_recv()
    theirs_at = {
        1: ggate.at[:, sib_ff],
        2: gup.at[:, sib_ff],
        3: gkv.at[1 - core],
        4: gout.at[sib_head],
        5: gq.at[:, sib_head],
    }
    for lane, (local, over) in zip((1, 2, 4, 3, 5), done):
        local.wait()
        over.wait_send()
        target = theirs_at[lane]
        remote(
            target, target, done_sems.at[8 + lane], done_sems.at[16 + lane], (core, row, col)
        ).wait_recv()


def run_backward(small_args, big_args):
    x_own, per_in, head_gains = small_args[0], small_args[2], small_args[4]
    own, width = x_own.shape
    block = width // 4
    gate = big_args[2]
    tokens, ff_part = gate.shape
    head_dim = head_gains.shape[1]
    rank = small_args[6].shape[1]
    small_rows = small_args[18].shape[1] + small_args[20].shape[0]
    vm = pl.BlockSpec(memory_space=pltpu.VMEM)
    hbm = pl.BlockSpec(memory_space=pl.ANY)
    shape = jax.ShapeDtypeStruct
    vmem = pltpu.VMEM
    dma = pltpu.SemaphoreType.DMA
    outs = [
        shape((4, own, block), BF),
        shape((4, own, block), BF),
        shape((8, block), F32),
        shape((8, 128), F32),
        shape((2, 4, small_rows, block // 4), BF),
        shape((block, 2 * head_dim), BF),
        shape((2, block, head_dim // 2), BF),
        shape((2 * head_dim, block), BF),
        shape((block, 2 * ff_part), BF),
        shape((block, 2 * ff_part), BF),
        shape((2 * ff_part, block), BF),
        shape((6, block // 2, ff_part), BF),
        shape((6, block // 2, ff_part), BF),
        shape((ff_part, tokens), BF),
        shape((2, ff_part - ff_part // TURNED_PART, tokens), BF),
    ]
    scratch = [
        vmem((width, head_dim), BF),
        vmem((width, head_dim), BF),
        vmem((head_dim, width), BF),
        vmem((width, ff_part), BF),
        vmem((width, ff_part), BF),
        vmem((ff_part, width), BF),
        vmem((tokens, width), BF),
        vmem((tokens, ff_part), BF),
        vmem((tokens, ff_part), BF),
        vmem((4 * tokens, block), BF),
        vmem((2, 256, block), BF),
        vmem((tokens, width), BF),
        vmem((tokens, width), BF),
        vmem((tokens, ff_part), BF),
        vmem((tokens, ff_part), BF),
        vmem((4 * own, width), BF),
        vmem((4 * own, width), F32),
        vmem((4 * own, width), BF),
        vmem((4, own, width), BF),
        vmem((3, own, width), BF),
        vmem((3, own, width), BF),
        vmem((own, width), F32),
        vmem((own, width), F32),
        vmem((own, width), F32),
        vmem((own, width), BF),
        vmem((16, width), F32),
        vmem((4, 16, block), F32),
        vmem((16, block), F32),
        vmem((8, 16, block), F32),
        vmem((small_rows, width), BF),
        vmem((small_rows, width), BF),
        vmem((small_rows, width), BF),
        vmem((6, small_rows // 2, block), BF),
        vmem((4, small_rows, block // 4), BF),
        vmem((tokens, head_dim), BF),
        vmem((2, 2 * tokens, head_dim), F32),
        vmem((2 * tokens, head_dim), BF),
        vmem((2 * tokens, head_dim), BF),
        vmem((tokens, head_dim), BF),
        vmem((tokens, head_dim), BF),
        vmem((width, head_dim // 2), BF),
        vmem((6, block // 2, head_dim), BF),
        vmem((6, block // 2, head_dim // 2), BF),
        vmem((6, head_dim // 2, block), BF),
        vmem((2, block // 2, ff_part), BF),
        dma((2,)),
        dma((11,)),
        dma((7, 12)),
        dma((4, 8 * PIECES)),
        dma((4, 8 * PIECES)),
        dma((4, 4 * PIECES)),
        dma((4, 4 * PIECES)),
        dma((24,)),
        dma((24,)),
        dma((12,)),
        dma((12,)),
        dma((24,)),
        dma((16,)),
        dma((12,)),
        dma((6,)),
        dma((8,)),
    ]
    return pl.pallas_call(
        backward_kernel,
        out_shape=outs,
        in_specs=[vm] * 21 + [hbm] * 11,
        out_specs=[vm] * 5 + [hbm] * 10,
        scratch_shapes=scratch,
        compiler_params=pltpu.CompilerParams(
            collective_id=1, has_side_effects=True, vmem_limit_bytes=VMEM_BYTES
        ),
        cost_estimate=pl.CostEstimate(
            flops=4 * 10**10, bytes_accessed=10**8, transcendentals=2 * 10**6
        ),
    )(*small_args, *big_args)


def finish_kernel(
    y_in,
    x_in,
    gains,
    tops,
    small,
    gq,
    gkv,
    gout,
    ggate,
    gup,
    gdown,
    head_gains,
    y_out,
    x_out,
    o_query,
    o_key,
    o_value,
    o_out,
    o_gate,
    o_up,
    o_down,
    o_left,
    o_right,
    o_per_gate,
    o_per_proj,
    o_gains,
    o_head,
    o_clip,
):
    o_query[...] = gq[...].astype(F32)
    o_key[...] = gkv[0].astype(F32)
    o_value[...] = gkv[1].astype(F32)
    o_out[...] = gout[...].astype(F32)
    o_gate[...] = ggate[...].astype(F32)
    o_up[...] = gup[...].astype(F32)
    o_down[...] = gdown[...].astype(F32)
    head_dim = head_gains.shape[1]
    quarter = small.shape[3]
    rank = o_right.shape[0]

    @pl.when(pl.program_id(0) == 0)
    def _():
        own = y_in.shape[1]
        for part in range(4):
            rows = pl.ds(part % 2 * own, own)
            y_out[part // 2, rows] = y_in[part]
            x_out[part // 2, rows] = x_in[part]

    @pl.when(pl.program_id(0) == 1)
    def _():
        for part in range(4):
            cols = pl.ds(part * quarter, quarter)
            first = small[0, part].astype(F32)
            o_right[:, cols] = first[:rank]
            o_per_proj[:, cols] = first[rank:]
            second = small[1, part].astype(F32)
            o_left[:, cols] = second[:rank]
            o_per_gate[cols] = second[rank:].T

    @pl.when(pl.program_id(0) == 1)
    def _():
        o_gains[...] = gains[pl.ds(0, 6)]
        o_head[pl.ds(0, 1)] = gains[pl.ds(6, 1), pl.ds(0, head_dim)]
        o_head[pl.ds(1, 1)] = gains[pl.ds(6, 1), pl.ds(head_dim, head_dim)]
        factor = jnp.sqrt(CLIP_LEVEL / jnp.maximum(tops[...], CLIP_LEVEL))[:, :1]
        o_clip[0] = factor * head_gains[pl.ds(0, 1)]
        o_clip[1] = factor * head_gains[pl.ds(1, 1)]


def run_finish(results, head_gains, rank):
    y_out, x_grad, g_gain, tops, small, gq, gkv, gout, ggate, gup, gdown = results
    steps = 2
    shape = jax.ShapeDtypeStruct

    def whole(array):
        dims = len(array.shape)
        return pl.BlockSpec(array.shape, lambda step: (0,) * dims)

    def rows(array):
        size = (array.shape[0] // steps, array.shape[1])
        return pl.BlockSpec(size, lambda step: (step, 0))

    own, block = y_out.shape[1:]
    key_width = gkv.shape[2]
    proj = small.shape[2] - rank
    tokens_shape = shape((2, 2 * own, block), BF)
    by_rows_out = [
        shape(gq.shape, F32),
        shape(gkv.shape[1:], F32),
        shape(gkv.shape[1:], F32),
        shape(gout.shape, F32),
        shape(ggate.shape, F32),
        shape(gup.shape, F32),
        shape(gdown.shape, F32),
    ]
    whole_out = [
        shape((rank, block), F32),
        shape((rank, block), F32),
        shape((block, proj), F32),
        shape((proj, block), F32),
        shape((6, block), F32),
        shape(head_gains.shape, F32),
        shape((2, tops.shape[0], head_gains.shape[1]), F32),
    ]
    kv_spec = pl.BlockSpec((2, block // steps, key_width), lambda step: (0, step, 0))
    return pl.pallas_call(
        finish_kernel,
        grid=(steps,),
        out_shape=[tokens_shape, tokens_shape] + by_rows_out + whole_out,
        in_specs=[whole(y_out), whole(x_grad), whole(g_gain), whole(tops), whole(small), rows(gq), kv_spec]
        + [rows(array) for array in (gout, ggate, gup, gdown)]
        + [whole(head_gains)],
        out_specs=[whole(tokens_shape)] * 2
        + [rows(array) for array in by_rows_out]
        + [whole(array) for array in whole_out],
        compiler_params=pltpu.CompilerParams(vmem_limit_bytes=VMEM_BYTES),
        cost_estimate=pl.CostEstimate(flops=10**7, bytes_accessed=3 * 10**7, transcendentals=0),
    )(*results, head_gains)


def body_pair(
    layer_in,
    per_layer_in,
    doc_lengths,
    w_query,
    w_key,
    w_value,
    w_out,
    w_gate,
    w_up,
    w_down,
    laurel_left,
    laurel_right,
    per_gate,
    per_proj,
    norm_gains,
    head_gains,
    out_grad,
):
    core, row, col = lax.axis_index("seq"), lax.axis_index("row"), lax.axis_index("col")
    rows, cols, cores = lax.axis_size("row"), lax.axis_size("col"), lax.axis_size("seq")
    seq_count = layer_in.shape[0]
    head_dim = head_gains.shape[1]
    key_width = w_key.shape[1]
    ff_part = w_gate.shape[1] // cores
    chunk = layer_in.shape[1]
    halves = rows // seq_count
    own_tokens = chunk // halves
    group_tokens = own_tokens * cores * cols
    even_col = col % 2 == 0

    rank = laurel_left.shape[1]
    saved = run_forward(
        layer_in.reshape(rows, own_tokens, -1),
        out_grad.reshape(rows, own_tokens, -1),
        norm_gains,
        (
            w_query,
            w_key,
            w_value,
            w_out,
            w_gate,
            w_up,
            w_down,
            laurel_left.T,
            laurel_right,
            per_gate,
            per_proj,
        ),
        doc_lengths,
        head_gains,
    )
    (x_own, g_own, gains, raw_q, raw_kv, q_low, kv, lse, top_tile, o_low, attn_val, lr_low, ff_val) = saved[
        :13
    ]
    laurels, p_gate, p_proj, cosine, sine, start = saved[13:19]
    w_q, w_kv_all, w_o, w_g, w_u, w_d, x_all, f_all, gate_val, up_val, turned = saved[19:]
    results = run_backward(
        (
            x_own,
            g_own,
            per_layer_in.reshape(rows, own_tokens, -1),
            gains,
            head_gains,
            attn_val,
            lr_low,
            ff_val,
            raw_q,
            raw_kv,
            q_low,
            kv,
            lse,
            top_tile,
            o_low,
            cosine,
            sine,
            start,
            laurels,
            p_gate,
            p_proj,
        ),
        (x_all, f_all, gate_val, up_val, turned, w_q, w_kv_all, w_o, w_g, w_u, w_d),
    )
    finished = list(run_finish(results[:11], head_gains, rank))
    finished[9] = finished[9].T
    return tuple(finished)


def solution(mesh):
    sizes = tuple(mesh.shape[axis] for axis in ("seq", "row", "col"))
    body = body_pair if sizes == (2, 4, 4) else body_any
    return jax.shard_map(
        body,
        mesh=mesh,
        in_specs=(
            P(None, ("seq", "col"), "row"),
            P(None, ("seq", "col"), None),
            P(),
            P("row", "col"),
            P("row", "col"),
            P("row", "col"),
            P("col", "row"),
            P("row", "col"),
            P("row", "col"),
            P("col", "row"),
            P("row", None),
            P(None, "row"),
            P("row", None),
            P(None, "row"),
            P(None, "row"),
            P(),
            P(None, ("seq", "col"), "row"),
        ),
        out_specs=(
            P(None, ("seq", "col"), "row"),
            P(None, ("seq", "col"), "row"),
            P("row", "col"),
            P("row", "col"),
            P("row", "col"),
            P("col", "row"),
            P("row", "col"),
            P("row", "col"),
            P("col", "row"),
            P("row", None),
            P(None, "row"),
            P("row", None),
            P(None, "row"),
            P(None, "row"),
            P(),
            P(),
        ),
        check_vma=False,
    )
```
